32 devices in a mesh: gx: 4 (over y, x), gy: 8 (over z, core).
Axes of the slice: x: 2, y: 2, z: 4, core: 2. Of those that a mesh axis runs over, the one named last changes fastest.
Arguments:
- adjoint_vel: float32 [128, 2, 62, 32, 128], P(('gx', 'gy')), may hold values from -6 to 6
- velocity: bfloat16 [128, 2, 62, 32, 128], P(('gx', 'gy')), may hold values from -6 to 6
- drag_coef: float32 [128, 32, 128], P(('gx', 'gy')), may hold values from 0.3 to 3
- level_count: int32 [128, 32, 128], P(('gx', 'gy')), may hold values from 1 to 62
- block_ids: int32 [128], P(('gx', 'gy')), may hold values from 0 to 64, as said below
- bathymetry: float32 [256, 1024], P('gy', 'gx'), may hold values from 0.25 to 1
- land_mask: int32 [256, 1024], P('gy', 'gx'), may hold values 0 or 1
Outputs:
- corrected_adjoint: float32 [128, 2, 62, 32, 128], P(('gx', 'gy'))
- drag_gradient: float32 [128, 32, 128], P(('gx', 'gy'))
- surface_height: float32 [256, 1024], P('gy', 'gx')
- bathy_sensitivity: float32 [256, 1024], P('gy', 'gx')
The draws below stay inside these ranges and needn't reach their ends.
Inputs may be any that keep to these rules, and one draw needn't show every extreme that they name: `block_ids`: each device's 4 entries name the blocks it holds, then 64 in unused slots; each block number below 64 appears exactly once over all devices; each device holds 1 to 4 blocks, and some device holds 4.
All inputs are finite; a program needn't handle non-finite values. No bound on the sum of `land_mask` on one device may be relied on, other than what follows from the above.
Results may differ from the reference program's by a relative error of at most 0.0003.
Values sent between devices are 32-bit elements; how exact they have to be, the bound alone decides.
No kernel may reach another device: no remote copies, remote signals or barrier semaphores. Data moves between devices by JAX's collectives and lax.ppermute only.
A program may use at most 128 MiB of HBM per device.

```python
import math
import jax
import jax.numpy as jnp
from jax import lax

LEV = 62
BY = 32
BX = 128
SLOTS = 4
STEPS = 32
NBLK = 64
NY = 256
NX = 1024
N_GX = 4
N_GY = 8
DEVICES = 32


def draw_block_ids(key, part):
    device_total = NBLK // 2
    first_key, second_key = jax.random.split(jax.random.fold_in(key, 7))
    pattern = jnp.array([4, 1, 1, 2], jnp.int32)
    ranking = jax.random.permutation(first_key, device_total).astype(jnp.int32)
    counts = pattern[ranking % 4]
    starts = jnp.cumsum(counts) - counts
    ordering = jax.random.permutation(second_key, NBLK).astype(jnp.int32)
    slot_index = jnp.arange(SLOTS, dtype=jnp.int32)
    position = jnp.minimum(starts[:, None] + slot_index[None, :], NBLK - 1)
    listed = jnp.where(slot_index[None, :] < counts[:, None], ordering[position], NBLK)
    return listed.reshape(-1).astype(jnp.int32)


def draw_adjoint_vel(key, part):
    noise_key, offset_key = jax.random.split(jax.random.fold_in(key, 11))
    slot_total = NBLK // 2 * SLOTS
    full_shape = (slot_total, 2, LEV, BY, BX)
    noise = jax.random.normal(noise_key, full_shape, jnp.float32)
    offset = jax.random.uniform(offset_key, (slot_total, 1, 1, 1, 1), jnp.float32, 0.003, 0.012)
    return jnp.clip(noise + offset, -6.0, 6.0).astype(jnp.float32)


def plant(values, stream_key, low, top_value):
    dims = values.shape
    place = [jax.random.randint(jax.random.fold_in(stream_key, axis), (), 0, dims[axis]) for axis in range(len(dims))]
    values = values.at[tuple(place)].set(low)
    longest = dims.index(max(dims))
    place[longest] = (place[longest] + 1) % dims[longest]
    return values.at[tuple(place)].set(top_value)


def shard_levels(own_key, shape, cuts, smallest, largest):
    def one(axis_at, shards_of):
        heights = jax.random.uniform(jax.random.fold_in(jax.random.fold_in(own_key, 6), axis_at), (shards_of,), jnp.float32, smallest / len(cuts), largest / len(cuts))
        return jnp.repeat(jnp.exp(heights), shape[axis_at] // shards_of).reshape((-1,) + (1,) * (len(shape) - axis_at - 1))

    factor_of = one(*cuts[0])
    for cut in cuts[1:]:
        factor_of = factor_of * one(*cut)
    return factor_of


def centred(own_key, extent, width, limit, pieces=(), held_as=jnp.bfloat16):
    values = jax.random.normal(own_key, extent, jnp.float32) * width
    if len(pieces) > 0:
        values = shard_levels(own_key, extent, pieces, -0.22, 0.18) * values
    return jnp.clip(values, min=-limit, max=limit).astype(held_as)


def setup_inputs(seed: int = 0) -> dict:
    seeds = jax.random.split(jax.random.key(seed), 8)
    adjoint_vel = draw_adjoint_vel(jax.random.fold_in(seeds[7], 71), 0)
    velocity = centred(seeds[1], (DEVICES * SLOTS, 2, LEV, BY, BX), 1.0, 6.0, ((0, 32),))
    drag_coef = jnp.clip(jnp.exp(math.log(3.0) - 2.3025851 * jax.random.uniform(seeds[2], (DEVICES * SLOTS, BY, BX), jnp.float32) ** shard_levels(seeds[2], (DEVICES * SLOTS, BY, BX), ((0, 32),), -0.2, 0.2)), 0.3, 3.0)
    level_count = plant(jax.random.randint(seeds[3], (DEVICES * SLOTS, BY, BX), 1, LEV + 1), jax.random.fold_in(seeds[3], 1), 1, LEV).astype(jnp.int32)
    block_ids = draw_block_ids(jax.random.fold_in(seeds[7], 71), 0)
    bathymetry = jnp.clip(jnp.exp(math.log(1.0) - 1.3862944 * jax.random.uniform(seeds[5], (NY, NX), jnp.float32) ** shard_levels(seeds[5], (NY, NX), ((0, 8), (1, 4)), -0.2, 0.2)), 0.25, 1.0)
    land_mask = plant((jax.random.randint(seeds[6], (NY, NX), 0, 8) < 7).astype(jnp.int32), jax.random.fold_in(seeds[6], 1), 0, 1)
    return {"adjoint_vel": adjoint_vel, "velocity": velocity, "drag_coef": drag_coef, "level_count": level_count, "block_ids": block_ids, "bathymetry": bathymetry, "land_mask": land_mask}


mix_rate = 0.25
mix_sweeps = 2
drag_step = 0.5
force_scale = 0.25
pressure_gain = 0.5
surface_shift = 1.0 / 64.0
speed_floor = 0.01

def chebyshev_table(total_steps):
    lowest = surface_shift
    highest = surface_shift + 8.0
    centre = 0.5 * (highest + lowest)
    radius = 0.5 * (highest - lowest)
    sigma_ratio = centre / radius
    ratio_prev = 1.0 / sigma_ratio
    table = []
    for _ in range(total_steps):
        ratio_next = 1.0 / (2.0 * sigma_ratio - ratio_prev)
        table.append((ratio_next * ratio_prev, 2.0 * ratio_next / radius))
        ratio_prev = ratio_next
    return (centre, table)

def column_block(adjoint, velocity, drag, levels):
    depth_index = lax.broadcasted_iota(jnp.int32, adjoint.shape[1:], 0)
    wetness = (depth_index < levels[None]).astype(jnp.float32)
    forcing = force_scale * lax.optimization_barrier(jnp.sum(wetness[None] * adjoint, axis=(0, 1)))
    column_field = adjoint * wetness[None]
    wet_below = wetness[None, 1:]
    for _ in range(mix_sweeps):
        level_flux = mix_rate * (column_field[:, 1:] - column_field[:, :-1]) * wet_below
        zeros_row = jnp.zeros_like(column_field[:, :1])
        column_field = column_field + jnp.concatenate([level_flux, zeros_row], axis=1) - jnp.concatenate([zeros_row, level_flux], axis=1)
    bottom = (depth_index == levels[None] - 1).astype(jnp.float32)
    flow_all = velocity.astype(jnp.float32)
    flow_bottom = lax.optimization_barrier(jnp.sum(bottom[None] * flow_all, axis=1))
    field_bottom = lax.optimization_barrier(jnp.sum(bottom[None] * column_field, axis=1))
    bottom_speed = jnp.sqrt(flow_bottom[0] * flow_bottom[0] + flow_bottom[1] * flow_bottom[1] + speed_floor)
    along_flow = flow_bottom[0] * field_bottom[0] + flow_bottom[1] * field_bottom[1]
    drag_pull = drag[None] * (bottom_speed[None] * field_bottom + flow_bottom * (along_flow / bottom_speed)[None])
    mixed_field = column_field - drag_step * bottom[None] * drag_pull[:, None]
    drag_grad = -drag_step * bottom_speed * along_flow
    return (mixed_field, drag_grad, forcing, wetness)

def face_weights(scaled):
    east = jnp.sqrt(scaled[:, :-1] * scaled[:, 1:])
    north = jnp.sqrt(scaled[:-1, :] * scaled[1:, :])
    return (east, north)

def operate(values, east, north):
    east_flux = east * (values[:, :-1] - values[:, 1:])
    north_flux = north * (values[:-1, :] - values[1:, :])
    result = surface_shift * values
    result = result + jnp.pad(east_flux, ((0, 0), (0, 1))) - jnp.pad(east_flux, ((0, 0), (1, 0)))
    result = result + jnp.pad(north_flux, ((0, 1), (0, 0))) - jnp.pad(north_flux, ((1, 0), (0, 0)))
    return result

def surface_terms(height, scaled):
    east, north = face_weights(scaled)
    east_step = height[:, 1:] - height[:, :-1]
    north_step = height[1:, :] - height[:-1, :]
    east_energy = east * east_step * east_step
    north_energy = north * north_step * north_step
    total = east_energy[1:-1, 1:] + east_energy[1:-1, :-1] + north_energy[1:, 1:-1] + north_energy[:-1, 1:-1]
    sensitivity = 0.25 * total / jnp.maximum(scaled[1:-1, 1:-1], 0.25)
    return (height[1:-1, 1:-1], east_step[1:-1, 1:], north_step[1:, 1:-1], sensitivity)

def to_grid(blocks):
    shaped = blocks.reshape(N_GX, N_GY, 2, BY, BX)
    return shaped.transpose(1, 3, 0, 2, 4).reshape(NY, NX)

def from_grid(planes):
    shaped = planes.reshape(2, N_GY, BY, N_GX, 2, BX)
    return shaped.transpose(3, 1, 4, 0, 2, 5).reshape(NBLK, 2, BY, BX)

def reference(adjoint_vel, velocity, drag_coef, level_count, block_ids, bathymetry, land_mask):

    def first_pass(inputs):
        mixed_field, drag_grad, forcing, wetness = column_block(inputs[0], inputs[1], inputs[2], inputs[3])
        return (mixed_field, drag_grad, forcing)
    mixed_all, drag_all, forcing_all = lax.map(first_pass, (adjoint_vel, velocity, drag_coef, level_count))
    valid = (block_ids < NBLK).astype(jnp.float32)
    even_blocks = jnp.zeros((NBLK + 1, BY, BX), jnp.float32).at[block_ids].add(forcing_all)[:NBLK]
    wet_mask = land_mask.astype(jnp.float32)
    scaled = bathymetry * wet_mask
    source = to_grid(even_blocks) * wet_mask
    east, north = face_weights(scaled)
    centre, table = chebyshev_table(STEPS)
    height = jnp.zeros_like(source)
    residual = source
    direction = source / centre
    for carry_coef, push_coef in table:
        height = height + direction
        residual = residual - operate(direction, east, north)
        direction = carry_coef * direction + push_coef * residual
    surface, east_step, north_step, sensitivity = surface_terms(jnp.pad(height, 1), jnp.pad(scaled, 1))
    grad_blocks = from_grid(jnp.stack([east_step, north_step]))
    grad_blocks = jnp.concatenate([grad_blocks, jnp.zeros((1, 2, BY, BX), jnp.float32)], axis=0)
    slot_grads = grad_blocks[block_ids]

    def second_pass(inputs):
        mixed_field, slot_grad, levels, flag = inputs
        depth_index = lax.broadcasted_iota(jnp.int32, mixed_field.shape[1:], 0)
        wetness = (depth_index < levels[None]).astype(jnp.float32)
        return flag * (mixed_field - pressure_gain * wetness[None] * slot_grad[:, None])
    corrected = lax.map(second_pass, (mixed_all, slot_grads, level_count, valid))
    return (corrected, drag_all * valid[:, None, None], surface, sensitivity)
```

```python
import functools

import jax
import jax.numpy as jnp
import numpy as np
from jax import lax
from jax.experimental import pallas as pl
from jax.experimental.pallas import tpu as pltpu
from jax.sharding import PartitionSpec as P

STEPS = 32

mix_rate = 0.25
drag_step = 0.5
force_scale = 0.25
pressure_gain = 0.5
surface_shift = 1.0 / 64.0
speed_floor = 0.01

LANES = 128
SUBLANES = 8
VMEM_LIMIT = 48 * 1024 * 1024


def chebyshev_sum(total_steps):
    highest = surface_shift + 8.0
    centre = 0.5 * (highest + surface_shift)
    radius = 0.5 * (highest - surface_shift)
    sigma_ratio = centre / radius

    def operate(series):
        shifted = np.zeros_like(series)
        shifted[1] += series[0]
        for k in range(1, len(series) - 1):
            shifted[k + 1] += 0.5 * series[k]
            shifted[k - 1] += 0.5 * series[k]
        return centre * series - radius * shifted

    height = np.zeros(total_steps + 2)
    residual = np.zeros(total_steps + 2)
    residual[0] = 1.0
    direction = residual / centre
    ratio_prev = 1.0 / sigma_ratio
    for _ in range(total_steps):
        height = height + direction
        residual = residual - operate(direction)
        ratio_next = 1.0 / (2.0 * sigma_ratio - ratio_prev)
        direction = ratio_next * ratio_prev * direction + 2.0 * ratio_next / radius * residual
        ratio_prev = ratio_next
    return [float(c) for c in height[:total_steps]], 2.0 / radius


def params(**kw):
    return pltpu.CompilerParams(vmem_limit_bytes=VMEM_LIMIT, **kw)


def forcing_kernel(levels_ref, adjoint_ref, out_ref):
    levels = levels_ref[0]
    depth = adjoint_ref.shape[2]
    total = jnp.zeros(levels.shape, jnp.float32)
    for k in range(depth):
        total = total + jnp.where(levels > k, adjoint_ref[0, 0, k] + adjoint_ref[0, 1, k], 0.0)
    out_ref[0] = force_scale * total


def column_forcing(adjoint_vel, level_count):
    slots, comps, depth, rows, cols = adjoint_vel.shape
    return pl.pallas_call(
        forcing_kernel,
        grid=(slots,),
        in_specs=[
            pl.BlockSpec((1, rows, cols), lambda b: (b, 0, 0)),
            pl.BlockSpec((1, comps, depth, rows, cols), lambda b: (b, 0, 0, 0, 0)),
        ],
        out_specs=pl.BlockSpec((1, rows, cols), lambda b: (b, 0, 0)),
        out_shape=jax.ShapeDtypeStruct((slots, rows, cols), jnp.float32),
        compiler_params=params(),
        cost_estimate=pl.CostEstimate(
            flops=2 * adjoint_vel.size, bytes_accessed=4 * adjoint_vel.size, transcendentals=0
        ),
        name="column_forcing",
    )(level_count, adjoint_vel)


def mixing_kernel(block_total, ids_ref, levels_ref, drag_ref, adjoint_ref, velocity_ref,
                  column_ref, bottom_ref, gradient_ref):
    flag = jnp.where(ids_ref[pl.program_id(0)] < block_total, 1.0, 0.0)
    depth = adjoint_ref.shape[2]
    rows = adjoint_ref.shape[3]
    group = 16

    def one_group(index, carry):
        span = pl.ds(pl.multiple_of(index * group, group), group)
        levels = levels_ref[0, span, :]
        flow = []
        field = []
        zero = jnp.zeros(levels.shape, jnp.float32)
        x = [None, None]
        first_flux = [zero, zero]
        second_flux = [zero, zero]
        once = [None, None]
        flow = [zero, zero]
        field = [zero, zero]
        rate_before = None
        for k in range(depth + 2):
            if k < depth:
                wet = levels > k
                rate = jnp.where(wet, mix_rate, 0.0)
                is_bottom_flow = levels == k + 1
            if 2 <= k:
                is_bottom = levels == k - 1
            for c in range(2):
                if k < depth:
                    fresh = jnp.where(wet, adjoint_ref[0, c, k, span, :], 0.0)
                    flow[c] = jnp.where(
                        is_bottom_flow, velocity_ref[0, c, k, span, :].astype(jnp.float32), flow[c]
                    )
                fresh_once = None
                if 1 <= k <= depth:
                    if k < depth:
                        flux = (fresh - x[c]) * rate
                        fresh_once = x[c] + flux - first_flux[c]
                        first_flux[c] = flux
                    else:
                        fresh_once = x[c] - first_flux[c]
                if k < depth:
                    x[c] = fresh
                if 2 <= k:
                    if k <= depth:
                        flux = (fresh_once - once[c]) * rate_before
                        twice = once[c] + flux - second_flux[c]
                        second_flux[c] = flux
                    else:
                        twice = once[c] - second_flux[c]
                    column_ref[0, c, k - 2, span, :] = twice
                    field[c] = jnp.where(is_bottom, twice, field[c])
                if fresh_once is not None:
                    once[c] = fresh_once
            if k < depth:
                rate_before = rate
        speed = jnp.sqrt(flow[0] * flow[0] + flow[1] * flow[1] + speed_floor)
        along = flow[0] * field[0] + flow[1] * field[1]
        ratio = along / speed
        drag = drag_ref[0, span, :]
        for c in range(2):
            bottom_ref[0, c, span, :] = field[c] - drag_step * drag * (
                speed * field[c] + flow[c] * ratio
            )
        gradient_ref[0, span, :] = -drag_step * speed * along * flag
        return carry

    lax.fori_loop(0, rows // group, one_group, 0)


def column_mixing(adjoint_vel, velocity, drag_coef, level_count, block_ids, block_total):
    slots, comps, depth, rows, cols = adjoint_vel.shape
    plane = pl.BlockSpec((1, rows, cols), lambda b, ids: (b, 0, 0))
    pair = pl.BlockSpec((1, comps, rows, cols), lambda b, ids: (b, 0, 0, 0))
    whole = pl.BlockSpec((1, comps, depth, rows, cols), lambda b, ids: (b, 0, 0, 0, 0))
    return pl.pallas_call(
        functools.partial(mixing_kernel, block_total),
        grid_spec=pltpu.PrefetchScalarGridSpec(
            num_scalar_prefetch=1,
            grid=(slots,),
            in_specs=[plane, plane, whole, whole],
            out_specs=[whole, pair, plane],
        ),
        out_shape=[
            jax.ShapeDtypeStruct(adjoint_vel.shape, jnp.float32),
            jax.ShapeDtypeStruct((slots, comps, rows, cols), jnp.float32),
            jax.ShapeDtypeStruct((slots, rows, cols), jnp.float32),
        ],
        compiler_params=params(),
        cost_estimate=pl.CostEstimate(
            flops=14 * adjoint_vel.size, bytes_accessed=10 * adjoint_vel.size, transcendentals=0
        ),
        name="column_mixing",
    )(block_ids, level_count, drag_coef, adjoint_vel, velocity)


def correct_kernel(block_total, ids_ref, levels_ref, bottom_ref, step_ref, column_ref, out_ref):
    flag = jnp.where(ids_ref[pl.program_id(0)] < block_total, 1, 0)
    levels = levels_ref[0] * flag
    push = pressure_gain * step_ref[0, 0]
    lowest = bottom_ref[0, 0] - push
    for k in range(column_ref.shape[2]):
        value = jnp.where(levels == k + 1, lowest, column_ref[0, 0, k] - push)
        out_ref[0, 0, k] = jnp.where(levels > k, value, 0.0)


def column_correct(column, bottom, steps, level_count, block_ids, block_total):
    slots, comps, depth, rows, cols = column.shape
    plane = pl.BlockSpec((1, rows, cols), lambda b, c, ids: (b, 0, 0))
    one = pl.BlockSpec((1, 1, rows, cols), lambda b, c, ids: (b, c, 0, 0))
    whole = pl.BlockSpec((1, 1, depth, rows, cols), lambda b, c, ids: (b, c, 0, 0, 0))
    return pl.pallas_call(
        functools.partial(correct_kernel, block_total),
        grid_spec=pltpu.PrefetchScalarGridSpec(
            num_scalar_prefetch=1,
            grid=(slots, comps),
            in_specs=[plane, one, one, whole],
            out_specs=whole,
        ),
        out_shape=jax.ShapeDtypeStruct(column.shape, jnp.float32),
        compiler_params=params(),
        cost_estimate=pl.CostEstimate(
            flops=4 * column.size, bytes_accessed=8 * column.size, transcendentals=0
        ),
        name="column_correct",
    )(block_ids, level_count, bottom, steps, column)


def window_rows(rows):
    return rows + 2 * STEPS


def window_places(me_ref, ids_ref, slots, lon_count, lat_count):
    places = []
    for w in range(slots + 2):
        if w < slots:
            block = jnp.where(ids_ref[w] < 2 * lon_count * lat_count, ids_ref[w], 0)
        else:
            block = (me_ref[0] * lat_count + me_ref[1]) * 2 + (w - slots)
        pair = lax.div(block, 2)
        lat = lax.rem(pair, lat_count)
        column = lax.div(pair, lat_count) * 2 + lax.rem(block, 2)
        places.append((lat, column))
    return places


def east_of(first, second, last_lane):
    first_roll = pltpu.roll(first, LANES - 1, 1)
    second_roll = pltpu.roll(second, LANES - 1, 1)
    return (
        jnp.where(last_lane, second_roll, first_roll),
        jnp.where(last_lane, first_roll, second_roll),
    )


def west_of(first, second, first_lane):
    first_roll = pltpu.roll(first, 1, 1)
    second_roll = pltpu.roll(second, 1, 1)
    return (
        jnp.where(first_lane, second_roll, first_roll),
        jnp.where(first_lane, first_roll, second_roll),
    )


def tile_at(row, tile):
    start = (row * 2 + tile) * SUBLANES
    if not isinstance(start, int):
        start = pl.multiple_of(start, SUBLANES)
    return pl.ds(start, SUBLANES)


def fill_windows(target, places, rows, load, lon_count, lat_count):
    lane = lax.broadcasted_iota(jnp.int32, (rows, LANES), 1)
    for w, (lat, column) in enumerate(places):
        for down in (-1, 0, 1):
            base = (down + 1) * rows * 2 * SUBLANES + w
            target[pl.ds(base, rows, stride=2 * SUBLANES), :] = load(lat + down, column)
            east = load(lat + down, column + 1)
            west = load(lat + down, column - 1)
            sides = jnp.where(lane < STEPS, east, jnp.where(lane >= LANES - STEPS, west, 0.0))
            target[pl.ds(base + SUBLANES, rows, stride=2 * SUBLANES), :] = sides


def weights_kernel(slots, lon_count, lat_count, me_ref, ids_ref, depth_ref,
                   scaled_ref, east_ref, north_ref):
    rows = depth_ref.shape[1] // 2 - SUBLANES // 2
    total = window_rows(rows)
    scaled_ref[...] = jnp.zeros_like(scaled_ref)
    column_count = 2 * lon_count

    def load(lat, column):
        inside = (lat >= 0) & (lat < lat_count) & (column >= 0) & (column < column_count)
        lat_safe = jnp.clip(lat, 0, lat_count - 1)
        column_safe = jnp.clip(column, 0, column_count - 1)
        device = lax.div(column_safe, 2) * lat_count + lat_safe
        start = pl.multiple_of(lax.rem(column_safe, 2) * rows, SUBLANES)
        return depth_ref[device, pl.ds(start, rows), :] * jnp.where(inside, 1.0, 0.0)

    places = window_places(me_ref, ids_ref, slots, lon_count, lat_count)
    fill_windows(scaled_ref, places, rows, load, lon_count, lat_count)

    last_lane = lax.broadcasted_iota(jnp.int32, (SUBLANES, LANES), 1) == LANES - 1
    scale = chebyshev_sum(STEPS)[1]

    def one_row(row, here):
        below = (scaled_ref[tile_at(row + 1, 0), :], scaled_ref[tile_at(row + 1, 1), :])
        easts = east_of(here[0], here[1], last_lane)
        for t in range(2):
            east_ref[tile_at(row, t), :] = scale * jnp.sqrt(here[t] * easts[t])
            north_ref[tile_at(row, t), :] = scale * jnp.sqrt(here[t] * below[t])
        return below

    first = (scaled_ref[tile_at(0, 0), :], scaled_ref[tile_at(0, 1), :])
    lax.fori_loop(0, total, one_row, first, unroll=4)


PAD_ROWS = 16


def surface_weights(depth_all, me, block_ids, slots, rows, lon_count, lat_count):
    total = (window_rows(rows) + PAD_ROWS) * 2 * SUBLANES
    shape = jax.ShapeDtypeStruct((total, LANES), jnp.float32)
    smem = pl.BlockSpec(memory_space=pltpu.SMEM)
    vmem = pl.BlockSpec(memory_space=pltpu.VMEM)
    return pl.pallas_call(
        functools.partial(weights_kernel, slots, lon_count, lat_count),
        in_specs=[smem, smem, vmem],
        out_specs=[vmem, vmem, vmem],
        out_shape=[shape, shape, shape],
        compiler_params=params(),
        cost_estimate=pl.CostEstimate(
            flops=8 * total * LANES, bytes_accessed=12 * total * LANES, transcendentals=0
        ),
        name="surface_weights",
    )(me, block_ids, depth_all)


UNROLL = 8


def solve_kernel(slots, lon_count, lat_count, pieces, me_ref, ids_ref, all_ids_ref,
                 scaled_ref, east_ref, north_ref, *rest):
    piece_refs = rest[:pieces]
    steps_ref, height_ref, sensitivity_ref = rest[pieces:pieces + 3]
    forcing, source, even, odd, places_of, sems = rest[pieces + 3:]
    rows = height_ref.shape[0]
    total = window_rows(rows)
    copies = [
        pltpu.make_async_copy(piece_refs[p], forcing.at[p], sems.at[p]) for p in range(pieces)
    ]
    for copy in copies:
        copy.start()

    block_total = 2 * lon_count * lat_count
    half = lat_count // 2

    def one_device(device, carry):
        lon_xor = lax.div(device, lat_count) ^ me_ref[0]
        lat_xor = lax.rem(device, lat_count) ^ me_ref[1]
        piece = lax.rem(lat_xor, 2) * lon_count + lon_xor
        start = (piece * half + lax.div(lat_xor, 2)) * slots
        for s in range(slots):
            places_of[all_ids_ref[device * slots + s]] = start + s
        return carry

    lax.fori_loop(0, lon_count * lat_count, one_device, 0)
    source[...] = jnp.zeros_like(source)
    for copy in copies:
        copy.wait()

    def load(lat, column):
        lat_safe = jnp.clip(lat, 0, lat_count - 1)
        column_safe = jnp.clip(column, 0, 2 * lon_count - 1)
        block = (lax.div(column_safe, 2) * lat_count + lat_safe) * 2 + lax.rem(column_safe, 2)
        place = places_of[block]
        return forcing[lax.div(place, half * slots), lax.rem(place, half * slots)]

    places = window_places(me_ref, ids_ref, slots, lon_count, lat_count)
    fill_windows(source, places, rows, load, lon_count, lat_count)

    coefs, _ = chebyshev_sum(STEPS)

    def first_row(row, carry):
        for t in range(2):
            at = tile_at(row, t)
            value = jnp.where(scaled_ref[at, :] > 0.0, source[at, :], 0.0)
            source[at, :] = value
            even[at, :] = coefs[STEPS - 1] * value
            odd[at, :] = jnp.zeros_like(value)
        return carry

    lax.fori_loop(0, total, first_row, 0, unroll=8)

    lane = lax.broadcasted_iota(jnp.int32, (SUBLANES, LANES), 1)
    last_lane = lane == LANES - 1
    first_lane = lane == 0

    def apply(current, target, coef, gain, low, count):
        def one(row, here, north_before):
            below = (current[tile_at(row + 1, 0), :], current[tile_at(row + 1, 1), :])
            easts = east_of(here[0], here[1], last_lane)
            east_flux = [
                east_ref[tile_at(row, t), :] * (here[t] - easts[t]) for t in range(2)
            ]
            west_flux = west_of(east_flux[0], east_flux[1], first_lane)
            north = []
            for t in range(2):
                at = tile_at(row, t)
                north.append(north_ref[at, :] * (here[t] - below[t]))
                spread = (east_flux[t] - west_flux[t]) + (north[t] - north_before[t])
                pushed = (here[t] + here[t]) - spread
                if gain != 1.0:
                    pushed = gain * pushed
                target[at, :] = (coef * source[at, :] - target[at, :]) + pushed
            return below, tuple(north)

        def group(index, carry):
            here, north_before = carry
            row = low + index * UNROLL
            for u in range(UNROLL):
                here, north_before = one(row + u, here, north_before)
            return here, north_before

        here = (current[tile_at(low, 0), :], current[tile_at(low, 1), :])
        before = tuple(
            north_ref[tile_at(low - 1, t), :] * (current[tile_at(low - 1, t), :] - here[t])
            for t in range(2)
        )
        lax.fori_loop(0, pl.cdiv(count, UNROLL), group, (here, before))

    current, target = even, odd
    for m in range(1, STEPS):
        k = STEPS - 1 - m
        apply(current, target, coefs[k], 1.0 if k > 0 else 0.5, m, total - 2 * m)
        current, target = target, current

    final, east_out, north_out = current, target, source

    def differences(row, here):
        below = (final[tile_at(row + 1, 0), :], final[tile_at(row + 1, 1), :])
        easts = east_of(here[0], here[1], last_lane)
        for t in range(2):
            east_out[tile_at(row, t), :] = easts[t] - here[t]
            north_out[tile_at(row, t), :] = below[t] - here[t]
        return below

    top = STEPS - 1
    lax.fori_loop(
        top, STEPS + rows, differences, (final[tile_at(top, 0), :], final[tile_at(top, 1), :])
    )

    def cut(ref, w):
        return ref[pl.ds(STEPS * 2 * SUBLANES + w, rows, stride=2 * SUBLANES), :]

    for w in range(slots):
        steps_ref[w, 0] = cut(east_out, w)
        steps_ref[w, 1] = cut(north_out, w)
    for h in range(2):
        height_ref[:, h * LANES:(h + 1) * LANES] = cut(final, slots + h)

    undo = 0.25 / chebyshev_sum(STEPS)[1]

    def energy_row(row, north_before):
        here = [east_out[tile_at(row, t), :] for t in range(2)]
        east_energy = [east_ref[tile_at(row, t), :] * here[t] * here[t] for t in range(2)]
        west_energy = west_of(east_energy[0], east_energy[1], first_lane)[0]
        at = tile_at(row, 0)
        north_step = north_out[at, :]
        north_energy = north_ref[at, :] * north_step * north_step
        energy = east_energy[0] + west_energy + north_energy + north_before
        east_out[at, :] = undo * energy / jnp.maximum(scaled_ref[at, :], 0.25)
        return north_energy

    at = tile_at(top, 0)
    step = north_out[at, :]
    lax.fori_loop(STEPS, STEPS + rows, energy_row, north_ref[at, :] * step * step)
    for h in range(2):
        sensitivity_ref[:, h * LANES:(h + 1) * LANES] = cut(east_out, slots + h)


def surface_solve(pieces, weights, me, block_ids, all_ids, slots, rows, lon_count, lat_count):
    scaled, east, north = weights
    cols = pieces[0].shape[-1]
    smem = pl.BlockSpec(memory_space=pltpu.SMEM)
    vmem = pl.BlockSpec(memory_space=pltpu.VMEM)
    anywhere = pl.BlockSpec(memory_space=pl.ANY)
    window = pltpu.VMEM(scaled.shape, jnp.float32)
    return pl.pallas_call(
        functools.partial(solve_kernel, slots, lon_count, lat_count, len(pieces)),
        in_specs=[smem, smem, smem, vmem, vmem, vmem] + [anywhere] * len(pieces),
        out_specs=[vmem, vmem, vmem],
        out_shape=[
            jax.ShapeDtypeStruct((slots, 2, rows, cols), jnp.float32),
            jax.ShapeDtypeStruct((rows, 2 * cols), jnp.float32),
            jax.ShapeDtypeStruct((rows, 2 * cols), jnp.float32),
        ],
        scratch_shapes=[
            pltpu.VMEM((len(pieces),) + pieces[0].shape, jnp.float32),
            window,
            window,
            window,
            pltpu.SMEM((2 * lon_count * lat_count + 1,), jnp.int32),
            pltpu.SemaphoreType.DMA((len(pieces),)),
        ],
        compiler_params=params(),
        cost_estimate=pl.CostEstimate(
            flops=14 * STEPS * scaled.size, bytes_accessed=16 * scaled.size, transcendentals=0
        ),
        name="surface_solve",
    )(me, block_ids, all_ids, scaled, east, north, *pieces)


def swap(values, axis, mask):
    count = lax.axis_size(axis)
    return lax.ppermute(values, axis, [(i, i ^ mask) for i in range(count)])


def gather_forcing(forcing, lon_count, lat_count):
    parts = [forcing] + [swap(forcing, "gy", 2 * m) for m in range(1, lat_count // 2)]
    line = jnp.concatenate(parts, axis=0)
    near = [line] + [swap(line, "gx", m) for m in range(1, lon_count)]
    far = [swap(piece, "gy", 1) for piece in near]
    return near + far


def per_device(adjoint_vel, velocity, drag_coef, level_count, block_ids, bathymetry, land_mask):
    slots = block_ids.shape[0]
    rows, cols = drag_coef.shape[1:]
    lon_count = lax.axis_size("gx")
    lat_count = lax.axis_size("gy")
    device_count = lon_count * lat_count
    block_total = 2 * device_count
    me = jnp.stack([lax.axis_index("gx"), lax.axis_index("gy")]).astype(jnp.int32)

    scaled = bathymetry * land_mask.astype(jnp.float32)
    id_rows = jnp.zeros((SUBLANES, cols), jnp.float32).at[0, :slots].set(
        block_ids.astype(jnp.float32)
    )
    sent = jnp.concatenate([scaled[:, :cols], scaled[:, cols:], id_rows], axis=0)
    depth_all = lax.all_gather(sent, ("gx", "gy"), axis=0, tiled=True)
    depth_all = depth_all.reshape(device_count, 2 * rows + SUBLANES, cols)
    all_ids = depth_all[:, 2 * rows, :slots].astype(jnp.int32).reshape(-1)

    forcing = column_forcing(adjoint_vel, level_count)
    pieces = gather_forcing(forcing, lon_count, lat_count)
    column, bottom, drag_gradient = column_mixing(
        adjoint_vel, velocity, drag_coef, level_count, block_ids, block_total
    )
    weights = surface_weights(depth_all, me, block_ids, slots, rows, lon_count, lat_count)
    steps, height, sensitivity = surface_solve(
        pieces, weights, me, block_ids, all_ids, slots, rows, lon_count, lat_count
    )
    corrected = column_correct(column, bottom, steps, level_count, block_ids, block_total)
    return corrected, drag_gradient, height, sensitivity


def solution(mesh):
    in_specs = (
        P(("gx", "gy"), None, None, None, None),
        P(("gx", "gy"), None, None, None, None),
        P(("gx", "gy"), None, None),
        P(("gx", "gy"), None, None),
        P(("gx", "gy")),
        P("gy", "gx"),
        P("gy", "gx"),
    )
    out_specs = (
        P(("gx", "gy"), None, None, None, None),
        P(("gx", "gy"), None, None),
        P("gy", "gx"),
        P("gy", "gx"),
    )
    return jax.shard_map(
        per_device, mesh=mesh, in_specs=in_specs, out_specs=out_specs, check_vma=False
    )
```

```python
import functools

import jax
import jax.numpy as jnp
import numpy as np
from jax import lax
from jax.experimental import pallas as pl
from jax.experimental.pallas import tpu as pltpu
from jax.sharding import PartitionSpec as P

STEPS = 32

mix_rate = 0.25
drag_step = 0.5
force_scale = 0.25
pressure_gain = 0.5
surface_shift = 1.0 / 64.0
speed_floor = 0.01

LANES = 128
SUBLANES = 8
MIB = 1024 * 1024
FORCING_VMEM = 48 * MIB
MIXING_VMEM = 4 * MIB
SURFACE_VMEM = 20 * MIB


def chebyshev_sum(total_steps):
    highest = surface_shift + 8.0
    centre = 0.5 * (highest + surface_shift)
    radius = 0.5 * (highest - surface_shift)
    sigma_ratio = centre / radius

    def operate(series):
        shifted = np.zeros_like(series)
        shifted[1] += series[0]
        for k in range(1, len(series) - 1):
            shifted[k + 1] += 0.5 * series[k]
            shifted[k - 1] += 0.5 * series[k]
        return centre * series - radius * shifted

    height = np.zeros(total_steps + 2)
    residual = np.zeros(total_steps + 2)
    residual[0] = 1.0
    direction = residual / centre
    ratio_prev = 1.0 / sigma_ratio
    for _ in range(total_steps):
        height = height + direction
        residual = residual - operate(direction)
        ratio_next = 1.0 / (2.0 * sigma_ratio - ratio_prev)
        direction = ratio_next * ratio_prev * direction + 2.0 * ratio_next / radius * residual
        ratio_prev = ratio_next
    return [float(c) for c in height[:total_steps]], 2.0 / radius


def params(limit):
    return pltpu.CompilerParams(vmem_limit_bytes=limit)


def forcing_kernel(levels_ref, adjoint_ref, out_ref, held, sems):
    slots, comps, depth, rows, cols = held.shape
    for b in range(slots):
        for c in range(comps):
            pltpu.make_async_copy(adjoint_ref.at[b, c], held.at[b, c], sems.at[b, c]).start()

    def one_slot(b, carry):
        levels = levels_ref[b]
        total = jnp.zeros((rows, cols), jnp.float32)
        for c in range(comps):
            pltpu.make_async_copy(adjoint_ref.at[b, c], held.at[b, c], sems.at[b, c]).wait()
            for k in range(depth):
                total = total + jnp.where(levels > k, held[b, c, k], 0.0)
        out_ref[b] = force_scale * total
        return carry

    lax.fori_loop(0, slots, one_slot, 0)


def column_forcing(adjoint_vel, level_count):
    slots, comps, depth, rows, cols = adjoint_vel.shape
    vmem = pl.BlockSpec(memory_space=pltpu.VMEM)
    return pl.pallas_call(
        forcing_kernel,
        in_specs=[vmem, pl.BlockSpec(memory_space=pl.ANY)],
        out_specs=[vmem, vmem],
        out_shape=[
            pltpu.VMEM((slots, rows, cols), jnp.float32),
            pltpu.VMEM(adjoint_vel.shape, jnp.float32),
        ],
        scratch_shapes=[pltpu.SemaphoreType.DMA((slots, comps))],
        compiler_params=params(FORCING_VMEM),
        cost_estimate=pl.CostEstimate(
            flops=2 * adjoint_vel.size, bytes_accessed=4 * adjoint_vel.size, transcendentals=0
        ),
        name="column_forcing",
    )(level_count, adjoint_vel)


CHUNK = 8


def mixing_kernel(block_total, ids_ref, levels_ref, drag_ref, adjoint_ref, velocity_ref,
                  line_ref, column_ref, bottom_ref, gradient_ref):
    slots, comps, depth, rows, cols = adjoint_ref.shape
    group = 16
    parts = rows // group

    def one_group(b, index):
        flag = jnp.where(ids_ref[b] < block_total, 1.0, 0.0)
        span = pl.ds(pl.multiple_of(index * group, group), group)
        levels = levels_ref[b, span, :]
        zero = jnp.zeros(levels.shape, jnp.float32)
        x = [zero, zero]
        once = [zero, zero]
        first_flux = [zero, zero]
        second_flux = [zero, zero]
        flow = [zero, zero]
        field = [zero, zero]
        rate_before = zero
        for low in range(0, depth + 2, CHUNK):
            here = range(low, min(low + CHUNK, depth + 2))
            loaded = {}
            for k in here:
                if k < depth:
                    for c in range(2):
                        loaded[k, c] = (
                            adjoint_ref[b, c, k, span, :],
                            velocity_ref[b, c, k, span, :],
                        )
            done = {}
            for k in here:
                if k < depth:
                    wet = levels > k
                    rate = jnp.where(wet, mix_rate, 0.0)
                    is_bottom_flow = levels == k + 1
                is_bottom = levels == k - 1
                for c in range(2):
                    if k < depth:
                        fresh = jnp.where(wet, loaded[k, c][0], 0.0)
                        flow[c] = jnp.where(
                            is_bottom_flow, loaded[k, c][1].astype(jnp.float32), flow[c]
                        )
                    fresh_once = None
                    if 1 <= k < depth:
                        flux = (fresh - x[c]) * rate
                        fresh_once = x[c] + (flux - first_flux[c])
                        first_flux[c] = flux
                    elif k == depth:
                        fresh_once = x[c] - first_flux[c]
                    if k < depth:
                        x[c] = fresh
                    if 2 <= k:
                        if k <= depth:
                            flux = (fresh_once - once[c]) * rate_before
                            twice = once[c] + (flux - second_flux[c])
                            second_flux[c] = flux
                        else:
                            twice = once[c] - second_flux[c]
                        done[k - 2, c] = twice
                        field[c] = jnp.where(is_bottom, twice, field[c])
                    if fresh_once is not None:
                        once[c] = fresh_once
                if k < depth:
                    rate_before = rate
            for (k, c), value in done.items():
                column_ref[b, c, k, span, :] = value
        speed = jnp.sqrt(flow[0] * flow[0] + flow[1] * flow[1] + speed_floor)
        along = flow[0] * field[0] + flow[1] * field[1]
        ratio = along / speed
        drag = drag_ref[b, span, :]
        for c in range(2):
            bottom_ref[b, c, span, :] = field[c] - drag_step * drag * (
                speed * field[c] + flow[c] * ratio
            )
        gradient_ref[b, span, :] = -drag_step * speed * along * flag

    def one(step, carry):
        one_group(lax.div(step, parts), lax.rem(step, parts))
        return carry

    lax.fori_loop(0, slots * parts, one, 0)


def column_mixing(adjoint_vel, velocity, drag_coef, level_count, block_ids, line, block_total):
    slots, comps, depth, rows, cols = adjoint_vel.shape
    vmem = pl.BlockSpec(memory_space=pltpu.VMEM)
    smem = pl.BlockSpec(memory_space=pltpu.SMEM)
    anywhere = pl.BlockSpec(memory_space=pl.ANY)
    return pl.pallas_call(
        functools.partial(mixing_kernel, block_total),
        in_specs=[smem, vmem, vmem, vmem, vmem, anywhere],
        out_specs=[vmem, vmem, vmem],
        out_shape=[
            jax.ShapeDtypeStruct(adjoint_vel.shape, jnp.float32),
            jax.ShapeDtypeStruct((slots, comps, rows, cols), jnp.float32),
            jax.ShapeDtypeStruct((slots, rows, cols), jnp.float32),
        ],
        compiler_params=params(MIXING_VMEM),
        cost_estimate=pl.CostEstimate(
            flops=14 * adjoint_vel.size, bytes_accessed=6 * adjoint_vel.size, transcendentals=0
        ),
        name="column_mixing",
    )(block_ids, level_count, drag_coef, adjoint_vel, velocity, line)


def window_rows(rows):
    return rows + 2 * STEPS


def window_places(me_ref, ids_ref, slots, lon_count, lat_count):
    places = []
    for w in range(slots + 2):
        if w < slots:
            block = jnp.where(ids_ref[w] < 2 * lon_count * lat_count, ids_ref[w], 0)
        else:
            block = (me_ref[0] * lat_count + me_ref[1]) * 2 + (w - slots)
        pair = lax.div(block, 2)
        lat = lax.rem(pair, lat_count)
        column = lax.div(pair, lat_count) * 2 + lax.rem(block, 2)
        places.append((lat, column))
    return places


def east_of(first, second, last_lane):
    first_roll = pltpu.roll(first, LANES - 1, 1)
    second_roll = pltpu.roll(second, LANES - 1, 1)
    return (
        jnp.where(last_lane, second_roll, first_roll),
        jnp.where(last_lane, first_roll, second_roll),
    )


def west_of(first, second, first_lane):
    first_roll = pltpu.roll(first, 1, 1)
    second_roll = pltpu.roll(second, 1, 1)
    return (
        jnp.where(first_lane, second_roll, first_roll),
        jnp.where(first_lane, first_roll, second_roll),
    )


def tile_at(row, tile):
    start = (row * 2 + tile) * SUBLANES
    if not isinstance(start, int):
        start = pl.multiple_of(start, SUBLANES)
    return pl.ds(start, SUBLANES)


def load_row(ref, row):
    return (ref[tile_at(row, 0), :], ref[tile_at(row, 1), :])


def put_window(target, w, rows, blocks, lane):
    for i in range(3):
        here, east, west = blocks[3 * i:3 * i + 3]
        sides = jnp.where(lane < STEPS, east, jnp.where(lane >= LANES - STEPS, west, 0.0))
        base = i * rows * 2 * SUBLANES + w
        target[pl.ds(base, rows, stride=2 * SUBLANES), :] = here
        target[pl.ds(base + SUBLANES, rows, stride=2 * SUBLANES), :] = sides


def fill_windows(target, places, rows, load):
    lane = lax.broadcasted_iota(jnp.int32, (rows, LANES), 1)
    for w, (lat, column) in enumerate(places):
        blocks = [load(lat + down, column + right) for down, right in NEIGHBOURS]
        put_window(target, w, rows, blocks, lane)


def depth_kernel(ids_ref, bathymetry_ref, mask_ref, out_ref):
    rows = bathymetry_ref.shape[0]
    scaled = bathymetry_ref[...] * mask_ref[...].astype(jnp.float32)
    out_ref[0:rows, :] = scaled[:, :LANES]
    out_ref[rows:2 * rows, :] = scaled[:, LANES:]
    lane = lax.broadcasted_iota(jnp.int32, (SUBLANES, LANES), 1)
    listed = jnp.zeros((SUBLANES, LANES), jnp.int32)
    for s in range(ids_ref.shape[0]):
        listed = jnp.where(lane == s, ids_ref[s], listed)
    out_ref[2 * rows:2 * rows + SUBLANES, :] = listed.astype(jnp.float32)


def depth_payload(bathymetry, land_mask, block_ids):
    rows = bathymetry.shape[0]
    vmem = pl.BlockSpec(memory_space=pltpu.VMEM)
    return pl.pallas_call(
        depth_kernel,
        in_specs=[pl.BlockSpec(memory_space=pltpu.SMEM), vmem, vmem],
        out_specs=vmem,
        out_shape=jax.ShapeDtypeStruct((2 * rows + SUBLANES, LANES), jnp.float32),
        compiler_params=params(SURFACE_VMEM),
        name="depth_payload",
    )(block_ids, bathymetry, land_mask)


def weights_kernel(slots, lon_count, lat_count, pieces, me_ref, ids_ref, *rest):
    piece_refs = rest[:pieces]
    scaled_ref, east_ref, north_ref, table_ref = rest[pieces:pieces + 4]
    depths, all_ids, places_of, sems = rest[pieces + 4:]
    half = lat_count // 2
    rows = (depths.shape[2] - SUBLANES) // 2
    total = window_rows(rows)
    column_count = 2 * lon_count
    copies = [
        pltpu.make_async_copy(
            piece_refs[p].at[:, pl.ds(2 * rows, SUBLANES), :], all_ids.at[p], sems.at[p]
        )
        for p in range(pieces)
    ]
    for copy in copies:
        copy.start()
    for p in range(pieces):
        depths[p] = piece_refs[p][...]
    scaled_ref[...] = jnp.zeros_like(scaled_ref)
    for copy in copies:
        copy.wait()

    def one_piece(p, carry):
        for z in range(half):
            for s in range(slots):
                block = all_ids[p, z, 0, s].astype(jnp.int32)
                places_of[block] = (p * half + z) * slots + s
        return carry

    lax.fori_loop(0, pieces, one_piece, 0)

    def load(lat, column):
        inside = (lat >= 0) & (lat < lat_count) & (column >= 0) & (column < column_count)
        lat_safe = jnp.clip(lat, 0, lat_count - 1)
        column_safe = jnp.clip(column, 0, column_count - 1)
        lon_xor = lax.div(column_safe, 2) ^ me_ref[0]
        lat_xor = lat_safe ^ me_ref[1]
        piece = lax.rem(lat_xor, 2) * lon_count + lon_xor
        start = pl.multiple_of(lax.rem(column_safe, 2) * rows, SUBLANES)
        block = depths[piece, lax.div(lat_xor, 2), pl.ds(start, rows), :]
        return block * jnp.where(inside, 1.0, 0.0)

    places = window_places(me_ref, ids_ref, slots, lon_count, lat_count)
    fill_windows(scaled_ref, places, rows, load)

    for w, (lat, column) in enumerate(places):
        for n, (down, right) in enumerate(NEIGHBOURS):
            lat_safe = jnp.clip(lat + down, 0, lat_count - 1)
            column_safe = jnp.clip(column + right, 0, column_count - 1)
            block = (lax.div(column_safe, 2) * lat_count + lat_safe) * 2 + lax.rem(column_safe, 2)
            table_ref[w * len(NEIGHBOURS) + n] = places_of[block]

    last_lane = lax.broadcasted_iota(jnp.int32, (SUBLANES, LANES), 1) == LANES - 1
    scale = chebyshev_sum(STEPS)[1]
    unroll = 8

    def some_rows(index, here):
        row = index * unroll
        out = []
        for u in range(unroll):
            below = load_row(scaled_ref, row + u + 1)
            easts = east_of(here[0], here[1], last_lane)
            for t in range(2):
                out.append((east_ref, u, t, scale * jnp.sqrt(here[t] * easts[t])))
                out.append((north_ref, u, t, scale * jnp.sqrt(here[t] * below[t])))
            here = below
        for ref, u, t, value in out:
            ref[tile_at(row + u, t), :] = value
        return here

    lax.fori_loop(0, total // unroll, some_rows, load_row(scaled_ref, 0))


PAD_ROWS = 16
NEIGHBOURS = [(down, right) for down in (-1, 0, 1) for right in (0, 1, -1)]


def surface_weights(pieces, me, block_ids, rows, lon_count, lat_count):
    slots = block_ids.shape[0]
    total = (window_rows(rows) + PAD_ROWS) * 2 * SUBLANES
    shape = jax.ShapeDtypeStruct((total, LANES), jnp.float32)
    smem = pl.BlockSpec(memory_space=pltpu.SMEM)
    vmem = pl.BlockSpec(memory_space=pltpu.VMEM)
    return pl.pallas_call(
        functools.partial(weights_kernel, slots, lon_count, lat_count, len(pieces)),
        in_specs=[smem, smem] + [vmem] * len(pieces),
        out_specs=[vmem, vmem, vmem, smem],
        out_shape=[shape, shape, shape]
        + [jax.ShapeDtypeStruct(((slots + 2) * len(NEIGHBOURS),), jnp.int32)],
        scratch_shapes=[
            pltpu.VMEM((len(pieces),) + pieces[0].shape, jnp.float32),
            pltpu.SMEM((len(pieces), pieces[0].shape[0], SUBLANES, LANES), jnp.float32),
            pltpu.SMEM((2 * lon_count * lat_count + 1,), jnp.int32),
            pltpu.SemaphoreType.DMA((len(pieces),)),
        ],
        compiler_params=params(SURFACE_VMEM),
        cost_estimate=pl.CostEstimate(
            flops=8 * total * LANES, bytes_accessed=12 * total * LANES, transcendentals=0
        ),
        name="surface_weights",
    )(me, block_ids, *pieces)


UNROLL = 16


def solve_kernel(block_total, pieces, ids_ref, table_ref, coefs_ref, scaled_ref, east_ref,
                 north_ref, levels_ref, bottom_ref, column_ref, *rest):
    piece_refs = rest[:pieces]
    corrected_ref, height_ref, sensitivity_ref = rest[pieces:pieces + 3]
    forcing, source, even, odd, staged, sems = rest[pieces + 3:]
    slots, comps, depth, rows, cols = staged.shape
    total = window_rows(rows)
    for p in range(pieces):
        forcing[p] = piece_refs[p][...]
    source[...] = jnp.zeros_like(source)

    lane = lax.broadcasted_iota(jnp.int32, (rows, LANES), 1)
    per_piece = forcing.shape[1]
    for w in range(slots + 2):
        blocks = []
        for n in range(len(NEIGHBOURS)):
            place = table_ref[w * len(NEIGHBOURS) + n]
            blocks.append(forcing[lax.div(place, per_piece), lax.rem(place, per_piece)])
        put_window(source, w, rows, blocks, lane)

    coefs, step_scale = chebyshev_sum(STEPS)
    unroll = 8

    def first_rows(index, carry):
        base = index * unroll
        out = []
        for u in range(unroll):
            for t in range(2):
                at = tile_at(base + u, t)
                out.append((at, jnp.where(scaled_ref[at, :] > 0.0, source[at, :], 0.0)))
        for at, value in out:
            source[at, :] = value
            even[at, :] = coefs[STEPS - 1] * value
            odd[at, :] = jnp.zeros_like(value)
        return carry

    lax.fori_loop(0, total // unroll, first_rows, 0)

    lane = lax.broadcasted_iota(jnp.int32, (SUBLANES, LANES), 1)
    last_lane = lane == LANES - 1
    first_lane = lane == 0

    def apply(current, target, coef, gain, low):
        def group(index, carry):
            here, north_before = carry
            row = low + index * UNROLL
            out = []
            for u in range(UNROLL):
                below = load_row(current, row + u + 1)
                easts = east_of(here[0], here[1], last_lane)
                east_weight = load_row(east_ref, row + u)
                north_weight = load_row(north_ref, row + u)
                fixed = load_row(source, row + u)
                old = load_row(target, row + u)
                east_flux = [east_weight[t] * (here[t] - easts[t]) for t in range(2)]
                west_flux = west_of(east_flux[0], east_flux[1], first_lane)
                north = [north_weight[t] * (here[t] - below[t]) for t in range(2)]
                for t in range(2):
                    spread = (east_flux[t] - west_flux[t]) + (north[t] - north_before[t])
                    pushed = (here[t] + here[t]) - spread
                    if gain != 1.0:
                        pushed = gain * pushed
                    out.append((u, t, (coef * fixed[t] - old[t]) + pushed))
                here = below
                north_before = tuple(north)
            for u, t, value in out:
                target[tile_at(row + u, t), :] = value
            return here, north_before

        here = load_row(current, low)
        above = load_row(current, low - 1)
        weight = load_row(north_ref, low - 1)
        before = tuple(weight[t] * (above[t] - here[t]) for t in range(2))
        groups = lax.div(total - 2 * low + UNROLL - 1, UNROLL)
        lax.fori_loop(0, groups, group, (here, before))

    def two_steps(pair, carry):
        low = 2 * pair + 1
        apply(even, odd, coefs_ref[low], 1.0, low)
        apply(odd, even, coefs_ref[low + 1], 1.0, low + 1)
        return carry

    lax.fori_loop(0, (STEPS - 2) // 2, two_steps, 0)
    apply(even, odd, coefs[0], 0.5, STEPS - 1)

    final, east_out, north_out = odd, even, source
    top = STEPS - 1

    def differences(row, here):
        below = load_row(final, row + 1)
        easts = east_of(here[0], here[1], last_lane)
        for t in range(2):
            east_out[tile_at(row, t), :] = easts[t] - here[t]
            north_out[tile_at(row, t), :] = below[t] - here[t]
        return below

    lax.fori_loop(top, STEPS + rows, differences, load_row(final, top), unroll=3)

    def cut(ref, w):
        return ref[pl.ds(STEPS * 2 * SUBLANES + w, rows, stride=2 * SUBLANES), :]

    for b in range(slots):
        flag = jnp.where(ids_ref[b] < block_total, 1, 0)
        levels = levels_ref[b] * flag
        for c in range(comps):
            push = pressure_gain * cut((east_out, north_out)[c], b)
            lowest = bottom_ref[b, c] - push
            for low in range(0, depth, 8):
                out = []
                for k in range(low, min(low + 8, depth)):
                    value = jnp.where(levels == k + 1, lowest, column_ref[b, c, k] - push)
                    out.append((k, jnp.where(levels > k, value, 0.0)))
                for k, value in out:
                    staged[b, c, k] = value
            pltpu.make_async_copy(
                staged.at[b, c], corrected_ref.at[b, c], sems.at[b, c]
            ).start()

    for h in range(2):
        height_ref[:, h * LANES:(h + 1) * LANES] = cut(final, slots + h)

    undo = 0.25 / step_scale

    def energy_row(row, north_before):
        here = load_row(east_out, row)
        weight = load_row(east_ref, row)
        east_energy = [weight[t] * here[t] * here[t] for t in range(2)]
        west_energy = west_of(east_energy[0], east_energy[1], first_lane)[0]
        at = tile_at(row, 0)
        north_step = north_out[at, :]
        north_energy = north_ref[at, :] * north_step * north_step
        energy = east_energy[0] + west_energy + north_energy + north_before
        east_out[at, :] = undo * energy / jnp.maximum(scaled_ref[at, :], 0.25)
        return north_energy

    at = tile_at(top, 0)
    step = north_out[at, :]
    lax.fori_loop(STEPS, STEPS + rows, energy_row, north_ref[at, :] * step * step, unroll=4)
    for h in range(2):
        sensitivity_ref[:, h * LANES:(h + 1) * LANES] = cut(east_out, slots + h)

    for b in range(slots):
        for c in range(comps):
            pltpu.make_async_copy(
                staged.at[b, c], corrected_ref.at[b, c], sems.at[b, c]
            ).wait()


def surface_solve(pieces, weights, block_ids, level_count, bottom, column, block_total):
    scaled, east, north, table = weights
    slots, comps, depth, rows, cols = column.shape
    smem = pl.BlockSpec(memory_space=pltpu.SMEM)
    vmem = pl.BlockSpec(memory_space=pltpu.VMEM)
    anywhere = pl.BlockSpec(memory_space=pl.ANY)
    window = pltpu.VMEM(scaled.shape, jnp.float32)
    coefs = jnp.array(chebyshev_sum(STEPS)[0][::-1], jnp.float32)
    return pl.pallas_call(
        functools.partial(solve_kernel, block_total, len(pieces)),
        in_specs=[smem, smem, smem] + [vmem] * (6 + len(pieces)),
        out_specs=[anywhere, vmem, vmem],
        out_shape=[
            jax.ShapeDtypeStruct(column.shape, jnp.float32),
            jax.ShapeDtypeStruct((rows, 2 * cols), jnp.float32),
            jax.ShapeDtypeStruct((rows, 2 * cols), jnp.float32),
        ],
        scratch_shapes=[
            pltpu.VMEM((len(pieces),) + pieces[0].shape, jnp.float32),
            window,
            window,
            window,
            pltpu.VMEM(column.shape, jnp.float32),
            pltpu.SemaphoreType.DMA((slots, comps)),
        ],
        compiler_params=params(SURFACE_VMEM),
        cost_estimate=pl.CostEstimate(
            flops=14 * STEPS * scaled.size, bytes_accessed=16 * scaled.size, transcendentals=0
        ),
        name="surface_solve",
    )(block_ids, table, coefs, scaled, east, north, level_count, bottom, column, *pieces)


def swap(values, axis, mask):
    count = lax.axis_size(axis)
    return lax.ppermute(values, axis, [(i, i ^ mask) for i in range(count)])


def gather(values, lon_count, lat_count):
    parts = [values] + [swap(values, "gy", 2 * m) for m in range(1, lat_count // 2)]
    line = jnp.stack(parts)
    near = [line] + [swap(line, "gx", m) for m in range(1, lon_count)]
    far = [swap(piece, "gy", 1) for piece in near]
    return near + far


def per_device(adjoint_vel, velocity, drag_coef, level_count, block_ids, bathymetry, land_mask):
    slots = block_ids.shape[0]
    rows, cols = drag_coef.shape[1:]
    lon_count = lax.axis_size("gx")
    lat_count = lax.axis_size("gy")
    block_total = 2 * lon_count * lat_count
    me = jnp.stack([lax.axis_index("gx"), lax.axis_index("gy")]).astype(jnp.int32)

    depths = gather(depth_payload(bathymetry, land_mask, block_ids), lon_count, lat_count)
    forcing, adjoint = column_forcing(adjoint_vel, level_count)
    pieces = gather(forcing, lon_count, lat_count)
    pieces = [piece.reshape((-1, rows, cols)) for piece in pieces]
    column, bottom, drag_gradient = column_mixing(
        adjoint, velocity, drag_coef, level_count, block_ids, pieces[0], block_total
    )
    weights = surface_weights(depths, me, block_ids, rows, lon_count, lat_count)
    corrected, height, sensitivity = surface_solve(
        pieces, weights, block_ids, level_count, bottom, column, block_total
    )
    return corrected, drag_gradient, height, sensitivity


def solution(mesh):
    in_specs = (
        P(("gx", "gy"), None, None, None, None),
        P(("gx", "gy"), None, None, None, None),
        P(("gx", "gy"), None, None),
        P(("gx", "gy"), None, None),
        P(("gx", "gy")),
        P("gy", "gx"),
        P("gy", "gx"),
    )
    out_specs = (
        P(("gx", "gy"), None, None, None, None),
        P(("gx", "gy"), None, None),
        P("gy", "gx"),
        P("gy", "gx"),
    )
    return jax.shard_map(
        per_device, mesh=mesh, in_specs=in_specs, out_specs=out_specs, check_vma=False
    )
```

```python
import functools

import jax
import jax.numpy as jnp
import numpy as np
from jax import lax
from jax.experimental import pallas as pl
from jax.experimental.pallas import tpu as pltpu
from jax.sharding import PartitionSpec as P

STEPS = 32

mix_rate = 0.25
drag_step = 0.5
force_scale = 0.25
pressure_gain = 0.5
surface_shift = 1.0 / 64.0
speed_floor = 0.01

LANES = 128
SUBLANES = 8
MIB = 1024 * 1024
STREAM_VMEM = 48 * MIB
WINDOW_VMEM = 16 * MIB


def chebyshev_sum(total_steps):
    highest = surface_shift + 8.0
    centre = 0.5 * (highest + surface_shift)
    radius = 0.5 * (highest - surface_shift)
    sigma_ratio = centre / radius

    def operate(series):
        shifted = np.zeros_like(series)
        shifted[1] += series[0]
        for k in range(1, len(series) - 1):
            shifted[k + 1] += 0.5 * series[k]
            shifted[k - 1] += 0.5 * series[k]
        return centre * series - radius * shifted

    height = np.zeros(total_steps + 2)
    residual = np.zeros(total_steps + 2)
    residual[0] = 1.0
    direction = residual / centre
    ratio_prev = 1.0 / sigma_ratio
    for _ in range(total_steps):
        height = height + direction
        residual = residual - operate(direction)
        ratio_next = 1.0 / (2.0 * sigma_ratio - ratio_prev)
        direction = ratio_next * ratio_prev * direction + 2.0 * ratio_next / radius * residual
        ratio_prev = ratio_next
    return [float(c) for c in height[:total_steps]], 2.0 / radius


def params(limit):
    return pltpu.CompilerParams(vmem_limit_bytes=limit)


SMEM = pl.BlockSpec(memory_space=pltpu.SMEM)
VMEM = pl.BlockSpec(memory_space=pltpu.VMEM)
ANYWHERE = pl.BlockSpec(memory_space=pl.ANY)
HBM = pl.BlockSpec(memory_space=pltpu.HBM)


def forcing_kernel(levels_ref, adjoint_ref, out_ref, held, sems):
    slots, comps, depth, rows, cols = held.shape
    for b in range(slots):
        for c in range(comps):
            pltpu.make_async_copy(adjoint_ref.at[b, c], held.at[b, c], sems.at[b, c]).start()

    def one_slot(b, carry):
        levels = levels_ref[b]
        total = jnp.zeros((rows, cols), jnp.float32)
        for c in range(comps):
            pltpu.make_async_copy(adjoint_ref.at[b, c], held.at[b, c], sems.at[b, c]).wait()
            for k in range(depth):
                total = total + jnp.where(levels > k, held[b, c, k], 0.0)
        out_ref[b] = force_scale * total
        return carry

    lax.fori_loop(0, slots, one_slot, 0)


def column_forcing(adjoint_vel, level_count):
    slots, comps, depth, rows, cols = adjoint_vel.shape
    return pl.pallas_call(
        forcing_kernel,
        in_specs=[VMEM, HBM],
        out_specs=VMEM,
        out_shape=pltpu.VMEM((slots, rows, cols), jnp.float32),
        scratch_shapes=[
            pltpu.VMEM(adjoint_vel.shape, jnp.float32),
            pltpu.SemaphoreType.DMA((slots, comps)),
        ],
        compiler_params=params(STREAM_VMEM),
        cost_estimate=pl.CostEstimate(
            flops=2 * adjoint_vel.size, bytes_accessed=4 * adjoint_vel.size, transcendentals=0
        ),
        name="column_forcing",
    )(level_count, adjoint_vel)


CHUNK = 8


def mixing_kernel(block_total, ids_ref, levels_ref, drag_ref, adjoint_ref, velocity_ref,
                  forcing_ref, column_ref, bottom_ref, gradient_ref, adjoint, velocity, column,
                  in_sems, out_sems):
    slots, comps, depth, rows, cols = adjoint.shape
    group = 16
    parts = rows // group

    def copies_in(b):
        return (
            pltpu.make_async_copy(adjoint_ref.at[b], adjoint.at[b], in_sems.at[0, b]),
            pltpu.make_async_copy(velocity_ref.at[b], velocity.at[b], in_sems.at[1, b]),
        )

    def copy_out(b):
        return pltpu.make_async_copy(column.at[b], column_ref.at[b], out_sems.at[b])

    for b in range(slots):
        for copy in copies_in(b):
            copy.start()

    def one_group(b, index):
        flag = jnp.where(ids_ref[b] < block_total, 1.0, 0.0)
        span = pl.ds(pl.multiple_of(index * group, group), group)
        levels = levels_ref[b, span, :]
        zero = jnp.zeros(levels.shape, jnp.float32)
        x = [zero, zero]
        once = [zero, zero]
        first_flux = [zero, zero]
        second_flux = [zero, zero]
        flow = [zero, zero]
        field = [zero, zero]
        rate_before = zero
        for low in range(0, depth + 2, CHUNK):
            here = range(low, min(low + CHUNK, depth + 2))
            loaded = {}
            for k in here:
                if k < depth:
                    for c in range(2):
                        loaded[k, c] = (
                            adjoint[b, c, k, span, :],
                            velocity[b, c, k, span, :],
                        )
            done = {}
            for k in here:
                if k < depth:
                    wet = levels > k
                    rate = jnp.where(wet, mix_rate, 0.0)
                    is_bottom_flow = levels == k + 1
                is_bottom = levels == k - 1
                for c in range(2):
                    if k < depth:
                        fresh = jnp.where(wet, loaded[k, c][0], 0.0)
                        flow[c] = jnp.where(
                            is_bottom_flow, loaded[k, c][1].astype(jnp.float32), flow[c]
                        )
                    fresh_once = None
                    if 1 <= k < depth:
                        flux = (fresh - x[c]) * rate
                        fresh_once = x[c] + (flux - first_flux[c])
                        first_flux[c] = flux
                    elif k == depth:
                        fresh_once = x[c] - first_flux[c]
                    if k < depth:
                        x[c] = fresh
                    if 2 <= k:
                        if k <= depth:
                            flux = (fresh_once - once[c]) * rate_before
                            twice = once[c] + (flux - second_flux[c])
                            second_flux[c] = flux
                        else:
                            twice = once[c] - second_flux[c]
                        done[k - 2, c] = twice
                        field[c] = jnp.where(is_bottom, twice, field[c])
                    if fresh_once is not None:
                        once[c] = fresh_once
                if k < depth:
                    rate_before = rate
            for (k, c), value in done.items():
                column[b, c, k, span, :] = value
        speed = jnp.sqrt(flow[0] * flow[0] + flow[1] * flow[1] + speed_floor)
        along = flow[0] * field[0] + flow[1] * field[1]
        ratio = along / speed
        drag = drag_ref[b, span, :]
        for c in range(2):
            bottom_ref[b, c, span, :] = field[c] - drag_step * drag * (
                speed * field[c] + flow[c] * ratio
            )
        gradient_ref[b, span, :] = -drag_step * speed * along * flag

    def one(step, carry):
        b = lax.div(step, parts)
        index = lax.rem(step, parts)

        @pl.when(index == 0)
        def _():
            for copy in copies_in(b):
                copy.wait()

        one_group(b, index)

        @pl.when(index == parts - 1)
        def _():
            copy_out(b).start()

        return carry

    lax.fori_loop(0, slots * parts, one, 0)
    for b in range(slots):
        copy_out(b).wait()


def column_mixing(adjoint_vel, velocity, drag_coef, level_count, block_ids, forcing, block_total):
    slots, comps, depth, rows, cols = adjoint_vel.shape
    return pl.pallas_call(
        functools.partial(mixing_kernel, block_total),
        in_specs=[SMEM, VMEM, VMEM, HBM, HBM, ANYWHERE],
        out_specs=[HBM, VMEM, VMEM],
        out_shape=[
            jax.ShapeDtypeStruct(adjoint_vel.shape, jnp.float32),
            jax.ShapeDtypeStruct((slots, comps, rows, cols), jnp.float32),
            jax.ShapeDtypeStruct((slots, rows, cols), jnp.float32),
        ],
        scratch_shapes=[
            pltpu.VMEM(adjoint_vel.shape, adjoint_vel.dtype),
            pltpu.VMEM(velocity.shape, velocity.dtype),
            pltpu.VMEM(adjoint_vel.shape, jnp.float32),
            pltpu.SemaphoreType.DMA((2, slots)),
            pltpu.SemaphoreType.DMA((slots,)),
        ],
        compiler_params=params(STREAM_VMEM),
        cost_estimate=pl.CostEstimate(
            flops=14 * adjoint_vel.size, bytes_accessed=10 * adjoint_vel.size, transcendentals=0
        ),
        name="column_mixing",
    )(block_ids, level_count, drag_coef, adjoint_vel, velocity, forcing)


WINDOWS = 8
STRIPS = LANES // WINDOWS
PAD = SUBLANES
WIDTH = LANES + 2 * STEPS
PITCH = WIDTH + 2 * PAD
NEIGHBOURS = [(down, right) for down in (-1, 0, 1) for right in (0, 1, -1)]


def window_height(rows):
    return rows + 2 * STEPS


def window_places(me_ref, ids_ref, slots, lon_count, lat_count):
    places = []
    for w in range(slots + 2):
        if w < slots:
            block = jnp.where(ids_ref[w] < 2 * lon_count * lat_count, ids_ref[w], 0)
        else:
            block = (me_ref[0] * lat_count + me_ref[1]) * 2 + (w - slots)
        pair = lax.div(block, 2)
        lat = lax.rem(pair, lat_count)
        column = lax.div(pair, lat_count) * 2 + lax.rem(block, 2)
        places.append((lat, column))
    return places


def put_window(natural, w, rows, blocks, lane):
    for i in range(3):
        here, east, west = blocks[3 * i:3 * i + 3]
        sides = jnp.where(lane < STEPS, east, jnp.where(lane >= LANES - STEPS, west, 0.0))
        start = w * window_height(rows) + i * rows
        natural[0, start:start + rows, :] = here
        natural[1, start:start + rows, :] = sides


def clear_rest(natural, windows, rows):
    start = windows * window_height(rows)
    natural[:, start:, :] = jnp.zeros((2, natural.shape[1] - start, LANES), jnp.float32)


def turn(natural, deep, put):
    for i in range(deep):
        put(i, STEPS, natural[0, pl.ds(i, LANES, stride=deep), :].T)
        sides = natural[1, pl.ds(i, LANES, stride=deep), :].T
        put(i, STEPS + LANES, sides[:STEPS])
        put(i, 0, sides[LANES - STEPS:])


def depth_kernel(ids_ref, bathymetry_ref, mask_ref, out_ref):
    rows = bathymetry_ref.shape[0]
    scaled = bathymetry_ref[...] * mask_ref[...].astype(jnp.float32)
    out_ref[0:rows, :] = scaled[:, :LANES]
    out_ref[rows:2 * rows, :] = scaled[:, LANES:]
    lane = lax.broadcasted_iota(jnp.int32, (SUBLANES, LANES), 1)
    listed = jnp.zeros((SUBLANES, LANES), jnp.int32)
    for s in range(ids_ref.shape[0]):
        listed = jnp.where(lane == s, ids_ref[s], listed)
    out_ref[2 * rows:2 * rows + SUBLANES, :] = listed.astype(jnp.float32)


def depth_payload(bathymetry, land_mask, block_ids):
    rows = bathymetry.shape[0]
    return pl.pallas_call(
        depth_kernel,
        in_specs=[SMEM, VMEM, VMEM],
        out_specs=VMEM,
        out_shape=pltpu.VMEM((2 * rows + SUBLANES, LANES), jnp.float32),
        compiler_params=params(STREAM_VMEM),
        name="depth_payload",
    )(block_ids, bathymetry, land_mask)


def weights_kernel(slots, lon_count, lat_count, me_ref, ids_ref, near_ref, far_ref,
                   scaled_ref, east_ref, north_ref, table_ref,
                   natural, all_ids, places_of, sems):
    half = lat_count // 2
    count = lon_count * half
    rows = (near_ref.shape[1] - SUBLANES) // 2
    deep = window_height(rows) // STRIPS
    column_count = 2 * lon_count
    parts = (near_ref, far_ref)
    copies = [
        pltpu.make_async_copy(
            parts[p].at[:, pl.ds(2 * rows, SUBLANES), :], all_ids.at[p], sems.at[p]
        )
        for p in range(2)
    ]
    for copy in copies:
        copy.start()

    def load(lat, column):
        inside = (lat >= 0) & (lat < lat_count) & (column >= 0) & (column < column_count)
        lat_safe = jnp.clip(lat, 0, lat_count - 1)
        column_safe = jnp.clip(column, 0, column_count - 1)
        lon_xor = lax.div(column_safe, 2) ^ me_ref[0]
        lat_xor = lat_safe ^ me_ref[1]
        place = lon_xor * half + lax.div(lat_xor, 2)
        start = pl.multiple_of(lax.rem(column_safe, 2) * rows, SUBLANES)
        near = near_ref[place, pl.ds(start, rows), :]
        far = far_ref[place, pl.ds(start, rows), :]
        here = jnp.where(lax.rem(lat_xor, 2) == 0, near, far)
        return here * jnp.where(inside, 1.0, 0.0)

    lane = lax.broadcasted_iota(jnp.int32, (rows, LANES), 1)
    places = window_places(me_ref, ids_ref, slots, lon_count, lat_count)
    for w, (lat, column) in enumerate(places):
        blocks = [load(lat + down, column + right) for down, right in NEIGHBOURS]
        put_window(natural, w, rows, blocks, lane)
    clear_rest(natural, slots + 2, rows)

    for copy in copies:
        copy.wait()

    def one_device(n, carry):
        for p in range(2):
            for s in range(slots):
                block = all_ids[p, n, 0, s].astype(jnp.int32)
                places_of[block] = (p * count + n) * slots + s
        return carry

    lax.fori_loop(0, count, one_device, 0)
    for w, (lat, column) in enumerate(places):
        for n, (down, right) in enumerate(NEIGHBOURS):
            lat_safe = jnp.clip(lat + down, 0, lat_count - 1)
            column_safe = jnp.clip(column + right, 0, column_count - 1)
            block = (lax.div(column_safe, 2) * lat_count + lat_safe) * 2 + lax.rem(column_safe, 2)
            table_ref[w * len(NEIGHBOURS) + n] = places_of[block]

    def put(i, x, values):
        start = i * PITCH + PAD + x
        scaled_ref[start:start + values.shape[0], :] = values

    turn(natural, deep, put)
    zeros = jnp.zeros((PAD, LANES), jnp.float32)
    for ref, count_of in ((scaled_ref, deep), (east_ref, deep), (north_ref, deep + 1)):
        for i in range(count_of):
            ref[i * PITCH:i * PITCH + PAD, :] = zeros
            ref[(i + 1) * PITCH - PAD:(i + 1) * PITCH, :] = zeros

    strip = lax.rem(lax.broadcasted_iota(jnp.int32, (SUBLANES, LANES), 1), STRIPS)
    scale = chebyshev_sum(STEPS)[1]
    first_scale = jnp.where(strip == 0, 0.0, scale)
    last_scale = jnp.where(strip == STRIPS - 1, 0.0, scale)

    def one_chunk(chunk, carry):
        at = [pl.multiple_of(i * PITCH + PAD + chunk * SUBLANES, SUBLANES) for i in range(deep)]
        here = [scaled_ref[pl.ds(a, SUBLANES), :] for a in at]
        easts = [scaled_ref[pl.ds(a + 1, SUBLANES), :] for a in at]
        above = pltpu.roll(here[-1], 1, 1)
        below = pltpu.roll(here[0], LANES - 1, 1)
        out = [(east_ref, at[i], scale * jnp.sqrt(here[i] * easts[i])) for i in range(deep)]
        out.append((north_ref, at[0], first_scale * jnp.sqrt(above * here[0])))
        for i in range(deep - 1):
            out.append((north_ref, at[i + 1], scale * jnp.sqrt(here[i] * here[i + 1])))
        out.append((north_ref, at[-1] + PITCH, last_scale * jnp.sqrt(here[-1] * below)))
        for ref, a, value in out:
            ref[pl.ds(pl.multiple_of(a, SUBLANES), SUBLANES), :] = value
        return carry

    lax.fori_loop(0, WIDTH // SUBLANES, one_chunk, 0)


def surface_weights(near, far, me, block_ids, rows, lon_count, lat_count):
    slots = block_ids.shape[0]
    height = window_height(rows)
    assert slots + 2 <= WINDOWS and height % STRIPS == 0 and near.shape[-1] == LANES
    deep = height // STRIPS
    shape = jax.ShapeDtypeStruct((deep * PITCH, LANES), jnp.float32)
    return pl.pallas_call(
        functools.partial(weights_kernel, slots, lon_count, lat_count),
        in_specs=[SMEM, SMEM, VMEM, VMEM],
        out_specs=[VMEM, VMEM, VMEM, SMEM],
        out_shape=[
            shape,
            shape,
            jax.ShapeDtypeStruct(((deep + 1) * PITCH, LANES), jnp.float32),
            jax.ShapeDtypeStruct(((slots + 2) * len(NEIGHBOURS),), jnp.int32),
        ],
        scratch_shapes=[
            pltpu.VMEM((2, WINDOWS * height, LANES), jnp.float32),
            pltpu.SMEM((2, near.shape[0], SUBLANES, LANES), jnp.float32),
            pltpu.SMEM((2 * lon_count * lat_count + 1,), jnp.int32),
            pltpu.SemaphoreType.DMA((2,)),
        ],
        compiler_params=params(WINDOW_VMEM),
        cost_estimate=pl.CostEstimate(
            flops=0, bytes_accessed=8 * MIB, transcendentals=0
        ),
        name="surface_weights",
    )(me, block_ids, near, far)


GROUP = 4


def solve_kernel(block_total, pieces, ids_ref, table_ref, coefs_ref, scaled_ref, east_ref,
                 north_ref, levels_ref, bottom_ref, column_ref, *rest):
    piece_refs = rest[:pieces]
    corrected_ref, height_ref, sensitivity_ref = rest[pieces:pieces + 3]
    (forcing, natural, source, even, odd, extra, column, in_sems, out_sems) = rest[pieces + 3:]
    slots, comps, depth, rows, cols = column.shape
    height = window_height(rows)
    deep = height // STRIPS
    for b in range(slots):
        pltpu.make_async_copy(column_ref.at[b], column.at[b], in_sems.at[b]).start()

    for p in range(pieces):
        forcing[p] = piece_refs[p][...]
    lane = lax.broadcasted_iota(jnp.int32, (rows, LANES), 1)
    per_piece = forcing.shape[1]
    for w in range(slots + 2):
        blocks = []
        for n in range(len(NEIGHBOURS)):
            place = table_ref[w * len(NEIGHBOURS) + n]
            blocks.append(forcing[lax.div(place, per_piece), lax.rem(place, per_piece)])
        put_window(natural, w, rows, blocks, lane)
    clear_rest(natural, slots + 2, rows)

    coefs, step_scale = chebyshev_sum(STEPS)

    def put(i, x, values):
        start = i * PITCH + PAD + x
        stop = start + values.shape[0]
        values = jnp.where(scaled_ref[start:stop, :] > 0.0, values, 0.0)
        source[start:stop, :] = values
        even[start:stop, :] = coefs[STEPS - 1] * values
        odd[start:stop, :] = jnp.zeros_like(values)

    zeros = jnp.zeros((PAD, LANES), jnp.float32)
    for ref in (even, odd):
        for i in range(deep):
            ref[i * PITCH:i * PITCH + PAD, :] = zeros
            ref[(i + 1) * PITCH - PAD:(i + 1) * PITCH, :] = zeros
    turn(natural, deep, put)

    def starts(chunk):
        return [pl.multiple_of(i * PITCH + PAD + chunk * SUBLANES, SUBLANES) for i in range(deep)]

    def at(ref, start, shift=0):
        return ref[pl.ds(start + shift, SUBLANES), :]

    def apply(current, target, coef, gain, low, count):
        def group(index, carry):
            out = []
            for g in range(GROUP):
                places = starts(low + index * GROUP + g)
                here = [at(current, a) for a in places]
                above = pltpu.roll(here[-1], 1, 1)
                below = pltpu.roll(here[0], LANES - 1, 1)
                north_before = at(north_ref, places[0]) * (above - here[0])
                for i, a in enumerate(places):
                    value = here[i]
                    under = here[i + 1] if i + 1 < deep else below
                    north = at(north_ref, a, PITCH) * (value - under)
                    east = at(east_ref, a) * (value - at(current, a, 1))
                    west = at(east_ref, a, -1) * (value - at(current, a, -1))
                    pushed = (value + value) - ((east + west) + (north - north_before))
                    if gain != 1.0:
                        pushed = gain * pushed
                    out.append((a, (coef * at(source, a) - at(target, a)) + pushed))
                    north_before = north
            for a, value in out:
                target[pl.ds(a, SUBLANES), :] = value
            return carry

        lax.fori_loop(0, count, group, 0)

    chunks = WIDTH // SUBLANES

    def bounds(m):
        low = m // (2 * SUBLANES) * 2
        return low, (chunks - 2 * low + GROUP - 1) // GROUP

    runs = []
    for m in range(1, STEPS - 1, 2):
        if runs and runs[-1][1] == bounds(m):
            runs[-1][2] += 1
        else:
            runs.append([m, bounds(m), 1])
    for first, (low, count), pairs in runs:
        def two_steps(pair, carry, first=first, low=low, count=count):
            m = first + 2 * pair
            apply(even, odd, coefs_ref[m], 1.0, low, count)
            apply(odd, even, coefs_ref[m + 1], 1.0, low, count)
            return carry

        lax.fori_loop(0, pairs, two_steps, 0)
    low, count = bounds(STEPS - 1)
    apply(even, odd, coefs[0], 0.5, low, count)

    undo = 0.25 / step_scale

    def differences(index, carry):
        places = starts(STEPS // SUBLANES + index)
        here = [at(odd, a) for a in places]
        above = pltpu.roll(here[-1], 1, 1)
        below = pltpu.roll(here[0], LANES - 1, 1)
        step = here[0] - above
        north_before = at(north_ref, places[0]) * step * step
        out = []
        for i, a in enumerate(places):
            value = here[i]
            under = here[i + 1] if i + 1 < deep else below
            north_step = under - value
            east_step = at(odd, a, 1) - value
            west_step = value - at(odd, a, -1)
            north = at(north_ref, a, PITCH) * north_step * north_step
            east = at(east_ref, a) * east_step * east_step
            west = at(east_ref, a, -1) * west_step * west_step
            energy = (east + west) + (north + north_before)
            out.append((even, a, east_step))
            out.append((source, a, north_step))
            out.append((extra, a, undo * energy / jnp.maximum(at(scaled_ref, a), 0.25)))
            north_before = north
        for ref, a, value in out:
            ref[pl.ds(a, SUBLANES), :] = value
        return carry

    lax.fori_loop(0, LANES // SUBLANES, differences, 0)

    def turn_back(ref, tile):
        for i in range(deep):
            start = i * PITCH + PAD + STEPS
            natural[tile, pl.ds(i, LANES, stride=deep), :] = ref[start:start + LANES, :].T

    def cut(tile, w):
        start = w * height + STEPS
        return natural[tile, start:start + rows, :]

    turn_back(even, 0)
    turn_back(source, 1)
    for b in range(slots):
        pltpu.make_async_copy(column_ref.at[b], column.at[b], in_sems.at[b]).wait()
        flag = jnp.where(ids_ref[b] < block_total, 1, 0)
        levels = levels_ref[b] * flag
        for c in range(comps):
            push = pressure_gain * cut(c, b)
            lowest = bottom_ref[b, c] - push
            for start in range(0, depth, 8):
                out = []
                for k in range(start, min(start + 8, depth)):
                    value = jnp.where(levels == k + 1, lowest, column[b, c, k] - push)
                    out.append((k, jnp.where(levels > k, value, 0.0)))
                for k, value in out:
                    column[b, c, k] = value
            pltpu.make_async_copy(
                column.at[b, c], corrected_ref.at[b, c], out_sems.at[b, c]
            ).start()

    turn_back(odd, 0)
    turn_back(extra, 1)
    for h in range(2):
        height_ref[:, h * LANES:(h + 1) * LANES] = cut(0, slots + h)
        sensitivity_ref[:, h * LANES:(h + 1) * LANES] = cut(1, slots + h)

    for b in range(slots):
        for c in range(comps):
            pltpu.make_async_copy(
                column.at[b, c], corrected_ref.at[b, c], out_sems.at[b, c]
            ).wait()


def surface_solve(pieces, weights, block_ids, level_count, bottom, column, block_total):
    scaled, east, north, table = weights
    slots, comps, depth, rows, cols = column.shape
    turned = pltpu.VMEM(scaled.shape, jnp.float32)
    coefs = jnp.array(chebyshev_sum(STEPS)[0][::-1], jnp.float32)
    return pl.pallas_call(
        functools.partial(solve_kernel, block_total, len(pieces)),
        in_specs=[SMEM, SMEM, SMEM] + [VMEM] * 5 + [HBM] + [VMEM] * len(pieces),
        out_specs=[HBM, VMEM, VMEM],
        out_shape=[
            jax.ShapeDtypeStruct(column.shape, jnp.float32),
            jax.ShapeDtypeStruct((rows, 2 * cols), jnp.float32),
            jax.ShapeDtypeStruct((rows, 2 * cols), jnp.float32),
        ],
        scratch_shapes=[
            pltpu.VMEM((len(pieces),) + pieces[0].shape, jnp.float32),
            pltpu.VMEM((2, WINDOWS * window_height(rows), LANES), jnp.float32),
            turned,
            turned,
            turned,
            turned,
            pltpu.VMEM(column.shape, jnp.float32),
            pltpu.SemaphoreType.DMA((slots,)),
            pltpu.SemaphoreType.DMA((slots, comps)),
        ],
        compiler_params=params(STREAM_VMEM),
        cost_estimate=pl.CostEstimate(
            flops=14 * STEPS * scaled.size, bytes_accessed=16 * scaled.size, transcendentals=0
        ),
        name="surface_solve",
    )(block_ids, table, coefs, scaled, east, north, level_count, bottom, column, *pieces)


def stack_kernel(parts, *refs):
    out_ref = refs[-1]
    for p in range(parts):
        out_ref[p] = refs[p][...]


def stack_after(parts, token):
    return pl.pallas_call(
        functools.partial(stack_kernel, len(parts)),
        in_specs=[VMEM] * len(parts) + [ANYWHERE],
        out_specs=VMEM,
        out_shape=jax.ShapeDtypeStruct((len(parts),) + parts[0].shape, jnp.float32),
        compiler_params=params(WINDOW_VMEM),
        name="stack_after",
    )(*parts, token)


def same_kernel(*refs):
    pass


def same_after(values, token):
    return pl.pallas_call(
        same_kernel,
        in_specs=[ANYWHERE, ANYWHERE],
        out_specs=ANYWHERE,
        out_shape=jax.ShapeDtypeStruct(values.shape, values.dtype),
        input_output_aliases={0: 0},
        name="same_after",
    )(values, token)


def swap(values, axis, mask):
    count = lax.axis_size(axis)
    return lax.ppermute(values, axis, [(i, i ^ mask) for i in range(count)])


def per_device(adjoint_vel, velocity, drag_coef, level_count, block_ids, bathymetry, land_mask):
    slots = block_ids.shape[0]
    rows, cols = drag_coef.shape[1:]
    lon_count = lax.axis_size("gx")
    lat_count = lax.axis_size("gy")
    half = lat_count // 2
    block_total = 2 * lon_count * lat_count
    me = jnp.stack([lax.axis_index("gx"), lax.axis_index("gy")]).astype(jnp.int32)

    depths = depth_payload(bathymetry, land_mask, block_ids)
    depth_parts = [depths] + [swap(depths, "gy", 2 * m) for m in range(1, half)]
    forcing = column_forcing(adjoint_vel, level_count)

    parts = [forcing] + [swap(forcing, "gy", 2 * m) for m in range(1, half)]
    near_depths = stack_after(depth_parts, forcing)
    near_depths = [near_depths] + [swap(near_depths, "gx", m) for m in range(1, lon_count)]
    column, bottom, drag_gradient = column_mixing(
        adjoint_vel, velocity, drag_coef, level_count, block_ids, forcing, block_total
    )
    line = stack_after(parts, bottom)

    near = [line] + [swap(line, "gx", m) for m in range(1, lon_count)]
    near_depths = stack_after(near_depths, line)
    near_depths = near_depths.reshape((lon_count * half,) + depths.shape)
    far_depths = swap(near_depths, "gy", 1)
    weights = surface_weights(
        near_depths, far_depths, me, block_ids, rows, lon_count, lat_count
    )
    near[1] = same_after(near[1], weights[1])
    far = [swap(piece, "gy", 1) for piece in near]
    pieces = [piece.reshape((-1, rows, cols)) for piece in near + far]

    corrected, height, sensitivity = surface_solve(
        pieces, weights, block_ids, level_count, bottom, column, block_total
    )
    return corrected, drag_gradient, height, sensitivity


def solution(mesh):
    in_specs = (
        P(("gx", "gy"), None, None, None, None),
        P(("gx", "gy"), None, None, None, None),
        P(("gx", "gy"), None, None),
        P(("gx", "gy"), None, None),
        P(("gx", "gy")),
        P("gy", "gx"),
        P("gy", "gx"),
    )
    out_specs = (
        P(("gx", "gy"), None, None, None, None),
        P(("gx", "gy"), None, None),
        P("gy", "gx"),
        P("gy", "gx"),
    )
    return jax.shard_map(
        per_device, mesh=mesh, in_specs=in_specs, out_specs=out_specs, check_vma=False
    )
```

```python
import functools

import jax
import jax.numpy as jnp
import numpy as np
from jax import lax
from jax.experimental import pallas as pl
from jax.experimental.pallas import tpu as pltpu
from jax.sharding import PartitionSpec as P

STEPS = 32

mix_rate = 0.25
drag_step = 0.5
force_scale = 0.25
pressure_gain = 0.5
surface_shift = 1.0 / 64.0
speed_floor = 0.01

LANES = 128
SUBLANES = 8
MIB = 1024 * 1024
FIRST_VMEM = 61 * MIB
MIXING_VMEM = 52 * MIB
SOLVE_VMEM = 50 * MIB
WINDOW_VMEM = 16 * MIB


def chebyshev_sum(total_steps):
    highest = surface_shift + 8.0
    centre = 0.5 * (highest + surface_shift)
    radius = 0.5 * (highest - surface_shift)
    sigma_ratio = centre / radius

    def operate(series):
        shifted = np.zeros_like(series)
        shifted[1] += series[0]
        for k in range(1, len(series) - 1):
            shifted[k + 1] += 0.5 * series[k]
            shifted[k - 1] += 0.5 * series[k]
        return centre * series - radius * shifted

    height = np.zeros(total_steps + 2)
    residual = np.zeros(total_steps + 2)
    residual[0] = 1.0
    direction = residual / centre
    ratio_prev = 1.0 / sigma_ratio
    for _ in range(total_steps):
        height = height + direction
        residual = residual - operate(direction)
        ratio_next = 1.0 / (2.0 * sigma_ratio - ratio_prev)
        direction = ratio_next * ratio_prev * direction + 2.0 * ratio_next / radius * residual
        ratio_prev = ratio_next
    return [float(c) for c in height[:total_steps]], 2.0 / radius


def params(limit):
    return pltpu.CompilerParams(vmem_limit_bytes=limit)


SMEM = pl.BlockSpec(memory_space=pltpu.SMEM)
VMEM = pl.BlockSpec(memory_space=pltpu.VMEM)
ANYWHERE = pl.BlockSpec(memory_space=pl.ANY)
HBM = pl.BlockSpec(memory_space=pltpu.HBM)


def forcing_kernel(levels_ref, adjoint_ref, out_ref, held, sems):
    slots, comps, depth, rows, cols = held.shape
    for b in range(slots):
        for c in range(comps):
            pltpu.make_async_copy(adjoint_ref.at[b, c], held.at[b, c], sems.at[b, c]).start()

    def one_slot(b, carry):
        levels = levels_ref[b]
        total = jnp.zeros((rows, cols), jnp.float32)
        for c in range(comps):
            pltpu.make_async_copy(adjoint_ref.at[b, c], held.at[b, c], sems.at[b, c]).wait()
            for k in range(depth):
                total = total + jnp.where(levels > k, held[b, c, k], 0.0)
        out_ref[b] = force_scale * total
        return carry

    lax.fori_loop(0, slots, one_slot, 0)


def column_forcing(adjoint_vel, level_count):
    slots, comps, depth, rows, cols = adjoint_vel.shape
    return pl.pallas_call(
        forcing_kernel,
        in_specs=[VMEM, HBM],
        out_specs=VMEM,
        out_shape=pltpu.VMEM((slots, rows, cols), jnp.float32),
        scratch_shapes=[
            pltpu.VMEM(adjoint_vel.shape, jnp.float32),
            pltpu.SemaphoreType.DMA((slots, comps)),
        ],
        compiler_params=params(FIRST_VMEM),
        cost_estimate=pl.CostEstimate(
            flops=2 * adjoint_vel.size, bytes_accessed=4 * adjoint_vel.size, transcendentals=0
        ),
        name="column_forcing",
    )(level_count, adjoint_vel)


CHUNK = 8


def mixing_kernel(block_total, first, earlier, ids_ref, levels_ref, drag_ref, adjoint_ref,
                  velocity_ref, after_ref, *rest):
    if earlier:
        for target, ref in zip(rest[3:5], rest[:2]):
            target[0:first] = ref[...]
        rest = rest[2:]
    column_ref, bottom_ref, gradient_ref, adjoint, velocity, column, in_sems, out_sems = rest
    slots, comps, depth, rows, cols = adjoint.shape
    group = 16
    parts = rows // group

    def copies_in(b):
        return (
            pltpu.make_async_copy(adjoint_ref.at[first + b], adjoint.at[b], in_sems.at[0, b]),
            pltpu.make_async_copy(velocity_ref.at[first + b], velocity.at[b], in_sems.at[1, b]),
        )

    def copy_out(b):
        return pltpu.make_async_copy(column.at[b], column_ref.at[b], out_sems.at[b])

    for b in range(slots):
        for copy in copies_in(b):
            copy.start()

    def one_group(b, index):
        flag = jnp.where(ids_ref[first + b] < block_total, 1.0, 0.0)
        span = pl.ds(pl.multiple_of(index * group, group), group)
        levels = levels_ref[first + b, span, :]
        zero = jnp.zeros(levels.shape, jnp.float32)
        x = [zero, zero]
        once = [zero, zero]
        first_flux = [zero, zero]
        second_flux = [zero, zero]
        flow = [zero, zero]
        field = [zero, zero]
        rate_before = zero
        for low in range(0, depth + 2, CHUNK):
            here = range(low, min(low + CHUNK, depth + 2))
            loaded = {}
            for k in here:
                if k < depth:
                    for c in range(2):
                        loaded[k, c] = (
                            adjoint[b, c, k, span, :],
                            velocity[b, c, k, span, :],
                        )
            done = {}
            for k in here:
                if k < depth:
                    wet = levels > k
                    rate = jnp.where(wet, mix_rate, 0.0)
                    is_bottom_flow = levels == k + 1
                is_bottom = levels == k - 1
                for c in range(2):
                    if k < depth:
                        fresh = jnp.where(wet, loaded[k, c][0], 0.0)
                        flow[c] = jnp.where(
                            is_bottom_flow, loaded[k, c][1].astype(jnp.float32), flow[c]
                        )
                    fresh_once = None
                    if 1 <= k < depth:
                        flux = (fresh - x[c]) * rate
                        fresh_once = x[c] + (flux - first_flux[c])
                        first_flux[c] = flux
                    elif k == depth:
                        fresh_once = x[c] - first_flux[c]
                    if k < depth:
                        x[c] = fresh
                    if 2 <= k:
                        if k <= depth:
                            flux = (fresh_once - once[c]) * rate_before
                            twice = once[c] + (flux - second_flux[c])
                            second_flux[c] = flux
                        else:
                            twice = once[c] - second_flux[c]
                        done[k - 2, c] = twice
                        field[c] = jnp.where(is_bottom, twice, field[c])
                    if fresh_once is not None:
                        once[c] = fresh_once
                if k < depth:
                    rate_before = rate
            for (k, c), value in done.items():
                column[b, c, k, span, :] = value
        speed = jnp.sqrt(flow[0] * flow[0] + flow[1] * flow[1] + speed_floor)
        along = flow[0] * field[0] + flow[1] * field[1]
        ratio = along / speed
        drag = drag_ref[first + b, span, :]
        for c in range(2):
            bottom_ref[first + b, c, span, :] = field[c] - drag_step * drag * (
                speed * field[c] + flow[c] * ratio
            )
        gradient_ref[first + b, span, :] = -drag_step * speed * along * flag

    def one(step, carry):
        b = lax.div(step, parts)
        index = lax.rem(step, parts)

        @pl.when(index == 0)
        def _():
            for copy in copies_in(b):
                copy.wait()

        one_group(b, index)

        @pl.when(index == parts - 1)
        def _():
            copy_out(b).start()

        return carry

    lax.fori_loop(0, slots * parts, one, 0)
    for b in range(slots):
        copy_out(b).wait()


def column_mixing(adjoint_vel, velocity, drag_coef, level_count, block_ids, after, block_total,
                  first, last, earlier=()):
    comps, depth, rows, cols = adjoint_vel.shape[1:]
    part = (last - first, comps, depth, rows, cols)
    size = (last - first) * comps * depth * rows * cols
    return pl.pallas_call(
        functools.partial(mixing_kernel, block_total, first, len(earlier)),
        in_specs=[SMEM, VMEM, VMEM, HBM, HBM, ANYWHERE] + [VMEM] * len(earlier),
        out_specs=[HBM, VMEM, VMEM],
        out_shape=[
            pltpu.HBM(part, jnp.float32),
            pltpu.VMEM((last, comps, rows, cols), jnp.float32),
            pltpu.HBM((last, rows, cols), jnp.float32),
        ],
        scratch_shapes=[
            pltpu.VMEM(part, adjoint_vel.dtype),
            pltpu.VMEM(part, velocity.dtype),
            pltpu.VMEM(part, jnp.float32),
            pltpu.SemaphoreType.DMA((2, last - first)),
            pltpu.SemaphoreType.DMA((last - first,)),
        ],
        compiler_params=params(MIXING_VMEM),
        cost_estimate=pl.CostEstimate(
            flops=14 * size, bytes_accessed=10 * size, transcendentals=0
        ),
        name="column_mixing",
    )(block_ids, level_count, drag_coef, adjoint_vel, velocity, after, *earlier)


PAD = SUBLANES
WIDTH = LANES + 2 * STEPS
PITCH = WIDTH + 2 * PAD
NEIGHBOURS = [(down, right) for down in (-1, 0, 1) for right in (0, 1, -1)]


def window_shape(slots, rows):
    strips = LANES // (slots + 2)
    deep = pl.cdiv(rows + 2 * STEPS, strips)
    return strips, deep, strips * deep


def window_places(me_ref, ids_ref, slots, lon_count, lat_count):
    places = []
    for w in range(slots + 2):
        if w < slots:
            block = jnp.where(ids_ref[w] < 2 * lon_count * lat_count, ids_ref[w], 0)
        else:
            block = (me_ref[0] * lat_count + me_ref[1]) * 2 + (w - slots)
        pair = lax.div(block, 2)
        lat = lax.rem(pair, lat_count)
        column = lax.div(pair, lat_count) * 2 + lax.rem(block, 2)
        places.append((lat, column))
    return places


def put_window(natural, base, rows, blocks, lane):
    for i in range(3):
        here, east, west = blocks[3 * i:3 * i + 3]
        sides = jnp.where(lane < STEPS, east, jnp.where(lane >= LANES - STEPS, west, 0.0))
        start = base + i * rows
        natural[0, start:start + rows, :] = here
        natural[1, start:start + rows, :] = sides


def turn(natural, deep, put):
    for i in range(deep):
        put(i, STEPS, natural[0, pl.ds(i, LANES, stride=deep), :].T)
        sides = natural[1, pl.ds(i, LANES, stride=deep), :].T
        put(i, STEPS + LANES, sides[:STEPS])
        put(i, 0, sides[LANES - STEPS:])


def depth_kernel(ids_ref, bathymetry_ref, mask_ref, out_ref, ids, bathymetry, mask, sems):
    copies = [
        pltpu.make_async_copy(ids_ref, ids, sems.at[0]),
        pltpu.make_async_copy(bathymetry_ref, bathymetry, sems.at[1]),
        pltpu.make_async_copy(mask_ref, mask, sems.at[2]),
    ]
    for copy in copies:
        copy.start()
    for copy in copies:
        copy.wait()
    rows = bathymetry.shape[0]
    scaled = bathymetry[...] * mask[...].astype(jnp.float32)
    out_ref[0:rows, :] = scaled[:, :LANES]
    out_ref[rows:2 * rows, :] = scaled[:, LANES:]
    lane = lax.broadcasted_iota(jnp.int32, (SUBLANES, LANES), 1)
    listed = jnp.zeros((SUBLANES, LANES), jnp.int32)
    for s in range(ids.shape[0]):
        listed = jnp.where(lane == s, ids[s], listed)
    out_ref[2 * rows:2 * rows + SUBLANES, :] = listed.astype(jnp.float32)


def depth_payload(bathymetry, land_mask, block_ids):
    rows = bathymetry.shape[0]
    return pl.pallas_call(
        depth_kernel,
        in_specs=[HBM, HBM, HBM],
        out_specs=VMEM,
        out_shape=pltpu.VMEM((2 * rows + SUBLANES, LANES), jnp.float32),
        scratch_shapes=[
            pltpu.SMEM(block_ids.shape, jnp.int32),
            pltpu.VMEM(bathymetry.shape, jnp.float32),
            pltpu.VMEM(land_mask.shape, jnp.int32),
            pltpu.SemaphoreType.DMA((3,)),
        ],
        compiler_params=params(FIRST_VMEM),
        name="depth_payload",
    )(block_ids, bathymetry, land_mask)


def weights_kernel(slots, lon_count, lat_count, me_ref, ids_ref, near_ref, far_ref,
                   scaled_ref, east_ref, north_ref, table_ref,
                   natural, all_ids, places_of, sems):
    half = lat_count // 2
    count = lon_count * half
    rows = (near_ref.shape[1] - SUBLANES) // 2
    strips, deep, tall = window_shape(slots, rows)
    column_count = 2 * lon_count
    parts = (near_ref, far_ref)
    copies = [
        pltpu.make_async_copy(
            parts[p].at[:, pl.ds(2 * rows, SUBLANES), :], all_ids.at[p], sems.at[p]
        )
        for p in range(2)
    ]
    for copy in copies:
        copy.start()
    natural[...] = jnp.zeros_like(natural)

    def load(lat, column):
        inside = (lat >= 0) & (lat < lat_count) & (column >= 0) & (column < column_count)
        lat_safe = jnp.clip(lat, 0, lat_count - 1)
        column_safe = jnp.clip(column, 0, column_count - 1)
        lon_xor = lax.div(column_safe, 2) ^ me_ref[0]
        lat_xor = lat_safe ^ me_ref[1]
        place = lon_xor * half + lax.div(lat_xor, 2)
        start = pl.multiple_of(lax.rem(column_safe, 2) * rows, SUBLANES)
        near = near_ref[place, pl.ds(start, rows), :]
        far = far_ref[place, pl.ds(start, rows), :]
        here = jnp.where(lax.rem(lat_xor, 2) == 0, near, far)
        return here * jnp.where(inside, 1.0, 0.0)

    lane = lax.broadcasted_iota(jnp.int32, (rows, LANES), 1)
    places = window_places(me_ref, ids_ref, slots, lon_count, lat_count)
    for w, (lat, column) in enumerate(places):
        blocks = [load(lat + down, column + right) for down, right in NEIGHBOURS]
        put_window(natural, w * tall, rows, blocks, lane)

    for copy in copies:
        copy.wait()

    def one_device(n, carry):
        for p in range(2):
            for s in range(slots):
                block = all_ids[p, n, 0, s].astype(jnp.int32)
                places_of[block] = (p * count + n) * slots + s
        return carry

    lax.fori_loop(0, count, one_device, 0)
    for w, (lat, column) in enumerate(places):
        for n, (down, right) in enumerate(NEIGHBOURS):
            lat_safe = jnp.clip(lat + down, 0, lat_count - 1)
            column_safe = jnp.clip(column + right, 0, column_count - 1)
            block = (lax.div(column_safe, 2) * lat_count + lat_safe) * 2 + lax.rem(column_safe, 2)
            table_ref[w * len(NEIGHBOURS) + n] = places_of[block]

    def put(i, x, values):
        start = i * PITCH + PAD + x
        scaled_ref[start:start + values.shape[0], :] = values

    turn(natural, deep, put)
    zeros = jnp.zeros((PAD, LANES), jnp.float32)
    for ref, count_of in ((scaled_ref, deep), (east_ref, deep), (north_ref, deep + 1)):
        for i in range(count_of):
            ref[i * PITCH:i * PITCH + PAD, :] = zeros
            ref[(i + 1) * PITCH - PAD:(i + 1) * PITCH, :] = zeros

    strip = lax.rem(lax.broadcasted_iota(jnp.int32, (SUBLANES, LANES), 1), strips)
    scale = chebyshev_sum(STEPS)[1]
    first_scale = jnp.where(strip == 0, 0.0, scale)
    last_scale = jnp.where(strip == strips - 1, 0.0, scale)

    def one_chunk(chunk, carry):
        at = [pl.multiple_of(i * PITCH + PAD + chunk * SUBLANES, SUBLANES) for i in range(deep)]
        here = [scaled_ref[pl.ds(a, SUBLANES), :] for a in at]
        easts = [scaled_ref[pl.ds(a + 1, SUBLANES), :] for a in at]
        above = pltpu.roll(here[-1], 1, 1)
        below = pltpu.roll(here[0], LANES - 1, 1)
        out = [(east_ref, at[i], scale * jnp.sqrt(here[i] * easts[i])) for i in range(deep)]
        out.append((north_ref, at[0], first_scale * jnp.sqrt(above * here[0])))
        for i in range(deep - 1):
            out.append((north_ref, at[i + 1], scale * jnp.sqrt(here[i] * here[i + 1])))
        out.append((north_ref, at[-1] + PITCH, last_scale * jnp.sqrt(here[-1] * below)))
        for ref, a, value in out:
            ref[pl.ds(pl.multiple_of(a, SUBLANES), SUBLANES), :] = value
        return carry

    lax.fori_loop(0, WIDTH // SUBLANES, one_chunk, 0)


def surface_weights(near, far, me, block_ids, rows, lon_count, lat_count):
    slots = block_ids.shape[0]
    assert near.shape[-1] == LANES
    strips, deep, tall = window_shape(slots, rows)
    shape = jax.ShapeDtypeStruct((deep * PITCH, LANES), jnp.float32)
    return pl.pallas_call(
        functools.partial(weights_kernel, slots, lon_count, lat_count),
        in_specs=[SMEM, SMEM, VMEM, VMEM],
        out_specs=[VMEM, VMEM, VMEM, SMEM],
        out_shape=[
            shape,
            shape,
            jax.ShapeDtypeStruct(((deep + 1) * PITCH, LANES), jnp.float32),
            jax.ShapeDtypeStruct(((slots + 2) * len(NEIGHBOURS),), jnp.int32),
        ],
        scratch_shapes=[
            pltpu.VMEM((2, LANES * deep, LANES), jnp.float32),
            pltpu.SMEM((2, near.shape[0], SUBLANES, LANES), jnp.float32),
            pltpu.SMEM((2 * lon_count * lat_count + 1,), jnp.int32),
            pltpu.SemaphoreType.DMA((2,)),
        ],
        compiler_params=params(WINDOW_VMEM),
        cost_estimate=pl.CostEstimate(
            flops=0, bytes_accessed=8 * MIB, transcendentals=0
        ),
        name="surface_weights",
    )(me, block_ids, near, far)


GROUP = 4


def solve_kernel(block_total, pieces, ids_ref, table_ref, coefs_ref, scaled_ref, east_ref,
                 north_ref, levels_ref, bottom_ref, *rest):
    column_refs, rest = rest[:2], rest[2:]
    piece_refs = rest[:pieces]
    corrected_ref, height_ref, sensitivity_ref = rest[pieces:pieces + 3]
    (forcing, natural, source, even, odd, extra, column, in_sems, out_sems) = rest[pieces + 3:]
    slots, comps, depth, rows, cols = column.shape
    strips, deep, tall = window_shape(slots, rows)
    first_slots = column_refs[0].shape[0]

    def copy_in(b):
        ref = column_refs[b // first_slots]
        return pltpu.make_async_copy(ref.at[b % first_slots], column.at[b], in_sems.at[b])

    for b in range(slots):
        copy_in(b).start()

    base = 0
    for ref in piece_refs:
        forcing[base:base + ref.shape[0]] = ref[...]
        base += ref.shape[0]
    lane = lax.broadcasted_iota(jnp.int32, (rows, LANES), 1)
    for w in range(slots + 2):
        places = [table_ref[w * len(NEIGHBOURS) + n] for n in range(len(NEIGHBOURS))]
        put_window(natural, w * tall, rows, [forcing[place] for place in places], lane)

    coefs, step_scale = chebyshev_sum(STEPS)

    def put(i, x, values):
        start = i * PITCH + PAD + x
        stop = start + values.shape[0]
        values = jnp.where(scaled_ref[start:stop, :] > 0.0, values, 0.0)
        source[start:stop, :] = values
        even[start:stop, :] = coefs[STEPS - 1] * values
        odd[start:stop, :] = jnp.zeros_like(values)

    zeros = jnp.zeros((PAD, LANES), jnp.float32)
    for ref in (even, odd):
        for i in range(deep):
            ref[i * PITCH:i * PITCH + PAD, :] = zeros
            ref[(i + 1) * PITCH - PAD:(i + 1) * PITCH, :] = zeros
    turn(natural, deep, put)

    def starts(chunk):
        return [pl.multiple_of(i * PITCH + PAD + chunk * SUBLANES, SUBLANES) for i in range(deep)]

    def at(ref, start, shift=0):
        return ref[pl.ds(start + shift, SUBLANES), :]

    def apply(current, target, coef, gain, low, count):
        def group(index, carry):
            out = []
            for g in range(GROUP):
                places = starts(low + index * GROUP + g)
                here = [at(current, a) for a in places]
                above = pltpu.roll(here[-1], 1, 1)
                below = pltpu.roll(here[0], LANES - 1, 1)
                north_before = at(north_ref, places[0]) * (above - here[0])
                for i, a in enumerate(places):
                    value = here[i]
                    under = here[i + 1] if i + 1 < deep else below
                    north = at(north_ref, a, PITCH) * (value - under)
                    east = at(east_ref, a) * (value - at(current, a, 1))
                    west = at(east_ref, a, -1) * (value - at(current, a, -1))
                    pushed = (value + value) - ((east + west) + (north - north_before))
                    if gain != 1.0:
                        pushed = gain * pushed
                    out.append((a, (coef * at(source, a) - at(target, a)) + pushed))
                    north_before = north
            for a, value in out:
                target[pl.ds(a, SUBLANES), :] = value
            return carry

        lax.fori_loop(0, count, group, 0)

    chunks = WIDTH // SUBLANES

    def bounds(m):
        low = m // (2 * SUBLANES) * 2
        return low, (chunks - 2 * low + GROUP - 1) // GROUP

    runs = []
    for m in range(1, STEPS - 1, 2):
        if runs and runs[-1][1] == bounds(m):
            runs[-1][2] += 1
        else:
            runs.append([m, bounds(m), 1])
    for first, (low, count), pairs in runs:
        def two_steps(pair, carry, first=first, low=low, count=count):
            m = first + 2 * pair
            apply(even, odd, coefs_ref[m], 1.0, low, count)
            apply(odd, even, coefs_ref[m + 1], 1.0, low, count)
            return carry

        lax.fori_loop(0, pairs, two_steps, 0)
    low, count = bounds(STEPS - 1)
    apply(even, odd, coefs[0], 0.5, low, count)

    undo = 0.25 / step_scale

    def differences(index, carry):
        places = starts(STEPS // SUBLANES + index)
        here = [at(odd, a) for a in places]
        above = pltpu.roll(here[-1], 1, 1)
        below = pltpu.roll(here[0], LANES - 1, 1)
        step = here[0] - above
        north_before = at(north_ref, places[0]) * step * step
        out = []
        for i, a in enumerate(places):
            value = here[i]
            under = here[i + 1] if i + 1 < deep else below
            north_step = under - value
            east_step = at(odd, a, 1) - value
            west_step = value - at(odd, a, -1)
            north = at(north_ref, a, PITCH) * north_step * north_step
            east = at(east_ref, a) * east_step * east_step
            west = at(east_ref, a, -1) * west_step * west_step
            energy = (east + west) + (north + north_before)
            out.append((even, a, east_step))
            out.append((source, a, north_step))
            out.append((extra, a, undo * energy / jnp.maximum(at(scaled_ref, a), 0.25)))
            north_before = north
        for ref, a, value in out:
            ref[pl.ds(a, SUBLANES), :] = value
        return carry

    lax.fori_loop(0, LANES // SUBLANES, differences, 0)

    def turn_back(ref, tile):
        for i in range(deep):
            start = i * PITCH + PAD + STEPS
            natural[tile, pl.ds(i, LANES, stride=deep), :] = ref[start:start + LANES, :].T

    def cut(tile, w):
        start = w * tall + STEPS
        return natural[tile, start:start + rows, :]

    turn_back(even, 0)
    turn_back(source, 1)
    for b in range(slots):
        copy_in(b).wait()
        flag = jnp.where(ids_ref[b] < block_total, 1, 0)
        levels = levels_ref[b] * flag
        for c in range(comps):
            push = pressure_gain * cut(c, b)
            lowest = bottom_ref[b, c] - push
            for start in range(0, depth, 8):
                out = []
                for k in range(start, min(start + 8, depth)):
                    value = jnp.where(levels == k + 1, lowest, column[b, c, k] - push)
                    out.append((k, jnp.where(levels > k, value, 0.0)))
                for k, value in out:
                    column[b, c, k] = value
            pltpu.make_async_copy(
                column.at[b, c], corrected_ref.at[b, c], out_sems.at[b, c]
            ).start()

    turn_back(odd, 0)
    turn_back(extra, 1)
    for h in range(2):
        height_ref[:, h * LANES:(h + 1) * LANES] = cut(0, slots + h)
        sensitivity_ref[:, h * LANES:(h + 1) * LANES] = cut(1, slots + h)

    for b in range(slots):
        for c in range(comps):
            pltpu.make_async_copy(
                column.at[b, c], corrected_ref.at[b, c], out_sems.at[b, c]
            ).wait()


def surface_solve(pieces, weights, block_ids, level_count, bottom, columns, block_total):
    scaled, east, north, table = weights
    comps, depth, rows, cols = columns[0].shape[1:]
    slots = level_count.shape[0]
    deep = window_shape(slots, rows)[1]
    full = (slots, comps, depth, rows, cols)
    turned = pltpu.VMEM(scaled.shape, jnp.float32)
    coefs = jnp.array(chebyshev_sum(STEPS)[0][::-1], jnp.float32)
    return pl.pallas_call(
        functools.partial(solve_kernel, block_total, len(pieces)),
        in_specs=[SMEM, SMEM, SMEM] + [VMEM] * 5 + [HBM] * 2 + [VMEM] * len(pieces),
        out_specs=[HBM, VMEM, VMEM],
        out_shape=[
            jax.ShapeDtypeStruct(full, jnp.float32),
            jax.ShapeDtypeStruct((rows, 2 * cols), jnp.float32),
            jax.ShapeDtypeStruct((rows, 2 * cols), jnp.float32),
        ],
        scratch_shapes=[
            pltpu.VMEM((sum(p.shape[0] for p in pieces), rows, cols), jnp.float32),
            pltpu.VMEM((2, LANES * deep, LANES), jnp.float32),
            turned,
            turned,
            turned,
            turned,
            pltpu.VMEM(full, jnp.float32),
            pltpu.SemaphoreType.DMA((slots,)),
            pltpu.SemaphoreType.DMA((slots, comps)),
        ],
        compiler_params=params(SOLVE_VMEM),
        cost_estimate=pl.CostEstimate(
            flops=14 * STEPS * scaled.size, bytes_accessed=16 * scaled.size, transcendentals=0
        ),
        name="surface_solve",
    )(block_ids, table, coefs, scaled, east, north, level_count, bottom, *columns, *pieces)


def stack_kernel(parts, *refs):
    out_ref = refs[-1]
    for p in range(parts):
        out_ref[p] = refs[p][...]


def stack_after(parts, *tokens):
    return pl.pallas_call(
        functools.partial(stack_kernel, len(parts)),
        in_specs=[VMEM] * len(parts) + [ANYWHERE] * len(tokens),
        out_specs=VMEM,
        out_shape=jax.ShapeDtypeStruct((len(parts),) + parts[0].shape, jnp.float32),
        compiler_params=params(WINDOW_VMEM),
        name="stack_after",
    )(*parts, *tokens)


def swap(values, axis, mask):
    count = lax.axis_size(axis)
    return lax.ppermute(values, axis, [(i, i ^ mask) for i in range(count)])


def per_device(adjoint_vel, velocity, drag_coef, level_count, block_ids, bathymetry, land_mask):
    slots = block_ids.shape[0]
    rows, cols = drag_coef.shape[1:]
    lon_count = lax.axis_size("gx")
    lat_count = lax.axis_size("gy")
    half = lat_count // 2
    block_total = 2 * lon_count * lat_count
    me = jnp.stack([lax.axis_index("gx"), lax.axis_index("gy")]).astype(jnp.int32)

    depths = depth_payload(bathymetry, land_mask, block_ids)
    depth_parts = [depths] + [swap(depths, "gy", 2 * m) for m in range(1, half)]
    forcing = column_forcing(adjoint_vel, level_count)

    parts = [forcing] + [swap(forcing, "gy", 2 * m) for m in range(1, half)]
    near_depths = stack_after(depth_parts, forcing)
    near_depths = [near_depths] + [swap(near_depths, "gx", m) for m in range(1, lon_count)]
    columns = (adjoint_vel, velocity, drag_coef, level_count, block_ids)
    middle = (slots + 1) // 2
    first_column, *first_rest = column_mixing(*columns, forcing, block_total, 0, middle)
    line = stack_after(parts, first_rest[0])

    near = [swap(line, "gx", m) for m in range(1, lon_count)]
    far_line = swap(line, "gy", 1)
    near_depths = stack_after(near_depths, line)
    near_depths = near_depths.reshape((lon_count * half,) + depths.shape)
    far_depths = swap(near_depths, "gy", 1)
    last_column, bottom, drag_gradient = column_mixing(
        *columns, line, block_total, middle, slots, first_rest
    )
    weights = surface_weights(
        near_depths, far_depths, me, block_ids, rows, lon_count, lat_count
    )

    near = stack_after(near, bottom, weights[0])
    far = swap(near, "gy", 1)
    pieces = [piece.reshape((-1, rows, cols)) for piece in (line, near, far_line, far)]

    corrected, height, sensitivity = surface_solve(
        pieces, weights, block_ids, level_count, bottom, (first_column, last_column), block_total
    )
    return corrected, drag_gradient, height, sensitivity


def solution(mesh):
    in_specs = (
        P(("gx", "gy"), None, None, None, None),
        P(("gx", "gy"), None, None, None, None),
        P(("gx", "gy"), None, None),
        P(("gx", "gy"), None, None),
        P(("gx", "gy")),
        P("gy", "gx"),
        P("gy", "gx"),
    )
    out_specs = (
        P(("gx", "gy"), None, None, None, None),
        P(("gx", "gy"), None, None),
        P("gy", "gx"),
        P("gy", "gx"),
    )
    return jax.shard_map(
        per_device, mesh=mesh, in_specs=in_specs, out_specs=out_specs, check_vma=False
    )
```

```python
import functools

import jax
import jax.numpy as jnp
import numpy as np
from jax import lax
from jax.experimental import pallas as pl
from jax.experimental.pallas import tpu as pltpu
from jax.sharding import PartitionSpec as P

STEPS = 32

mix_rate = 0.25
drag_step = 0.5
force_scale = 0.25
pressure_gain = 0.5
surface_shift = 1.0 / 64.0
speed_floor = 0.01

LANES = 128
SUBLANES = 8
MIB = 1024 * 1024
FIRST_VMEM = 61 * MIB
MIXING_VMEM = 52 * MIB
SOLVE_VMEM = 50 * MIB
WINDOW_VMEM = 16 * MIB


def chebyshev_sum(total_steps):
    highest = surface_shift + 8.0
    centre = 0.5 * (highest + surface_shift)
    radius = 0.5 * (highest - surface_shift)
    sigma_ratio = centre / radius

    def operate(series):
        shifted = np.zeros_like(series)
        shifted[1] += series[0]
        for k in range(1, len(series) - 1):
            shifted[k + 1] += 0.5 * series[k]
            shifted[k - 1] += 0.5 * series[k]
        return centre * series - radius * shifted

    height = np.zeros(total_steps + 2)
    residual = np.zeros(total_steps + 2)
    residual[0] = 1.0
    direction = residual / centre
    ratio_prev = 1.0 / sigma_ratio
    for _ in range(total_steps):
        height = height + direction
        residual = residual - operate(direction)
        ratio_next = 1.0 / (2.0 * sigma_ratio - ratio_prev)
        direction = ratio_next * ratio_prev * direction + 2.0 * ratio_next / radius * residual
        ratio_prev = ratio_next
    return [float(c) for c in height[:total_steps]], 2.0 / radius


def params(limit):
    return pltpu.CompilerParams(vmem_limit_bytes=limit)


SMEM = pl.BlockSpec(memory_space=pltpu.SMEM)
VMEM = pl.BlockSpec(memory_space=pltpu.VMEM)
ANYWHERE = pl.BlockSpec(memory_space=pl.ANY)
HBM = pl.BlockSpec(memory_space=pltpu.HBM)


def forcing_kernel(levels_ref, adjoint_ref, out_ref, levels_held, held, level_sem, sems):
    slots, comps, depth, rows, cols = held.shape
    level_copy = pltpu.make_async_copy(levels_ref, levels_held, level_sem)
    level_copy.start()
    for b in range(slots):
        for c in range(comps):
            pltpu.make_async_copy(adjoint_ref.at[b, c], held.at[b, c], sems.at[b, c]).start()
    level_copy.wait()

    def one_slot(b, carry):
        levels = levels_held[b]
        total = jnp.zeros((rows, cols), jnp.float32)
        for c in range(comps):
            pltpu.make_async_copy(adjoint_ref.at[b, c], held.at[b, c], sems.at[b, c]).wait()
            for k in range(depth):
                total = total + jnp.where(levels > k, held[b, c, k], 0.0)
        out_ref[b] = force_scale * total
        return carry

    lax.fori_loop(0, slots, one_slot, 0)


def column_forcing(adjoint_vel, level_count):
    slots, comps, depth, rows, cols = adjoint_vel.shape
    return pl.pallas_call(
        forcing_kernel,
        in_specs=[HBM, HBM],
        out_specs=VMEM,
        out_shape=pltpu.VMEM((slots, rows, cols), jnp.float32),
        scratch_shapes=[
            pltpu.VMEM(level_count.shape, jnp.int32),
            pltpu.VMEM(adjoint_vel.shape, jnp.float32),
            pltpu.SemaphoreType.DMA,
            pltpu.SemaphoreType.DMA((slots, comps)),
        ],
        compiler_params=params(FIRST_VMEM),
        cost_estimate=pl.CostEstimate(
            flops=2 * adjoint_vel.size, bytes_accessed=4 * adjoint_vel.size, transcendentals=0
        ),
        name="column_forcing",
    )(level_count, adjoint_vel)


CHUNK = 8


def mixing_kernel(block_total, ids_ref, levels_ref, drag_ref, adjoint_ref, velocity_ref,
                  after_ref, column_ref, bottom_ref, gradient_ref, adjoint, velocity, column,
                  in_sems, out_sems):
    slots, comps, depth, rows, cols = adjoint.shape
    group = 16
    parts = rows // group

    def copies_in(b):
        return (
            pltpu.make_async_copy(adjoint_ref.at[b], adjoint.at[b], in_sems.at[0, b]),
            pltpu.make_async_copy(velocity_ref.at[b], velocity.at[b], in_sems.at[1, b]),
        )

    def copy_out(b):
        return pltpu.make_async_copy(
            column.at[b, :, pl.ds(2, depth)], column_ref.at[b], out_sems.at[b]
        )

    for b in range(slots):
        for copy in copies_in(b):
            copy.start()

    def one_group(b, index):
        flag = jnp.where(ids_ref[b] < block_total, 1.0, 0.0)
        span = pl.ds(pl.multiple_of(index * group, group), group)
        levels = levels_ref[b, span, :]
        zero = jnp.zeros(levels.shape, jnp.float32)

        def some_levels(chunk, carry):
            x, once, first_flux, second_flux, flow, field, rate_before = carry
            x, once, first_flux, second_flux = list(x), list(once), list(first_flux), list(second_flux)
            flow, field = list(flow), list(field)
            base = chunk * CHUNK
            loaded = []
            for j in range(CHUNK):
                k = jnp.minimum(base + j, depth - 1)
                loaded.append([
                    (adjoint[b, c, k, span, :], velocity[b, c, k, span, :]) for c in range(2)
                ])
            done = []
            for j in range(CHUNK):
                k = base + j
                wet = levels > k
                rate = jnp.where(wet, jnp.where(k > 0, mix_rate, 0.0), 0.0)
                is_bottom_flow = levels == k + 1
                is_bottom = levels == k - 1
                for c in range(2):
                    fresh = jnp.where(wet, loaded[j][c][0], 0.0)
                    flow[c] = jnp.where(
                        is_bottom_flow, loaded[j][c][1].astype(jnp.float32), flow[c]
                    )
                    flux = (fresh - x[c]) * rate
                    fresh_once = x[c] + (flux - first_flux[c])
                    first_flux[c] = flux
                    x[c] = fresh
                    flux = (fresh_once - once[c]) * rate_before
                    twice = once[c] + (flux - second_flux[c])
                    second_flux[c] = flux
                    once[c] = fresh_once
                    field[c] = jnp.where(is_bottom, twice, field[c])
                    done.append((c, k, twice))
                rate_before = rate
            for c, k, value in done:
                column[b, c, k, span, :] = value
            return (
                tuple(x), tuple(once), tuple(first_flux), tuple(second_flux),
                tuple(flow), tuple(field), rate_before,
            )

        start = ((zero, zero),) * 6 + (zero,)
        end = lax.fori_loop(0, (depth + 2) // CHUNK, some_levels, start)
        flow, field = end[4], end[5]
        speed = jnp.sqrt(flow[0] * flow[0] + flow[1] * flow[1] + speed_floor)
        along = flow[0] * field[0] + flow[1] * field[1]
        ratio = along / speed
        drag = drag_ref[b, span, :]
        for c in range(2):
            bottom_ref[b, c, span, :] = field[c] - drag_step * drag * (
                speed * field[c] + flow[c] * ratio
            )
        gradient_ref[b, span, :] = -drag_step * speed * along * flag

    def one(step, carry):
        b = lax.div(step, parts)
        index = lax.rem(step, parts)

        @pl.when(index == 0)
        def _():
            for copy in copies_in(b):
                copy.wait()

        one_group(b, index)

        @pl.when(index == parts - 1)
        def _():
            copy_out(b).start()

        return carry

    lax.fori_loop(0, slots * parts, one, 0)
    for b in range(slots):
        copy_out(b).wait()


def column_mixing(adjoint_vel, velocity, drag_coef, level_count, block_ids, after, block_total):
    slots, comps, depth, rows, cols = adjoint_vel.shape
    assert (depth + 2) % CHUNK == 0
    size = adjoint_vel.size
    return pl.pallas_call(
        functools.partial(mixing_kernel, block_total),
        in_specs=[SMEM, VMEM, VMEM, HBM, HBM, ANYWHERE],
        out_specs=[HBM, VMEM, VMEM],
        out_shape=[
            pltpu.HBM(adjoint_vel.shape, jnp.float32),
            pltpu.VMEM((slots, comps, rows, cols), jnp.float32),
            pltpu.HBM((slots, rows, cols), jnp.float32),
        ],
        scratch_shapes=[
            pltpu.VMEM(adjoint_vel.shape, adjoint_vel.dtype),
            pltpu.VMEM(velocity.shape, velocity.dtype),
            pltpu.VMEM((slots, comps, depth + 2, rows, cols), jnp.float32),
            pltpu.SemaphoreType.DMA((2, slots)),
            pltpu.SemaphoreType.DMA((slots,)),
        ],
        compiler_params=params(MIXING_VMEM),
        cost_estimate=pl.CostEstimate(
            flops=14 * size, bytes_accessed=10 * size, transcendentals=0
        ),
        name="column_mixing",
    )(block_ids, level_count, drag_coef, adjoint_vel, velocity, after)


PAD = SUBLANES
WIDTH = LANES + 2 * STEPS
PITCH = WIDTH + 2 * PAD
NEIGHBOURS = [(down, right) for down in (-1, 0, 1) for right in (0, 1, -1)]


def window_shape(slots, rows):
    strips = LANES // (slots + 2)
    deep = pl.cdiv(rows + 2 * STEPS, strips)
    return strips, deep, strips * deep


def log2(count):
    bits = count.bit_length() - 1
    assert 1 << bits == count
    return bits


def window_places(me_ref, ids_ref, slots, lon_count, lat_count):
    places = []
    for w in range(slots + 2):
        if w < slots:
            block = jnp.where(ids_ref[w] < 2 * lon_count * lat_count, ids_ref[w], 0)
        else:
            block = (me_ref[0] * lat_count + me_ref[1]) * 2 + (w - slots)
        pair = block >> 1
        column = (pair >> log2(lat_count)) * 2 + (block & 1)
        places.append((pair & (lat_count - 1), column))
    return places


def put_window(natural, base, rows, blocks, lane):
    for i in range(3):
        here, east, west = blocks[3 * i:3 * i + 3]
        sides = jnp.where(lane < STEPS, east, jnp.where(lane >= LANES - STEPS, west, 0.0))
        start = base + i * rows
        natural[0, start:start + rows, :] = here
        natural[1, start:start + rows, :] = sides


def turn(natural, deep, put):
    for i in range(deep):
        put(i, STEPS, natural[0, pl.ds(i, LANES, stride=deep), :].T)
        sides = natural[1, pl.ds(i, LANES, stride=deep), :].T
        put(i, STEPS + LANES, sides[:STEPS])
        put(i, 0, sides[LANES - STEPS:])


def depth_kernel(ids_ref, bathymetry_ref, mask_ref, out_ref, ids, bathymetry, mask, sems):
    copies = [
        pltpu.make_async_copy(ids_ref, ids, sems.at[0]),
        pltpu.make_async_copy(bathymetry_ref, bathymetry, sems.at[1]),
        pltpu.make_async_copy(mask_ref, mask, sems.at[2]),
    ]
    for copy in copies:
        copy.start()
    for copy in copies:
        copy.wait()
    rows = bathymetry.shape[0]
    scaled = bathymetry[...] * mask[...].astype(jnp.float32)
    out_ref[0:rows, :] = scaled[:, :LANES]
    out_ref[rows:2 * rows, :] = scaled[:, LANES:]
    lane = lax.broadcasted_iota(jnp.int32, (SUBLANES, LANES), 1)
    listed = jnp.zeros((SUBLANES, LANES), jnp.int32)
    for s in range(ids.shape[0]):
        listed = jnp.where(lane == s, ids[s], listed)
    out_ref[2 * rows:2 * rows + SUBLANES, :] = listed.astype(jnp.float32)


def depth_payload(bathymetry, land_mask, block_ids):
    rows = bathymetry.shape[0]
    return pl.pallas_call(
        depth_kernel,
        in_specs=[HBM, HBM, HBM],
        out_specs=VMEM,
        out_shape=pltpu.VMEM((2 * rows + SUBLANES, LANES), jnp.float32),
        scratch_shapes=[
            pltpu.SMEM(block_ids.shape, jnp.int32),
            pltpu.VMEM(bathymetry.shape, jnp.float32),
            pltpu.VMEM(land_mask.shape, jnp.int32),
            pltpu.SemaphoreType.DMA((3,)),
        ],
        compiler_params=params(FIRST_VMEM),
        name="depth_payload",
    )(block_ids, bathymetry, land_mask)


def weights_kernel(slots, lon_count, lat_count, me_ref, ids_ref, near_ref, far_ref,
                   scaled_ref, east_ref, north_ref, table_ref,
                   natural, all_ids, places_of, sems):
    half = lat_count // 2
    count = lon_count * half
    rows = (near_ref.shape[1] - SUBLANES) // 2
    strips, deep, tall = window_shape(slots, rows)
    column_count = 2 * lon_count
    parts = (near_ref, far_ref)
    copies = [
        pltpu.make_async_copy(
            parts[p].at[:, pl.ds(2 * rows, 1), :], all_ids.at[p], sems.at[p]
        )
        for p in range(2)
    ]
    for copy in copies:
        copy.start()
    natural[...] = jnp.zeros_like(natural)

    def load(lat, column):
        inside = (lat >= 0) & (lat < lat_count) & (column >= 0) & (column < column_count)
        lat_safe = jnp.clip(lat, 0, lat_count - 1)
        column_safe = jnp.clip(column, 0, column_count - 1)
        lon_xor = (column_safe >> 1) ^ me_ref[0]
        lat_xor = lat_safe ^ me_ref[1]
        place = lon_xor * half + (lat_xor >> 1)
        start = pl.multiple_of((column_safe & 1) * rows, SUBLANES)
        near = near_ref[place, pl.ds(start, rows), :]
        far = far_ref[place, pl.ds(start, rows), :]
        here = jnp.where((lat_xor & 1) == 0, near, far)
        return here * jnp.where(inside, 1.0, 0.0)

    lane = lax.broadcasted_iota(jnp.int32, (rows, LANES), 1)
    places = window_places(me_ref, ids_ref, slots, lon_count, lat_count)
    for w, (lat, column) in enumerate(places):
        blocks = [load(lat + down, column + right) for down, right in NEIGHBOURS]
        put_window(natural, w * tall, rows, blocks, lane)

    for copy in copies:
        copy.wait()

    def one_device(n, carry):
        for p in range(2):
            for s in range(slots):
                block = all_ids[p, n, 0, s].astype(jnp.int32)
                places_of[block] = (p * count + n) * slots + s
        return carry

    lax.fori_loop(0, count, one_device, 0)
    for w, (lat, column) in enumerate(places):
        for n, (down, right) in enumerate(NEIGHBOURS):
            lat_safe = jnp.clip(lat + down, 0, lat_count - 1)
            column_safe = jnp.clip(column + right, 0, column_count - 1)
            block = ((column_safe >> 1) * lat_count + lat_safe) * 2 + (column_safe & 1)
            table_ref[w * len(NEIGHBOURS) + n] = places_of[block]

    def put(i, x, values):
        start = i * PITCH + PAD + x
        scaled_ref[start:start + values.shape[0], :] = values

    turn(natural, deep, put)
    zeros = jnp.zeros((PAD, LANES), jnp.float32)
    for ref, count_of in ((scaled_ref, deep), (east_ref, deep), (north_ref, deep + 1)):
        for i in range(count_of):
            ref[i * PITCH:i * PITCH + PAD, :] = zeros
            ref[(i + 1) * PITCH - PAD:(i + 1) * PITCH, :] = zeros

    strip = lax.rem(lax.broadcasted_iota(jnp.int32, (SUBLANES, LANES), 1), strips)
    scale = chebyshev_sum(STEPS)[1]
    first_scale = jnp.where(strip == 0, 0.0, scale)
    last_scale = jnp.where(strip == strips - 1, 0.0, scale)

    def one_chunk(chunk, carry):
        at = [pl.multiple_of(i * PITCH + PAD + chunk * SUBLANES, SUBLANES) for i in range(deep)]
        here = [scaled_ref[pl.ds(a, SUBLANES), :] for a in at]
        easts = [scaled_ref[pl.ds(a + 1, SUBLANES), :] for a in at]
        above = pltpu.roll(here[-1], 1, 1)
        below = pltpu.roll(here[0], LANES - 1, 1)
        out = [(east_ref, at[i], scale * jnp.sqrt(here[i] * easts[i])) for i in range(deep)]
        out.append((north_ref, at[0], first_scale * jnp.sqrt(above * here[0])))
        for i in range(deep - 1):
            out.append((north_ref, at[i + 1], scale * jnp.sqrt(here[i] * here[i + 1])))
        out.append((north_ref, at[-1] + PITCH, last_scale * jnp.sqrt(here[-1] * below)))
        for ref, a, value in out:
            ref[pl.ds(pl.multiple_of(a, SUBLANES), SUBLANES), :] = value
        return carry

    lax.fori_loop(0, WIDTH // SUBLANES, one_chunk, 0)


def surface_weights(near, far, me, block_ids, rows, lon_count, lat_count):
    slots = block_ids.shape[0]
    assert near.shape[-1] == LANES
    strips, deep, tall = window_shape(slots, rows)
    shape = jax.ShapeDtypeStruct((deep * PITCH, LANES), jnp.float32)
    return pl.pallas_call(
        functools.partial(weights_kernel, slots, lon_count, lat_count),
        in_specs=[SMEM, SMEM, VMEM, VMEM],
        out_specs=[VMEM, VMEM, VMEM, SMEM],
        out_shape=[
            shape,
            shape,
            jax.ShapeDtypeStruct(((deep + 1) * PITCH, LANES), jnp.float32),
            jax.ShapeDtypeStruct(((slots + 2) * len(NEIGHBOURS),), jnp.int32),
        ],
        scratch_shapes=[
            pltpu.VMEM((2, LANES * deep, LANES), jnp.float32),
            pltpu.SMEM((2, near.shape[0], 1, LANES), jnp.float32),
            pltpu.SMEM((2 * lon_count * lat_count + 1,), jnp.int32),
            pltpu.SemaphoreType.DMA((2,)),
        ],
        compiler_params=params(WINDOW_VMEM),
        cost_estimate=pl.CostEstimate(
            flops=0, bytes_accessed=8 * MIB, transcendentals=0
        ),
        name="surface_weights",
    )(me, block_ids, near, far)


def solve_kernel(block_total, ids_ref, table_ref, coefs_ref, scaled_ref, east_ref, north_ref,
                 levels_ref, bottom_ref, column_ref, near_ref, far_ref,
                 corrected_ref, height_ref, sensitivity_ref,
                 natural, source, even, odd, extra, column, in_sems, out_sems):
    slots, comps, depth, rows, cols = column.shape
    strips, deep, tall = window_shape(slots, rows)

    def copy_in(b):
        return pltpu.make_async_copy(column_ref.at[b], column.at[b], in_sems.at[b])

    for b in range(slots):
        copy_in(b).start()

    count = near_ref.shape[0]

    def load(place):
        inner = place & (count - 1)
        return jnp.where(place < count, near_ref[inner], far_ref[inner])

    lane = lax.broadcasted_iota(jnp.int32, (rows, LANES), 1)
    for w in range(slots + 2):
        places = [table_ref[w * len(NEIGHBOURS) + n] for n in range(len(NEIGHBOURS))]
        put_window(natural, w * tall, rows, [load(place) for place in places], lane)

    coefs, step_scale = chebyshev_sum(STEPS)

    def put(i, x, values):
        start = i * PITCH + PAD + x
        stop = start + values.shape[0]
        values = jnp.where(scaled_ref[start:stop, :] > 0.0, values, 0.0)
        source[start:stop, :] = values
        even[start:stop, :] = coefs[STEPS - 1] * values
        odd[start:stop, :] = jnp.zeros_like(values)

    zeros = jnp.zeros((PAD, LANES), jnp.float32)
    for ref in (even, odd):
        for i in range(deep):
            ref[i * PITCH:i * PITCH + PAD, :] = zeros
            ref[(i + 1) * PITCH - PAD:(i + 1) * PITCH, :] = zeros
    turn(natural, deep, put)

    def starts(chunk):
        return [pl.multiple_of(i * PITCH + PAD + chunk * SUBLANES, SUBLANES) for i in range(deep)]

    def at(ref, start, shift=0):
        return ref[pl.ds(start + shift, SUBLANES), :]

    chunks = WIDTH // SUBLANES

    def apply(current, target, coef, gain, low, count):
        size = (chunks - 2 * low) // count

        def group(index, carry):
            out = []
            for g in range(size):
                places = starts(low + index * size + g)
                here = [at(current, a) for a in places]
                above = pltpu.roll(here[-1], 1, 1)
                below = pltpu.roll(here[0], LANES - 1, 1)
                north_before = at(north_ref, places[0]) * (above - here[0])
                for i, a in enumerate(places):
                    value = here[i]
                    under = here[i + 1] if i + 1 < deep else below
                    north = at(north_ref, a, PITCH) * (value - under)
                    east = at(east_ref, a) * (value - at(current, a, 1))
                    west = at(east_ref, a, -1) * (value - at(current, a, -1))
                    pushed = (value + value) - ((east + west) + (north - north_before))
                    if gain != 1.0:
                        pushed = gain * pushed
                    out.append((a, (coef * at(source, a) - at(target, a)) + pushed))
                    north_before = north
            for a, value in out:
                target[pl.ds(a, SUBLANES), :] = value
            return carry

        lax.fori_loop(0, count, group, 0)

    def bounds(m):
        low = m // (2 * SUBLANES) * 2
        count = chunks - 2 * low
        return low, count // (5 if count % 5 == 0 else 4)

    runs = []
    for m in range(1, STEPS - 1, 2):
        if runs and runs[-1][1] == bounds(m):
            runs[-1][2] += 1
        else:
            runs.append([m, bounds(m), 1])
    for first, (low, count), pairs in runs:
        def two_steps(pair, carry, first=first, low=low, count=count):
            m = first + 2 * pair
            apply(even, odd, coefs_ref[m], 1.0, low, count)
            apply(odd, even, coefs_ref[m + 1], 1.0, low, count)
            return carry

        lax.fori_loop(0, pairs, two_steps, 0)
    low, count = bounds(STEPS - 1)
    apply(even, odd, coefs[0], 0.5, low, count)

    undo = 0.25 / step_scale

    def differences(index, carry):
        places = starts(STEPS // SUBLANES + index)
        here = [at(odd, a) for a in places]
        above = pltpu.roll(here[-1], 1, 1)
        below = pltpu.roll(here[0], LANES - 1, 1)
        step = here[0] - above
        north_before = at(north_ref, places[0]) * step * step
        out = []
        for i, a in enumerate(places):
            value = here[i]
            under = here[i + 1] if i + 1 < deep else below
            north_step = under - value
            east_step = at(odd, a, 1) - value
            west_step = value - at(odd, a, -1)
            north = at(north_ref, a, PITCH) * north_step * north_step
            east = at(east_ref, a) * east_step * east_step
            west = at(east_ref, a, -1) * west_step * west_step
            energy = (east + west) + (north + north_before)
            out.append((even, a, east_step))
            out.append((source, a, north_step))
            out.append((extra, a, undo * energy / jnp.maximum(at(scaled_ref, a), 0.25)))
            north_before = north
        for ref, a, value in out:
            ref[pl.ds(a, SUBLANES), :] = value
        return carry

    lax.fori_loop(0, LANES // SUBLANES, differences, 0)

    def turn_back(ref, tile):
        for i in range(deep):
            start = i * PITCH + PAD + STEPS
            natural[tile, pl.ds(i, LANES, stride=deep), :] = ref[start:start + LANES, :].T

    def cut(tile, w):
        start = w * tall + STEPS
        return natural[tile, start:start + rows, :]

    turn_back(even, 0)
    turn_back(source, 1)

    def copy_out(b, c):
        return pltpu.make_async_copy(column.at[b, c], corrected_ref.at[b, c], out_sems.at[b, c])

    def one_part(part, carry):
        b = part >> 1
        c = part & 1

        @pl.when(c == 0)
        def _():
            copy_in(b).wait()

        levels = levels_ref[b] * jnp.where(ids_ref[b] < block_total, 1, 0)
        push = pressure_gain * natural[c, pl.ds(b * tall + STEPS, rows), :]
        lowest = bottom_ref[b, c] - push

        def some_levels(base, size):
            out = []
            for j in range(size):
                k = base + j
                value = jnp.where(levels == k + 1, lowest, column[b, c, k] - push)
                out.append((k, jnp.where(levels > k, value, 0.0)))
            for k, value in out:
                column[b, c, k] = value

        def one_chunk(chunk, inner):
            some_levels(chunk * CHUNK, CHUNK)
            return inner

        lax.fori_loop(0, depth // CHUNK, one_chunk, 0)
        some_levels(depth // CHUNK * CHUNK, depth % CHUNK)
        copy_out(b, c).start()
        return carry

    lax.fori_loop(0, slots * comps, one_part, 0)

    turn_back(odd, 0)
    turn_back(extra, 1)
    for h in range(2):
        height_ref[:, h * LANES:(h + 1) * LANES] = cut(0, slots + h)
        sensitivity_ref[:, h * LANES:(h + 1) * LANES] = cut(1, slots + h)

    for b in range(slots):
        for c in range(comps):
            copy_out(b, c).wait()


def surface_solve(near, far, weights, block_ids, level_count, bottom, column, block_total):
    scaled, east, north, table = weights
    slots, comps, depth, rows, cols = column.shape
    assert comps == 2
    deep = window_shape(slots, rows)[1]
    turned = pltpu.VMEM(scaled.shape, jnp.float32)
    coefs = jnp.array(chebyshev_sum(STEPS)[0][::-1], jnp.float32)
    return pl.pallas_call(
        functools.partial(solve_kernel, block_total),
        in_specs=[SMEM, SMEM, SMEM] + [VMEM] * 5 + [HBM] + [VMEM] * 2,
        out_specs=[HBM, VMEM, VMEM],
        out_shape=[
            jax.ShapeDtypeStruct(column.shape, jnp.float32),
            jax.ShapeDtypeStruct((rows, 2 * cols), jnp.float32),
            jax.ShapeDtypeStruct((rows, 2 * cols), jnp.float32),
        ],
        scratch_shapes=[
            pltpu.VMEM((2, LANES * deep, LANES), jnp.float32),
            turned,
            turned,
            turned,
            turned,
            pltpu.VMEM(column.shape, jnp.float32),
            pltpu.SemaphoreType.DMA((slots,)),
            pltpu.SemaphoreType.DMA((slots, comps)),
        ],
        compiler_params=params(SOLVE_VMEM),
        cost_estimate=pl.CostEstimate(
            flops=14 * STEPS * scaled.size, bytes_accessed=16 * scaled.size, transcendentals=0
        ),
        name="surface_solve",
    )(block_ids, table, coefs, scaled, east, north, level_count, bottom, column, near, far)


def stack_kernel(parts, *refs):
    out_ref = refs[-1]
    for p in range(parts):
        out_ref[p] = refs[p][...]


def stack_after(parts, *tokens):
    return pl.pallas_call(
        functools.partial(stack_kernel, len(parts)),
        in_specs=[VMEM] * len(parts) + [ANYWHERE] * len(tokens),
        out_specs=VMEM,
        out_shape=jax.ShapeDtypeStruct((len(parts),) + parts[0].shape, jnp.float32),
        compiler_params=params(WINDOW_VMEM),
        name="stack_after",
    )(*parts, *tokens)


def swap(values, axis, mask):
    count = lax.axis_size(axis)
    return lax.ppermute(values, axis, [(i, i ^ mask) for i in range(count)])


def per_device(adjoint_vel, velocity, drag_coef, level_count, block_ids, bathymetry, land_mask):
    slots = block_ids.shape[0]
    rows, cols = drag_coef.shape[1:]
    lon_count = lax.axis_size("gx")
    lat_count = lax.axis_size("gy")
    half = lat_count // 2
    block_total = 2 * lon_count * lat_count
    me = jnp.stack([lax.axis_index("gx"), lax.axis_index("gy")]).astype(jnp.int32)

    depths = depth_payload(bathymetry, land_mask, block_ids)
    depth_parts = [depths] + [swap(depths, "gy", 2 * m) for m in range(1, half)]
    forcing = column_forcing(adjoint_vel, level_count)

    parts = [forcing] + [swap(forcing, "gy", 2 * m) for m in range(1, half)]
    near_depths = stack_after(depth_parts, forcing)
    near_depths = [near_depths] + [swap(near_depths, "gx", m) for m in range(1, lon_count)]
    line = stack_after(parts)

    near = [line] + [swap(line, "gx", m) for m in range(1, lon_count)]
    near_depths = stack_after(near_depths, line)
    near_depths = near_depths.reshape((lon_count * half,) + depths.shape)
    far_depths = swap(near_depths, "gy", 1)
    column, bottom, drag_gradient = column_mixing(
        adjoint_vel, velocity, drag_coef, level_count, block_ids, line, block_total
    )
    weights = surface_weights(
        near_depths, far_depths, me, block_ids, rows, lon_count, lat_count
    )

    near = stack_after(near, bottom, weights[0])
    far = swap(near, "gy", 1)

    corrected, height, sensitivity = surface_solve(
        near.reshape((-1, rows, cols)), far.reshape((-1, rows, cols)), weights,
        block_ids, level_count, bottom, column, block_total,
    )
    return corrected, drag_gradient, height, sensitivity


def solution(mesh):
    in_specs = (
        P(("gx", "gy"), None, None, None, None),
        P(("gx", "gy"), None, None, None, None),
        P(("gx", "gy"), None, None),
        P(("gx", "gy"), None, None),
        P(("gx", "gy")),
        P("gy", "gx"),
        P("gy", "gx"),
    )
    out_specs = (
        P(("gx", "gy"), None, None, None, None),
        P(("gx", "gy"), None, None),
        P("gy", "gx"),
        P("gy", "gx"),
    )
    return jax.shard_map(
        per_device, mesh=mesh, in_specs=in_specs, out_specs=out_specs, check_vma=False
    )
```

```python
import functools

import jax
import jax.numpy as jnp
import numpy as np
from jax import lax
from jax.experimental import pallas as pl
from jax.experimental.pallas import tpu as pltpu
from jax.sharding import PartitionSpec as P

STEPS = 32

mix_rate = 0.25
drag_step = 0.5
force_scale = 0.25
pressure_gain = 0.5
surface_shift = 1.0 / 64.0
speed_floor = 0.01

LANES = 128
SUBLANES = 8
MIB = 1024 * 1024
FIRST_VMEM = 61 * MIB
MIXING_VMEM = 52 * MIB
SOLVE_VMEM = 50 * MIB
WINDOW_VMEM = 16 * MIB


def chebyshev_sum(total_steps):
    highest = surface_shift + 8.0
    centre = 0.5 * (highest + surface_shift)
    radius = 0.5 * (highest - surface_shift)
    sigma_ratio = centre / radius

    def operate(series):
        shifted = np.zeros_like(series)
        shifted[1] += series[0]
        for k in range(1, len(series) - 1):
            shifted[k + 1] += 0.5 * series[k]
            shifted[k - 1] += 0.5 * series[k]
        return centre * series - radius * shifted

    height = np.zeros(total_steps + 2)
    residual = np.zeros(total_steps + 2)
    residual[0] = 1.0
    direction = residual / centre
    ratio_prev = 1.0 / sigma_ratio
    for _ in range(total_steps):
        height = height + direction
        residual = residual - operate(direction)
        ratio_next = 1.0 / (2.0 * sigma_ratio - ratio_prev)
        direction = ratio_next * ratio_prev * direction + 2.0 * ratio_next / radius * residual
        ratio_prev = ratio_next
    return [float(c) for c in height[:total_steps]], 2.0 / radius


def params(limit):
    return pltpu.CompilerParams(vmem_limit_bytes=limit)


SMEM = pl.BlockSpec(memory_space=pltpu.SMEM)
VMEM = pl.BlockSpec(memory_space=pltpu.VMEM)
ANYWHERE = pl.BlockSpec(memory_space=pl.ANY)
HBM = pl.BlockSpec(memory_space=pltpu.HBM)


def forcing_kernel(levels_ref, adjoint_ref, out_ref, levels_held, held, level_sem, sems):
    slots, comps, depth, rows, cols = held.shape
    level_copy = pltpu.make_async_copy(levels_ref, levels_held, level_sem)
    level_copy.start()
    for b in range(slots):
        for c in range(comps):
            pltpu.make_async_copy(adjoint_ref.at[b, c], held.at[b, c], sems.at[b, c]).start()
    level_copy.wait()

    def one_slot(b, carry):
        levels = levels_held[b]
        total = jnp.zeros((rows, cols), jnp.float32)
        for c in range(comps):
            pltpu.make_async_copy(adjoint_ref.at[b, c], held.at[b, c], sems.at[b, c]).wait()
            for k in range(depth):
                total = total + jnp.where(levels > k, held[b, c, k], 0.0)
        out_ref[b] = force_scale * total
        return carry

    lax.fori_loop(0, slots, one_slot, 0)


def column_forcing(adjoint_vel, level_count):
    slots, comps, depth, rows, cols = adjoint_vel.shape
    return pl.pallas_call(
        forcing_kernel,
        in_specs=[HBM, HBM],
        out_specs=VMEM,
        out_shape=pltpu.VMEM((slots, rows, cols), jnp.float32),
        scratch_shapes=[
            pltpu.VMEM(level_count.shape, jnp.int32),
            pltpu.VMEM(adjoint_vel.shape, jnp.float32),
            pltpu.SemaphoreType.DMA,
            pltpu.SemaphoreType.DMA((slots, comps)),
        ],
        compiler_params=params(FIRST_VMEM),
        cost_estimate=pl.CostEstimate(
            flops=2 * adjoint_vel.size, bytes_accessed=4 * adjoint_vel.size, transcendentals=0
        ),
        name="column_forcing",
    )(level_count, adjoint_vel)


DEEP_CHUNK = 16


def mixing_kernel(block_total, first, earlier, ids_ref, levels_ref, drag_ref, adjoint_ref,
                  velocity_ref, after_ref, *rest):
    if earlier:
        for target, ref in zip(rest[3:5], rest[:2]):
            target[0:first] = ref[...]
        rest = rest[2:]
    column_ref, bottom_ref, gradient_ref, adjoint, velocity, column, in_sems, out_sems = rest
    slots, comps, depth, rows, cols = adjoint.shape
    group = 16
    parts = rows // group

    def copies_in(b, index):
        span = pl.ds(pl.multiple_of(index * group, group), group)
        return (
            pltpu.make_async_copy(
                adjoint_ref.at[first + b, :, :, span], adjoint.at[b, :, :, span],
                in_sems.at[0, b, index],
            ),
            pltpu.make_async_copy(
                velocity_ref.at[first + b, :, :, span], velocity.at[b, :, :, span],
                in_sems.at[1, b, index],
            ),
        )

    def copy_out(b, index):
        span = pl.ds(pl.multiple_of(index * group, group), group)
        return pltpu.make_async_copy(
            column.at[b, :, pl.ds(2, depth), span], column_ref.at[b, :, :, span],
            out_sems.at[b, index],
        )

    for b in range(slots):
        for index in range(parts):
            for copy in copies_in(b, index):
                copy.start()

    def one_group(b, index):
        flag = jnp.where(ids_ref[first + b] < block_total, 1.0, 0.0)
        span = pl.ds(pl.multiple_of(index * group, group), group)
        levels = levels_ref[first + b, span, :]
        zero = jnp.zeros(levels.shape, jnp.float32)

        def one_component(c):
            def some_levels(chunk, carry):
                x, once, first_flux, second_flux, flow, field, rate_before = carry
                base = chunk * DEEP_CHUNK
                done = []
                for j in range(DEEP_CHUNK):
                    k = base + j
                    inside = jnp.minimum(k, depth - 1)
                    wet = levels > k
                    rate = jnp.where(wet, jnp.where(k > 0, mix_rate, 0.0), 0.0)
                    fresh = jnp.where(wet, adjoint[b, c, inside, span, :], 0.0)
                    flow = jnp.where(
                        levels == k + 1, velocity[b, c, inside, span, :].astype(jnp.float32), flow
                    )
                    flux = (fresh - x) * rate
                    fresh_once = x + (flux - first_flux)
                    first_flux = flux
                    x = fresh
                    flux = (fresh_once - once) * rate_before
                    twice = once + (flux - second_flux)
                    second_flux = flux
                    once = fresh_once
                    rate_before = rate
                    field = jnp.where(levels == k - 1, twice, field)
                    done.append((k, twice))
                for k, value in done:
                    column[b, c, k, span, :] = value
                return x, once, first_flux, second_flux, flow, field, rate_before

            end = lax.fori_loop(0, (depth + 2) // DEEP_CHUNK, some_levels, (zero,) * 7)
            return end[4], end[5]

        flow, field = zip(one_component(0), one_component(1))
        speed = jnp.sqrt(flow[0] * flow[0] + flow[1] * flow[1] + speed_floor)
        along = flow[0] * field[0] + flow[1] * field[1]
        ratio = along / speed
        drag = drag_ref[first + b, span, :]
        for c in range(2):
            bottom_ref[first + b, c, span, :] = field[c] - drag_step * drag * (
                speed * field[c] + flow[c] * ratio
            )
        gradient_ref[first + b, span, :] = -drag_step * speed * along * flag

    def one(step, carry):
        b = lax.div(step, parts)
        index = lax.rem(step, parts)
        for copy in copies_in(b, index):
            copy.wait()
        one_group(b, index)
        copy_out(b, index).start()
        return carry

    lax.fori_loop(0, slots * parts, one, 0)
    for b in range(slots):
        for index in range(parts):
            copy_out(b, index).wait()


def column_mixing(adjoint_vel, velocity, drag_coef, level_count, block_ids, after, block_total,
                  first, last, earlier=()):
    comps, depth, rows, cols = adjoint_vel.shape[1:]
    assert (depth + 2) % DEEP_CHUNK == 0
    slots = last - first
    part = (slots, comps, depth, rows, cols)
    size = slots * comps * depth * rows * cols
    return pl.pallas_call(
        functools.partial(mixing_kernel, block_total, first, len(earlier)),
        in_specs=[SMEM, VMEM, VMEM, HBM, HBM, ANYWHERE] + [VMEM] * len(earlier),
        out_specs=[HBM, VMEM, VMEM],
        out_shape=[
            pltpu.HBM(part, jnp.float32),
            pltpu.VMEM((last, comps, rows, cols), jnp.float32),
            pltpu.HBM((last, rows, cols), jnp.float32),
        ],
        scratch_shapes=[
            pltpu.VMEM(part, adjoint_vel.dtype),
            pltpu.VMEM(part, velocity.dtype),
            pltpu.VMEM((slots, comps, depth + 2, rows, cols), jnp.float32),
            pltpu.SemaphoreType.DMA((2, slots, rows // 16)),
            pltpu.SemaphoreType.DMA((slots, rows // 16)),
        ],
        compiler_params=params(MIXING_VMEM),
        cost_estimate=pl.CostEstimate(
            flops=14 * size, bytes_accessed=10 * size, transcendentals=0
        ),
        name="column_mixing",
    )(block_ids, level_count, drag_coef, adjoint_vel, velocity, after, *earlier)


CHUNK = 8
PAD = SUBLANES
WIDTH = LANES + 2 * STEPS
PITCH = WIDTH + 2 * PAD
NEIGHBOURS = [(down, right) for down in (-1, 0, 1) for right in (0, 1, -1)]


def window_shape(slots, rows):
    strips = LANES // (slots + 2)
    deep = pl.cdiv(rows + 2 * STEPS, strips)
    return strips, deep, strips * deep


def log2(count):
    bits = count.bit_length() - 1
    assert 1 << bits == count
    return bits


def window_places(me_ref, ids_ref, slots, lon_count, lat_count):
    places = []
    for w in range(slots + 2):
        if w < slots:
            block = jnp.where(ids_ref[w] < 2 * lon_count * lat_count, ids_ref[w], 0)
        else:
            block = (me_ref[0] * lat_count + me_ref[1]) * 2 + (w - slots)
        pair = block >> 1
        column = (pair >> log2(lat_count)) * 2 + (block & 1)
        places.append((pair & (lat_count - 1), column))
    return places


def put_window(natural, base, rows, blocks, lane):
    for i in range(3):
        here, east, west = blocks[3 * i:3 * i + 3]
        sides = jnp.where(lane < STEPS, east, jnp.where(lane >= LANES - STEPS, west, 0.0))
        start = base + i * rows
        natural[0, start:start + rows, :] = here
        natural[1, start:start + rows, :] = sides


def turn(natural, deep, put):
    for i in range(deep):
        put(i, STEPS, natural[0, pl.ds(i, LANES, stride=deep), :].T)
        sides = natural[1, pl.ds(i, LANES, stride=deep), :].T
        put(i, STEPS + LANES, sides[:STEPS])
        put(i, 0, sides[LANES - STEPS:])


def rows_at(ref, start, shift=0):
    return ref[pl.ds(start + shift, SUBLANES), :]


def strip_rows(ref, chunk, deep):
    at = [pl.multiple_of(i * PITCH + PAD + chunk * SUBLANES, SUBLANES) for i in range(deep)]
    here = [rows_at(ref, a) for a in at]
    above = [pltpu.roll(here[-1], 1, 1)] + here[:-1]
    below = here[1:] + [pltpu.roll(here[0], LANES - 1, 1)]
    return here, above, below, at


def depth_kernel(ids_ref, bathymetry_ref, mask_ref, out_ref, ids, bathymetry, mask, sems):
    copies = [
        pltpu.make_async_copy(ids_ref, ids, sems.at[0]),
        pltpu.make_async_copy(bathymetry_ref, bathymetry, sems.at[1]),
        pltpu.make_async_copy(mask_ref, mask, sems.at[2]),
    ]
    for copy in copies:
        copy.start()
    for copy in copies:
        copy.wait()
    rows = bathymetry.shape[0]
    scaled = bathymetry[...] * mask[...].astype(jnp.float32)
    out_ref[0:rows, :] = scaled[:, :LANES]
    out_ref[rows:2 * rows, :] = scaled[:, LANES:]
    lane = lax.broadcasted_iota(jnp.int32, (SUBLANES, LANES), 1)
    listed = jnp.zeros((SUBLANES, LANES), jnp.int32)
    for s in range(ids.shape[0]):
        listed = jnp.where(lane == s, ids[s], listed)
    out_ref[2 * rows:2 * rows + SUBLANES, :] = listed.astype(jnp.float32)


def depth_payload(bathymetry, land_mask, block_ids):
    rows = bathymetry.shape[0]
    return pl.pallas_call(
        depth_kernel,
        in_specs=[HBM, HBM, HBM],
        out_specs=VMEM,
        out_shape=pltpu.VMEM((2 * rows + SUBLANES, LANES), jnp.float32),
        scratch_shapes=[
            pltpu.SMEM(block_ids.shape, jnp.int32),
            pltpu.VMEM(bathymetry.shape, jnp.float32),
            pltpu.VMEM(land_mask.shape, jnp.int32),
            pltpu.SemaphoreType.DMA((3,)),
        ],
        compiler_params=params(FIRST_VMEM),
        name="depth_payload",
    )(block_ids, bathymetry, land_mask)


def weights_kernel(slots, lon_count, lat_count, me_ref, ids_ref, near_ref, far_ref,
                   root_ref, centre_ref, around_ref, table_ref,
                   natural, all_ids, places_of, sems):
    half = lat_count // 2
    count = lon_count * half
    rows = (near_ref.shape[1] - SUBLANES) // 2
    strips, deep, tall = window_shape(slots, rows)
    column_count = 2 * lon_count
    parts = (near_ref, far_ref)
    copies = [
        pltpu.make_async_copy(
            parts[p].at[:, pl.ds(2 * rows, 1), :], all_ids.at[p], sems.at[p]
        )
        for p in range(2)
    ]
    for copy in copies:
        copy.start()
    natural[...] = jnp.zeros_like(natural)

    def load(lat, column):
        inside = (lat >= 0) & (lat < lat_count) & (column >= 0) & (column < column_count)
        lat_safe = jnp.clip(lat, 0, lat_count - 1)
        column_safe = jnp.clip(column, 0, column_count - 1)
        lon_xor = (column_safe >> 1) ^ me_ref[0]
        lat_xor = lat_safe ^ me_ref[1]
        place = lon_xor * half + (lat_xor >> 1)
        start = pl.multiple_of((column_safe & 1) * rows, SUBLANES)
        near = near_ref[place, pl.ds(start, rows), :]
        far = far_ref[place, pl.ds(start, rows), :]
        here = jnp.where((lat_xor & 1) == 0, near, far)
        return here * jnp.where(inside, 1.0, 0.0)

    lane = lax.broadcasted_iota(jnp.int32, (rows, LANES), 1)
    places = window_places(me_ref, ids_ref, slots, lon_count, lat_count)
    for w, (lat, column) in enumerate(places):
        blocks = [load(lat + down, column + right) for down, right in NEIGHBOURS]
        put_window(natural, w * tall, rows, blocks, lane)

    for copy in copies:
        copy.wait()

    def one_device(n, carry):
        for p in range(2):
            for s in range(slots):
                block = all_ids[p, n, 0, s].astype(jnp.int32)
                places_of[block] = (p * count + n) * slots + s
        return carry

    lax.fori_loop(0, count, one_device, 0)
    for w, (lat, column) in enumerate(places):
        for n, (down, right) in enumerate(NEIGHBOURS):
            lat_safe = jnp.clip(lat + down, 0, lat_count - 1)
            column_safe = jnp.clip(column + right, 0, column_count - 1)
            block = ((column_safe >> 1) * lat_count + lat_safe) * 2 + (column_safe & 1)
            table_ref[w * len(NEIGHBOURS) + n] = places_of[block]

    scale = chebyshev_sum(STEPS)[1]

    def put(i, x, values):
        start = i * PITCH + PAD + x
        root_ref[start:start + values.shape[0], :] = jnp.sqrt(values)
        around_ref[start:start + values.shape[0], :] = scale * values

    turn(natural, deep, put)
    zeros = jnp.zeros((PAD, LANES), jnp.float32)
    for i in range(deep):
        root_ref[i * PITCH:i * PITCH + PAD, :] = zeros
        root_ref[(i + 1) * PITCH - PAD:(i + 1) * PITCH, :] = zeros

    def one_chunk(chunk, carry):
        out = []
        here, above, below, at = strip_rows(root_ref, chunk, deep)
        for i, a in enumerate(at):
            others = (rows_at(root_ref, a, 1) + rows_at(root_ref, a, -1)) + (above[i] + below[i])
            out.append((a, 2.0 - scale * here[i] * others))
        for a, value in out:
            centre_ref[pl.ds(a, SUBLANES), :] = value
        return carry

    lax.fori_loop(0, WIDTH // SUBLANES, one_chunk, 0)


def surface_weights(near, far, me, block_ids, rows, lon_count, lat_count):
    slots = block_ids.shape[0]
    assert near.shape[-1] == LANES
    strips, deep, tall = window_shape(slots, rows)
    shape = jax.ShapeDtypeStruct((deep * PITCH, LANES), jnp.float32)
    return pl.pallas_call(
        functools.partial(weights_kernel, slots, lon_count, lat_count),
        in_specs=[SMEM, SMEM, VMEM, VMEM],
        out_specs=[VMEM, VMEM, VMEM, SMEM],
        out_shape=[
            shape,
            shape,
            shape,
            jax.ShapeDtypeStruct(((slots + 2) * len(NEIGHBOURS),), jnp.int32),
        ],
        scratch_shapes=[
            pltpu.VMEM((2, LANES * deep, LANES), jnp.float32),
            pltpu.SMEM((2, near.shape[0], 1, LANES), jnp.float32),
            pltpu.SMEM((2 * lon_count * lat_count + 1,), jnp.int32),
            pltpu.SemaphoreType.DMA((2,)),
        ],
        compiler_params=params(WINDOW_VMEM),
        cost_estimate=pl.CostEstimate(
            flops=0, bytes_accessed=8 * MIB, transcendentals=0
        ),
        name="surface_weights",
    )(me, block_ids, near, far)


def solve_kernel(block_total, ids_ref, table_ref, coefs_ref, root_ref, centre_ref, around_ref,
                 levels_ref, bottom_ref, first_column_ref, last_column_ref, near_ref, far_ref,
                 corrected_ref, height_ref, sensitivity_ref,
                 natural, source, even, odd, extra, column, in_sems, out_sems):
    slots, comps, depth, rows, cols = column.shape
    strips, deep, tall = window_shape(slots, rows)

    middle = first_column_ref.shape[0]
    copies_in = [
        pltpu.make_async_copy(first_column_ref, column.at[pl.ds(0, middle)], in_sems.at[0]),
        pltpu.make_async_copy(
            last_column_ref, column.at[pl.ds(middle, slots - middle)], in_sems.at[1]
        ),
    ]
    for copy in copies_in:
        copy.start()

    count = near_ref.shape[0]

    def load(place):
        inner = place & (count - 1)
        return jnp.where(place < count, near_ref[inner], far_ref[inner])

    lane = lax.broadcasted_iota(jnp.int32, (rows, LANES), 1)
    for w in range(slots + 2):
        places = [table_ref[w * len(NEIGHBOURS) + n] for n in range(len(NEIGHBOURS))]
        put_window(natural, w * tall, rows, [load(place) for place in places], lane)

    coefs, step_scale = chebyshev_sum(STEPS)

    def put(i, x, values):
        start = i * PITCH + PAD + x
        stop = start + values.shape[0]
        root = root_ref[start:stop, :]
        values = jnp.where(root > 0.0, root * values, 0.0)
        source[start:stop, :] = values
        even[start:stop, :] = coefs[STEPS - 1] * values
        odd[start:stop, :] = jnp.zeros_like(values)

    zeros = jnp.zeros((PAD, LANES), jnp.float32)
    for ref in (even, odd):
        for i in range(deep):
            ref[i * PITCH:i * PITCH + PAD, :] = zeros
            ref[(i + 1) * PITCH - PAD:(i + 1) * PITCH, :] = zeros
    turn(natural, deep, put)

    chunks = WIDTH // SUBLANES

    def apply(current, target, coef, gain, low, count):
        size = (chunks - 2 * low) // count

        def group(index, carry):
            out = []
            for n in range(size):
                here, above, below, at = strip_rows(current, low + index * size + n, deep)
                for i, a in enumerate(at):
                    others = (rows_at(current, a, 1) + rows_at(current, a, -1)) + (
                        above[i] + below[i]
                    )
                    pushed = rows_at(centre_ref, a) * here[i] + rows_at(around_ref, a) * others
                    if gain != 1.0:
                        pushed = gain * pushed
                    kept = coef * rows_at(source, a) - rows_at(target, a)
                    out.append((a, kept + pushed))
            for a, value in out:
                target[pl.ds(a, SUBLANES), :] = value
            return carry

        lax.fori_loop(0, count, group, 0)

    def bounds(m):
        low = m // (2 * SUBLANES) * 2
        count = chunks - 2 * low
        return low, count // (5 if count % 5 == 0 else 4)

    runs = []
    for m in range(1, STEPS - 1, 2):
        if runs and runs[-1][1] == bounds(m):
            runs[-1][2] += 1
        else:
            runs.append([m, bounds(m), 1])
    for first, (low, count), pairs in runs:
        def two_steps(pair, carry, first=first, low=low, count=count):
            m = first + 2 * pair
            apply(even, odd, coefs_ref[m], 1.0, low, count)
            apply(odd, even, coefs_ref[m + 1], 1.0, low, count)
            return carry

        lax.fori_loop(0, pairs, two_steps, 0)
    low, count = bounds(STEPS - 1)
    apply(even, odd, coefs[0], 0.5, low, count)

    low = STEPS // SUBLANES - 1

    def one_height(chunk, carry):
        out = []
        for i in range(deep):
            a = pl.multiple_of(i * PITCH + PAD + chunk * SUBLANES, SUBLANES)
            root = rows_at(root_ref, a)
            out.append((a, jnp.where(root > 0.0, rows_at(odd, a) / root, 0.0)))
        for a, value in out:
            extra[pl.ds(a, SUBLANES), :] = value
        return carry

    lax.fori_loop(low, chunks - low, one_height, 0)

    def differences(chunk, carry):
        here, above, below, at = strip_rows(extra, chunk, deep)
        root, root_above, root_below, _ = strip_rows(root_ref, chunk, deep)
        out = []
        for i, a in enumerate(at):
            east_step = rows_at(extra, a, 1) - here[i]
            west_step = here[i] - rows_at(extra, a, -1)
            south_step = below[i] - here[i]
            north_step = here[i] - above[i]
            energy = root[i] * (
                (rows_at(root_ref, a, 1) * east_step * east_step
                 + rows_at(root_ref, a, -1) * west_step * west_step)
                + (root_below[i] * south_step * south_step
                   + root_above[i] * north_step * north_step)
            )
            scaled = rows_at(around_ref, a) * (1.0 / step_scale)
            out.append((even, a, east_step))
            out.append((source, a, 0.25 * energy / jnp.maximum(scaled, 0.25)))
        for ref, a, value in out:
            ref[pl.ds(a, SUBLANES), :] = value
        return carry

    lax.fori_loop(low + 1, chunks - low - 1, differences, 0)

    def turn_back(ref, tile):
        for i in range(deep):
            start = i * PITCH + PAD + STEPS
            natural[tile, pl.ds(i, LANES, stride=deep), :] = ref[start:start + LANES, :].T

    def cut(tile, w, shift=0):
        return natural[tile, pl.ds(w * tall + STEPS + shift, rows), :]

    def copy_out(b, c):
        return pltpu.make_async_copy(column.at[b, c], corrected_ref.at[b, c], out_sems.at[b, c])

    def correct(b, c, step):
        levels = levels_ref[b] * jnp.where(ids_ref[b] < block_total, 1, 0)
        push = pressure_gain * step
        lowest = bottom_ref[b, c] - push

        def some_levels(base, size):
            out = []
            for j in range(size):
                k = base + j
                value = jnp.where(levels == k + 1, lowest, column[b, c, k] - push)
                out.append((k, jnp.where(levels > k, value, 0.0)))
            for k, value in out:
                column[b, c, k] = value

        def one_chunk(chunk, inner):
            some_levels(chunk * CHUNK, CHUNK)
            return inner

        lax.fori_loop(0, depth // CHUNK, one_chunk, 0)
        some_levels(depth // CHUNK * CHUNK, depth % CHUNK)
        copy_out(b, c).start()

    turn_back(even, 0)
    for copy in copies_in:
        copy.wait()

    def correct_east(b, carry):
        correct(b, 0, cut(0, b))
        return carry

    def correct_north(b, carry):
        correct(b, 1, cut(1, b, 1) - cut(1, b))
        return carry

    lax.fori_loop(0, slots, correct_east, 0)
    turn_back(extra, 1)
    lax.fori_loop(0, slots, correct_north, 0)
    turn_back(source, 0)
    for h in range(2):
        height_ref[:, h * LANES:(h + 1) * LANES] = cut(1, slots + h)
        sensitivity_ref[:, h * LANES:(h + 1) * LANES] = cut(0, slots + h)

    for b in range(slots):
        for c in range(comps):
            copy_out(b, c).wait()


def surface_solve(near, far, weights, block_ids, level_count, bottom, columns, block_total):
    root, centre, around, table = weights
    comps, depth, rows, cols = columns[0].shape[1:]
    slots = level_count.shape[0]
    assert comps == 2
    full = (slots, comps, depth, rows, cols)
    deep = window_shape(slots, rows)[1]
    turned = pltpu.VMEM(root.shape, jnp.float32)
    coefs = jnp.array(chebyshev_sum(STEPS)[0][::-1], jnp.float32)
    return pl.pallas_call(
        functools.partial(solve_kernel, block_total),
        in_specs=[SMEM, SMEM, SMEM] + [VMEM] * 5 + [HBM] * 2 + [VMEM] * 2,
        out_specs=[HBM, VMEM, VMEM],
        out_shape=[
            jax.ShapeDtypeStruct(full, jnp.float32),
            jax.ShapeDtypeStruct((rows, 2 * cols), jnp.float32),
            jax.ShapeDtypeStruct((rows, 2 * cols), jnp.float32),
        ],
        scratch_shapes=[
            pltpu.VMEM((2, LANES * deep, LANES), jnp.float32),
            turned,
            turned,
            turned,
            turned,
            pltpu.VMEM(full, jnp.float32),
            pltpu.SemaphoreType.DMA((2,)),
            pltpu.SemaphoreType.DMA((slots, comps)),
        ],
        compiler_params=params(SOLVE_VMEM),
        cost_estimate=pl.CostEstimate(
            flops=9 * STEPS * root.size, bytes_accessed=16 * root.size, transcendentals=0
        ),
        name="surface_solve",
    )(block_ids, table, coefs, root, centre, around, level_count, bottom, *columns, near, far)


def stack_kernel(parts, *refs):
    out_ref = refs[-1]
    for p in range(parts):
        out_ref[p] = refs[p][...]


def stack_after(parts, *tokens):
    return pl.pallas_call(
        functools.partial(stack_kernel, len(parts)),
        in_specs=[VMEM] * len(parts) + [ANYWHERE] * len(tokens),
        out_specs=VMEM,
        out_shape=jax.ShapeDtypeStruct((len(parts),) + parts[0].shape, jnp.float32),
        compiler_params=params(WINDOW_VMEM),
        name="stack_after",
    )(*parts, *tokens)


def swap(values, axis, mask):
    count = lax.axis_size(axis)
    return lax.ppermute(values, axis, [(i, i ^ mask) for i in range(count)])


def per_device(adjoint_vel, velocity, drag_coef, level_count, block_ids, bathymetry, land_mask):
    slots = block_ids.shape[0]
    rows, cols = drag_coef.shape[1:]
    lon_count = lax.axis_size("gx")
    lat_count = lax.axis_size("gy")
    half = lat_count // 2
    block_total = 2 * lon_count * lat_count
    me = jnp.stack([lax.axis_index("gx"), lax.axis_index("gy")]).astype(jnp.int32)

    depths = depth_payload(bathymetry, land_mask, block_ids)
    depth_parts = [depths] + [swap(depths, "gy", 2 * m) for m in range(1, half)]
    forcing = column_forcing(adjoint_vel, level_count)

    parts = [forcing] + [swap(forcing, "gy", 2 * m) for m in range(1, half)]
    near_depths = stack_after(depth_parts, forcing)
    near_depths = [near_depths] + [swap(near_depths, "gx", m) for m in range(1, lon_count)]
    columns = (adjoint_vel, velocity, drag_coef, level_count, block_ids)
    middle = (slots + 1) // 2
    first_column, *first_rest = column_mixing(*columns, forcing, block_total, 0, middle)
    line = stack_after(parts, first_rest[0])

    near = [line] + [swap(line, "gx", m) for m in range(1, lon_count)]
    near_depths = stack_after(near_depths, line)
    near_depths = near_depths.reshape((lon_count * half,) + depths.shape)
    far_depths = swap(near_depths, "gy", 1)
    last_column, bottom, drag_gradient = column_mixing(
        *columns, line, block_total, middle, slots, first_rest
    )
    weights = surface_weights(
        near_depths, far_depths, me, block_ids, rows, lon_count, lat_count
    )

    near = stack_after(near, bottom, weights[0])
    far = swap(near, "gy", 1)

    corrected, height, sensitivity = surface_solve(
        near.reshape((-1, rows, cols)), far.reshape((-1, rows, cols)), weights,
        block_ids, level_count, bottom, (first_column, last_column), block_total,
    )
    return corrected, drag_gradient, height, sensitivity


def solution(mesh):
    in_specs = (
        P(("gx", "gy"), None, None, None, None),
        P(("gx", "gy"), None, None, None, None),
        P(("gx", "gy"), None, None),
        P(("gx", "gy"), None, None),
        P(("gx", "gy")),
        P("gy", "gx"),
        P("gy", "gx"),
    )
    out_specs = (
        P(("gx", "gy"), None, None, None, None),
        P(("gx", "gy"), None, None),
        P("gy", "gx"),
        P("gy", "gx"),
    )
    return jax.shard_map(
        per_device, mesh=mesh, in_specs=in_specs, out_specs=out_specs, check_vma=False
    )
```

```python
import functools

import jax
import jax.numpy as jnp
import numpy as np
from jax import lax
from jax.experimental import pallas as pl
from jax.experimental.pallas import tpu as pltpu
from jax.sharding import PartitionSpec as P

STEPS = 32

mix_rate = 0.25
drag_step = 0.5
force_scale = 0.25
pressure_gain = 0.5
surface_shift = 1.0 / 64.0
speed_floor = 0.01

LANES = 128
SUBLANES = 8
MIB = 1024 * 1024
FIRST_VMEM = 61 * MIB
MIXING_VMEM = 52 * MIB
SOLVE_VMEM = 50 * MIB
WINDOW_VMEM = 16 * MIB


def chebyshev_sum(total_steps):
    highest = surface_shift + 8.0
    centre = 0.5 * (highest + surface_shift)
    radius = 0.5 * (highest - surface_shift)
    sigma_ratio = centre / radius

    def operate(series):
        shifted = np.zeros_like(series)
        shifted[1] += series[0]
        for k in range(1, len(series) - 1):
            shifted[k + 1] += 0.5 * series[k]
            shifted[k - 1] += 0.5 * series[k]
        return centre * series - radius * shifted

    height = np.zeros(total_steps + 2)
    residual = np.zeros(total_steps + 2)
    residual[0] = 1.0
    direction = residual / centre
    ratio_prev = 1.0 / sigma_ratio
    for _ in range(total_steps):
        height = height + direction
        residual = residual - operate(direction)
        ratio_next = 1.0 / (2.0 * sigma_ratio - ratio_prev)
        direction = ratio_next * ratio_prev * direction + 2.0 * ratio_next / radius * residual
        ratio_prev = ratio_next
    return [float(c) for c in height[:total_steps]], 2.0 / radius


def params(limit):
    return pltpu.CompilerParams(vmem_limit_bytes=limit)


SMEM = pl.BlockSpec(memory_space=pltpu.SMEM)
VMEM = pl.BlockSpec(memory_space=pltpu.VMEM)
ANYWHERE = pl.BlockSpec(memory_space=pl.ANY)
HBM = pl.BlockSpec(memory_space=pltpu.HBM)


AHEAD = 2


def forcing_kernel(levels_ref, adjoint_ref, out_ref, levels_held, held, level_sem, sems):
    slots, comps, depth, rows, cols = held.shape
    level_copy = pltpu.make_async_copy(levels_ref, levels_held, level_sem)
    level_copy.start()

    def copies_in(b):
        return [
            pltpu.make_async_copy(adjoint_ref.at[b, c], held.at[b, c], sems.at[b, c])
            for c in range(comps)
        ]

    for b in range(min(AHEAD, slots)):
        for copy in copies_in(b):
            copy.start()
    level_copy.wait()

    def one_slot(b, carry):
        for copy in copies_in(b):
            copy.wait()

        @pl.when(b + AHEAD < slots)
        def _():
            for copy in copies_in(b + AHEAD):
                copy.start()

        levels = levels_held[b]
        total = jnp.zeros((rows, cols), jnp.float32)
        for c in range(comps):
            for k in range(depth):
                total = total + jnp.where(levels > k, held[b, c, k], 0.0)
        out_ref[b] = force_scale * total
        return carry

    lax.fori_loop(0, slots, one_slot, 0)


def column_forcing(adjoint_vel, level_count):
    slots, comps, depth, rows, cols = adjoint_vel.shape
    return pl.pallas_call(
        forcing_kernel,
        in_specs=[HBM, HBM],
        out_specs=VMEM,
        out_shape=pltpu.VMEM((slots, rows, cols), jnp.float32),
        scratch_shapes=[
            pltpu.VMEM(level_count.shape, jnp.int32),
            pltpu.VMEM(adjoint_vel.shape, jnp.float32),
            pltpu.SemaphoreType.DMA,
            pltpu.SemaphoreType.DMA((slots, comps)),
        ],
        compiler_params=params(FIRST_VMEM),
        cost_estimate=pl.CostEstimate(
            flops=2 * adjoint_vel.size, bytes_accessed=4 * adjoint_vel.size, transcendentals=0
        ),
        name="column_forcing",
    )(level_count, adjoint_vel)


DEEP_CHUNK = 16


def mixing_kernel(block_total, first, earlier, ids_ref, levels_ref, drag_ref, adjoint_ref,
                  velocity_ref, after_ref, *rest):
    if earlier:
        for target, ref in zip(rest[3:5], rest[:2]):
            target[0:first] = ref[...]
        rest = rest[2:]
    column_ref, bottom_ref, gradient_ref, adjoint, velocity, column, in_sems, out_sems = rest
    slots, comps, depth, rows, cols = adjoint.shape
    group = 16
    parts = rows // group

    def copies_in(b, index):
        span = pl.ds(pl.multiple_of(index * group, group), group)
        return (
            pltpu.make_async_copy(
                adjoint_ref.at[first + b, :, :, span], adjoint.at[b, :, :, span],
                in_sems.at[0, b, index],
            ),
            pltpu.make_async_copy(
                velocity_ref.at[first + b, :, :, span], velocity.at[b, :, :, span],
                in_sems.at[1, b, index],
            ),
        )

    def copy_out(b, index):
        span = pl.ds(pl.multiple_of(index * group, group), group)
        return pltpu.make_async_copy(
            column.at[b, :, pl.ds(2, depth), span], column_ref.at[b, :, :, span],
            out_sems.at[b, index],
        )

    for step in range(min(AHEAD, slots * parts)):
        for copy in copies_in(step // parts, step % parts):
            copy.start()

    def one_group(b, index):
        flag = jnp.where(ids_ref[first + b] < block_total, 1.0, 0.0)
        span = pl.ds(pl.multiple_of(index * group, group), group)
        levels = levels_ref[first + b, span, :]
        zero = jnp.zeros(levels.shape, jnp.float32)

        def one_component(c):
            def some_levels(chunk, carry):
                x, once, first_flux, second_flux, flow, field, rate_before = carry
                base = chunk * DEEP_CHUNK
                done = []
                for j in range(DEEP_CHUNK):
                    k = base + j
                    inside = jnp.minimum(k, depth - 1)
                    wet = levels > k
                    rate = jnp.where(wet, jnp.where(k > 0, mix_rate, 0.0), 0.0)
                    fresh = jnp.where(wet, adjoint[b, c, inside, span, :], 0.0)
                    flow = jnp.where(
                        levels == k + 1, velocity[b, c, inside, span, :].astype(jnp.float32), flow
                    )
                    flux = (fresh - x) * rate
                    fresh_once = x + (flux - first_flux)
                    first_flux = flux
                    x = fresh
                    flux = (fresh_once - once) * rate_before
                    twice = once + (flux - second_flux)
                    second_flux = flux
                    once = fresh_once
                    rate_before = rate
                    field = jnp.where(levels == k - 1, twice, field)
                    done.append((k, twice))
                for k, value in done:
                    column[b, c, k, span, :] = value
                return x, once, first_flux, second_flux, flow, field, rate_before

            end = lax.fori_loop(0, (depth + 2) // DEEP_CHUNK, some_levels, (zero,) * 7)
            return end[4], end[5]

        flow, field = zip(one_component(0), one_component(1))
        speed = jnp.sqrt(flow[0] * flow[0] + flow[1] * flow[1] + speed_floor)
        along = flow[0] * field[0] + flow[1] * field[1]
        ratio = along / speed
        drag = drag_ref[first + b, span, :]
        for c in range(2):
            bottom_ref[first + b, c, span, :] = field[c] - drag_step * drag * (
                speed * field[c] + flow[c] * ratio
            )
        gradient_ref[first + b, span, :] = -drag_step * speed * along * flag

    def one(step, carry):
        b = lax.div(step, parts)
        index = lax.rem(step, parts)
        for copy in copies_in(b, index):
            copy.wait()

        @pl.when(step + AHEAD < slots * parts)
        def _():
            later = step + AHEAD
            for copy in copies_in(lax.div(later, parts), lax.rem(later, parts)):
                copy.start()

        one_group(b, index)
        copy_out(b, index).start()
        return carry

    lax.fori_loop(0, slots * parts, one, 0)
    for b in range(slots):
        for index in range(parts):
            copy_out(b, index).wait()


def column_mixing(adjoint_vel, velocity, drag_coef, level_count, block_ids, after, block_total,
                  first, last, earlier=()):
    comps, depth, rows, cols = adjoint_vel.shape[1:]
    assert (depth + 2) % DEEP_CHUNK == 0
    slots = last - first
    part = (slots, comps, depth, rows, cols)
    size = slots * comps * depth * rows * cols
    return pl.pallas_call(
        functools.partial(mixing_kernel, block_total, first, len(earlier)),
        in_specs=[SMEM, VMEM, VMEM, HBM, HBM, ANYWHERE] + [VMEM] * len(earlier),
        out_specs=[HBM, VMEM, VMEM],
        out_shape=[
            pltpu.HBM(part, jnp.float32),
            pltpu.VMEM((last, comps, rows, cols), jnp.float32),
            pltpu.HBM((last, rows, cols), jnp.float32),
        ],
        scratch_shapes=[
            pltpu.VMEM(part, adjoint_vel.dtype),
            pltpu.VMEM(part, velocity.dtype),
            pltpu.VMEM((slots, comps, depth + 2, rows, cols), jnp.float32),
            pltpu.SemaphoreType.DMA((2, slots, rows // 16)),
            pltpu.SemaphoreType.DMA((slots, rows // 16)),
        ],
        compiler_params=params(MIXING_VMEM),
        cost_estimate=pl.CostEstimate(
            flops=14 * size, bytes_accessed=10 * size, transcendentals=0
        ),
        name="column_mixing",
    )(block_ids, level_count, drag_coef, adjoint_vel, velocity, after, *earlier)


CHUNK = 8
PAD = SUBLANES
WIDTH = LANES + 2 * STEPS
PITCH = WIDTH + 2 * PAD
NEIGHBOURS = [(down, right) for down in (-1, 0, 1) for right in (0, 1, -1)]


def window_shape(slots, rows):
    strips = LANES // (slots + 2)
    deep = pl.cdiv(rows + 2 * STEPS, strips)
    return strips, deep, strips * deep


def log2(count):
    bits = count.bit_length() - 1
    assert 1 << bits == count
    return bits


def window_places(me_ref, ids_ref, slots, lon_count, lat_count):
    places = []
    for w in range(slots + 2):
        if w < slots:
            block = jnp.where(ids_ref[w] < 2 * lon_count * lat_count, ids_ref[w], 0)
        else:
            block = (me_ref[0] * lat_count + me_ref[1]) * 2 + (w - slots)
        pair = block >> 1
        column = (pair >> log2(lat_count)) * 2 + (block & 1)
        places.append((pair & (lat_count - 1), column))
    return places


def put_window(natural, base, rows, blocks, lane):
    for i in range(3):
        here, east, west = blocks[3 * i:3 * i + 3]
        sides = jnp.where(lane < STEPS, east, jnp.where(lane >= LANES - STEPS, west, 0.0))
        start = base + i * rows
        natural[0, start:start + rows, :] = here
        natural[1, start:start + rows, :] = sides


def flip(tiles):
    index = lax.broadcasted_iota(jnp.int32, (LANES, LANES), 0)
    unit = index == lax.broadcasted_iota(jnp.int32, (LANES, LANES), 1)
    unit = jnp.where(unit, 1.0, 0.0).astype(jnp.bfloat16)
    values = jnp.concatenate(tiles, axis=0)
    total = None
    for _ in range(3):
        part = values.astype(jnp.bfloat16)
        values = values - part.astype(jnp.float32)
        product = lax.dot_general(
            unit, part, (((1,), (1,)), ((), ())), preferred_element_type=jnp.float32
        )
        total = product if total is None else total + product
    return [total[:, i * LANES:(i + 1) * LANES] for i in range(len(tiles))]


def turn(natural, deep, put):
    for tile in range(2):
        turned = flip([natural[tile, pl.ds(i, LANES, stride=deep), :] for i in range(deep)])
        for i, values in enumerate(turned):
            if tile == 0:
                put(i, STEPS, values)
            else:
                put(i, STEPS + LANES, values[:STEPS])
                put(i, 0, values[LANES - STEPS:])


def rows_at(ref, start, shift=0):
    return ref[pl.ds(start + shift, SUBLANES), :]


def strip_rows(ref, chunk, deep):
    at = [pl.multiple_of(i * PITCH + PAD + chunk * SUBLANES, SUBLANES) for i in range(deep)]
    here = [rows_at(ref, a) for a in at]
    above = [pltpu.roll(here[-1], 1, 1)] + here[:-1]
    below = here[1:] + [pltpu.roll(here[0], LANES - 1, 1)]
    return here, above, below, at


def depth_kernel(ids_ref, bathymetry_ref, mask_ref, out_ref, ids, bathymetry, mask, sems):
    copies = [
        pltpu.make_async_copy(ids_ref, ids, sems.at[0]),
        pltpu.make_async_copy(bathymetry_ref, bathymetry, sems.at[1]),
        pltpu.make_async_copy(mask_ref, mask, sems.at[2]),
    ]
    for copy in copies:
        copy.start()
    for copy in copies:
        copy.wait()
    rows = bathymetry.shape[0]
    scaled = bathymetry[...] * mask[...].astype(jnp.float32)
    out_ref[0:rows, :] = scaled[:, :LANES]
    out_ref[rows:2 * rows, :] = scaled[:, LANES:]
    lane = lax.broadcasted_iota(jnp.int32, (SUBLANES, LANES), 1)
    listed = jnp.zeros((SUBLANES, LANES), jnp.int32)
    for s in range(ids.shape[0]):
        listed = jnp.where(lane == s, ids[s], listed)
    out_ref[2 * rows:2 * rows + SUBLANES, :] = listed.astype(jnp.float32)


def depth_payload(bathymetry, land_mask, block_ids):
    rows = bathymetry.shape[0]
    return pl.pallas_call(
        depth_kernel,
        in_specs=[HBM, HBM, HBM],
        out_specs=VMEM,
        out_shape=pltpu.VMEM((2 * rows + SUBLANES, LANES), jnp.float32),
        scratch_shapes=[
            pltpu.SMEM(block_ids.shape, jnp.int32),
            pltpu.VMEM(bathymetry.shape, jnp.float32),
            pltpu.VMEM(land_mask.shape, jnp.int32),
            pltpu.SemaphoreType.DMA((3,)),
        ],
        compiler_params=params(FIRST_VMEM),
        name="depth_payload",
    )(block_ids, bathymetry, land_mask)


def weights_kernel(slots, lon_count, lat_count, me_ref, ids_ref, near_ref, far_ref,
                   root_ref, centre_ref, around_ref, table_ref,
                   natural, all_ids, places_of, sems):
    half = lat_count // 2
    count = lon_count * half
    rows = (near_ref.shape[1] - SUBLANES) // 2
    strips, deep, tall = window_shape(slots, rows)
    column_count = 2 * lon_count
    parts = (near_ref, far_ref)
    copies = [
        pltpu.make_async_copy(
            parts[p].at[:, pl.ds(2 * rows, 1), :], all_ids.at[p], sems.at[p]
        )
        for p in range(2)
    ]
    for copy in copies:
        copy.start()
    natural[...] = jnp.zeros_like(natural)

    def load(lat, column):
        inside = (lat >= 0) & (lat < lat_count) & (column >= 0) & (column < column_count)
        lat_safe = jnp.clip(lat, 0, lat_count - 1)
        column_safe = jnp.clip(column, 0, column_count - 1)
        lon_xor = (column_safe >> 1) ^ me_ref[0]
        lat_xor = lat_safe ^ me_ref[1]
        place = lon_xor * half + (lat_xor >> 1)
        start = pl.multiple_of((column_safe & 1) * rows, SUBLANES)
        near = near_ref[place, pl.ds(start, rows), :]
        far = far_ref[place, pl.ds(start, rows), :]
        here = jnp.where((lat_xor & 1) == 0, near, far)
        return here * jnp.where(inside, 1.0, 0.0)

    lane = lax.broadcasted_iota(jnp.int32, (rows, LANES), 1)
    places = window_places(me_ref, ids_ref, slots, lon_count, lat_count)
    for w, (lat, column) in enumerate(places):
        blocks = [load(lat + down, column + right) for down, right in NEIGHBOURS]
        put_window(natural, w * tall, rows, blocks, lane)

    for copy in copies:
        copy.wait()

    def one_device(n, carry):
        for p in range(2):
            for s in range(slots):
                block = all_ids[p, n, 0, s].astype(jnp.int32)
                places_of[block] = (p * count + n) * slots + s
        return carry

    lax.fori_loop(0, count, one_device, 0)
    for w, (lat, column) in enumerate(places):
        for n, (down, right) in enumerate(NEIGHBOURS):
            lat_safe = jnp.clip(lat + down, 0, lat_count - 1)
            column_safe = jnp.clip(column + right, 0, column_count - 1)
            block = ((column_safe >> 1) * lat_count + lat_safe) * 2 + (column_safe & 1)
            table_ref[w * len(NEIGHBOURS) + n] = places_of[block]

    scale = chebyshev_sum(STEPS)[1]

    def put(i, x, values):
        start = i * PITCH + PAD + x
        root_ref[start:start + values.shape[0], :] = jnp.sqrt(values)
        around_ref[start:start + values.shape[0], :] = scale * values

    turn(natural, deep, put)
    zeros = jnp.zeros((PAD, LANES), jnp.float32)
    for i in range(deep):
        root_ref[i * PITCH:i * PITCH + PAD, :] = zeros
        root_ref[(i + 1) * PITCH - PAD:(i + 1) * PITCH, :] = zeros

    def one_chunk(chunk, carry):
        out = []
        here, above, below, at = strip_rows(root_ref, chunk, deep)
        for i, a in enumerate(at):
            others = (rows_at(root_ref, a, 1) + rows_at(root_ref, a, -1)) + (above[i] + below[i])
            out.append((a, 2.0 - scale * here[i] * others))
        for a, value in out:
            centre_ref[pl.ds(a, SUBLANES), :] = value
        return carry

    lax.fori_loop(0, WIDTH // SUBLANES, one_chunk, 0)


def surface_weights(near, far, me, block_ids, rows, lon_count, lat_count):
    slots = block_ids.shape[0]
    assert near.shape[-1] == LANES
    strips, deep, tall = window_shape(slots, rows)
    shape = jax.ShapeDtypeStruct((deep * PITCH, LANES), jnp.float32)
    return pl.pallas_call(
        functools.partial(weights_kernel, slots, lon_count, lat_count),
        in_specs=[SMEM, SMEM, VMEM, VMEM],
        out_specs=[VMEM, VMEM, VMEM, SMEM],
        out_shape=[
            shape,
            shape,
            shape,
            jax.ShapeDtypeStruct(((slots + 2) * len(NEIGHBOURS),), jnp.int32),
        ],
        scratch_shapes=[
            pltpu.VMEM((2, LANES * deep, LANES), jnp.float32),
            pltpu.SMEM((2, near.shape[0], 1, LANES), jnp.float32),
            pltpu.SMEM((2 * lon_count * lat_count + 1,), jnp.int32),
            pltpu.SemaphoreType.DMA((2,)),
        ],
        compiler_params=params(WINDOW_VMEM),
        cost_estimate=pl.CostEstimate(
            flops=0, bytes_accessed=8 * MIB, transcendentals=0
        ),
        name="surface_weights",
    )(me, block_ids, near, far)


def solve_kernel(block_total, ids_ref, table_ref, coefs_ref, root_ref, centre_ref, around_ref,
                 levels_ref, bottom_ref, first_column_ref, last_column_ref, near_ref, far_ref,
                 corrected_ref, height_ref, sensitivity_ref,
                 natural, source, even, odd, extra, column, in_sems, out_sems):
    slots, comps, depth, rows, cols = column.shape
    strips, deep, tall = window_shape(slots, rows)

    middle = first_column_ref.shape[0]
    copies_in = [
        pltpu.make_async_copy(first_column_ref, column.at[pl.ds(0, middle)], in_sems.at[0]),
        pltpu.make_async_copy(
            last_column_ref, column.at[pl.ds(middle, slots - middle)], in_sems.at[1]
        ),
    ]
    for copy in copies_in:
        copy.start()

    count = near_ref.shape[0]

    def load(place):
        inner = place & (count - 1)
        return jnp.where(place < count, near_ref[inner], far_ref[inner])

    lane = lax.broadcasted_iota(jnp.int32, (rows, LANES), 1)
    for w in range(slots + 2):
        places = [table_ref[w * len(NEIGHBOURS) + n] for n in range(len(NEIGHBOURS))]
        put_window(natural, w * tall, rows, [load(place) for place in places], lane)

    coefs, step_scale = chebyshev_sum(STEPS)

    def put(i, x, values):
        start = i * PITCH + PAD + x
        stop = start + values.shape[0]
        root = root_ref[start:stop, :]
        values = jnp.where(root > 0.0, root * values, 0.0)
        source[start:stop, :] = values
        even[start:stop, :] = coefs[STEPS - 1] * values
        odd[start:stop, :] = jnp.zeros_like(values)

    zeros = jnp.zeros((PAD, LANES), jnp.float32)
    for ref in (even, odd):
        for i in range(deep):
            ref[i * PITCH:i * PITCH + PAD, :] = zeros
            ref[(i + 1) * PITCH - PAD:(i + 1) * PITCH, :] = zeros
    turn(natural, deep, put)

    chunks = WIDTH // SUBLANES

    def apply(current, target, coef, gain, low, count):
        size = (chunks - 2 * low) // count
        assert size * count == chunks - 2 * low

        def group(index, carry):
            out = []
            for n in range(size):
                here, above, below, at = strip_rows(current, low + index * size + n, deep)
                for i, a in enumerate(at):
                    others = (rows_at(current, a, 1) + rows_at(current, a, -1)) + (
                        above[i] + below[i]
                    )
                    pushed = rows_at(centre_ref, a) * here[i] + rows_at(around_ref, a) * others
                    if gain != 1.0:
                        pushed = gain * pushed
                    kept = coef * rows_at(source, a) - rows_at(target, a)
                    out.append((a, kept + pushed))
            for a, value in out:
                target[pl.ds(a, SUBLANES), :] = value
            return carry

        lax.fori_loop(0, count, group, 0)

    def bounds(m):
        low = m // (2 * SUBLANES) * 2
        return low, 4

    runs = []
    for m in range(1, STEPS - 1, 2):
        if runs and runs[-1][1] == bounds(m):
            runs[-1][2] += 1
        else:
            runs.append([m, bounds(m), 1])
    for first, (low, count), pairs in runs:
        def two_steps(pair, carry, first=first, low=low, count=count):
            m = first + 2 * pair
            apply(even, odd, coefs_ref[m], 1.0, low, count)
            apply(odd, even, coefs_ref[m + 1], 1.0, low, count)
            return carry

        lax.fori_loop(0, pairs, two_steps, 0)
    low, count = bounds(STEPS - 1)
    apply(even, odd, coefs[0], 0.5, low, count)

    low = STEPS // SUBLANES - 1

    def one_height(chunk, carry):
        out = []
        for i in range(deep):
            a = pl.multiple_of(i * PITCH + PAD + chunk * SUBLANES, SUBLANES)
            root = rows_at(root_ref, a)
            out.append((a, jnp.where(root > 0.0, rows_at(odd, a) / root, 0.0)))
        for a, value in out:
            extra[pl.ds(a, SUBLANES), :] = value
        return carry

    lax.fori_loop(low, chunks - low, one_height, 0)

    def differences(chunk, carry):
        here, above, below, at = strip_rows(extra, chunk, deep)
        root, root_above, root_below, _ = strip_rows(root_ref, chunk, deep)
        out = []
        for i, a in enumerate(at):
            east_step = rows_at(extra, a, 1) - here[i]
            west_step = here[i] - rows_at(extra, a, -1)
            south_step = below[i] - here[i]
            north_step = here[i] - above[i]
            energy = root[i] * (
                (rows_at(root_ref, a, 1) * east_step * east_step
                 + rows_at(root_ref, a, -1) * west_step * west_step)
                + (root_below[i] * south_step * south_step
                   + root_above[i] * north_step * north_step)
            )
            scaled = rows_at(around_ref, a) * (1.0 / step_scale)
            out.append((even, a, east_step))
            out.append((source, a, 0.25 * energy / jnp.maximum(scaled, 0.25)))
        for ref, a, value in out:
            ref[pl.ds(a, SUBLANES), :] = value
        return carry

    lax.fori_loop(low + 1, chunks - low - 1, differences, 0)

    def turn_back(ref, tile):
        starts = [i * PITCH + PAD + STEPS for i in range(deep)]
        turned = flip([ref[start:start + LANES, :] for start in starts])
        for i, values in enumerate(turned):
            natural[tile, pl.ds(i, LANES, stride=deep), :] = values

    def cut(tile, w, shift=0):
        return natural[tile, pl.ds(w * tall + STEPS + shift, rows), :]

    def copy_out(b, c):
        return pltpu.make_async_copy(column.at[b, c], corrected_ref.at[b, c], out_sems.at[b, c])

    def correct(b, c, step):
        levels = levels_ref[b] * jnp.where(ids_ref[b] < block_total, 1, 0)
        push = pressure_gain * step
        lowest = bottom_ref[b, c] - push

        def some_levels(base, size):
            out = []
            for j in range(size):
                k = base + j
                value = jnp.where(levels == k + 1, lowest, column[b, c, k] - push)
                out.append((k, jnp.where(levels > k, value, 0.0)))
            for k, value in out:
                column[b, c, k] = value

        def one_chunk(chunk, inner):
            some_levels(chunk * CHUNK, CHUNK)
            return inner

        lax.fori_loop(0, depth // CHUNK, one_chunk, 0)
        some_levels(depth // CHUNK * CHUNK, depth % CHUNK)
        copy_out(b, c).start()

    turn_back(even, 0)
    for copy in copies_in:
        copy.wait()

    def correct_east(b, carry):
        correct(b, 0, cut(0, b))
        return carry

    def correct_north(b, carry):
        correct(b, 1, cut(1, b, 1) - cut(1, b))
        return carry

    lax.fori_loop(0, slots, correct_east, 0)
    turn_back(extra, 1)
    lax.fori_loop(0, slots, correct_north, 0)
    turn_back(source, 0)
    for h in range(2):
        height_ref[:, h * LANES:(h + 1) * LANES] = cut(1, slots + h)
        sensitivity_ref[:, h * LANES:(h + 1) * LANES] = cut(0, slots + h)

    for b in range(slots):
        for c in range(comps):
            copy_out(b, c).wait()


def surface_solve(near, far, weights, block_ids, level_count, bottom, columns, block_total):
    root, centre, around, table = weights
    comps, depth, rows, cols = columns[0].shape[1:]
    slots = level_count.shape[0]
    assert comps == 2
    full = (slots, comps, depth, rows, cols)
    deep = window_shape(slots, rows)[1]
    turned = pltpu.VMEM(root.shape, jnp.float32)
    coefs = jnp.array(chebyshev_sum(STEPS)[0][::-1], jnp.float32)
    return pl.pallas_call(
        functools.partial(solve_kernel, block_total),
        in_specs=[SMEM, SMEM, SMEM] + [VMEM] * 5 + [HBM] * 2 + [VMEM] * 2,
        out_specs=[HBM, VMEM, VMEM],
        out_shape=[
            jax.ShapeDtypeStruct(full, jnp.float32),
            jax.ShapeDtypeStruct((rows, 2 * cols), jnp.float32),
            jax.ShapeDtypeStruct((rows, 2 * cols), jnp.float32),
        ],
        scratch_shapes=[
            pltpu.VMEM((2, LANES * deep, LANES), jnp.float32),
            turned,
            turned,
            turned,
            turned,
            pltpu.VMEM(full, jnp.float32),
            pltpu.SemaphoreType.DMA((2,)),
            pltpu.SemaphoreType.DMA((slots, comps)),
        ],
        compiler_params=params(SOLVE_VMEM),
        cost_estimate=pl.CostEstimate(
            flops=9 * STEPS * root.size, bytes_accessed=16 * root.size, transcendentals=0
        ),
        name="surface_solve",
    )(block_ids, table, coefs, root, centre, around, level_count, bottom, *columns, near, far)


def stack_kernel(parts, *refs):
    out_ref = refs[-1]
    for p in range(parts):
        out_ref[p] = refs[p][...]


def stack_after(parts, *tokens):
    return pl.pallas_call(
        functools.partial(stack_kernel, len(parts)),
        in_specs=[VMEM] * len(parts) + [ANYWHERE] * len(tokens),
        out_specs=VMEM,
        out_shape=jax.ShapeDtypeStruct((len(parts),) + parts[0].shape, jnp.float32),
        compiler_params=params(WINDOW_VMEM),
        name="stack_after",
    )(*parts, *tokens)


def swap(values, axis, mask):
    count = lax.axis_size(axis)
    return lax.ppermute(values, axis, [(i, i ^ mask) for i in range(count)])


def per_device(adjoint_vel, velocity, drag_coef, level_count, block_ids, bathymetry, land_mask):
    slots = block_ids.shape[0]
    rows, cols = drag_coef.shape[1:]
    lon_count = lax.axis_size("gx")
    lat_count = lax.axis_size("gy")
    half = lat_count // 2
    block_total = 2 * lon_count * lat_count
    me = jnp.stack([lax.axis_index("gx"), lax.axis_index("gy")]).astype(jnp.int32)

    depths = depth_payload(bathymetry, land_mask, block_ids)
    depth_parts = [depths] + [swap(depths, "gy", 2 * m) for m in range(1, half)]
    forcing = column_forcing(adjoint_vel, level_count)

    parts = [forcing] + [swap(forcing, "gy", 2 * m) for m in range(1, half)]
    near_depths = stack_after(depth_parts, forcing)
    near_depths = [near_depths] + [swap(near_depths, "gx", m) for m in range(1, lon_count)]
    columns = (adjoint_vel, velocity, drag_coef, level_count, block_ids)
    middle = (slots + 1) // 2
    first_column, *first_rest = column_mixing(*columns, forcing, block_total, 0, middle)
    line = stack_after(parts, first_rest[0])

    near = [line] + [swap(line, "gx", m) for m in range(1, lon_count)]
    near_depths = stack_after(near_depths, line)
    near_depths = near_depths.reshape((lon_count * half,) + depths.shape)
    far_depths = swap(near_depths, "gy", 1)
    last_column, bottom, drag_gradient = column_mixing(
        *columns, line, block_total, middle, slots, first_rest
    )
    weights = surface_weights(
        near_depths, far_depths, me, block_ids, rows, lon_count, lat_count
    )

    near = stack_after(near, bottom, weights[0])
    far = swap(near, "gy", 1)

    corrected, height, sensitivity = surface_solve(
        near.reshape((-1, rows, cols)), far.reshape((-1, rows, cols)), weights,
        block_ids, level_count, bottom, (first_column, last_column), block_total,
    )
    return corrected, drag_gradient, height, sensitivity


def solution(mesh):
    in_specs = (
        P(("gx", "gy"), None, None, None, None),
        P(("gx", "gy"), None, None, None, None),
        P(("gx", "gy"), None, None),
        P(("gx", "gy"), None, None),
        P(("gx", "gy")),
        P("gy", "gx"),
        P("gy", "gx"),
    )
    out_specs = (
        P(("gx", "gy"), None, None, None, None),
        P(("gx", "gy"), None, None),
        P("gy", "gx"),
        P("gy", "gx"),
    )
    return jax.shard_map(
        per_device, mesh=mesh, in_specs=in_specs, out_specs=out_specs, check_vma=False
    )
```

```python
import functools

import jax
import jax.numpy as jnp
import numpy as np
from jax import lax
from jax.experimental import pallas as pl
from jax.experimental.pallas import tpu as pltpu
from jax.sharding import PartitionSpec as P

STEPS = 32

mix_rate = 0.25
drag_step = 0.5
force_scale = 0.25
pressure_gain = 0.5
surface_shift = 1.0 / 64.0
speed_floor = 0.01

LANES = 128
SUBLANES = 8
MIB = 1024 * 1024
FIRST_VMEM = 61 * MIB
MIXING_VMEM = 52 * MIB
SOLVE_VMEM = 50 * MIB
WINDOW_VMEM = 16 * MIB


def chebyshev_sum(total_steps):
    highest = surface_shift + 8.0
    centre = 0.5 * (highest + surface_shift)
    radius = 0.5 * (highest - surface_shift)
    sigma_ratio = centre / radius

    def operate(series):
        shifted = np.zeros_like(series)
        shifted[1] += series[0]
        for k in range(1, len(series) - 1):
            shifted[k + 1] += 0.5 * series[k]
            shifted[k - 1] += 0.5 * series[k]
        return centre * series - radius * shifted

    height = np.zeros(total_steps + 2)
    residual = np.zeros(total_steps + 2)
    residual[0] = 1.0
    direction = residual / centre
    ratio_prev = 1.0 / sigma_ratio
    for _ in range(total_steps):
        height = height + direction
        residual = residual - operate(direction)
        ratio_next = 1.0 / (2.0 * sigma_ratio - ratio_prev)
        direction = ratio_next * ratio_prev * direction + 2.0 * ratio_next / radius * residual
        ratio_prev = ratio_next
    return [float(c) for c in height[:total_steps]], 2.0 / radius


def params(limit):
    return pltpu.CompilerParams(vmem_limit_bytes=limit)


SMEM = pl.BlockSpec(memory_space=pltpu.SMEM)
VMEM = pl.BlockSpec(memory_space=pltpu.VMEM)
ANYWHERE = pl.BlockSpec(memory_space=pl.ANY)
HBM = pl.BlockSpec(memory_space=pltpu.HBM)


def payload_kernel(ids_ref, bathymetry_ref, mask_ref, levels_ref, adjoint_ref, out_ref,
                   ids, bathymetry, mask, levels_held, held, small_sems, sems):
    slots, comps, depth, rows, cols = held.shape
    small = [
        pltpu.make_async_copy(ref, buffer, small_sems.at[n])
        for n, (ref, buffer) in enumerate((
            (ids_ref, ids), (bathymetry_ref, bathymetry), (mask_ref, mask),
            (levels_ref, levels_held),
        ))
    ]
    for copy in small:
        copy.start()
    for b in range(slots):
        for c in range(comps):
            pltpu.make_async_copy(adjoint_ref.at[b, c], held.at[b, c], sems.at[b, c]).start()
    for copy in small:
        copy.wait()

    base = slots * rows
    scaled = bathymetry[...] * mask[...].astype(jnp.float32)
    out_ref[base:base + rows, :] = scaled[:, :cols]
    out_ref[base + rows:base + 2 * rows, :] = scaled[:, cols:]
    lane = lax.broadcasted_iota(jnp.int32, (SUBLANES, cols), 1)
    listed = jnp.zeros((SUBLANES, cols), jnp.int32)
    for s in range(slots):
        listed = jnp.where(lane == s, ids[s], listed)
    out_ref[base + 2 * rows:base + 2 * rows + SUBLANES, :] = listed.astype(jnp.float32)

    def one_slot(b, carry):
        levels = levels_held[b]
        total = jnp.zeros((rows, cols), jnp.float32)
        for c in range(comps):
            pltpu.make_async_copy(adjoint_ref.at[b, c], held.at[b, c], sems.at[b, c]).wait()
            for k in range(depth):
                total = total + jnp.where(levels > k, held[b, c, k], 0.0)
        out_ref[pl.ds(pl.multiple_of(b * rows, SUBLANES), rows), :] = force_scale * total
        return carry

    lax.fori_loop(0, slots, one_slot, 0)


def device_payload(adjoint_vel, level_count, bathymetry, land_mask, block_ids):
    slots, comps, depth, rows, cols = adjoint_vel.shape
    return pl.pallas_call(
        payload_kernel,
        in_specs=[HBM] * 5,
        out_specs=VMEM,
        out_shape=pltpu.VMEM(((slots + 2) * rows + SUBLANES, cols), jnp.float32),
        scratch_shapes=[
            pltpu.SMEM(block_ids.shape, jnp.int32),
            pltpu.VMEM(bathymetry.shape, jnp.float32),
            pltpu.VMEM(land_mask.shape, jnp.int32),
            pltpu.VMEM(level_count.shape, jnp.int32),
            pltpu.VMEM(adjoint_vel.shape, jnp.float32),
            pltpu.SemaphoreType.DMA((4,)),
            pltpu.SemaphoreType.DMA((slots, comps)),
        ],
        compiler_params=params(FIRST_VMEM),
        cost_estimate=pl.CostEstimate(
            flops=2 * adjoint_vel.size, bytes_accessed=4 * adjoint_vel.size, transcendentals=0
        ),
        name="device_payload",
    )(block_ids, bathymetry, land_mask, level_count, adjoint_vel)


CHUNK = 8


def mixing_kernel(block_total, ids_ref, levels_ref, drag_ref, adjoint_ref, velocity_ref, after_ref,
                  column_ref, bottom_ref, gradient_ref, adjoint, velocity, column,
                  in_sems, out_sems):
    slots, comps, depth, rows, cols = adjoint.shape
    group = 16
    parts = rows // group

    def copies_in(b):
        return (
            pltpu.make_async_copy(adjoint_ref.at[b], adjoint.at[b], in_sems.at[0, b]),
            pltpu.make_async_copy(velocity_ref.at[b], velocity.at[b], in_sems.at[1, b]),
        )

    def copy_out(b):
        return pltpu.make_async_copy(column.at[b], column_ref.at[b], out_sems.at[b])

    for b in range(slots):
        for copy in copies_in(b):
            copy.start()

    def one_group(b, index):
        flag = jnp.where(ids_ref[b] < block_total, 1.0, 0.0)
        span = pl.ds(pl.multiple_of(index * group, group), group)
        levels = levels_ref[b, span, :]
        zero = jnp.zeros(levels.shape, jnp.float32)
        x = [zero, zero]
        once = [zero, zero]
        first_flux = [zero, zero]
        second_flux = [zero, zero]
        flow = [zero, zero]
        field = [zero, zero]
        rate_before = zero
        for low in range(0, depth + 2, CHUNK):
            here = range(low, min(low + CHUNK, depth + 2))
            loaded = {}
            for k in here:
                if k < depth:
                    for c in range(2):
                        loaded[k, c] = (
                            adjoint[b, c, k, span, :],
                            velocity[b, c, k, span, :],
                        )
            done = {}
            for k in here:
                if k < depth:
                    wet = levels > k
                    rate = jnp.where(wet, mix_rate, 0.0)
                    is_bottom_flow = levels == k + 1
                is_bottom = levels == k - 1
                for c in range(2):
                    if k < depth:
                        fresh = jnp.where(wet, loaded[k, c][0], 0.0)
                        flow[c] = jnp.where(
                            is_bottom_flow, loaded[k, c][1].astype(jnp.float32), flow[c]
                        )
                    fresh_once = None
                    if 1 <= k < depth:
                        flux = (fresh - x[c]) * rate
                        fresh_once = x[c] + (flux - first_flux[c])
                        first_flux[c] = flux
                    elif k == depth:
                        fresh_once = x[c] - first_flux[c]
                    if k < depth:
                        x[c] = fresh
                    if 2 <= k:
                        if k <= depth:
                            flux = (fresh_once - once[c]) * rate_before
                            twice = once[c] + (flux - second_flux[c])
                            second_flux[c] = flux
                        else:
                            twice = once[c] - second_flux[c]
                        done[k - 2, c] = twice
                        field[c] = jnp.where(is_bottom, twice, field[c])
                    if fresh_once is not None:
                        once[c] = fresh_once
                if k < depth:
                    rate_before = rate
            for (k, c), value in done.items():
                column[b, c, k, span, :] = value
        speed = jnp.sqrt(flow[0] * flow[0] + flow[1] * flow[1] + speed_floor)
        along = flow[0] * field[0] + flow[1] * field[1]
        ratio = along / speed
        drag = drag_ref[b, span, :]
        for c in range(2):
            bottom_ref[b, c, span, :] = field[c] - drag_step * drag * (
                speed * field[c] + flow[c] * ratio
            )
        gradient_ref[b, span, :] = -drag_step * speed * along * flag

    def one(step, carry):
        b = lax.div(step, parts)
        index = lax.rem(step, parts)

        @pl.when(index == 0)
        def _():
            for copy in copies_in(b):
                copy.wait()

        one_group(b, index)

        @pl.when(index == parts - 1)
        def _():
            copy_out(b).start()

        return carry

    lax.fori_loop(0, slots * parts, one, 0)
    for b in range(slots):
        copy_out(b).wait()


def column_mixing(adjoint_vel, velocity, drag_coef, level_count, block_ids, after, block_total):
    slots, comps, depth, rows, cols = adjoint_vel.shape
    return pl.pallas_call(
        functools.partial(mixing_kernel, block_total),
        in_specs=[SMEM, VMEM, VMEM, HBM, HBM, ANYWHERE],
        out_specs=[HBM, VMEM, VMEM],
        out_shape=[
            pltpu.HBM(adjoint_vel.shape, jnp.float32),
            pltpu.VMEM((slots, comps, rows, cols), jnp.float32),
            pltpu.HBM((slots, rows, cols), jnp.float32),
        ],
        scratch_shapes=[
            pltpu.VMEM(adjoint_vel.shape, adjoint_vel.dtype),
            pltpu.VMEM(velocity.shape, velocity.dtype),
            pltpu.VMEM(adjoint_vel.shape, jnp.float32),
            pltpu.SemaphoreType.DMA((2, slots)),
            pltpu.SemaphoreType.DMA((slots,)),
        ],
        compiler_params=params(MIXING_VMEM),
        cost_estimate=pl.CostEstimate(
            flops=14 * adjoint_vel.size, bytes_accessed=10 * adjoint_vel.size, transcendentals=0
        ),
        name="column_mixing",
    )(block_ids, level_count, drag_coef, adjoint_vel, velocity, after)


PAD = SUBLANES
WIDTH = LANES + 2 * STEPS
PITCH = WIDTH + 2 * PAD
NEIGHBOURS = [(down, right) for down in (-1, 0, 1) for right in (0, 1, -1)]


def window_shape(slots, rows):
    strips = LANES // (slots + 2)
    deep = pl.cdiv(rows + 2 * STEPS, strips)
    return strips, deep, strips * deep


def log2(count):
    bits = count.bit_length() - 1
    assert 1 << bits == count
    return bits


def window_places(me_ref, ids_ref, slots, lon_count, lat_count):
    places = []
    for w in range(slots + 2):
        if w < slots:
            block = jnp.where(ids_ref[w] < 2 * lon_count * lat_count, ids_ref[w], 0)
        else:
            block = (me_ref[0] * lat_count + me_ref[1]) * 2 + (w - slots)
        pair = block >> 1
        column = (pair >> log2(lat_count)) * 2 + (block & 1)
        places.append((pair & (lat_count - 1), column))
    return places


def put_window(natural, base, rows, blocks, lane):
    for i in range(3):
        here, east, west = blocks[3 * i:3 * i + 3]
        sides = jnp.where(lane < STEPS, east, jnp.where(lane >= LANES - STEPS, west, 0.0))
        start = base + i * rows
        natural[0, start:start + rows, :] = here
        natural[1, start:start + rows, :] = sides


def turn(natural, deep, put):
    for i in range(deep):
        put(i, STEPS, natural[0, pl.ds(i, LANES, stride=deep), :].T)
        sides = natural[1, pl.ds(i, LANES, stride=deep), :].T
        put(i, STEPS + LANES, sides[:STEPS])
        put(i, 0, sides[LANES - STEPS:])


def rows_at(ref, start, shift=0):
    return ref[pl.ds(start + shift, SUBLANES), :]


def strip_rows(ref, chunk, deep):
    at = [i * PITCH + PAD + chunk * SUBLANES for i in range(deep)]
    if not isinstance(chunk, int):
        at = [pl.multiple_of(a, SUBLANES) for a in at]
    here = [rows_at(ref, a) for a in at]
    above = [pltpu.roll(here[-1], 1, 1)] + here[:-1]
    below = here[1:] + [pltpu.roll(here[0], LANES - 1, 1)]
    return here, above, below, at


def weights_kernel(slots, lon_count, lat_count, me_ref, ids_ref, near_ref, far_ref,
                   root_ref, centre_ref, around_ref, table_ref,
                   natural, all_ids, places_of, sems):
    half = lat_count // 2
    count = lon_count * half
    rows = (near_ref.shape[1] - SUBLANES) // 2
    strips, deep, tall = window_shape(slots, rows)
    column_count = 2 * lon_count
    parts = (near_ref, far_ref)
    copies = [
        pltpu.make_async_copy(
            parts[p].at[:, pl.ds(2 * rows, 1), :], all_ids.at[p], sems.at[p]
        )
        for p in range(2)
    ]
    for copy in copies:
        copy.start()
    natural[...] = jnp.zeros_like(natural)

    def load(lat, column):
        inside = (lat >= 0) & (lat < lat_count) & (column >= 0) & (column < column_count)
        lat_safe = jnp.clip(lat, 0, lat_count - 1)
        column_safe = jnp.clip(column, 0, column_count - 1)
        lon_xor = (column_safe >> 1) ^ me_ref[0]
        lat_xor = lat_safe ^ me_ref[1]
        place = lon_xor * half + (lat_xor >> 1)
        start = pl.multiple_of((column_safe & 1) * rows, SUBLANES)
        near = near_ref[place, pl.ds(start, rows), :]
        far = far_ref[place, pl.ds(start, rows), :]
        here = jnp.where((lat_xor & 1) == 0, near, far)
        return here * jnp.where(inside, 1.0, 0.0)

    lane = lax.broadcasted_iota(jnp.int32, (rows, LANES), 1)
    places = window_places(me_ref, ids_ref, slots, lon_count, lat_count)
    for w, (lat, column) in enumerate(places):
        blocks = [load(lat + down, column + right) for down, right in NEIGHBOURS]
        put_window(natural, w * tall, rows, blocks, lane)

    for copy in copies:
        copy.wait()

    def one_device(n, carry):
        for p in range(2):
            for s in range(slots):
                block = all_ids[p, n, 0, s].astype(jnp.int32)
                places_of[block] = (p * count + n) * slots + s
        return carry

    lax.fori_loop(0, count, one_device, 0)
    for w, (lat, column) in enumerate(places):
        for n, (down, right) in enumerate(NEIGHBOURS):
            lat_safe = jnp.clip(lat + down, 0, lat_count - 1)
            column_safe = jnp.clip(column + right, 0, column_count - 1)
            block = ((column_safe >> 1) * lat_count + lat_safe) * 2 + (column_safe & 1)
            table_ref[w * len(NEIGHBOURS) + n] = places_of[block]

    scale = chebyshev_sum(STEPS)[1]

    def put(i, x, values):
        start = i * PITCH + PAD + x
        root_ref[start:start + values.shape[0], :] = jnp.sqrt(values)
        around_ref[start:start + values.shape[0], :] = scale * values

    turn(natural, deep, put)
    zeros = jnp.zeros((PAD, LANES), jnp.float32)
    for i in range(deep):
        root_ref[i * PITCH:i * PITCH + PAD, :] = zeros
        root_ref[(i + 1) * PITCH - PAD:(i + 1) * PITCH, :] = zeros

    def one_chunk(chunk, carry):
        out = []
        here, above, below, at = strip_rows(root_ref, chunk, deep)
        for i, a in enumerate(at):
            others = (rows_at(root_ref, a, 1) + rows_at(root_ref, a, -1)) + (above[i] + below[i])
            out.append((a, 2.0 - scale * here[i] * others))
        for a, value in out:
            centre_ref[pl.ds(a, SUBLANES), :] = value
        return carry

    lax.fori_loop(0, WIDTH // SUBLANES, one_chunk, 0)


def surface_weights(near, far, me, block_ids, rows, lon_count, lat_count):
    slots = block_ids.shape[0]
    assert near.shape[-1] == LANES
    strips, deep, tall = window_shape(slots, rows)
    shape = jax.ShapeDtypeStruct((deep * PITCH, LANES), jnp.float32)
    return pl.pallas_call(
        functools.partial(weights_kernel, slots, lon_count, lat_count),
        in_specs=[SMEM, SMEM, VMEM, VMEM],
        out_specs=[VMEM, VMEM, VMEM, SMEM],
        out_shape=[
            shape,
            shape,
            shape,
            jax.ShapeDtypeStruct(((slots + 2) * len(NEIGHBOURS),), jnp.int32),
        ],
        scratch_shapes=[
            pltpu.VMEM((2, LANES * deep, LANES), jnp.float32),
            pltpu.SMEM((2, near.shape[0], 1, LANES), jnp.float32),
            pltpu.SMEM((2 * lon_count * lat_count + 1,), jnp.int32),
            pltpu.SemaphoreType.DMA((2,)),
        ],
        compiler_params=params(WINDOW_VMEM),
        cost_estimate=pl.CostEstimate(
            flops=0, bytes_accessed=8 * MIB, transcendentals=0
        ),
        name="surface_weights",
    )(me, block_ids, near, far)


BATCH = 3


def solve_kernel(block_total, ids_ref, table_ref, coefs_ref, root_ref, centre_ref, around_ref,
                 levels_ref, bottom_ref, column_ref, near_ref, far_ref,
                 corrected_ref, height_ref, sensitivity_ref,
                 natural, source, even, odd, extra, column, in_sems, out_sems):
    slots, comps, depth, rows, cols = column.shape
    strips, deep, tall = window_shape(slots, rows)

    copies_in = [
        pltpu.make_async_copy(column_ref.at[b], column.at[b], in_sems.at[b]) for b in range(slots)
    ]
    for copy in copies_in:
        copy.start()

    count = near_ref.shape[0]

    def load(place):
        inner = place & (count - 1)
        return jnp.where(place < count, near_ref[inner], far_ref[inner])

    lane = lax.broadcasted_iota(jnp.int32, (rows, LANES), 1)
    for w in range(slots + 2):
        places = [table_ref[w * len(NEIGHBOURS) + n] for n in range(len(NEIGHBOURS))]
        put_window(natural, w * tall, rows, [load(place) for place in places], lane)

    coefs, step_scale = chebyshev_sum(STEPS)

    def put(i, x, values):
        start = i * PITCH + PAD + x
        stop = start + values.shape[0]
        root = root_ref[start:stop, :]
        values = jnp.where(root > 0.0, root * values, 0.0)
        source[start:stop, :] = values
        even[start:stop, :] = coefs[STEPS - 1] * values
        odd[start:stop, :] = jnp.zeros_like(values)

    zeros = jnp.zeros((PAD, LANES), jnp.float32)
    for ref in (even, odd):
        for i in range(deep):
            ref[i * PITCH:i * PITCH + PAD, :] = zeros
            ref[(i + 1) * PITCH - PAD:(i + 1) * PITCH, :] = zeros
    turn(natural, deep, put)

    chunks = WIDTH // SUBLANES

    def apply(current, target, coef, gain, m):
        first = m // SUBLANES

        def store(batch):
            for a, value in batch:
                target[pl.ds(a, SUBLANES), :] = value

        late = []
        for start in range(first, chunks - first, BATCH):
            batch = []
            for chunk in range(start, min(start + BATCH, chunks - first)):
                here, above, below, at = strip_rows(current, chunk, deep)
                for i, a in enumerate(at):
                    others = (rows_at(current, a, 1) + rows_at(current, a, -1)) + (
                        above[i] + below[i]
                    )
                    pushed = rows_at(centre_ref, a) * here[i] + rows_at(around_ref, a) * others
                    if gain != 1.0:
                        pushed = gain * pushed
                    kept = coef * rows_at(source, a) - rows_at(target, a)
                    batch.append((a, kept + pushed))
            store(late)
            late = batch
        store(late)

    runs = []
    for m in range(1, STEPS - 1, 2):
        if runs and runs[-1][0] // SUBLANES == m // SUBLANES:
            runs[-1][1] += 1
        else:
            runs.append([m, 1])
    for first, pairs in runs:
        def two_steps(pair, carry, first=first):
            m = first + 2 * pair
            apply(even, odd, coefs_ref[m], 1.0, first)
            apply(odd, even, coefs_ref[m + 1], 1.0, first)
            return carry

        lax.fori_loop(0, pairs, two_steps, 0)
    apply(even, odd, coefs[0], 0.5, STEPS - 1)

    low = STEPS // SUBLANES - 1

    def one_height(chunk, carry):
        out = []
        for i in range(deep):
            a = pl.multiple_of(i * PITCH + PAD + chunk * SUBLANES, SUBLANES)
            root = rows_at(root_ref, a)
            out.append((a, jnp.where(root > 0.0, rows_at(odd, a) / root, 0.0)))
        for a, value in out:
            extra[pl.ds(a, SUBLANES), :] = value
        return carry

    lax.fori_loop(low, chunks - low, one_height, 0)

    def differences(chunk, carry):
        here, above, below, at = strip_rows(extra, chunk, deep)
        root, root_above, root_below, _ = strip_rows(root_ref, chunk, deep)
        out = []
        for i, a in enumerate(at):
            east_step = rows_at(extra, a, 1) - here[i]
            west_step = here[i] - rows_at(extra, a, -1)
            south_step = below[i] - here[i]
            north_step = here[i] - above[i]
            energy = root[i] * (
                (rows_at(root_ref, a, 1) * east_step * east_step
                 + rows_at(root_ref, a, -1) * west_step * west_step)
                + (root_below[i] * south_step * south_step
                   + root_above[i] * north_step * north_step)
            )
            scaled = rows_at(around_ref, a) * (1.0 / step_scale)
            out.append((even, a, east_step))
            out.append((source, a, 0.25 * energy / jnp.maximum(scaled, 0.25)))
        for ref, a, value in out:
            ref[pl.ds(a, SUBLANES), :] = value
        return carry

    lax.fori_loop(low + 1, chunks - low - 1, differences, 0)

    def turn_back(ref, tile):
        for i in range(deep):
            start = i * PITCH + PAD + STEPS
            natural[tile, pl.ds(i, LANES, stride=deep), :] = ref[start:start + LANES, :].T

    def cut(tile, w, shift=0):
        return natural[tile, pl.ds(w * tall + STEPS + shift, rows), :]

    def copy_out(b, c):
        return pltpu.make_async_copy(column.at[b, c], corrected_ref.at[b, c], out_sems.at[b, c])

    def correct(b, c, step):
        levels = levels_ref[b] * jnp.where(ids_ref[b] < block_total, 1, 0)
        push = pressure_gain * step
        lowest = bottom_ref[b, c] - push

        def some_levels(base, size):
            out = []
            for j in range(size):
                k = base + j
                value = jnp.where(levels == k + 1, lowest, column[b, c, k] - push)
                out.append((k, jnp.where(levels > k, value, 0.0)))
            for k, value in out:
                column[b, c, k] = value

        def one_chunk(chunk, inner):
            some_levels(chunk * CHUNK, CHUNK)
            return inner

        lax.fori_loop(0, depth // CHUNK, one_chunk, 0)
        some_levels(depth // CHUNK * CHUNK, depth % CHUNK)
        copy_out(b, c).start()

    turn_back(even, 0)
    for copy in copies_in:
        copy.wait()

    def correct_east(b, carry):
        correct(b, 0, cut(0, b))
        return carry

    def correct_north(b, carry):
        correct(b, 1, cut(1, b, 1) - cut(1, b))
        return carry

    lax.fori_loop(0, slots, correct_east, 0)
    turn_back(extra, 1)
    lax.fori_loop(0, slots, correct_north, 0)
    turn_back(source, 0)
    for h in range(2):
        height_ref[:, h * LANES:(h + 1) * LANES] = cut(1, slots + h)
        sensitivity_ref[:, h * LANES:(h + 1) * LANES] = cut(0, slots + h)

    for b in range(slots):
        for c in range(comps):
            copy_out(b, c).wait()


def surface_solve(near, far, weights, block_ids, level_count, bottom, column, block_total):
    root, centre, around, table = weights
    slots, comps, depth, rows, cols = column.shape
    assert comps == 2
    deep = window_shape(slots, rows)[1]
    turned = pltpu.VMEM(root.shape, jnp.float32)
    coefs = jnp.array(chebyshev_sum(STEPS)[0][::-1], jnp.float32)
    return pl.pallas_call(
        functools.partial(solve_kernel, block_total),
        in_specs=[SMEM, SMEM, SMEM] + [VMEM] * 5 + [HBM] + [VMEM] * 2,
        out_specs=[HBM, VMEM, VMEM],
        out_shape=[
            jax.ShapeDtypeStruct(column.shape, jnp.float32),
            jax.ShapeDtypeStruct((rows, 2 * cols), jnp.float32),
            jax.ShapeDtypeStruct((rows, 2 * cols), jnp.float32),
        ],
        scratch_shapes=[
            pltpu.VMEM((2, LANES * deep, LANES), jnp.float32),
            turned,
            turned,
            turned,
            turned,
            pltpu.VMEM(column.shape, jnp.float32),
            pltpu.SemaphoreType.DMA((slots,)),
            pltpu.SemaphoreType.DMA((slots, comps)),
        ],
        compiler_params=params(SOLVE_VMEM),
        cost_estimate=pl.CostEstimate(
            flops=9 * STEPS * root.size, bytes_accessed=16 * root.size, transcendentals=0
        ),
        name="surface_solve",
    )(block_ids, table, coefs, root, centre, around, level_count, bottom, column, near, far)


def stack_kernel(parts, *refs):
    out_ref = refs[-1]
    for p in range(parts):
        out_ref[p] = refs[p][...]


def stack_after(parts, *tokens):
    return pl.pallas_call(
        functools.partial(stack_kernel, len(parts)),
        in_specs=[VMEM] * len(parts) + [ANYWHERE] * len(tokens),
        out_specs=VMEM,
        out_shape=jax.ShapeDtypeStruct((len(parts),) + parts[0].shape, jnp.float32),
        compiler_params=params(WINDOW_VMEM),
        name="stack_after",
    )(*parts, *tokens)


def split_kernel(parts, *refs):
    head_ref, tail_ref = refs[-2:]
    head = head_ref.shape[1]
    for p in range(parts):
        head_ref[p] = refs[p][:head, :]
        tail_ref[p] = refs[p][head:, :]


def split_after(parts, head, *tokens):
    rows, cols = parts[0].shape
    return pl.pallas_call(
        functools.partial(split_kernel, len(parts)),
        in_specs=[VMEM] * len(parts) + [ANYWHERE] * len(tokens),
        out_specs=[VMEM, VMEM],
        out_shape=[
            jax.ShapeDtypeStruct((len(parts), head, cols), jnp.float32),
            jax.ShapeDtypeStruct((len(parts), rows - head, cols), jnp.float32),
        ],
        compiler_params=params(WINDOW_VMEM),
        name="split_after",
    )(*parts, *tokens)


def swap(values, axis, mask):
    count = lax.axis_size(axis)
    return lax.ppermute(values, axis, [(i, i ^ mask) for i in range(count)])


def per_device(adjoint_vel, velocity, drag_coef, level_count, block_ids, bathymetry, land_mask):
    slots = block_ids.shape[0]
    rows, cols = drag_coef.shape[1:]
    lon_count = lax.axis_size("gx")
    lat_count = lax.axis_size("gy")
    half = lat_count // 2
    block_total = 2 * lon_count * lat_count
    me = jnp.stack([lax.axis_index("gx"), lax.axis_index("gy")]).astype(jnp.int32)

    payload = device_payload(adjoint_vel, level_count, bathymetry, land_mask, block_ids)
    parts = [payload] + [swap(payload, "gy", 2 * m) for m in range(1, half)]
    column, bottom, drag_gradient = column_mixing(
        adjoint_vel, velocity, drag_coef, level_count, block_ids, payload, block_total
    )
    line, depths = split_after(parts, slots * rows, bottom)

    near_depths = [depths] + [swap(depths, "gx", m) for m in range(1, lon_count)]
    near = [line] + [swap(line, "gx", m) for m in range(1, lon_count)]
    near_depths = stack_after(near_depths)
    near_depths = near_depths.reshape((lon_count * half,) + depths.shape[1:])
    far_depths = swap(near_depths, "gy", 1)
    weights = surface_weights(
        near_depths, far_depths, me, block_ids, rows, lon_count, lat_count
    )

    near = stack_after(near, weights[0])
    far = swap(near, "gy", 1)

    corrected, height, sensitivity = surface_solve(
        near.reshape((-1, rows, cols)), far.reshape((-1, rows, cols)), weights,
        block_ids, level_count, bottom, column, block_total,
    )
    return corrected, drag_gradient, height, sensitivity


def solution(mesh):
    in_specs = (
        P(("gx", "gy"), None, None, None, None),
        P(("gx", "gy"), None, None, None, None),
        P(("gx", "gy"), None, None),
        P(("gx", "gy"), None, None),
        P(("gx", "gy")),
        P("gy", "gx"),
        P("gy", "gx"),
    )
    out_specs = (
        P(("gx", "gy"), None, None, None, None),
        P(("gx", "gy"), None, None),
        P("gy", "gx"),
        P("gy", "gx"),
    )
    return jax.shard_map(
        per_device, mesh=mesh, in_specs=in_specs, out_specs=out_specs, check_vma=False
    )
```

```python
import functools

import jax
import jax.numpy as jnp
import numpy as np
from jax import lax
from jax.experimental import pallas as pl
from jax.experimental.pallas import tpu as pltpu
from jax.sharding import PartitionSpec as P

STEPS = 32

mix_rate = 0.25
drag_step = 0.5
force_scale = 0.25
pressure_gain = 0.5
surface_shift = 1.0 / 64.0
speed_floor = 0.01

LANES = 128
SUBLANES = 8
MIB = 1024 * 1024
FIRST_VMEM = 61 * MIB
MIXING_VMEM = 52 * MIB
SOLVE_VMEM = 50 * MIB
WINDOW_VMEM = 16 * MIB


def chebyshev_sum(total_steps):
    highest = surface_shift + 8.0
    centre = 0.5 * (highest + surface_shift)
    radius = 0.5 * (highest - surface_shift)
    sigma_ratio = centre / radius

    def operate(series):
        shifted = np.zeros_like(series)
        shifted[1] += series[0]
        for k in range(1, len(series) - 1):
            shifted[k + 1] += 0.5 * series[k]
            shifted[k - 1] += 0.5 * series[k]
        return centre * series - radius * shifted

    height = np.zeros(total_steps + 2)
    residual = np.zeros(total_steps + 2)
    residual[0] = 1.0
    direction = residual / centre
    ratio_prev = 1.0 / sigma_ratio
    for _ in range(total_steps):
        height = height + direction
        residual = residual - operate(direction)
        ratio_next = 1.0 / (2.0 * sigma_ratio - ratio_prev)
        direction = ratio_next * ratio_prev * direction + 2.0 * ratio_next / radius * residual
        ratio_prev = ratio_next
    return [float(c) for c in height[:total_steps]], 2.0 / radius


def params(limit):
    return pltpu.CompilerParams(vmem_limit_bytes=limit)


SMEM = pl.BlockSpec(memory_space=pltpu.SMEM)
VMEM = pl.BlockSpec(memory_space=pltpu.VMEM)
ANYWHERE = pl.BlockSpec(memory_space=pl.ANY)
HBM = pl.BlockSpec(memory_space=pltpu.HBM)


CUTS = 2


def level_cuts(depth):
    step = pl.cdiv(depth, CUTS)
    return [(n, n * step, min(step, depth - n * step)) for n in range(CUTS)]


def forcing_kernel(levels_ref, adjoint_ref, out_ref, levels_held, held, level_sem, sems):
    slots, comps, depth, rows, cols = held.shape
    level_copy = pltpu.make_async_copy(levels_ref, levels_held, level_sem)
    level_copy.start()

    def copies_in(b):
        return [
            pltpu.make_async_copy(
                adjoint_ref.at[b, c, pl.ds(low, size)], held.at[b, c, pl.ds(low, size)],
                sems.at[b, c, n],
            )
            for c in range(comps)
            for n, low, size in level_cuts(depth)
        ]

    for b in range(slots):
        for copy in copies_in(b):
            copy.start()
    level_copy.wait()

    def one_slot(b, carry):
        for copy in copies_in(b):
            copy.wait()
        levels = levels_held[b]
        totals = [jnp.zeros((rows, cols), jnp.float32) for _ in range(4)]
        for k in range(depth):
            both = held[b, 0, k] + held[b, 1, k]
            totals[k % 4] = totals[k % 4] + jnp.where(levels > k, both, 0.0)
        out_ref[b] = force_scale * ((totals[0] + totals[1]) + (totals[2] + totals[3]))
        return carry

    lax.fori_loop(0, slots, one_slot, 0)


def column_forcing(adjoint_vel, level_count):
    slots, comps, depth, rows, cols = adjoint_vel.shape
    return pl.pallas_call(
        forcing_kernel,
        in_specs=[HBM, HBM],
        out_specs=VMEM,
        out_shape=pltpu.VMEM((slots, rows, cols), jnp.float32),
        scratch_shapes=[
            pltpu.VMEM(level_count.shape, jnp.int32),
            pltpu.VMEM(adjoint_vel.shape, jnp.float32),
            pltpu.SemaphoreType.DMA,
            pltpu.SemaphoreType.DMA((slots, comps, CUTS)),
        ],
        compiler_params=params(FIRST_VMEM),
        cost_estimate=pl.CostEstimate(
            flops=2 * adjoint_vel.size, bytes_accessed=4 * adjoint_vel.size, transcendentals=0
        ),
        name="column_forcing",
    )(level_count, adjoint_vel)


CHUNK = 8


def mixing_kernel(block_total, first, earlier, ids_ref, levels_ref, drag_ref, adjoint_ref,
                  velocity_ref, after_ref, *rest):
    if earlier:
        for target, ref in zip(rest[3:5], rest[:2]):
            target[0:first] = ref[...]
        rest = rest[2:]
    column_ref, bottom_ref, gradient_ref, adjoint, velocity, column, in_sems, out_sems = rest
    slots, comps, depth, rows, cols = adjoint.shape
    group = 16
    parts = rows // group

    def copies_in(b):
        return [
            pltpu.make_async_copy(
                source.at[first + b, c, pl.ds(low, size)], target.at[b, c, pl.ds(low, size)],
                in_sems.at[which, b, c, n],
            )
            for which, (source, target) in enumerate(
                ((adjoint_ref, adjoint), (velocity_ref, velocity))
            )
            for c in range(comps)
            for n, low, size in level_cuts(depth)
        ]

    def copies_out(b):
        return [
            pltpu.make_async_copy(column.at[b, c], column_ref.at[b, c], out_sems.at[b, c])
            for c in range(comps)
        ]

    for b in range(slots):
        for copy in copies_in(b):
            copy.start()

    def one_component(b, c, span, levels):
        zero = jnp.zeros(levels.shape, jnp.float32)
        x = once = first_flux = second_flux = flow = field = rate_before = zero

        def store(batch):
            for k, value in batch:
                column[b, c, k, span, :] = value

        late = []
        for low in range(0, depth + 2, CHUNK):
            batch = []
            for k in range(low, min(low + CHUNK, depth + 2)):
                fresh_once = None
                if k < depth:
                    wet = levels > k
                    rate = jnp.where(wet, mix_rate, 0.0)
                    fresh = jnp.where(wet, adjoint[b, c, k, span, :], 0.0)
                    flow = jnp.where(
                        levels == k + 1, velocity[b, c, k, span, :].astype(jnp.float32), flow
                    )
                    if 1 <= k:
                        flux = (fresh - x) * rate
                        fresh_once = x + (flux - first_flux)
                        first_flux = flux
                    x = fresh
                elif k == depth:
                    fresh_once = x - first_flux
                if 2 <= k:
                    if k <= depth:
                        flux = (fresh_once - once) * rate_before
                        twice = once + (flux - second_flux)
                        second_flux = flux
                    else:
                        twice = once - second_flux
                    batch.append((k - 2, twice))
                    field = jnp.where(levels == k - 1, twice, field)
                if fresh_once is not None:
                    once = fresh_once
                rate_before = rate
            store(late)
            late = batch
        store(late)
        return flow, field

    def one_group(b, index):
        flag = jnp.where(ids_ref[first + b] < block_total, 1.0, 0.0)
        span = pl.ds(pl.multiple_of(index * group, group), group)
        levels = levels_ref[first + b, span, :]
        flow, field = zip(*[one_component(b, c, span, levels) for c in range(2)])
        speed = jnp.sqrt(flow[0] * flow[0] + flow[1] * flow[1] + speed_floor)
        along = flow[0] * field[0] + flow[1] * field[1]
        ratio = along / speed
        drag = drag_ref[first + b, span, :]
        for c in range(2):
            bottom_ref[first + b, c, span, :] = field[c] - drag_step * drag * (
                speed * field[c] + flow[c] * ratio
            )
        gradient_ref[first + b, span, :] = -drag_step * speed * along * flag

    def one(step, carry):
        b = lax.div(step, parts)
        index = lax.rem(step, parts)

        @pl.when(index == 0)
        def _():
            for copy in copies_in(b):
                copy.wait()

        one_group(b, index)

        @pl.when(index == parts - 1)
        def _():
            for copy in copies_out(b):
                copy.start()

        return carry

    lax.fori_loop(0, slots * parts, one, 0)
    for b in range(slots):
        for copy in copies_out(b):
            copy.wait()


def column_mixing(adjoint_vel, velocity, drag_coef, level_count, block_ids, after, block_total,
                  first, last, earlier=()):
    comps, depth, rows, cols = adjoint_vel.shape[1:]
    slots = last - first
    part = (slots, comps, depth, rows, cols)
    size = slots * comps * depth * rows * cols
    return pl.pallas_call(
        functools.partial(mixing_kernel, block_total, first, len(earlier)),
        in_specs=[SMEM, VMEM, VMEM, HBM, HBM, ANYWHERE] + [VMEM] * len(earlier),
        out_specs=[HBM, VMEM, VMEM],
        out_shape=[
            pltpu.HBM(part, jnp.float32),
            pltpu.VMEM((last, comps, rows, cols), jnp.float32),
            (pltpu.HBM if last == level_count.shape[0] else pltpu.VMEM)((last, rows, cols), jnp.float32),
        ],
        scratch_shapes=[
            pltpu.VMEM(part, adjoint_vel.dtype),
            pltpu.VMEM(part, velocity.dtype),
            pltpu.VMEM(part, jnp.float32),
            pltpu.SemaphoreType.DMA((2, slots, comps, CUTS)),
            pltpu.SemaphoreType.DMA((slots, comps)),
        ],
        compiler_params=params(MIXING_VMEM),
        cost_estimate=pl.CostEstimate(
            flops=14 * size, bytes_accessed=10 * size, transcendentals=0
        ),
        name="column_mixing",
    )(block_ids, level_count, drag_coef, adjoint_vel, velocity, after, *earlier)


PAD = SUBLANES
BATCH = 3
WIDTH = LANES + 2 * STEPS
PITCH = WIDTH + 2 * PAD
NEIGHBOURS = [(down, right) for down in (-1, 0, 1) for right in (0, 1, -1)]


def window_shape(slots, rows):
    strips = LANES // (slots + 2)
    deep = pl.cdiv(rows + 2 * STEPS, strips)
    return strips, deep, strips * deep


def log2(count):
    bits = count.bit_length() - 1
    assert 1 << bits == count
    return bits


def window_places(me_ref, ids_ref, slots, lon_count, lat_count):
    places = []
    for w in range(slots + 2):
        if w < slots:
            block = jnp.where(ids_ref[w] < 2 * lon_count * lat_count, ids_ref[w], 0)
        else:
            block = (me_ref[0] * lat_count + me_ref[1]) * 2 + (w - slots)
        pair = block >> 1
        column = (pair >> log2(lat_count)) * 2 + (block & 1)
        places.append((pair & (lat_count - 1), column))
    return places


def put_window(natural, base, rows, blocks, lane):
    for i in range(3):
        here, east, west = blocks[3 * i:3 * i + 3]
        sides = jnp.where(lane < STEPS, east, jnp.where(lane >= LANES - STEPS, west, 0.0))
        start = base + i * rows
        natural[0, start:start + rows, :] = here
        natural[1, start:start + rows, :] = sides


def turn(natural, deep, put):
    for i in range(deep):
        put(i, STEPS, natural[0, pl.ds(i, LANES, stride=deep), :].T)
        sides = natural[1, pl.ds(i, LANES, stride=deep), :].T
        put(i, STEPS + LANES, sides[:STEPS])
        put(i, 0, sides[LANES - STEPS:])


def rows_at(ref, start, shift=0):
    return ref[pl.ds(start + shift, SUBLANES), :]


def in_batches(chunks, work):
    late = []
    for start in range(0, len(chunks), BATCH):
        batch = [item for chunk in chunks[start:start + BATCH] for item in work(chunk)]
        for ref, a, value in late:
            ref[pl.ds(a, SUBLANES), :] = value
        late = batch
    for ref, a, value in late:
        ref[pl.ds(a, SUBLANES), :] = value


def strip_rows(ref, chunk, deep):
    at = [i * PITCH + PAD + chunk * SUBLANES for i in range(deep)]
    here = [rows_at(ref, a) for a in at]
    above = [pltpu.roll(here[-1], 1, 1)] + here[:-1]
    below = here[1:] + [pltpu.roll(here[0], LANES - 1, 1)]
    return here, above, below, at


def depth_kernel(ids_ref, bathymetry_ref, mask_ref, out_ref, ids, bathymetry, mask, sems):
    copies = [
        pltpu.make_async_copy(ids_ref, ids, sems.at[0]),
        pltpu.make_async_copy(bathymetry_ref, bathymetry, sems.at[1]),
        pltpu.make_async_copy(mask_ref, mask, sems.at[2]),
    ]
    for copy in copies:
        copy.start()
    for copy in copies:
        copy.wait()
    rows = bathymetry.shape[0]
    scaled = bathymetry[...] * mask[...].astype(jnp.float32)
    out_ref[0:rows, :] = scaled[:, :LANES]
    out_ref[rows:2 * rows, :] = scaled[:, LANES:]
    lane = lax.broadcasted_iota(jnp.int32, (SUBLANES, LANES), 1)
    listed = jnp.zeros((SUBLANES, LANES), jnp.int32)
    for s in range(ids.shape[0]):
        listed = jnp.where(lane == s, ids[s], listed)
    out_ref[2 * rows:2 * rows + SUBLANES, :] = listed.astype(jnp.float32)


def depth_payload(bathymetry, land_mask, block_ids):
    rows = bathymetry.shape[0]
    return pl.pallas_call(
        depth_kernel,
        in_specs=[HBM, HBM, HBM],
        out_specs=VMEM,
        out_shape=pltpu.VMEM((2 * rows + SUBLANES, LANES), jnp.float32),
        scratch_shapes=[
            pltpu.SMEM(block_ids.shape, jnp.int32),
            pltpu.VMEM(bathymetry.shape, jnp.float32),
            pltpu.VMEM(land_mask.shape, jnp.int32),
            pltpu.SemaphoreType.DMA((3,)),
        ],
        compiler_params=params(FIRST_VMEM),
        name="depth_payload",
    )(block_ids, bathymetry, land_mask)


def weights_kernel(slots, lon_count, lat_count, me_ref, ids_ref, near_ref, far_ref,
                   root_ref, centre_ref, around_ref, table_ref,
                   natural, all_ids, places_of, sems):
    half = lat_count // 2
    count = lon_count * half
    rows = (near_ref.shape[1] - SUBLANES) // 2
    strips, deep, tall = window_shape(slots, rows)
    column_count = 2 * lon_count
    parts = (near_ref, far_ref)
    copies = [
        pltpu.make_async_copy(
            parts[p].at[:, pl.ds(2 * rows, 1), :], all_ids.at[p], sems.at[p]
        )
        for p in range(2)
    ]
    for copy in copies:
        copy.start()
    natural[...] = jnp.zeros_like(natural)

    def load(lat, column):
        inside = (lat >= 0) & (lat < lat_count) & (column >= 0) & (column < column_count)
        lat_safe = jnp.clip(lat, 0, lat_count - 1)
        column_safe = jnp.clip(column, 0, column_count - 1)
        lon_xor = (column_safe >> 1) ^ me_ref[0]
        lat_xor = lat_safe ^ me_ref[1]
        place = lon_xor * half + (lat_xor >> 1)
        start = pl.multiple_of((column_safe & 1) * rows, SUBLANES)
        near = near_ref[place, pl.ds(start, rows), :]
        far = far_ref[place, pl.ds(start, rows), :]
        here = jnp.where((lat_xor & 1) == 0, near, far)
        return here * jnp.where(inside, 1.0, 0.0)

    lane = lax.broadcasted_iota(jnp.int32, (rows, LANES), 1)
    places = window_places(me_ref, ids_ref, slots, lon_count, lat_count)
    for w, (lat, column) in enumerate(places):
        blocks = [load(lat + down, column + right) for down, right in NEIGHBOURS]
        put_window(natural, w * tall, rows, blocks, lane)

    for copy in copies:
        copy.wait()

    def one_device(n, carry):
        for p in range(2):
            for s in range(slots):
                block = all_ids[p, n, 0, s].astype(jnp.int32)
                places_of[block] = (p * count + n) * slots + s
        return carry

    lax.fori_loop(0, count, one_device, 0)
    for w, (lat, column) in enumerate(places):
        for n, (down, right) in enumerate(NEIGHBOURS):
            lat_safe = jnp.clip(lat + down, 0, lat_count - 1)
            column_safe = jnp.clip(column + right, 0, column_count - 1)
            block = ((column_safe >> 1) * lat_count + lat_safe) * 2 + (column_safe & 1)
            table_ref[w * len(NEIGHBOURS) + n] = places_of[block]

    scale = chebyshev_sum(STEPS)[1]

    def put(i, x, values):
        start = i * PITCH + PAD + x
        root_ref[start:start + values.shape[0], :] = jnp.sqrt(values)
        around_ref[start:start + values.shape[0], :] = scale * values

    turn(natural, deep, put)
    zeros = jnp.zeros((PAD, LANES), jnp.float32)
    for i in range(deep):
        root_ref[i * PITCH:i * PITCH + PAD, :] = zeros
        root_ref[(i + 1) * PITCH - PAD:(i + 1) * PITCH, :] = zeros

    def work(chunk):
        here, above, below, at = strip_rows(root_ref, chunk, deep)
        out = []
        for i, a in enumerate(at):
            others = (rows_at(root_ref, a, 1) + rows_at(root_ref, a, -1)) + (above[i] + below[i])
            out.append((centre_ref, a, 2.0 - scale * here[i] * others))
        return out

    in_batches(range(WIDTH // SUBLANES), work)


def surface_weights(near, far, me, block_ids, rows, lon_count, lat_count):
    slots = block_ids.shape[0]
    assert near.shape[-1] == LANES
    strips, deep, tall = window_shape(slots, rows)
    shape = jax.ShapeDtypeStruct((deep * PITCH, LANES), jnp.float32)
    return pl.pallas_call(
        functools.partial(weights_kernel, slots, lon_count, lat_count),
        in_specs=[SMEM, SMEM, VMEM, VMEM],
        out_specs=[VMEM, VMEM, VMEM, SMEM],
        out_shape=[
            shape,
            shape,
            shape,
            jax.ShapeDtypeStruct(((slots + 2) * len(NEIGHBOURS),), jnp.int32),
        ],
        scratch_shapes=[
            pltpu.VMEM((2, LANES * deep, LANES), jnp.float32),
            pltpu.SMEM((2, near.shape[0], 1, LANES), jnp.float32),
            pltpu.SMEM((2 * lon_count * lat_count + 1,), jnp.int32),
            pltpu.SemaphoreType.DMA((2,)),
        ],
        compiler_params=params(WINDOW_VMEM),
        cost_estimate=pl.CostEstimate(
            flops=0, bytes_accessed=8 * MIB, transcendentals=0
        ),
        name="surface_weights",
    )(me, block_ids, near, far)


def solve_kernel(block_total, ids_ref, table_ref, coefs_ref, root_ref, centre_ref, around_ref,
                 levels_ref, bottom_ref, first_column_ref, last_column_ref, near_ref, far_ref,
                 corrected_ref, height_ref, sensitivity_ref,
                 natural, source, even, odd, extra, column, in_sems, out_sems):
    slots, comps, depth, rows, cols = column.shape
    strips, deep, tall = window_shape(slots, rows)

    middle = first_column_ref.shape[0]
    copies_in = [
        pltpu.make_async_copy(first_column_ref, column.at[pl.ds(0, middle)], in_sems.at[0]),
        pltpu.make_async_copy(
            last_column_ref, column.at[pl.ds(middle, slots - middle)], in_sems.at[1]
        ),
    ]
    for copy in copies_in:
        copy.start()

    count = near_ref.shape[0]

    def load(place):
        inner = place & (count - 1)
        return jnp.where(place < count, near_ref[inner], far_ref[inner])

    lane = lax.broadcasted_iota(jnp.int32, (rows, LANES), 1)
    for w in range(slots + 2):
        places = [table_ref[w * len(NEIGHBOURS) + n] for n in range(len(NEIGHBOURS))]
        put_window(natural, w * tall, rows, [load(place) for place in places], lane)

    coefs, step_scale = chebyshev_sum(STEPS)

    def put(i, x, values):
        start = i * PITCH + PAD + x
        stop = start + values.shape[0]
        root = root_ref[start:stop, :]
        values = jnp.where(root > 0.0, root * values, 0.0)
        source[start:stop, :] = values
        even[start:stop, :] = coefs[STEPS - 1] * values
        odd[start:stop, :] = jnp.zeros_like(values)

    zeros = jnp.zeros((PAD, LANES), jnp.float32)
    for ref in (even, odd):
        for i in range(deep):
            ref[i * PITCH:i * PITCH + PAD, :] = zeros
            ref[(i + 1) * PITCH - PAD:(i + 1) * PITCH, :] = zeros
    turn(natural, deep, put)

    chunks = WIDTH // SUBLANES

    def apply(current, target, coef, gain, m):
        def work(chunk):
            here, above, below, at = strip_rows(current, chunk, deep)
            out = []
            for i, a in enumerate(at):
                others = (rows_at(current, a, 1) + rows_at(current, a, -1)) + (
                    above[i] + below[i]
                )
                pushed = rows_at(centre_ref, a) * here[i] + rows_at(around_ref, a) * others
                if gain != 1.0:
                    pushed = gain * pushed
                kept = coef * rows_at(source, a) - rows_at(target, a)
                out.append((target, a, kept + pushed))
            return out

        in_batches(range(m // SUBLANES, chunks - m // SUBLANES), work)

    runs = []
    for m in range(1, STEPS - 1, 2):
        if runs and runs[-1][0] // SUBLANES == m // SUBLANES:
            runs[-1][1] += 1
        else:
            runs.append([m, 1])
    for first, pairs in runs:
        def two_steps(pair, carry, first=first):
            m = first + 2 * pair
            apply(even, odd, coefs_ref[m], 1.0, first)
            apply(odd, even, coefs_ref[m + 1], 1.0, first)
            return carry

        lax.fori_loop(0, pairs, two_steps, 0)
    apply(even, odd, coefs[0], 0.5, STEPS - 1)

    low = STEPS // SUBLANES - 1

    def one_height(chunk):
        out = []
        for i in range(deep):
            a = i * PITCH + PAD + chunk * SUBLANES
            root = rows_at(root_ref, a)
            out.append((extra, a, jnp.where(root > 0.0, rows_at(odd, a) / root, 0.0)))
        return out

    in_batches(range(low, chunks - low), one_height)

    def differences(chunk):
        here, above, below, at = strip_rows(extra, chunk, deep)
        root, root_above, root_below, _ = strip_rows(root_ref, chunk, deep)
        out = []
        for i, a in enumerate(at):
            east_step = rows_at(extra, a, 1) - here[i]
            west_step = here[i] - rows_at(extra, a, -1)
            south_step = below[i] - here[i]
            north_step = here[i] - above[i]
            energy = root[i] * (
                (rows_at(root_ref, a, 1) * east_step * east_step
                 + rows_at(root_ref, a, -1) * west_step * west_step)
                + (root_below[i] * south_step * south_step
                   + root_above[i] * north_step * north_step)
            )
            scaled = rows_at(around_ref, a) * (1.0 / step_scale)
            out.append((even, a, east_step))
            out.append((source, a, 0.25 * energy / jnp.maximum(scaled, 0.25)))
        return out

    in_batches(range(low + 1, chunks - low - 1), differences)

    def turn_back(ref, tile):
        for i in range(deep):
            start = i * PITCH + PAD + STEPS
            natural[tile, pl.ds(i, LANES, stride=deep), :] = ref[start:start + LANES, :].T

    def cut(tile, w, shift=0):
        return natural[tile, pl.ds(w * tall + STEPS + shift, rows), :]

    def copy_out(b, c):
        return pltpu.make_async_copy(column.at[b, c], corrected_ref.at[b, c], out_sems.at[b, c])

    def correct(b, c, step):
        levels = levels_ref[b] * jnp.where(ids_ref[b] < block_total, 1, 0)
        push = pressure_gain * step
        lowest = bottom_ref[b, c] - push

        late = []
        for low in range(0, depth, CHUNK):
            batch = []
            for k in range(low, min(low + CHUNK, depth)):
                value = jnp.where(levels == k + 1, lowest, column[b, c, k] - push)
                batch.append((k, jnp.where(levels > k, value, 0.0)))
            for k, value in late:
                column[b, c, k] = value
            late = batch
        for k, value in late:
            column[b, c, k] = value
        copy_out(b, c).start()

    turn_back(even, 0)
    for copy in copies_in:
        copy.wait()

    def correct_east(b, carry):
        correct(b, 0, cut(0, b))
        return carry

    def correct_north(b, carry):
        correct(b, 1, cut(1, b, 1) - cut(1, b))
        return carry

    lax.fori_loop(0, slots, correct_east, 0)
    turn_back(extra, 1)
    lax.fori_loop(0, slots, correct_north, 0)
    turn_back(source, 0)
    for h in range(2):
        height_ref[:, h * LANES:(h + 1) * LANES] = cut(1, slots + h)
        sensitivity_ref[:, h * LANES:(h + 1) * LANES] = cut(0, slots + h)

    for b in range(slots):
        for c in range(comps):
            copy_out(b, c).wait()


def surface_solve(near, far, weights, block_ids, level_count, bottom, columns, block_total):
    root, centre, around, table = weights
    comps, depth, rows, cols = columns[0].shape[1:]
    slots = level_count.shape[0]
    assert comps == 2
    full = (slots, comps, depth, rows, cols)
    deep = window_shape(slots, rows)[1]
    turned = pltpu.VMEM(root.shape, jnp.float32)
    coefs = jnp.array(chebyshev_sum(STEPS)[0][::-1], jnp.float32)
    return pl.pallas_call(
        functools.partial(solve_kernel, block_total),
        in_specs=[SMEM, SMEM, SMEM] + [VMEM] * 5 + [HBM] * 2 + [VMEM] * 2,
        out_specs=[HBM, VMEM, VMEM],
        out_shape=[
            jax.ShapeDtypeStruct(full, jnp.float32),
            jax.ShapeDtypeStruct((rows, 2 * cols), jnp.float32),
            jax.ShapeDtypeStruct((rows, 2 * cols), jnp.float32),
        ],
        scratch_shapes=[
            pltpu.VMEM((2, LANES * deep, LANES), jnp.float32),
            turned,
            turned,
            turned,
            turned,
            pltpu.VMEM(full, jnp.float32),
            pltpu.SemaphoreType.DMA((2,)),
            pltpu.SemaphoreType.DMA((slots, comps)),
        ],
        compiler_params=params(SOLVE_VMEM),
        cost_estimate=pl.CostEstimate(
            flops=9 * STEPS * root.size, bytes_accessed=16 * root.size, transcendentals=0
        ),
        name="surface_solve",
    )(block_ids, table, coefs, root, centre, around, level_count, bottom, *columns, near, far)


def stack_kernel(parts, *refs):
    out_ref = refs[-1]
    for p in range(parts):
        out_ref[p] = refs[p][...]


def stack_after(parts, *tokens):
    return pl.pallas_call(
        functools.partial(stack_kernel, len(parts)),
        in_specs=[VMEM] * len(parts) + [ANYWHERE] * len(tokens),
        out_specs=VMEM,
        out_shape=jax.ShapeDtypeStruct((len(parts),) + parts[0].shape, jnp.float32),
        compiler_params=params(WINDOW_VMEM),
        name="stack_after",
    )(*parts, *tokens)


def swap(values, axis, mask):
    count = lax.axis_size(axis)
    return lax.ppermute(values, axis, [(i, i ^ mask) for i in range(count)])


def per_device(adjoint_vel, velocity, drag_coef, level_count, block_ids, bathymetry, land_mask):
    slots = block_ids.shape[0]
    rows, cols = drag_coef.shape[1:]
    lon_count = lax.axis_size("gx")
    lat_count = lax.axis_size("gy")
    half = lat_count // 2
    block_total = 2 * lon_count * lat_count
    me = jnp.stack([lax.axis_index("gx"), lax.axis_index("gy")]).astype(jnp.int32)

    depths = depth_payload(bathymetry, land_mask, block_ids)
    depth_parts = [depths] + [swap(depths, "gy", 2 * m) for m in range(1, half)]
    forcing = column_forcing(adjoint_vel, level_count)

    parts = [forcing] + [swap(forcing, "gy", 2 * m) for m in range(1, half)]
    near_depths = stack_after(depth_parts, forcing)
    near_depths = [near_depths] + [swap(near_depths, "gx", m) for m in range(1, lon_count)]
    columns = (adjoint_vel, velocity, drag_coef, level_count, block_ids)
    middle = (slots + 1) // 2
    first_column, *first_rest = column_mixing(*columns, forcing, block_total, 0, middle)
    line = stack_after(parts, first_rest[0])

    near = [line] + [swap(line, "gx", m) for m in range(1, lon_count)]
    near_depths = stack_after(near_depths, line)
    near_depths = near_depths.reshape((lon_count * half,) + depths.shape)
    far_depths = swap(near_depths, "gy", 1)
    last_column, bottom, drag_gradient = column_mixing(
        *columns, line, block_total, middle, slots, first_rest
    )
    weights = surface_weights(
        near_depths, far_depths, me, block_ids, rows, lon_count, lat_count
    )

    near = stack_after(near, bottom, weights[0])
    far = swap(near, "gy", 1)

    corrected, height, sensitivity = surface_solve(
        near.reshape((-1, rows, cols)), far.reshape((-1, rows, cols)), weights,
        block_ids, level_count, bottom, (first_column, last_column), block_total,
    )
    return corrected, drag_gradient, height, sensitivity


def solution(mesh):
    in_specs = (
        P(("gx", "gy"), None, None, None, None),
        P(("gx", "gy"), None, None, None, None),
        P(("gx", "gy"), None, None),
        P(("gx", "gy"), None, None),
        P(("gx", "gy")),
        P("gy", "gx"),
        P("gy", "gx"),
    )
    out_specs = (
        P(("gx", "gy"), None, None, None, None),
        P(("gx", "gy"), None, None),
        P("gy", "gx"),
        P("gy", "gx"),
    )
    return jax.shard_map(
        per_device, mesh=mesh, in_specs=in_specs, out_specs=out_specs, check_vma=False
    )
```

```python
import functools

import jax
import jax.numpy as jnp
import numpy as np
from jax import lax
from jax.experimental import pallas as pl
from jax.experimental.pallas import tpu as pltpu
from jax.sharding import PartitionSpec as P

STEPS = 32

mix_rate = 0.25
drag_step = 0.5
force_scale = 0.25
pressure_gain = 0.5
surface_shift = 1.0 / 64.0
speed_floor = 0.01

LANES = 128
SUBLANES = 8
MIB = 1024 * 1024
FIRST_VMEM = 61 * MIB
MIXING_VMEM = 52 * MIB
SOLVE_VMEM = 50 * MIB
WINDOW_VMEM = 16 * MIB


def chebyshev_sum(total_steps):
    highest = surface_shift + 8.0
    centre = 0.5 * (highest + surface_shift)
    radius = 0.5 * (highest - surface_shift)
    sigma_ratio = centre / radius

    def operate(series):
        shifted = np.zeros_like(series)
        shifted[1] += series[0]
        for k in range(1, len(series) - 1):
            shifted[k + 1] += 0.5 * series[k]
            shifted[k - 1] += 0.5 * series[k]
        return centre * series - radius * shifted

    height = np.zeros(total_steps + 2)
    residual = np.zeros(total_steps + 2)
    residual[0] = 1.0
    direction = residual / centre
    ratio_prev = 1.0 / sigma_ratio
    for _ in range(total_steps):
        height = height + direction
        residual = residual - operate(direction)
        ratio_next = 1.0 / (2.0 * sigma_ratio - ratio_prev)
        direction = ratio_next * ratio_prev * direction + 2.0 * ratio_next / radius * residual
        ratio_prev = ratio_next
    return [float(c) for c in height[:total_steps]], 2.0 / radius


def params(limit):
    return pltpu.CompilerParams(vmem_limit_bytes=limit)


SMEM = pl.BlockSpec(memory_space=pltpu.SMEM)
VMEM = pl.BlockSpec(memory_space=pltpu.VMEM)
ANYWHERE = pl.BlockSpec(memory_space=pl.ANY)
HBM = pl.BlockSpec(memory_space=pltpu.HBM)


def forcing_kernel(levels_ref, adjoint_ref, out_ref, levels_held, held, level_sem, sems):
    slots, comps, depth, rows, cols = held.shape
    level_copy = pltpu.make_async_copy(levels_ref, levels_held, level_sem)
    level_copy.start()

    def copy_in(b, c):
        return pltpu.make_async_copy(adjoint_ref.at[b, c], held.at[b, c], sems.at[b, c])

    for b in range(slots):
        for c in range(comps):
            copy_in(b, c).start()
    level_copy.wait()

    def one_slot(b, carry):
        levels = levels_held[b]
        totals = [jnp.zeros((rows, cols), jnp.float32) for _ in range(4)]
        for c in range(comps):
            copy_in(b, c).wait()
            for k in range(depth):
                totals[k % 4] = totals[k % 4] + jnp.where(levels > k, held[b, c, k], 0.0)
        out_ref[b] = force_scale * ((totals[0] + totals[1]) + (totals[2] + totals[3]))
        return carry

    lax.fori_loop(0, slots, one_slot, 0)


def column_forcing(adjoint_vel, level_count):
    slots, comps, depth, rows, cols = adjoint_vel.shape
    return pl.pallas_call(
        forcing_kernel,
        in_specs=[HBM, HBM],
        out_specs=VMEM,
        out_shape=pltpu.VMEM((slots, rows, cols), jnp.float32),
        scratch_shapes=[
            pltpu.VMEM(level_count.shape, jnp.int32),
            pltpu.VMEM(adjoint_vel.shape, jnp.float32),
            pltpu.SemaphoreType.DMA,
            pltpu.SemaphoreType.DMA((slots, comps)),
        ],
        compiler_params=params(FIRST_VMEM),
        cost_estimate=pl.CostEstimate(
            flops=2 * adjoint_vel.size, bytes_accessed=4 * adjoint_vel.size, transcendentals=0
        ),
        name="column_forcing",
    )(level_count, adjoint_vel)


CHUNK = 8


def mixing_kernel(block_total, first, earlier, ids_ref, levels_ref, drag_ref, adjoint_ref,
                  velocity_ref, after_ref, *rest):
    if earlier:
        for target, ref in zip(rest[3:5], rest[:2]):
            target[0:first] = ref[...]
        rest = rest[2:]
    column_ref, bottom_ref, gradient_ref, adjoint, velocity, column, in_sems, out_sems = rest
    slots, comps, depth, rows, cols = adjoint.shape
    group = 16
    parts = rows // group

    def copies_in(b):
        return [
            pltpu.make_async_copy(source.at[first + b, c], target.at[b, c], in_sems.at[n, b, c])
            for n, (source, target) in enumerate(
                ((adjoint_ref, adjoint), (velocity_ref, velocity))
            )
            for c in range(comps)
        ]

    def copy_out(b, index):
        span = pl.ds(pl.multiple_of(index * group, group), group)
        return pltpu.make_async_copy(
            column.at[b, :, :, span], column_ref.at[b, :, :, span], out_sems.at[b, index]
        )

    for b in range(slots):
        for copy in copies_in(b):
            copy.start()

    def one_component(b, c, span, levels):
        zero = jnp.zeros(levels.shape, jnp.float32)
        x = once = first_flux = second_flux = flow = field = rate_before = zero

        def store(batch):
            for k, value in batch:
                column[b, c, k, span, :] = value

        late = []
        for low in range(0, depth + 2, CHUNK):
            batch = []
            for k in range(low, min(low + CHUNK, depth + 2)):
                fresh_once = None
                if k < depth:
                    wet = levels > k
                    rate = jnp.where(wet, mix_rate, 0.0)
                    fresh = jnp.where(wet, adjoint[b, c, k, span, :], 0.0)
                    flow = jnp.where(
                        levels == k + 1, velocity[b, c, k, span, :].astype(jnp.float32), flow
                    )
                    if 1 <= k:
                        flux = (fresh - x) * rate
                        fresh_once = x + (flux - first_flux)
                        first_flux = flux
                    x = fresh
                elif k == depth:
                    fresh_once = x - first_flux
                if 2 <= k:
                    if k <= depth:
                        flux = (fresh_once - once) * rate_before
                        twice = once + (flux - second_flux)
                        second_flux = flux
                    else:
                        twice = once - second_flux
                    batch.append((k - 2, twice))
                    field = jnp.where(levels == k - 1, twice, field)
                if fresh_once is not None:
                    once = fresh_once
                rate_before = rate
            store(late)
            late = batch
        store(late)
        return flow, field

    def one_group(b, index):
        flag = jnp.where(ids_ref[first + b] < block_total, 1.0, 0.0)
        span = pl.ds(pl.multiple_of(index * group, group), group)
        levels = levels_ref[first + b, span, :]
        flow, field = zip(*[one_component(b, c, span, levels) for c in range(2)])
        speed = jnp.sqrt(flow[0] * flow[0] + flow[1] * flow[1] + speed_floor)
        along = flow[0] * field[0] + flow[1] * field[1]
        ratio = along / speed
        drag = drag_ref[first + b, span, :]
        for c in range(2):
            bottom_ref[first + b, c, span, :] = field[c] - drag_step * drag * (
                speed * field[c] + flow[c] * ratio
            )
        gradient_ref[first + b, span, :] = -drag_step * speed * along * flag

    def one(step, carry):
        b = lax.div(step, parts)
        index = lax.rem(step, parts)

        @pl.when(index == 0)
        def _():
            for copy in copies_in(b):
                copy.wait()

        one_group(b, index)
        copy_out(b, index).start()
        return carry

    lax.fori_loop(0, slots * parts, one, 0)
    for b in range(slots):
        for index in range(parts):
            copy_out(b, index).wait()


def column_mixing(adjoint_vel, velocity, drag_coef, level_count, block_ids, after, block_total,
                  first, last, earlier=()):
    comps, depth, rows, cols = adjoint_vel.shape[1:]
    slots = last - first
    part = (slots, comps, depth, rows, cols)
    size = slots * comps * depth * rows * cols
    return pl.pallas_call(
        functools.partial(mixing_kernel, block_total, first, len(earlier)),
        in_specs=[SMEM, VMEM, VMEM, HBM, HBM, ANYWHERE] + [VMEM] * len(earlier),
        out_specs=[HBM, VMEM, VMEM],
        out_shape=[
            pltpu.HBM(part, jnp.float32),
            pltpu.VMEM((last, comps, rows, cols), jnp.float32),
            (pltpu.HBM if last == level_count.shape[0] else pltpu.VMEM)((last, rows, cols), jnp.float32),
        ],
        scratch_shapes=[
            pltpu.VMEM(part, adjoint_vel.dtype),
            pltpu.VMEM(part, velocity.dtype),
            pltpu.VMEM(part, jnp.float32),
            pltpu.SemaphoreType.DMA((2, slots, comps)),
            pltpu.SemaphoreType.DMA((slots, rows // 16)),
        ],
        compiler_params=params(MIXING_VMEM),
        cost_estimate=pl.CostEstimate(
            flops=14 * size, bytes_accessed=10 * size, transcendentals=0
        ),
        name="column_mixing",
    )(block_ids, level_count, drag_coef, adjoint_vel, velocity, after, *earlier)


PAD = SUBLANES
BATCH = 3
WIDTH = LANES + 2 * STEPS
PITCH = WIDTH + 2 * PAD
NEIGHBOURS = [(down, right) for down in (-1, 0, 1) for right in (0, 1, -1)]


def window_shape(slots, rows):
    strips = LANES // (slots + 2)
    deep = pl.cdiv(rows + 2 * STEPS, strips)
    return strips, deep, strips * deep


def log2(count):
    bits = count.bit_length() - 1
    assert 1 << bits == count
    return bits


def window_places(me_ref, ids_ref, slots, lon_count, lat_count):
    places = []
    for w in range(slots + 2):
        if w < slots:
            block = jnp.where(ids_ref[w] < 2 * lon_count * lat_count, ids_ref[w], 0)
        else:
            block = (me_ref[0] * lat_count + me_ref[1]) * 2 + (w - slots)
        pair = block >> 1
        column = (pair >> log2(lat_count)) * 2 + (block & 1)
        places.append((pair & (lat_count - 1), column))
    return places


def put_window(natural, base, rows, blocks, lane):
    for i in range(3):
        here, east, west = blocks[3 * i:3 * i + 3]
        sides = jnp.where(lane < STEPS, east, jnp.where(lane >= LANES - STEPS, west, 0.0))
        start = base + i * rows
        natural[0, start:start + rows, :] = here
        natural[1, start:start + rows, :] = sides


def turn(natural, deep, put):
    for i in range(deep):
        put(i, STEPS, natural[0, pl.ds(i, LANES, stride=deep), :].T)
        sides = natural[1, pl.ds(i, LANES, stride=deep), :].T
        put(i, STEPS + LANES, sides[:STEPS])
        put(i, 0, sides[LANES - STEPS:])


def rows_at(ref, start, shift=0):
    return ref[pl.ds(start + shift, SUBLANES), :]


def in_batches(chunks, work):
    late = []
    for start in range(0, len(chunks), BATCH):
        batch = [item for chunk in chunks[start:start + BATCH] for item in work(chunk)]
        for ref, a, value in late:
            ref[pl.ds(a, SUBLANES), :] = value
        late = batch
    for ref, a, value in late:
        ref[pl.ds(a, SUBLANES), :] = value


def strip_rows(ref, chunk, deep):
    at = [i * PITCH + PAD + chunk * SUBLANES for i in range(deep)]
    here = [rows_at(ref, a) for a in at]
    above = [pltpu.roll(here[-1], 1, 1)] + here[:-1]
    below = here[1:] + [pltpu.roll(here[0], LANES - 1, 1)]
    return here, above, below, at


def depth_kernel(ids_ref, bathymetry_ref, mask_ref, out_ref, ids, bathymetry, mask, sems):
    copies = [
        pltpu.make_async_copy(ids_ref, ids, sems.at[0]),
        pltpu.make_async_copy(bathymetry_ref, bathymetry, sems.at[1]),
        pltpu.make_async_copy(mask_ref, mask, sems.at[2]),
    ]
    for copy in copies:
        copy.start()
    for copy in copies:
        copy.wait()
    rows = bathymetry.shape[0]
    scaled = bathymetry[...] * mask[...].astype(jnp.float32)
    out_ref[0:rows, :] = scaled[:, :LANES]
    out_ref[rows:2 * rows, :] = scaled[:, LANES:]
    lane = lax.broadcasted_iota(jnp.int32, (SUBLANES, LANES), 1)
    listed = jnp.zeros((SUBLANES, LANES), jnp.int32)
    for s in range(ids.shape[0]):
        listed = jnp.where(lane == s, ids[s], listed)
    out_ref[2 * rows:2 * rows + SUBLANES, :] = listed.astype(jnp.float32)


def depth_payload(bathymetry, land_mask, block_ids):
    rows = bathymetry.shape[0]
    return pl.pallas_call(
        depth_kernel,
        in_specs=[HBM, HBM, HBM],
        out_specs=VMEM,
        out_shape=pltpu.VMEM((2 * rows + SUBLANES, LANES), jnp.float32),
        scratch_shapes=[
            pltpu.SMEM(block_ids.shape, jnp.int32),
            pltpu.VMEM(bathymetry.shape, jnp.float32),
            pltpu.VMEM(land_mask.shape, jnp.int32),
            pltpu.SemaphoreType.DMA((3,)),
        ],
        compiler_params=params(FIRST_VMEM),
        name="depth_payload",
    )(block_ids, bathymetry, land_mask)


def weights_kernel(slots, lon_count, lat_count, me_ref, ids_ref, near_ref, far_ref,
                   root_ref, centre_ref, around_ref, table_ref,
                   natural, all_ids, places_of, sems):
    half = lat_count // 2
    count = lon_count * half
    rows = (near_ref.shape[1] - SUBLANES) // 2
    strips, deep, tall = window_shape(slots, rows)
    column_count = 2 * lon_count
    parts = (near_ref, far_ref)
    copies = [
        pltpu.make_async_copy(
            parts[p].at[:, pl.ds(2 * rows, 1), :], all_ids.at[p], sems.at[p]
        )
        for p in range(2)
    ]
    for copy in copies:
        copy.start()
    natural[...] = jnp.zeros_like(natural)

    def load(lat, column):
        inside = (lat >= 0) & (lat < lat_count) & (column >= 0) & (column < column_count)
        lat_safe = jnp.clip(lat, 0, lat_count - 1)
        column_safe = jnp.clip(column, 0, column_count - 1)
        lon_xor = (column_safe >> 1) ^ me_ref[0]
        lat_xor = lat_safe ^ me_ref[1]
        place = lon_xor * half + (lat_xor >> 1)
        start = pl.multiple_of((column_safe & 1) * rows, SUBLANES)
        near = near_ref[place, pl.ds(start, rows), :]
        far = far_ref[place, pl.ds(start, rows), :]
        here = jnp.where((lat_xor & 1) == 0, near, far)
        return here * jnp.where(inside, 1.0, 0.0)

    lane = lax.broadcasted_iota(jnp.int32, (rows, LANES), 1)
    places = window_places(me_ref, ids_ref, slots, lon_count, lat_count)
    for w, (lat, column) in enumerate(places):
        blocks = [load(lat + down, column + right) for down, right in NEIGHBOURS]
        put_window(natural, w * tall, rows, blocks, lane)

    for copy in copies:
        copy.wait()

    def one_device(n, carry):
        for p in range(2):
            for s in range(slots):
                block = all_ids[p, n, 0, s].astype(jnp.int32)
                places_of[block] = (p * count + n) * slots + s
        return carry

    lax.fori_loop(0, count, one_device, 0)
    for w, (lat, column) in enumerate(places):
        for n, (down, right) in enumerate(NEIGHBOURS):
            lat_safe = jnp.clip(lat + down, 0, lat_count - 1)
            column_safe = jnp.clip(column + right, 0, column_count - 1)
            block = ((column_safe >> 1) * lat_count + lat_safe) * 2 + (column_safe & 1)
            table_ref[w * len(NEIGHBOURS) + n] = places_of[block]

    scale = chebyshev_sum(STEPS)[1]

    def put(i, x, values):
        start = i * PITCH + PAD + x
        root_ref[start:start + values.shape[0], :] = jnp.sqrt(values)
        around_ref[start:start + values.shape[0], :] = scale * values

    turn(natural, deep, put)
    zeros = jnp.zeros((PAD, LANES), jnp.float32)
    for i in range(deep):
        root_ref[i * PITCH:i * PITCH + PAD, :] = zeros
        root_ref[(i + 1) * PITCH - PAD:(i + 1) * PITCH, :] = zeros

    def work(chunk):
        here, above, below, at = strip_rows(root_ref, chunk, deep)
        out = []
        for i, a in enumerate(at):
            others = (rows_at(root_ref, a, 1) + rows_at(root_ref, a, -1)) + (above[i] + below[i])
            out.append((centre_ref, a, 2.0 - scale * here[i] * others))
        return out

    in_batches(range(WIDTH // SUBLANES), work)


def surface_weights(near, far, me, block_ids, rows, lon_count, lat_count):
    slots = block_ids.shape[0]
    assert near.shape[-1] == LANES
    strips, deep, tall = window_shape(slots, rows)
    shape = jax.ShapeDtypeStruct((deep * PITCH, LANES), jnp.float32)
    return pl.pallas_call(
        functools.partial(weights_kernel, slots, lon_count, lat_count),
        in_specs=[SMEM, SMEM, VMEM, VMEM],
        out_specs=[VMEM, VMEM, VMEM, SMEM],
        out_shape=[
            shape,
            shape,
            shape,
            jax.ShapeDtypeStruct(((slots + 2) * len(NEIGHBOURS),), jnp.int32),
        ],
        scratch_shapes=[
            pltpu.VMEM((2, LANES * deep, LANES), jnp.float32),
            pltpu.SMEM((2, near.shape[0], 1, LANES), jnp.float32),
            pltpu.SMEM((2 * lon_count * lat_count + 1,), jnp.int32),
            pltpu.SemaphoreType.DMA((2,)),
        ],
        compiler_params=params(WINDOW_VMEM),
        cost_estimate=pl.CostEstimate(
            flops=0, bytes_accessed=8 * MIB, transcendentals=0
        ),
        name="surface_weights",
    )(me, block_ids, near, far)


def solve_kernel(block_total, ids_ref, table_ref, coefs_ref, root_ref, centre_ref, around_ref,
                 levels_ref, bottom_ref, first_column_ref, last_column_ref, near_ref, far_ref,
                 corrected_ref, height_ref, sensitivity_ref,
                 natural, source, even, odd, extra, column, in_sems, out_sems):
    slots, comps, depth, rows, cols = column.shape
    strips, deep, tall = window_shape(slots, rows)

    middle = first_column_ref.shape[0]
    copies_in = [
        pltpu.make_async_copy(first_column_ref, column.at[pl.ds(0, middle)], in_sems.at[0]),
        pltpu.make_async_copy(
            last_column_ref, column.at[pl.ds(middle, slots - middle)], in_sems.at[1]
        ),
    ]
    for copy in copies_in:
        copy.start()

    count = near_ref.shape[0]

    def load(place):
        inner = place & (count - 1)
        return jnp.where(place < count, near_ref[inner], far_ref[inner])

    lane = lax.broadcasted_iota(jnp.int32, (rows, LANES), 1)
    for w in range(slots + 2):
        places = [table_ref[w * len(NEIGHBOURS) + n] for n in range(len(NEIGHBOURS))]
        put_window(natural, w * tall, rows, [load(place) for place in places], lane)

    coefs, step_scale = chebyshev_sum(STEPS)

    def put(i, x, values):
        start = i * PITCH + PAD + x
        stop = start + values.shape[0]
        root = root_ref[start:stop, :]
        values = jnp.where(root > 0.0, root * values, 0.0)
        source[start:stop, :] = values
        even[start:stop, :] = coefs[STEPS - 1] * values
        odd[start:stop, :] = jnp.zeros_like(values)

    zeros = jnp.zeros((PAD, LANES), jnp.float32)
    for ref in (even, odd):
        for i in range(deep):
            ref[i * PITCH:i * PITCH + PAD, :] = zeros
            ref[(i + 1) * PITCH - PAD:(i + 1) * PITCH, :] = zeros
    turn(natural, deep, put)

    chunks = WIDTH // SUBLANES

    def apply(current, target, coef, gain, m):
        def work(chunk):
            here, above, below, at = strip_rows(current, chunk, deep)
            out = []
            for i, a in enumerate(at):
                others = (rows_at(current, a, 1) + rows_at(current, a, -1)) + (
                    above[i] + below[i]
                )
                pushed = rows_at(centre_ref, a) * here[i] + rows_at(around_ref, a) * others
                if gain != 1.0:
                    pushed = gain * pushed
                kept = coef * rows_at(source, a) - rows_at(target, a)
                out.append((target, a, kept + pushed))
            return out

        in_batches(range(m // SUBLANES, chunks - m // SUBLANES), work)

    runs = []
    for m in range(1, STEPS - 1, 2):
        if runs and runs[-1][0] // SUBLANES == m // SUBLANES:
            runs[-1][1] += 1
        else:
            runs.append([m, 1])
    for first, pairs in runs:
        def two_steps(pair, carry, first=first):
            m = first + 2 * pair
            apply(even, odd, coefs_ref[m], 1.0, first)
            apply(odd, even, coefs_ref[m + 1], 1.0, first)
            return carry

        lax.fori_loop(0, pairs, two_steps, 0)
    apply(even, odd, coefs[0], 0.5, STEPS - 1)

    low = STEPS // SUBLANES - 1

    def one_height(chunk):
        out = []
        for i in range(deep):
            a = i * PITCH + PAD + chunk * SUBLANES
            root = rows_at(root_ref, a)
            out.append((extra, a, jnp.where(root > 0.0, rows_at(odd, a) / root, 0.0)))
        return out

    in_batches(range(low, chunks - low), one_height)

    def differences(chunk):
        here, above, below, at = strip_rows(extra, chunk, deep)
        root, root_above, root_below, _ = strip_rows(root_ref, chunk, deep)
        out = []
        for i, a in enumerate(at):
            east_step = rows_at(extra, a, 1) - here[i]
            west_step = here[i] - rows_at(extra, a, -1)
            south_step = below[i] - here[i]
            north_step = here[i] - above[i]
            energy = root[i] * (
                (rows_at(root_ref, a, 1) * east_step * east_step
                 + rows_at(root_ref, a, -1) * west_step * west_step)
                + (root_below[i] * south_step * south_step
                   + root_above[i] * north_step * north_step)
            )
            scaled = rows_at(around_ref, a) * (1.0 / step_scale)
            out.append((even, a, east_step))
            out.append((source, a, 0.25 * energy / jnp.maximum(scaled, 0.25)))
        return out

    in_batches(range(low + 1, chunks - low - 1), differences)

    def turn_back(ref, tile):
        for i in range(deep):
            start = i * PITCH + PAD + STEPS
            natural[tile, pl.ds(i, LANES, stride=deep), :] = ref[start:start + LANES, :].T

    def cut(tile, w, shift=0):
        return natural[tile, pl.ds(w * tall + STEPS + shift, rows), :]

    def copy_out(b, c):
        return pltpu.make_async_copy(column.at[b, c], corrected_ref.at[b, c], out_sems.at[b, c])

    def correct(b, c, step):
        levels = levels_ref[b] * jnp.where(ids_ref[b] < block_total, 1, 0)
        push = pressure_gain * step
        lowest = bottom_ref[b, c] - push

        late = []
        for low in range(0, depth, CHUNK):
            batch = []
            for k in range(low, min(low + CHUNK, depth)):
                value = jnp.where(levels == k + 1, lowest, column[b, c, k] - push)
                batch.append((k, jnp.where(levels > k, value, 0.0)))
            for k, value in late:
                column[b, c, k] = value
            late = batch
        for k, value in late:
            column[b, c, k] = value
        copy_out(b, c).start()

    turn_back(even, 0)
    for copy in copies_in:
        copy.wait()

    def correct_east(b, carry):
        correct(b, 0, cut(0, b))
        return carry

    def correct_north(b, carry):
        correct(b, 1, cut(1, b, 1) - cut(1, b))
        return carry

    lax.fori_loop(0, slots, correct_east, 0)
    turn_back(extra, 1)
    lax.fori_loop(0, slots, correct_north, 0)
    turn_back(source, 0)
    for h in range(2):
        height_ref[:, h * LANES:(h + 1) * LANES] = cut(1, slots + h)
        sensitivity_ref[:, h * LANES:(h + 1) * LANES] = cut(0, slots + h)

    for b in range(slots):
        for c in range(comps):
            copy_out(b, c).wait()


def surface_solve(near, far, weights, block_ids, level_count, bottom, columns, block_total):
    root, centre, around, table = weights
    comps, depth, rows, cols = columns[0].shape[1:]
    slots = level_count.shape[0]
    assert comps == 2
    full = (slots, comps, depth, rows, cols)
    deep = window_shape(slots, rows)[1]
    turned = pltpu.VMEM(root.shape, jnp.float32)
    coefs = jnp.array(chebyshev_sum(STEPS)[0][::-1], jnp.float32)
    return pl.pallas_call(
        functools.partial(solve_kernel, block_total),
        in_specs=[SMEM, SMEM, SMEM] + [VMEM] * 5 + [HBM] * 2 + [VMEM] * 2,
        out_specs=[HBM, VMEM, VMEM],
        out_shape=[
            jax.ShapeDtypeStruct(full, jnp.float32),
            jax.ShapeDtypeStruct((rows, 2 * cols), jnp.float32),
            jax.ShapeDtypeStruct((rows, 2 * cols), jnp.float32),
        ],
        scratch_shapes=[
            pltpu.VMEM((2, LANES * deep, LANES), jnp.float32),
            turned,
            turned,
            turned,
            turned,
            pltpu.VMEM(full, jnp.float32),
            pltpu.SemaphoreType.DMA((2,)),
            pltpu.SemaphoreType.DMA((slots, comps)),
        ],
        compiler_params=params(SOLVE_VMEM),
        cost_estimate=pl.CostEstimate(
            flops=9 * STEPS * root.size, bytes_accessed=16 * root.size, transcendentals=0
        ),
        name="surface_solve",
    )(block_ids, table, coefs, root, centre, around, level_count, bottom, *columns, near, far)


def stack_kernel(parts, *refs):
    out_ref = refs[-1]
    for p in range(parts):
        out_ref[p] = refs[p][...]


def stack_after(parts, *tokens):
    return pl.pallas_call(
        functools.partial(stack_kernel, len(parts)),
        in_specs=[VMEM] * len(parts) + [ANYWHERE] * len(tokens),
        out_specs=VMEM,
        out_shape=jax.ShapeDtypeStruct((len(parts),) + parts[0].shape, jnp.float32),
        compiler_params=params(WINDOW_VMEM),
        name="stack_after",
    )(*parts, *tokens)


def swap(values, axis, mask):
    count = lax.axis_size(axis)
    return lax.ppermute(values, axis, [(i, i ^ mask) for i in range(count)])


def per_device(adjoint_vel, velocity, drag_coef, level_count, block_ids, bathymetry, land_mask):
    slots = block_ids.shape[0]
    rows, cols = drag_coef.shape[1:]
    lon_count = lax.axis_size("gx")
    lat_count = lax.axis_size("gy")
    half = lat_count // 2
    block_total = 2 * lon_count * lat_count
    me = jnp.stack([lax.axis_index("gx"), lax.axis_index("gy")]).astype(jnp.int32)

    depths = depth_payload(bathymetry, land_mask, block_ids)
    depth_parts = [depths] + [swap(depths, "gy", 2 * m) for m in range(1, half)]
    forcing = column_forcing(adjoint_vel, level_count)

    parts = [forcing] + [swap(forcing, "gy", 2 * m) for m in range(1, half)]
    near_depths = stack_after(depth_parts, parts[1])
    near_depths = [near_depths] + [swap(near_depths, "gx", m) for m in range(1, lon_count)]
    columns = (adjoint_vel, velocity, drag_coef, level_count, block_ids)
    middle = (slots + 1) // 2
    first_column, *first_rest = column_mixing(*columns, forcing, block_total, 0, middle)
    line = stack_after(parts, first_rest[0])

    near = [line] + [swap(line, "gx", m) for m in range(1, lon_count)]
    near_depths = stack_after(near_depths, line)
    near_depths = near_depths.reshape((lon_count * half,) + depths.shape)
    far_depths = swap(near_depths, "gy", 1)
    last_column, bottom, drag_gradient = column_mixing(
        *columns, line, block_total, middle, slots, first_rest
    )
    weights = surface_weights(
        near_depths, far_depths, me, block_ids, rows, lon_count, lat_count
    )

    near = stack_after(near, bottom, weights[0])
    far = swap(near, "gy", 1)

    corrected, height, sensitivity = surface_solve(
        near.reshape((-1, rows, cols)), far.reshape((-1, rows, cols)), weights,
        block_ids, level_count, bottom, (first_column, last_column), block_total,
    )
    return corrected, drag_gradient, height, sensitivity


def solution(mesh):
    in_specs = (
        P(("gx", "gy"), None, None, None, None),
        P(("gx", "gy"), None, None, None, None),
        P(("gx", "gy"), None, None),
        P(("gx", "gy"), None, None),
        P(("gx", "gy")),
        P("gy", "gx"),
        P("gy", "gx"),
    )
    out_specs = (
        P(("gx", "gy"), None, None, None, None),
        P(("gx", "gy"), None, None),
        P("gy", "gx"),
        P("gy", "gx"),
    )
    return jax.shard_map(
        per_device, mesh=mesh, in_specs=in_specs, out_specs=out_specs, check_vma=False
    )
```

```python
import functools

import jax
import jax.numpy as jnp
import numpy as np
from jax import lax
from jax.experimental import pallas as pl
from jax.experimental.pallas import tpu as pltpu
from jax.sharding import PartitionSpec as P

STEPS = 32

mix_rate = 0.25
drag_step = 0.5
force_scale = 0.25
pressure_gain = 0.5
surface_shift = 1.0 / 64.0
speed_floor = 0.01

LANES = 128
SUBLANES = 8
MIB = 1024 * 1024
FIRST_VMEM = 61 * MIB
MIXING_VMEM = 52 * MIB
SOLVE_VMEM = 50 * MIB
WINDOW_VMEM = 16 * MIB


def chebyshev_sum(total_steps):
    highest = surface_shift + 8.0
    centre = 0.5 * (highest + surface_shift)
    radius = 0.5 * (highest - surface_shift)
    sigma_ratio = centre / radius

    def operate(series):
        shifted = np.zeros_like(series)
        shifted[1] += series[0]
        for k in range(1, len(series) - 1):
            shifted[k + 1] += 0.5 * series[k]
            shifted[k - 1] += 0.5 * series[k]
        return centre * series - radius * shifted

    height = np.zeros(total_steps + 2)
    residual = np.zeros(total_steps + 2)
    residual[0] = 1.0
    direction = residual / centre
    ratio_prev = 1.0 / sigma_ratio
    for _ in range(total_steps):
        height = height + direction
        residual = residual - operate(direction)
        ratio_next = 1.0 / (2.0 * sigma_ratio - ratio_prev)
        direction = ratio_next * ratio_prev * direction + 2.0 * ratio_next / radius * residual
        ratio_prev = ratio_next
    return [float(c) for c in height[:total_steps]], 2.0 / radius


def params(limit):
    return pltpu.CompilerParams(vmem_limit_bytes=limit)


SMEM = pl.BlockSpec(memory_space=pltpu.SMEM)
VMEM = pl.BlockSpec(memory_space=pltpu.VMEM)
ANYWHERE = pl.BlockSpec(memory_space=pl.ANY)
HBM = pl.BlockSpec(memory_space=pltpu.HBM)


def forcing_kernel(levels_ref, adjoint_ref, out_ref, levels_held, held, level_sem, sems):
    slots, comps, depth, rows, cols = held.shape
    level_copy = pltpu.make_async_copy(levels_ref, levels_held, level_sem)
    level_copy.start()

    def copy_in(b, c):
        return pltpu.make_async_copy(adjoint_ref.at[b, c], held.at[b, c], sems.at[b, c])

    for b in range(slots):
        for c in range(comps):
            copy_in(b, c).start()
    level_copy.wait()

    def one_slot(b, carry):
        levels = levels_held[b]
        totals = [jnp.zeros((rows, cols), jnp.float32) for _ in range(4)]
        for c in range(comps):
            copy_in(b, c).wait()
            for k in range(depth):
                totals[k % 4] = totals[k % 4] + jnp.where(levels > k, held[b, c, k], 0.0)
        out_ref[b] = force_scale * ((totals[0] + totals[1]) + (totals[2] + totals[3]))
        return carry

    lax.fori_loop(0, slots, one_slot, 0)


def column_forcing(adjoint_vel, level_count):
    slots, comps, depth, rows, cols = adjoint_vel.shape
    return pl.pallas_call(
        forcing_kernel,
        in_specs=[HBM, HBM],
        out_specs=VMEM,
        out_shape=pltpu.VMEM((slots, rows, cols), jnp.float32),
        scratch_shapes=[
            pltpu.VMEM(level_count.shape, jnp.int32),
            pltpu.VMEM(adjoint_vel.shape, jnp.float32),
            pltpu.SemaphoreType.DMA,
            pltpu.SemaphoreType.DMA((slots, comps)),
        ],
        compiler_params=params(FIRST_VMEM),
        cost_estimate=pl.CostEstimate(
            flops=2 * adjoint_vel.size, bytes_accessed=4 * adjoint_vel.size, transcendentals=0
        ),
        name="column_forcing",
    )(level_count, adjoint_vel)


CHUNK = 8


def mixing_kernel(block_total, ids_ref, levels_ref, drag_ref, adjoint_ref, velocity_ref, after_ref,
                  column_ref, bottom_ref, gradient_ref, adjoint, velocity, column,
                  in_sems, out_sems):
    slots, comps, depth, rows, cols = adjoint.shape
    group = 16
    parts = rows // group

    def copies_in(b):
        return [
            pltpu.make_async_copy(source.at[b, c], target.at[b, c], in_sems.at[n, b, c])
            for n, (source, target) in enumerate(
                ((adjoint_ref, adjoint), (velocity_ref, velocity))
            )
            for c in range(comps)
        ]

    def copy_out(b, index):
        span = pl.ds(pl.multiple_of(index * group, group), group)
        return pltpu.make_async_copy(
            column.at[b, :, :, span], column_ref.at[b, :, :, span], out_sems.at[b, index]
        )

    for b in range(slots):
        for copy in copies_in(b):
            copy.start()

    def one_component(b, c, span, levels):
        zero = jnp.zeros(levels.shape, jnp.float32)
        x = once = first_flux = second_flux = flow = field = zero
        wets = []
        rates = []

        def store(batch):
            for k, value in batch:
                column[b, c, k, span, :] = value

        late = []
        for low in range(0, depth + 2, CHUNK):
            batch = []
            for k in range(low, min(low + CHUNK, depth + 2)):
                fresh_once = None
                if k < depth:
                    wets.append(levels > k)
                    rates.append(jnp.where(wets[k], mix_rate, 0.0))
                    fresh = adjoint[b, c, k, span, :]
                    flow = jnp.where(
                        wets[k], velocity[b, c, k, span, :].astype(jnp.float32), flow
                    )
                    if 1 <= k:
                        flux = (fresh - x) * rates[k]
                        fresh_once = x + (flux - first_flux)
                        first_flux = flux
                    x = fresh
                elif k == depth:
                    fresh_once = x - first_flux
                if 2 <= k:
                    if k <= depth:
                        flux = (fresh_once - once) * rates[k - 1]
                        twice = once + (flux - second_flux)
                        second_flux = flux
                    else:
                        twice = once - second_flux
                    batch.append((k - 2, twice))
                    field = jnp.where(wets[k - 2], twice, field)
                if fresh_once is not None:
                    once = fresh_once
            store(late)
            late = batch
        store(late)
        return flow, field

    def one_group(b, index):
        flag = jnp.where(ids_ref[b] < block_total, 1.0, 0.0)
        span = pl.ds(pl.multiple_of(index * group, group), group)
        levels = levels_ref[b, span, :]
        flow, field = zip(*[one_component(b, c, span, levels) for c in range(2)])
        speed = jnp.sqrt(flow[0] * flow[0] + flow[1] * flow[1] + speed_floor)
        along = flow[0] * field[0] + flow[1] * field[1]
        ratio = along / speed
        drag = drag_ref[b, span, :]
        for c in range(2):
            bottom_ref[b, c, span, :] = field[c] - drag_step * drag * (
                speed * field[c] + flow[c] * ratio
            )
        gradient_ref[b, span, :] = -drag_step * speed * along * flag

    def one(step, carry):
        b = lax.div(step, parts)
        index = lax.rem(step, parts)

        @pl.when(index == 0)
        def _():
            for copy in copies_in(b):
                copy.wait()

        one_group(b, index)
        copy_out(b, index).start()
        return carry

    lax.fori_loop(0, slots * parts, one, 0)
    for b in range(slots):
        for index in range(parts):
            copy_out(b, index).wait()


def column_mixing(adjoint_vel, velocity, drag_coef, level_count, block_ids, after, block_total):
    slots, comps, depth, rows, cols = adjoint_vel.shape
    size = adjoint_vel.size
    return pl.pallas_call(
        functools.partial(mixing_kernel, block_total),
        in_specs=[SMEM, VMEM, VMEM, HBM, HBM, ANYWHERE],
        out_specs=[HBM, VMEM, VMEM],
        out_shape=[
            pltpu.HBM(adjoint_vel.shape, jnp.float32),
            pltpu.VMEM((slots, comps, rows, cols), jnp.float32),
            pltpu.HBM((slots, rows, cols), jnp.float32),
        ],
        scratch_shapes=[
            pltpu.VMEM(adjoint_vel.shape, adjoint_vel.dtype),
            pltpu.VMEM(velocity.shape, velocity.dtype),
            pltpu.VMEM(adjoint_vel.shape, jnp.float32),
            pltpu.SemaphoreType.DMA((2, slots, comps)),
            pltpu.SemaphoreType.DMA((slots, rows // 16)),
        ],
        compiler_params=params(MIXING_VMEM),
        cost_estimate=pl.CostEstimate(
            flops=14 * size, bytes_accessed=10 * size, transcendentals=0
        ),
        name="column_mixing",
    )(block_ids, level_count, drag_coef, adjoint_vel, velocity, after)


PAD = SUBLANES
BATCH = 3
WIDTH = LANES + 2 * STEPS
PITCH = WIDTH + 2 * PAD
NEIGHBOURS = [(down, right) for down in (-1, 0, 1) for right in (0, 1, -1)]


def window_shape(slots, rows):
    strips = LANES // (slots + 2)
    deep = pl.cdiv(rows + 2 * STEPS, strips)
    return strips, deep, strips * deep


def log2(count):
    bits = count.bit_length() - 1
    assert 1 << bits == count
    return bits


def window_places(me_ref, ids_ref, slots, lon_count, lat_count):
    places = []
    for w in range(slots + 2):
        if w < slots:
            block = jnp.where(ids_ref[w] < 2 * lon_count * lat_count, ids_ref[w], 0)
        else:
            block = (me_ref[0] * lat_count + me_ref[1]) * 2 + (w - slots)
        pair = block >> 1
        column = (pair >> log2(lat_count)) * 2 + (block & 1)
        places.append((pair & (lat_count - 1), column))
    return places


def put_window(natural, base, rows, blocks, lane):
    for i in range(3):
        here, east, west = blocks[3 * i:3 * i + 3]
        sides = jnp.where(lane < STEPS, east, jnp.where(lane >= LANES - STEPS, west, 0.0))
        start = base + i * rows
        natural[0, start:start + rows, :] = here
        natural[1, start:start + rows, :] = sides


def turn(natural, deep, put):
    for i in range(deep):
        put(i, STEPS, natural[0, pl.ds(i, LANES, stride=deep), :].T)
        sides = natural[1, pl.ds(i, LANES, stride=deep), :].T
        put(i, STEPS + LANES, sides[:STEPS])
        put(i, 0, sides[LANES - STEPS:])


def rows_at(ref, start, shift=0):
    return ref[pl.ds(start + shift, SUBLANES), :]


def in_batches(chunks, work):
    late = []
    for start in range(0, len(chunks), BATCH):
        batch = [item for chunk in chunks[start:start + BATCH] for item in work(chunk)]
        for ref, a, value in late:
            ref[pl.ds(a, SUBLANES), :] = value
        late = batch
    for ref, a, value in late:
        ref[pl.ds(a, SUBLANES), :] = value


def strip_rows(ref, chunk, deep):
    at = [i * PITCH + PAD + chunk * SUBLANES for i in range(deep)]
    here = [rows_at(ref, a) for a in at]
    above = [pltpu.roll(here[-1], 1, 1)] + here[:-1]
    below = here[1:] + [pltpu.roll(here[0], LANES - 1, 1)]
    return here, above, below, at


def depth_kernel(ids_ref, bathymetry_ref, mask_ref, out_ref, ids, bathymetry, mask, sems):
    copies = [
        pltpu.make_async_copy(ids_ref, ids, sems.at[0]),
        pltpu.make_async_copy(bathymetry_ref, bathymetry, sems.at[1]),
        pltpu.make_async_copy(mask_ref, mask, sems.at[2]),
    ]
    for copy in copies:
        copy.start()
    for copy in copies:
        copy.wait()
    rows = bathymetry.shape[0]
    scaled = bathymetry[...] * mask[...].astype(jnp.float32)
    out_ref[0:rows, :] = scaled[:, :LANES]
    out_ref[rows:2 * rows, :] = scaled[:, LANES:]
    lane = lax.broadcasted_iota(jnp.int32, (SUBLANES, LANES), 1)
    listed = jnp.zeros((SUBLANES, LANES), jnp.int32)
    for s in range(ids.shape[0]):
        listed = jnp.where(lane == s, ids[s], listed)
    out_ref[2 * rows:2 * rows + SUBLANES, :] = listed.astype(jnp.float32)


def depth_payload(bathymetry, land_mask, block_ids):
    rows = bathymetry.shape[0]
    return pl.pallas_call(
        depth_kernel,
        in_specs=[HBM, HBM, HBM],
        out_specs=VMEM,
        out_shape=pltpu.VMEM((2 * rows + SUBLANES, LANES), jnp.float32),
        scratch_shapes=[
            pltpu.SMEM(block_ids.shape, jnp.int32),
            pltpu.VMEM(bathymetry.shape, jnp.float32),
            pltpu.VMEM(land_mask.shape, jnp.int32),
            pltpu.SemaphoreType.DMA((3,)),
        ],
        compiler_params=params(FIRST_VMEM),
        name="depth_payload",
    )(block_ids, bathymetry, land_mask)


def weights_kernel(slots, lon_count, lat_count, me_ref, ids_ref, near_ref, far_ref,
                   root_ref, centre_ref, around_ref, table_ref,
                   natural, all_ids, places_of, sems):
    half = lat_count // 2
    count = lon_count * half
    rows = (near_ref.shape[1] - SUBLANES) // 2
    strips, deep, tall = window_shape(slots, rows)
    column_count = 2 * lon_count
    parts = (near_ref, far_ref)
    copies = [
        pltpu.make_async_copy(
            parts[p].at[:, pl.ds(2 * rows, 1), :], all_ids.at[p], sems.at[p]
        )
        for p in range(2)
    ]
    for copy in copies:
        copy.start()
    natural[...] = jnp.zeros_like(natural)

    def load(lat, column):
        inside = (lat >= 0) & (lat < lat_count) & (column >= 0) & (column < column_count)
        lat_safe = jnp.clip(lat, 0, lat_count - 1)
        column_safe = jnp.clip(column, 0, column_count - 1)
        lon_xor = (column_safe >> 1) ^ me_ref[0]
        lat_xor = lat_safe ^ me_ref[1]
        place = lon_xor * half + (lat_xor >> 1)
        start = pl.multiple_of((column_safe & 1) * rows, SUBLANES)
        near = near_ref[place, pl.ds(start, rows), :]
        far = far_ref[place, pl.ds(start, rows), :]
        here = jnp.where((lat_xor & 1) == 0, near, far)
        return here * jnp.where(inside, 1.0, 0.0)

    lane = lax.broadcasted_iota(jnp.int32, (rows, LANES), 1)
    places = window_places(me_ref, ids_ref, slots, lon_count, lat_count)
    for w, (lat, column) in enumerate(places):
        blocks = [load(lat + down, column + right) for down, right in NEIGHBOURS]
        put_window(natural, w * tall, rows, blocks, lane)

    for copy in copies:
        copy.wait()

    def one_device(n, carry):
        for p in range(2):
            for s in range(slots):
                block = all_ids[p, n, 0, s].astype(jnp.int32)
                places_of[block] = (p * count + n) * slots + s
        return carry

    lax.fori_loop(0, count, one_device, 0)
    for w, (lat, column) in enumerate(places):
        for n, (down, right) in enumerate(NEIGHBOURS):
            lat_safe = jnp.clip(lat + down, 0, lat_count - 1)
            column_safe = jnp.clip(column + right, 0, column_count - 1)
            block = ((column_safe >> 1) * lat_count + lat_safe) * 2 + (column_safe & 1)
            table_ref[w * len(NEIGHBOURS) + n] = places_of[block]

    scale = chebyshev_sum(STEPS)[1]

    def put(i, x, values):
        start = i * PITCH + PAD + x
        root_ref[start:start + values.shape[0], :] = jnp.sqrt(values)
        around_ref[start:start + values.shape[0], :] = scale * values

    turn(natural, deep, put)
    zeros = jnp.zeros((PAD, LANES), jnp.float32)
    for i in range(deep):
        root_ref[i * PITCH:i * PITCH + PAD, :] = zeros
        root_ref[(i + 1) * PITCH - PAD:(i + 1) * PITCH, :] = zeros

    def work(chunk):
        here, above, below, at = strip_rows(root_ref, chunk, deep)
        out = []
        for i, a in enumerate(at):
            others = (rows_at(root_ref, a, 1) + rows_at(root_ref, a, -1)) + (above[i] + below[i])
            out.append((centre_ref, a, 2.0 - scale * here[i] * others))
        return out

    in_batches(range(WIDTH // SUBLANES), work)


def surface_weights(near, far, me, block_ids, rows, lon_count, lat_count):
    slots = block_ids.shape[0]
    assert near.shape[-1] == LANES
    strips, deep, tall = window_shape(slots, rows)
    shape = jax.ShapeDtypeStruct((deep * PITCH, LANES), jnp.float32)
    return pl.pallas_call(
        functools.partial(weights_kernel, slots, lon_count, lat_count),
        in_specs=[SMEM, SMEM, VMEM, VMEM],
        out_specs=[VMEM, VMEM, VMEM, SMEM],
        out_shape=[
            shape,
            shape,
            shape,
            jax.ShapeDtypeStruct(((slots + 2) * len(NEIGHBOURS),), jnp.int32),
        ],
        scratch_shapes=[
            pltpu.VMEM((2, LANES * deep, LANES), jnp.float32),
            pltpu.SMEM((2, near.shape[0], 1, LANES), jnp.float32),
            pltpu.SMEM((2 * lon_count * lat_count + 1,), jnp.int32),
            pltpu.SemaphoreType.DMA((2,)),
        ],
        compiler_params=params(WINDOW_VMEM),
        cost_estimate=pl.CostEstimate(
            flops=0, bytes_accessed=8 * MIB, transcendentals=0
        ),
        name="surface_weights",
    )(me, block_ids, near, far)


def solve_kernel(block_total, ids_ref, table_ref, coefs_ref, root_ref, centre_ref, around_ref,
                 levels_ref, bottom_ref, column_ref, near_ref, far_ref,
                 corrected_ref, height_ref, sensitivity_ref,
                 natural, source, even, odd, extra, column, in_sems, out_sems):
    slots, comps, depth, rows, cols = column.shape
    strips, deep, tall = window_shape(slots, rows)

    copies_in = [
        pltpu.make_async_copy(column_ref.at[b], column.at[b], in_sems.at[b]) for b in range(slots)
    ]
    for copy in copies_in:
        copy.start()

    count = near_ref.shape[0]

    def load(place):
        inner = place & (count - 1)
        return jnp.where(place < count, near_ref[inner], far_ref[inner])

    lane = lax.broadcasted_iota(jnp.int32, (rows, LANES), 1)
    for w in range(slots + 2):
        places = [table_ref[w * len(NEIGHBOURS) + n] for n in range(len(NEIGHBOURS))]
        put_window(natural, w * tall, rows, [load(place) for place in places], lane)

    coefs, step_scale = chebyshev_sum(STEPS)

    def put(i, x, values):
        start = i * PITCH + PAD + x
        stop = start + values.shape[0]
        root = root_ref[start:stop, :]
        values = jnp.where(root > 0.0, root * values, 0.0)
        source[start:stop, :] = values
        even[start:stop, :] = coefs[STEPS - 1] * values
        odd[start:stop, :] = jnp.zeros_like(values)

    zeros = jnp.zeros((PAD, LANES), jnp.float32)
    for ref in (even, odd):
        for i in range(deep):
            ref[i * PITCH:i * PITCH + PAD, :] = zeros
            ref[(i + 1) * PITCH - PAD:(i + 1) * PITCH, :] = zeros
    turn(natural, deep, put)

    chunks = WIDTH // SUBLANES

    def apply(current, target, coef, gain, m):
        def work(chunk):
            here, above, below, at = strip_rows(current, chunk, deep)
            out = []
            for i, a in enumerate(at):
                others = (rows_at(current, a, 1) + rows_at(current, a, -1)) + (
                    above[i] + below[i]
                )
                pushed = rows_at(centre_ref, a) * here[i] + rows_at(around_ref, a) * others
                if gain != 1.0:
                    pushed = gain * pushed
                kept = coef * rows_at(source, a) - rows_at(target, a)
                out.append((target, a, kept + pushed))
            return out

        in_batches(range(m // SUBLANES, chunks - m // SUBLANES), work)

    runs = []
    for m in range(1, STEPS - 1, 2):
        if runs and runs[-1][0] // SUBLANES == m // SUBLANES:
            runs[-1][1] += 1
        else:
            runs.append([m, 1])
    for first, pairs in runs:
        def two_steps(pair, carry, first=first):
            m = first + 2 * pair
            apply(even, odd, coefs_ref[m], 1.0, first)
            apply(odd, even, coefs_ref[m + 1], 1.0, first)
            return carry

        lax.fori_loop(0, pairs, two_steps, 0)
    apply(even, odd, coefs[0], 0.5, STEPS - 1)

    low = STEPS // SUBLANES - 1

    def one_height(chunk):
        out = []
        for i in range(deep):
            a = i * PITCH + PAD + chunk * SUBLANES
            root = rows_at(root_ref, a)
            out.append((extra, a, jnp.where(root > 0.0, rows_at(odd, a) / root, 0.0)))
        return out

    in_batches(range(low, chunks - low), one_height)

    def differences(chunk):
        here, above, below, at = strip_rows(extra, chunk, deep)
        root, root_above, root_below, _ = strip_rows(root_ref, chunk, deep)
        out = []
        for i, a in enumerate(at):
            east_step = rows_at(extra, a, 1) - here[i]
            west_step = here[i] - rows_at(extra, a, -1)
            south_step = below[i] - here[i]
            north_step = here[i] - above[i]
            energy = root[i] * (
                (rows_at(root_ref, a, 1) * east_step * east_step
                 + rows_at(root_ref, a, -1) * west_step * west_step)
                + (root_below[i] * south_step * south_step
                   + root_above[i] * north_step * north_step)
            )
            scaled = rows_at(around_ref, a) * (1.0 / step_scale)
            out.append((even, a, east_step))
            out.append((source, a, 0.25 * energy / jnp.maximum(scaled, 0.25)))
        return out

    in_batches(range(low + 1, chunks - low - 1), differences)

    def turn_back(ref, tile):
        for i in range(deep):
            start = i * PITCH + PAD + STEPS
            natural[tile, pl.ds(i, LANES, stride=deep), :] = ref[start:start + LANES, :].T

    def cut(tile, w, shift=0):
        return natural[tile, pl.ds(w * tall + STEPS + shift, rows), :]

    def copy_out(b, c):
        return pltpu.make_async_copy(column.at[b, c], corrected_ref.at[b, c], out_sems.at[b, c])

    def correct(b, c, step):
        levels = levels_ref[b] * jnp.where(ids_ref[b] < block_total, 1, 0)
        push = pressure_gain * step
        lowest = bottom_ref[b, c] - push

        late = []
        for low in range(0, depth, CHUNK):
            batch = []
            for k in range(low, min(low + CHUNK, depth)):
                value = jnp.where(levels == k + 1, lowest, column[b, c, k] - push)
                batch.append((k, jnp.where(levels > k, value, 0.0)))
            for k, value in late:
                column[b, c, k] = value
            late = batch
        for k, value in late:
            column[b, c, k] = value
        copy_out(b, c).start()

    turn_back(even, 0)
    for copy in copies_in:
        copy.wait()

    def correct_east(b, carry):
        correct(b, 0, cut(0, b))
        return carry

    def correct_north(b, carry):
        correct(b, 1, cut(1, b, 1) - cut(1, b))
        return carry

    lax.fori_loop(0, slots, correct_east, 0)
    turn_back(extra, 1)
    lax.fori_loop(0, slots, correct_north, 0)
    turn_back(source, 0)
    for h in range(2):
        height_ref[:, h * LANES:(h + 1) * LANES] = cut(1, slots + h)
        sensitivity_ref[:, h * LANES:(h + 1) * LANES] = cut(0, slots + h)

    for b in range(slots):
        for c in range(comps):
            copy_out(b, c).wait()


def surface_solve(near, far, weights, block_ids, level_count, bottom, column, block_total):
    root, centre, around, table = weights
    slots, comps, depth, rows, cols = column.shape
    assert comps == 2
    deep = window_shape(slots, rows)[1]
    turned = pltpu.VMEM(root.shape, jnp.float32)
    coefs = jnp.array(chebyshev_sum(STEPS)[0][::-1], jnp.float32)
    return pl.pallas_call(
        functools.partial(solve_kernel, block_total),
        in_specs=[SMEM, SMEM, SMEM] + [VMEM] * 5 + [HBM] + [VMEM] * 2,
        out_specs=[HBM, VMEM, VMEM],
        out_shape=[
            jax.ShapeDtypeStruct(column.shape, jnp.float32),
            jax.ShapeDtypeStruct((rows, 2 * cols), jnp.float32),
            jax.ShapeDtypeStruct((rows, 2 * cols), jnp.float32),
        ],
        scratch_shapes=[
            pltpu.VMEM((2, LANES * deep, LANES), jnp.float32),
            turned,
            turned,
            turned,
            turned,
            pltpu.VMEM(column.shape, jnp.float32),
            pltpu.SemaphoreType.DMA((slots,)),
            pltpu.SemaphoreType.DMA((slots, comps)),
        ],
        compiler_params=params(SOLVE_VMEM),
        cost_estimate=pl.CostEstimate(
            flops=9 * STEPS * root.size, bytes_accessed=16 * root.size, transcendentals=0
        ),
        name="surface_solve",
    )(block_ids, table, coefs, root, centre, around, level_count, bottom, column, near, far)


def stack_kernel(parts, *refs):
    out_ref = refs[-1]
    for p in range(parts):
        out_ref[p] = refs[p][...]


def stack_after(parts, *tokens):
    return pl.pallas_call(
        functools.partial(stack_kernel, len(parts)),
        in_specs=[VMEM] * len(parts) + [ANYWHERE] * len(tokens),
        out_specs=VMEM,
        out_shape=jax.ShapeDtypeStruct((len(parts),) + parts[0].shape, jnp.float32),
        compiler_params=params(WINDOW_VMEM),
        name="stack_after",
    )(*parts, *tokens)


def swap(values, axis, mask):
    count = lax.axis_size(axis)
    return lax.ppermute(values, axis, [(i, i ^ mask) for i in range(count)])


def per_device(adjoint_vel, velocity, drag_coef, level_count, block_ids, bathymetry, land_mask):
    slots = block_ids.shape[0]
    rows, cols = drag_coef.shape[1:]
    lon_count = lax.axis_size("gx")
    lat_count = lax.axis_size("gy")
    half = lat_count // 2
    block_total = 2 * lon_count * lat_count
    me = jnp.stack([lax.axis_index("gx"), lax.axis_index("gy")]).astype(jnp.int32)

    depths = depth_payload(bathymetry, land_mask, block_ids)
    depth_parts = [depths] + [swap(depths, "gy", 2 * m) for m in range(1, half)]
    forcing = column_forcing(adjoint_vel, level_count)

    parts = [forcing] + [swap(forcing, "gy", 2 * m) for m in range(1, half)]
    near_depths = stack_after(depth_parts, forcing)
    near_depths = [near_depths] + [swap(near_depths, "gx", m) for m in range(1, lon_count)]
    line = stack_after(parts)

    near = [line] + [swap(line, "gx", m) for m in range(1, lon_count)]
    near_depths = stack_after(near_depths, line)
    near_depths = near_depths.reshape((lon_count * half,) + depths.shape)
    far_depths = swap(near_depths, "gy", 1)
    column, bottom, drag_gradient = column_mixing(
        adjoint_vel, velocity, drag_coef, level_count, block_ids, line, block_total
    )
    weights = surface_weights(
        near_depths, far_depths, me, block_ids, rows, lon_count, lat_count
    )

    near = stack_after(near, bottom, weights[0])
    far = swap(near, "gy", 1)

    corrected, height, sensitivity = surface_solve(
        near.reshape((-1, rows, cols)), far.reshape((-1, rows, cols)), weights,
        block_ids, level_count, bottom, column, block_total,
    )
    return corrected, drag_gradient, height, sensitivity


def solution(mesh):
    in_specs = (
        P(("gx", "gy"), None, None, None, None),
        P(("gx", "gy"), None, None, None, None),
        P(("gx", "gy"), None, None),
        P(("gx", "gy"), None, None),
        P(("gx", "gy")),
        P("gy", "gx"),
        P("gy", "gx"),
    )
    out_specs = (
        P(("gx", "gy"), None, None, None, None),
        P(("gx", "gy"), None, None),
        P("gy", "gx"),
        P("gy", "gx"),
    )
    return jax.shard_map(
        per_device, mesh=mesh, in_specs=in_specs, out_specs=out_specs, check_vma=False
    )
```

```python
import functools

import jax
import jax.numpy as jnp
import numpy as np
from jax import lax
from jax.experimental import pallas as pl
from jax.experimental.pallas import tpu as pltpu
from jax.sharding import PartitionSpec as P

STEPS = 32

mix_rate = 0.25
drag_step = 0.5
force_scale = 0.25
pressure_gain = 0.5
surface_shift = 1.0 / 64.0
speed_floor = 0.01

LANES = 128
SUBLANES = 8
MIB = 1024 * 1024
FIRST_VMEM = 61 * MIB
MIXING_VMEM = 52 * MIB
SOLVE_VMEM = 50 * MIB
WINDOW_VMEM = 16 * MIB


def chebyshev_sum(total_steps):
    highest = surface_shift + 8.0
    centre = 0.5 * (highest + surface_shift)
    radius = 0.5 * (highest - surface_shift)
    sigma_ratio = centre / radius

    def operate(series):
        shifted = np.zeros_like(series)
        shifted[1] += series[0]
        for k in range(1, len(series) - 1):
            shifted[k + 1] += 0.5 * series[k]
            shifted[k - 1] += 0.5 * series[k]
        return centre * series - radius * shifted

    height = np.zeros(total_steps + 2)
    residual = np.zeros(total_steps + 2)
    residual[0] = 1.0
    direction = residual / centre
    ratio_prev = 1.0 / sigma_ratio
    for _ in range(total_steps):
        height = height + direction
        residual = residual - operate(direction)
        ratio_next = 1.0 / (2.0 * sigma_ratio - ratio_prev)
        direction = ratio_next * ratio_prev * direction + 2.0 * ratio_next / radius * residual
        ratio_prev = ratio_next
    return [float(c) for c in height[:total_steps]], 2.0 / radius


def params(limit):
    return pltpu.CompilerParams(vmem_limit_bytes=limit)


SMEM = pl.BlockSpec(memory_space=pltpu.SMEM)
VMEM = pl.BlockSpec(memory_space=pltpu.VMEM)
ANYWHERE = pl.BlockSpec(memory_space=pl.ANY)
HBM = pl.BlockSpec(memory_space=pltpu.HBM)


def forcing_kernel(levels_ref, adjoint_ref, out_ref, levels_held, held, level_sem, sems):
    slots, comps, depth, rows, cols = held.shape
    level_copy = pltpu.make_async_copy(levels_ref, levels_held, level_sem)
    level_copy.start()

    def copy_in(b, c):
        return pltpu.make_async_copy(adjoint_ref.at[b, c], held.at[b, c], sems.at[b, c])

    for b in range(slots):
        for c in range(comps):
            copy_in(b, c).start()
    level_copy.wait()

    def one_slot(b, carry):
        levels = levels_held[b]
        totals = [jnp.zeros((rows, cols), jnp.float32) for _ in range(4)]
        for c in range(comps):
            copy_in(b, c).wait()
            for k in range(depth):
                totals[k % 4] = totals[k % 4] + jnp.where(levels > k, held[b, c, k], 0.0)
        out_ref[b] = force_scale * ((totals[0] + totals[1]) + (totals[2] + totals[3]))
        return carry

    lax.fori_loop(0, slots, one_slot, 0)


def column_forcing(adjoint_vel, level_count):
    slots, comps, depth, rows, cols = adjoint_vel.shape
    return pl.pallas_call(
        forcing_kernel,
        in_specs=[HBM, HBM],
        out_specs=VMEM,
        out_shape=pltpu.VMEM((slots, rows, cols), jnp.float32),
        scratch_shapes=[
            pltpu.VMEM(level_count.shape, jnp.int32),
            pltpu.VMEM(adjoint_vel.shape, jnp.float32),
            pltpu.SemaphoreType.DMA,
            pltpu.SemaphoreType.DMA((slots, comps)),
        ],
        compiler_params=params(FIRST_VMEM),
        cost_estimate=pl.CostEstimate(
            flops=2 * adjoint_vel.size, bytes_accessed=4 * adjoint_vel.size, transcendentals=0
        ),
        name="column_forcing",
    )(level_count, adjoint_vel)


CHUNK = 8


def mixing_kernel(block_total, first, earlier, ids_ref, levels_ref, drag_ref, adjoint_ref,
                  velocity_ref, after_ref, *rest):
    if earlier:
        for target, ref in zip(rest[3:5], rest[:2]):
            target[0:first] = ref[...]
        rest = rest[2:]
    column_ref, bottom_ref, gradient_ref, adjoint, velocity, column, in_sems, out_sems = rest
    slots, comps, depth, rows, cols = adjoint.shape
    group = 16
    parts = rows // group

    def copies_in(b):
        return [
            pltpu.make_async_copy(source.at[first + b, c], target.at[b, c], in_sems.at[n, b, c])
            for n, (source, target) in enumerate(
                ((adjoint_ref, adjoint), (velocity_ref, velocity))
            )
            for c in range(comps)
        ]

    def copy_out(b, index):
        span = pl.ds(pl.multiple_of(index * group, group), group)
        return pltpu.make_async_copy(
            column.at[b, :, :, span], column_ref.at[b, :, :, span], out_sems.at[b, index]
        )

    for b in range(slots):
        for copy in copies_in(b):
            copy.start()

    def one_group(b, index):
        flag = jnp.where(ids_ref[first + b] < block_total, 1.0, 0.0)
        span = pl.ds(pl.multiple_of(index * group, group), group)
        levels = levels_ref[first + b, span, :]
        zero = jnp.zeros(levels.shape, jnp.float32)
        x = [zero, zero]
        once = [zero, zero]
        first_flux = [zero, zero]
        second_flux = [zero, zero]
        flow = [zero, zero]
        field = [zero, zero]
        wets = []
        rates = []
        for low in range(0, depth + 2, CHUNK):
            here = range(low, min(low + CHUNK, depth + 2))
            loaded = {}
            for k in here:
                if k < depth:
                    for c in range(2):
                        loaded[k, c] = (adjoint[b, c, k, span, :], velocity[b, c, k, span, :])
            done = []
            for k in here:
                if k < depth:
                    wets.append(levels > k)
                    rates.append(jnp.where(wets[k], mix_rate, 0.0))
                for c in range(2):
                    fresh_once = None
                    if k < depth:
                        fresh = loaded[k, c][0]
                        flow[c] = jnp.where(
                            wets[k], loaded[k, c][1].astype(jnp.float32), flow[c]
                        )
                        if 1 <= k:
                            flux = (fresh - x[c]) * rates[k]
                            fresh_once = x[c] + (flux - first_flux[c])
                            first_flux[c] = flux
                        x[c] = fresh
                    elif k == depth:
                        fresh_once = x[c] - first_flux[c]
                    if 2 <= k:
                        if k <= depth:
                            flux = (fresh_once - once[c]) * rates[k - 1]
                            twice = once[c] + (flux - second_flux[c])
                            second_flux[c] = flux
                        else:
                            twice = once[c] - second_flux[c]
                        done.append((c, k - 2, twice))
                        field[c] = jnp.where(wets[k - 2], twice, field[c])
                    if fresh_once is not None:
                        once[c] = fresh_once
            for c, k, value in done:
                column[b, c, k, span, :] = value
        speed = jnp.sqrt(flow[0] * flow[0] + flow[1] * flow[1] + speed_floor)
        along = flow[0] * field[0] + flow[1] * field[1]
        ratio = along / speed
        drag = drag_ref[first + b, span, :]
        for c in range(2):
            bottom_ref[first + b, c, span, :] = field[c] - drag_step * drag * (
                speed * field[c] + flow[c] * ratio
            )
        gradient_ref[first + b, span, :] = -drag_step * speed * along * flag

    def one(step, carry):
        b = lax.div(step, parts)
        index = lax.rem(step, parts)

        @pl.when(index == 0)
        def _():
            for copy in copies_in(b):
                copy.wait()

        one_group(b, index)
        copy_out(b, index).start()
        return carry

    lax.fori_loop(0, slots * parts, one, 0)
    for b in range(slots):
        for index in range(parts):
            copy_out(b, index).wait()


def column_mixing(adjoint_vel, velocity, drag_coef, level_count, block_ids, after, block_total,
                  first, last, earlier=()):
    comps, depth, rows, cols = adjoint_vel.shape[1:]
    slots = last - first
    part = (slots, comps, depth, rows, cols)
    size = slots * comps * depth * rows * cols
    return pl.pallas_call(
        functools.partial(mixing_kernel, block_total, first, len(earlier)),
        in_specs=[SMEM, VMEM, VMEM, HBM, HBM, ANYWHERE] + [VMEM] * len(earlier),
        out_specs=[HBM, VMEM, VMEM],
        out_shape=[
            pltpu.HBM(part, jnp.float32),
            pltpu.VMEM((last, comps, rows, cols), jnp.float32),
            (pltpu.HBM if last == level_count.shape[0] else pltpu.VMEM)((last, rows, cols), jnp.float32),
        ],
        scratch_shapes=[
            pltpu.VMEM(part, adjoint_vel.dtype),
            pltpu.VMEM(part, velocity.dtype),
            pltpu.VMEM(part, jnp.float32),
            pltpu.SemaphoreType.DMA((2, slots, comps)),
            pltpu.SemaphoreType.DMA((slots, rows // 16)),
        ],
        compiler_params=params(MIXING_VMEM),
        cost_estimate=pl.CostEstimate(
            flops=14 * size, bytes_accessed=10 * size, transcendentals=0
        ),
        name="column_mixing",
    )(block_ids, level_count, drag_coef, adjoint_vel, velocity, after, *earlier)


WIDTH = LANES + 2 * STEPS
SPAN = WIDTH // SUBLANES
BATCH = 3
NEIGHBOURS = [(down, right) for down in (-1, 0, 1) for right in (0, 1, -1)]


def window_shape(slots, rows):
    strips = LANES // (slots + 2)
    deep = pl.cdiv(rows + 2 * STEPS, strips)
    return strips, deep, strips * deep


def log2(count):
    bits = count.bit_length() - 1
    assert 1 << bits == count
    return bits


def window_places(me_ref, ids_ref, slots, lon_count, lat_count):
    places = []
    for w in range(slots + 2):
        if w < slots:
            block = jnp.where(ids_ref[w] < 2 * lon_count * lat_count, ids_ref[w], 0)
        else:
            block = (me_ref[0] * lat_count + me_ref[1]) * 2 + (w - slots)
        pair = block >> 1
        column = (pair >> log2(lat_count)) * 2 + (block & 1)
        places.append((pair & (lat_count - 1), column))
    return places


def put_window(natural, base, rows, blocks, lane):
    for i in range(3):
        here, east, west = blocks[3 * i:3 * i + 3]
        sides = jnp.where(lane < STEPS, east, jnp.where(lane >= LANES - STEPS, west, 0.0))
        start = base + i * rows
        natural[0, start:start + rows, :] = here
        natural[1, start:start + rows, :] = sides


def strip_pieces(first, count):
    pieces = []
    x = first
    while x < first + count:
        length = min(SPAN - x % SPAN, first + count - x)
        pieces.append((x - first, x // SPAN, x % SPAN, length))
        x += length
    return pieces


def turned_rows(i, sublane, n, length):
    return pl.ds(i * WIDTH + n * SUBLANES + sublane, length, stride=SUBLANES)


def turn(natural, deep, target):
    def put(i, first, values):
        for offset, sublane, n, length in strip_pieces(first, values.shape[0]):
            target[turned_rows(i, sublane, n, length), :] = values[offset:offset + length]

    for i in range(deep):
        put(i, STEPS, natural[0, pl.ds(i, LANES, stride=deep), :].T)
        sides = natural[1, pl.ds(i, LANES, stride=deep), :].T
        put(i, STEPS + LANES, sides[:STEPS])
        put(i, 0, sides[LANES - STEPS:])


def turn_back(source, natural, tile, deep):
    for i in range(deep):
        values = jnp.concatenate(
            [
                source[turned_rows(i, sublane, n, length), :]
                for _, sublane, n, length in strip_pieces(STEPS, LANES)
            ],
            axis=0,
        )
        natural[tile, pl.ds(i, LANES, stride=deep), :] = values.T


def vector(i, n):
    start = (i * SPAN + n) * SUBLANES
    return slice(start, start + SUBLANES)


def in_batches(deep, work):
    late = []
    for start in range(0, SPAN, BATCH):
        batch = [
            (ref, vector(i, n), value)
            for n in range(start, min(start + BATCH, SPAN))
            for i in range(deep)
            for ref, value in work(i, n)
        ]
        for ref, at, value in late:
            ref[at, :] = value
        late = batch
    for ref, at, value in late:
        ref[at, :] = value


class Around:
    def __init__(self, ref, deep):
        self.ref = ref
        self.deep = deep
        self.held = {}

    def here(self, i, n):
        if (i, n) not in self.held:
            self.held[i, n] = self.ref[vector(i, n), :]
        return self.held[i, n]

    def east(self, i, n):
        if n + 1 < SPAN:
            return self.here(i, n + 1)
        return pltpu.roll(self.ref[vector(i, 0), :], SUBLANES - 1, 0)

    def west(self, i, n):
        if n > 0:
            return self.here(i, n - 1)
        return pltpu.roll(self.ref[vector(i, SPAN - 1), :], 1, 0)

    def north(self, i, n):
        if i > 0:
            return self.here(i - 1, n)
        return pltpu.roll(self.here(self.deep - 1, n), 1, 1)

    def south(self, i, n):
        if i + 1 < self.deep:
            return self.here(i + 1, n)
        return pltpu.roll(self.here(0, n), LANES - 1, 1)

    def total(self, i, n):
        return (self.east(i, n) + self.west(i, n)) + (self.north(i, n) + self.south(i, n))


def depth_kernel(ids_ref, bathymetry_ref, mask_ref, out_ref, ids, bathymetry, mask, sems):
    copies = [
        pltpu.make_async_copy(ids_ref, ids, sems.at[0]),
        pltpu.make_async_copy(bathymetry_ref, bathymetry, sems.at[1]),
        pltpu.make_async_copy(mask_ref, mask, sems.at[2]),
    ]
    for copy in copies:
        copy.start()
    for copy in copies:
        copy.wait()
    rows = bathymetry.shape[0]
    scaled = bathymetry[...] * mask[...].astype(jnp.float32)
    out_ref[0:rows, :] = scaled[:, :LANES]
    out_ref[rows:2 * rows, :] = scaled[:, LANES:]
    lane = lax.broadcasted_iota(jnp.int32, (SUBLANES, LANES), 1)
    listed = jnp.zeros((SUBLANES, LANES), jnp.int32)
    for s in range(ids.shape[0]):
        listed = jnp.where(lane == s, ids[s], listed)
    out_ref[2 * rows:2 * rows + SUBLANES, :] = listed.astype(jnp.float32)


def depth_payload(bathymetry, land_mask, block_ids):
    rows = bathymetry.shape[0]
    return pl.pallas_call(
        depth_kernel,
        in_specs=[HBM, HBM, HBM],
        out_specs=VMEM,
        out_shape=pltpu.VMEM((2 * rows + SUBLANES, LANES), jnp.float32),
        scratch_shapes=[
            pltpu.SMEM(block_ids.shape, jnp.int32),
            pltpu.VMEM(bathymetry.shape, jnp.float32),
            pltpu.VMEM(land_mask.shape, jnp.int32),
            pltpu.SemaphoreType.DMA((3,)),
        ],
        compiler_params=params(FIRST_VMEM),
        name="depth_payload",
    )(block_ids, bathymetry, land_mask)


def weights_kernel(slots, lon_count, lat_count, me_ref, ids_ref, near_ref, far_ref,
                   root_ref, centre_ref, around_ref, table_ref,
                   natural, all_ids, places_of, sems):
    half = lat_count // 2
    count = lon_count * half
    rows = (near_ref.shape[1] - SUBLANES) // 2
    strips, deep, tall = window_shape(slots, rows)
    column_count = 2 * lon_count
    parts = (near_ref, far_ref)
    copies = [
        pltpu.make_async_copy(
            parts[p].at[:, pl.ds(2 * rows, 1), :], all_ids.at[p], sems.at[p]
        )
        for p in range(2)
    ]
    for copy in copies:
        copy.start()
    natural[...] = jnp.zeros_like(natural)

    def load(lat, column):
        inside = (lat >= 0) & (lat < lat_count) & (column >= 0) & (column < column_count)
        lat_safe = jnp.clip(lat, 0, lat_count - 1)
        column_safe = jnp.clip(column, 0, column_count - 1)
        lon_xor = (column_safe >> 1) ^ me_ref[0]
        lat_xor = lat_safe ^ me_ref[1]
        place = lon_xor * half + (lat_xor >> 1)
        start = pl.multiple_of((column_safe & 1) * rows, SUBLANES)
        near = near_ref[place, pl.ds(start, rows), :]
        far = far_ref[place, pl.ds(start, rows), :]
        here = jnp.where((lat_xor & 1) == 0, near, far)
        return here * jnp.where(inside, 1.0, 0.0)

    lane = lax.broadcasted_iota(jnp.int32, (rows, LANES), 1)
    places = window_places(me_ref, ids_ref, slots, lon_count, lat_count)
    for w, (lat, column) in enumerate(places):
        blocks = [load(lat + down, column + right) for down, right in NEIGHBOURS]
        put_window(natural, w * tall, rows, blocks, lane)

    for copy in copies:
        copy.wait()

    def one_device(n, carry):
        for p in range(2):
            for s in range(slots):
                block = all_ids[p, n, 0, s].astype(jnp.int32)
                places_of[block] = (p * count + n) * slots + s
        return carry

    lax.fori_loop(0, count, one_device, 0)
    for w, (lat, column) in enumerate(places):
        for n, (down, right) in enumerate(NEIGHBOURS):
            lat_safe = jnp.clip(lat + down, 0, lat_count - 1)
            column_safe = jnp.clip(column + right, 0, column_count - 1)
            block = ((column_safe >> 1) * lat_count + lat_safe) * 2 + (column_safe & 1)
            table_ref[w * len(NEIGHBOURS) + n] = places_of[block]

    scale = chebyshev_sum(STEPS)[1]

    turn(natural, deep, around_ref)

    def roots(i, n):
        scaled = around_ref[vector(i, n), :]
        return [(root_ref, jnp.sqrt(scaled)), (around_ref, scale * scaled)]

    in_batches(deep, roots)
    root = Around(root_ref, deep)

    def centres(i, n):
        return [(centre_ref, 2.0 - scale * root.here(i, n) * root.total(i, n))]

    in_batches(deep, centres)


def surface_weights(near, far, me, block_ids, rows, lon_count, lat_count):
    slots = block_ids.shape[0]
    assert near.shape[-1] == LANES
    strips, deep, tall = window_shape(slots, rows)
    shape = jax.ShapeDtypeStruct((deep * WIDTH, LANES), jnp.float32)
    return pl.pallas_call(
        functools.partial(weights_kernel, slots, lon_count, lat_count),
        in_specs=[SMEM, SMEM, VMEM, VMEM],
        out_specs=[VMEM, VMEM, VMEM, SMEM],
        out_shape=[
            shape,
            shape,
            shape,
            jax.ShapeDtypeStruct(((slots + 2) * len(NEIGHBOURS),), jnp.int32),
        ],
        scratch_shapes=[
            pltpu.VMEM((2, LANES * deep, LANES), jnp.float32),
            pltpu.SMEM((2, near.shape[0], 1, LANES), jnp.float32),
            pltpu.SMEM((2 * lon_count * lat_count + 1,), jnp.int32),
            pltpu.SemaphoreType.DMA((2,)),
        ],
        compiler_params=params(WINDOW_VMEM),
        cost_estimate=pl.CostEstimate(
            flops=0, bytes_accessed=8 * MIB, transcendentals=0
        ),
        name="surface_weights",
    )(me, block_ids, near, far)


def solve_kernel(block_total, ids_ref, table_ref, coefs_ref, root_ref, centre_ref, around_ref,
                 levels_ref, bottom_ref, first_column_ref, last_column_ref, near_ref, far_ref,
                 corrected_ref, height_ref, sensitivity_ref,
                 natural, source, even, odd, extra, column, in_sems, out_sems):
    slots, comps, depth, rows, cols = column.shape
    strips, deep, tall = window_shape(slots, rows)

    middle = first_column_ref.shape[0]
    copies_in = [
        pltpu.make_async_copy(first_column_ref, column.at[pl.ds(0, middle)], in_sems.at[0]),
        pltpu.make_async_copy(
            last_column_ref, column.at[pl.ds(middle, slots - middle)], in_sems.at[1]
        ),
    ]
    for copy in copies_in:
        copy.start()

    count = near_ref.shape[0]

    def load(place):
        inner = place & (count - 1)
        return jnp.where(place < count, near_ref[inner], far_ref[inner])

    lane = lax.broadcasted_iota(jnp.int32, (rows, LANES), 1)
    for w in range(slots + 2):
        places = [table_ref[w * len(NEIGHBOURS) + n] for n in range(len(NEIGHBOURS))]
        put_window(natural, w * tall, rows, [load(place) for place in places], lane)

    coefs, step_scale = chebyshev_sum(STEPS)

    turn(natural, deep, source)

    def starts(i, n):
        at = vector(i, n)
        root = root_ref[at, :]
        value = jnp.where(root > 0.0, root * source[at, :], 0.0)
        return [(source, value), (even, coefs[STEPS - 1] * value), (odd, jnp.zeros_like(value))]

    in_batches(deep, starts)

    def apply(current, target, coef, gain):
        values = Around(current, deep)

        def work(i, n):
            at = vector(i, n)
            pushed = centre_ref[at, :] * values.here(i, n) + around_ref[at, :] * values.total(i, n)
            if gain != 1.0:
                pushed = gain * pushed
            return [(target, (coef * source[at, :] - target[at, :]) + pushed)]

        in_batches(deep, work)

    def two_steps(pair, carry):
        apply(even, odd, coefs_ref[2 * pair + 1], 1.0)
        apply(odd, even, coefs_ref[2 * pair + 2], 1.0)
        return carry

    lax.fori_loop(0, (STEPS - 2) // 2, two_steps, 0)
    apply(even, odd, coefs[0], 0.5)

    def heights(i, n):
        at = vector(i, n)
        root = root_ref[at, :]
        return [(extra, jnp.where(root > 0.0, odd[at, :] / root, 0.0))]

    in_batches(deep, heights)
    height = Around(extra, deep)
    root = Around(root_ref, deep)

    def differences(i, n):
        here = height.here(i, n)
        energy = None
        east_step = height.east(i, n) - here
        for step, weight in (
            (east_step, root.east(i, n)),
            (here - height.west(i, n), root.west(i, n)),
            (height.south(i, n) - here, root.south(i, n)),
            (here - height.north(i, n), root.north(i, n)),
        ):
            part = weight * step * step
            energy = part if energy is None else energy + part
        energy = root.here(i, n) * energy
        scaled = around_ref[vector(i, n), :] * (1.0 / step_scale)
        return [(even, east_step), (source, 0.25 * energy / jnp.maximum(scaled, 0.25))]

    in_batches(deep, differences)

    def cut(tile, w, shift=0):
        return natural[tile, pl.ds(w * tall + STEPS + shift, rows), :]

    def copy_out(b, c):
        return pltpu.make_async_copy(column.at[b, c], corrected_ref.at[b, c], out_sems.at[b, c])

    def correct(b, c, step):
        levels = levels_ref[b] * jnp.where(ids_ref[b] < block_total, 1, 0)
        push = pressure_gain * step
        lowest = bottom_ref[b, c] - push

        late = []
        for low in range(0, depth, CHUNK):
            batch = []
            for k in range(low, min(low + CHUNK, depth)):
                value = jnp.where(levels == k + 1, lowest, column[b, c, k] - push)
                batch.append((k, jnp.where(levels > k, value, 0.0)))
            for k, value in late:
                column[b, c, k] = value
            late = batch
        for k, value in late:
            column[b, c, k] = value
        copy_out(b, c).start()

    turn_back(even, natural, 0, deep)
    for copy in copies_in:
        copy.wait()

    def correct_east(b, carry):
        correct(b, 0, cut(0, b))
        return carry

    def correct_north(b, carry):
        correct(b, 1, cut(1, b, 1) - cut(1, b))
        return carry

    lax.fori_loop(0, slots, correct_east, 0)
    turn_back(extra, natural, 1, deep)
    lax.fori_loop(0, slots, correct_north, 0)
    turn_back(source, natural, 0, deep)
    for h in range(2):
        height_ref[:, h * LANES:(h + 1) * LANES] = cut(1, slots + h)
        sensitivity_ref[:, h * LANES:(h + 1) * LANES] = cut(0, slots + h)

    for b in range(slots):
        for c in range(comps):
            copy_out(b, c).wait()


def surface_solve(near, far, weights, block_ids, level_count, bottom, columns, block_total):
    root, centre, around, table = weights
    comps, depth, rows, cols = columns[0].shape[1:]
    slots = level_count.shape[0]
    assert comps == 2
    full = (slots, comps, depth, rows, cols)
    deep = window_shape(slots, rows)[1]
    turned = pltpu.VMEM(root.shape, jnp.float32)
    coefs = jnp.array(chebyshev_sum(STEPS)[0][::-1], jnp.float32)
    return pl.pallas_call(
        functools.partial(solve_kernel, block_total),
        in_specs=[SMEM, SMEM, SMEM] + [VMEM] * 5 + [HBM] * 2 + [VMEM] * 2,
        out_specs=[HBM, VMEM, VMEM],
        out_shape=[
            jax.ShapeDtypeStruct(full, jnp.float32),
            jax.ShapeDtypeStruct((rows, 2 * cols), jnp.float32),
            jax.ShapeDtypeStruct((rows, 2 * cols), jnp.float32),
        ],
        scratch_shapes=[
            pltpu.VMEM((2, LANES * deep, LANES), jnp.float32),
            turned,
            turned,
            turned,
            turned,
            pltpu.VMEM(full, jnp.float32),
            pltpu.SemaphoreType.DMA((2,)),
            pltpu.SemaphoreType.DMA((slots, comps)),
        ],
        compiler_params=params(SOLVE_VMEM),
        cost_estimate=pl.CostEstimate(
            flops=9 * STEPS * root.size, bytes_accessed=16 * root.size, transcendentals=0
        ),
        name="surface_solve",
    )(block_ids, table, coefs, root, centre, around, level_count, bottom, *columns, near, far)


def stack_kernel(parts, *refs):
    out_ref = refs[-1]
    for p in range(parts):
        out_ref[p] = refs[p][...]


def stack_after(parts, *tokens):
    return pl.pallas_call(
        functools.partial(stack_kernel, len(parts)),
        in_specs=[VMEM] * len(parts) + [ANYWHERE] * len(tokens),
        out_specs=VMEM,
        out_shape=jax.ShapeDtypeStruct((len(parts),) + parts[0].shape, jnp.float32),
        compiler_params=params(WINDOW_VMEM),
        name="stack_after",
    )(*parts, *tokens)


FIRST_SLOTS = 1


def swap(values, axis, mask):
    count = lax.axis_size(axis)
    return lax.ppermute(values, axis, [(i, i ^ mask) for i in range(count)])


def per_device(adjoint_vel, velocity, drag_coef, level_count, block_ids, bathymetry, land_mask):
    slots = block_ids.shape[0]
    rows, cols = drag_coef.shape[1:]
    lon_count = lax.axis_size("gx")
    lat_count = lax.axis_size("gy")
    half = lat_count // 2
    block_total = 2 * lon_count * lat_count
    me = jnp.stack([lax.axis_index("gx"), lax.axis_index("gy")]).astype(jnp.int32)

    depths = depth_payload(bathymetry, land_mask, block_ids)
    depth_parts = [depths] + [swap(depths, "gy", 2 * m) for m in range(1, half)]
    forcing = column_forcing(adjoint_vel, level_count)

    parts = [forcing] + [swap(forcing, "gy", 2 * m) for m in range(1, half)]
    near_depths = stack_after(depth_parts, forcing)
    near_depths = [near_depths] + [swap(near_depths, "gx", m) for m in range(1, lon_count)]
    columns = (adjoint_vel, velocity, drag_coef, level_count, block_ids)
    first_column, *first_rest = column_mixing(*columns, forcing, block_total, 0, FIRST_SLOTS)
    line = stack_after(parts, first_rest[0])

    near = [line] + [swap(line, "gx", m) for m in range(1, lon_count)]
    near_depths = stack_after(near_depths, line)
    near_depths = near_depths.reshape((lon_count * half,) + depths.shape)
    far_depths = swap(near_depths, "gy", 1)
    last_column, bottom, drag_gradient = column_mixing(
        *columns, line, block_total, FIRST_SLOTS, slots, first_rest
    )
    weights = surface_weights(
        near_depths, far_depths, me, block_ids, rows, lon_count, lat_count
    )

    near = stack_after(near, bottom, weights[0])
    far = swap(near, "gy", 1)

    corrected, height, sensitivity = surface_solve(
        near.reshape((-1, rows, cols)), far.reshape((-1, rows, cols)), weights,
        block_ids, level_count, bottom, (first_column, last_column), block_total,
    )
    return corrected, drag_gradient, height, sensitivity


def solution(mesh):
    in_specs = (
        P(("gx", "gy"), None, None, None, None),
        P(("gx", "gy"), None, None, None, None),
        P(("gx", "gy"), None, None),
        P(("gx", "gy"), None, None),
        P(("gx", "gy")),
        P("gy", "gx"),
        P("gy", "gx"),
    )
    out_specs = (
        P(("gx", "gy"), None, None, None, None),
        P(("gx", "gy"), None, None),
        P("gy", "gx"),
        P("gy", "gx"),
    )
    return jax.shard_map(
        per_device, mesh=mesh, in_specs=in_specs, out_specs=out_specs, check_vma=False
    )
```

```python
import functools

import jax
import jax.numpy as jnp
import numpy as np
from jax import lax
from jax.experimental import pallas as pl
from jax.experimental.pallas import tpu as pltpu
from jax.sharding import PartitionSpec as P

STEPS = 32

mix_rate = 0.25
drag_step = 0.5
force_scale = 0.25
pressure_gain = 0.5
surface_shift = 1.0 / 64.0
speed_floor = 0.01

LANES = 128
SUBLANES = 8
MIB = 1024 * 1024
FIRST_VMEM = 61 * MIB
MIXING_VMEM = 52 * MIB
SOLVE_VMEM = 50 * MIB
WINDOW_VMEM = 16 * MIB


def chebyshev_sum(total_steps):
    highest = surface_shift + 8.0
    centre = 0.5 * (highest + surface_shift)
    radius = 0.5 * (highest - surface_shift)
    sigma_ratio = centre / radius

    def operate(series):
        shifted = np.zeros_like(series)
        shifted[1] += series[0]
        for k in range(1, len(series) - 1):
            shifted[k + 1] += 0.5 * series[k]
            shifted[k - 1] += 0.5 * series[k]
        return centre * series - radius * shifted

    height = np.zeros(total_steps + 2)
    residual = np.zeros(total_steps + 2)
    residual[0] = 1.0
    direction = residual / centre
    ratio_prev = 1.0 / sigma_ratio
    for _ in range(total_steps):
        height = height + direction
        residual = residual - operate(direction)
        ratio_next = 1.0 / (2.0 * sigma_ratio - ratio_prev)
        direction = ratio_next * ratio_prev * direction + 2.0 * ratio_next / radius * residual
        ratio_prev = ratio_next
    return [float(c) for c in height[:total_steps]], 2.0 / radius


def params(limit):
    return pltpu.CompilerParams(vmem_limit_bytes=limit)


SMEM = pl.BlockSpec(memory_space=pltpu.SMEM)
VMEM = pl.BlockSpec(memory_space=pltpu.VMEM)
ANYWHERE = pl.BlockSpec(memory_space=pl.ANY)
HBM = pl.BlockSpec(memory_space=pltpu.HBM)


def forcing_kernel(levels_ref, adjoint_ref, out_ref, levels_held, held, level_sem, sems):
    slots, comps, depth, rows, cols = held.shape
    level_copy = pltpu.make_async_copy(levels_ref, levels_held, level_sem)
    level_copy.start()

    def copy_in(b, c):
        return pltpu.make_async_copy(adjoint_ref.at[b, c], held.at[b, c], sems.at[b, c])

    for b in range(slots):
        for c in range(comps):
            copy_in(b, c).start()
    level_copy.wait()

    def one_slot(b, carry):
        levels = levels_held[b]
        totals = [jnp.zeros((rows, cols), jnp.float32) for _ in range(4)]
        for c in range(comps):
            copy_in(b, c).wait()
            for k in range(depth):
                totals[k % 4] = totals[k % 4] + jnp.where(levels > k, held[b, c, k], 0.0)
        out_ref[b] = force_scale * ((totals[0] + totals[1]) + (totals[2] + totals[3]))
        return carry

    lax.fori_loop(0, slots, one_slot, 0)


def column_forcing(adjoint_vel, level_count):
    slots, comps, depth, rows, cols = adjoint_vel.shape
    return pl.pallas_call(
        forcing_kernel,
        in_specs=[HBM, HBM],
        out_specs=VMEM,
        out_shape=pltpu.VMEM((slots, rows, cols), jnp.float32),
        scratch_shapes=[
            pltpu.VMEM(level_count.shape, jnp.int32),
            pltpu.VMEM(adjoint_vel.shape, jnp.float32),
            pltpu.SemaphoreType.DMA,
            pltpu.SemaphoreType.DMA((slots, comps)),
        ],
        compiler_params=params(FIRST_VMEM),
        cost_estimate=pl.CostEstimate(
            flops=2 * adjoint_vel.size, bytes_accessed=4 * adjoint_vel.size, transcendentals=0
        ),
        name="column_forcing",
    )(level_count, adjoint_vel)


CHUNK = 8


def mixing_kernel(block_total, first, earlier, ids_ref, levels_ref, drag_ref, adjoint_ref,
                  velocity_ref, after_ref, *rest):
    if earlier:
        for target, ref in zip(rest[3:5], rest[:2]):
            target[0:first] = ref[...]
        rest = rest[2:]
    column_ref, bottom_ref, gradient_ref, adjoint, velocity, column, in_sems, out_sems = rest
    slots, comps, depth, rows, cols = adjoint.shape
    group = 16
    parts = rows // group

    def copies_in(b, index):
        span = pl.ds(pl.multiple_of(index * group, group), group)
        return [
            pltpu.make_async_copy(
                source.at[first + b, :, :, span], target.at[b, :, :, span],
                in_sems.at[n, b, index],
            )
            for n, (source, target) in enumerate(
                ((adjoint_ref, adjoint), (velocity_ref, velocity))
            )
        ]

    def copy_out(b, index):
        span = pl.ds(pl.multiple_of(index * group, group), group)
        return pltpu.make_async_copy(
            column.at[b, :, :, span], column_ref.at[b, :, :, span], out_sems.at[b, index]
        )

    for b in range(slots):
        for index in range(parts):
            for copy in copies_in(b, index):
                copy.start()

    def one_group(b, index):
        flag = jnp.where(ids_ref[first + b] < block_total, 1.0, 0.0)
        span = pl.ds(pl.multiple_of(index * group, group), group)
        levels = levels_ref[first + b, span, :]
        zero = jnp.zeros(levels.shape, jnp.float32)
        x = [zero, zero]
        once = [zero, zero]
        first_flux = [zero, zero]
        second_flux = [zero, zero]
        flow = [zero, zero]
        field = [zero, zero]
        wets = []
        rates = []
        for low in range(0, depth + 2, CHUNK):
            here = range(low, min(low + CHUNK, depth + 2))
            loaded = {}
            for k in here:
                if k < depth:
                    for c in range(2):
                        loaded[k, c] = (adjoint[b, c, k, span, :], velocity[b, c, k, span, :])
            done = []
            for k in here:
                if k < depth:
                    wets.append(levels > k)
                    rates.append(jnp.where(wets[k], mix_rate, 0.0))
                for c in range(2):
                    fresh_once = None
                    if k < depth:
                        fresh = loaded[k, c][0]
                        flow[c] = jnp.where(
                            wets[k], loaded[k, c][1].astype(jnp.float32), flow[c]
                        )
                        if 1 <= k:
                            flux = (fresh - x[c]) * rates[k]
                            fresh_once = x[c] + (flux - first_flux[c])
                            first_flux[c] = flux
                        x[c] = fresh
                    elif k == depth:
                        fresh_once = x[c] - first_flux[c]
                    if 2 <= k:
                        if k <= depth:
                            flux = (fresh_once - once[c]) * rates[k - 1]
                            twice = once[c] + (flux - second_flux[c])
                            second_flux[c] = flux
                        else:
                            twice = once[c] - second_flux[c]
                        done.append((c, k - 2, twice))
                        field[c] = jnp.where(wets[k - 2], twice, field[c])
                    if fresh_once is not None:
                        once[c] = fresh_once
            for c, k, value in done:
                column[b, c, k, span, :] = value
        speed = jnp.sqrt(flow[0] * flow[0] + flow[1] * flow[1] + speed_floor)
        along = flow[0] * field[0] + flow[1] * field[1]
        ratio = along / speed
        drag = drag_ref[first + b, span, :]
        for c in range(2):
            bottom_ref[first + b, c, span, :] = field[c] - drag_step * drag * (
                speed * field[c] + flow[c] * ratio
            )
        gradient_ref[first + b, span, :] = -drag_step * speed * along * flag

    def one(step, carry):
        b = lax.div(step, parts)
        index = lax.rem(step, parts)

        for copy in copies_in(b, index):
            copy.wait()
        one_group(b, index)
        copy_out(b, index).start()
        return carry

    lax.fori_loop(0, slots * parts, one, 0)
    for b in range(slots):
        for index in range(parts):
            copy_out(b, index).wait()


def column_mixing(adjoint_vel, velocity, drag_coef, level_count, block_ids, after, block_total,
                  first, last, earlier=()):
    comps, depth, rows, cols = adjoint_vel.shape[1:]
    slots = last - first
    part = (slots, comps, depth, rows, cols)
    size = slots * comps * depth * rows * cols
    return pl.pallas_call(
        functools.partial(mixing_kernel, block_total, first, len(earlier)),
        in_specs=[SMEM, VMEM, VMEM, HBM, HBM, ANYWHERE] + [VMEM] * len(earlier),
        out_specs=[HBM, VMEM, VMEM],
        out_shape=[
            pltpu.HBM(part, jnp.float32),
            pltpu.VMEM((last, comps, rows, cols), jnp.float32),
            (pltpu.HBM if last == level_count.shape[0] else pltpu.VMEM)((last, rows, cols), jnp.float32),
        ],
        scratch_shapes=[
            pltpu.VMEM(part, adjoint_vel.dtype),
            pltpu.VMEM(part, velocity.dtype),
            pltpu.VMEM(part, jnp.float32),
            pltpu.SemaphoreType.DMA((2, slots, rows // 16)),
            pltpu.SemaphoreType.DMA((slots, rows // 16)),
        ],
        compiler_params=params(MIXING_VMEM),
        cost_estimate=pl.CostEstimate(
            flops=14 * size, bytes_accessed=10 * size, transcendentals=0
        ),
        name="column_mixing",
    )(block_ids, level_count, drag_coef, adjoint_vel, velocity, after, *earlier)


PAD = SUBLANES
BATCH = 2
WIDTH = LANES + 2 * STEPS
PITCH = WIDTH + 2 * PAD
NEIGHBOURS = [(down, right) for down in (-1, 0, 1) for right in (0, 1, -1)]


def window_shape(slots, rows):
    strips = LANES // (slots + 2)
    deep = pl.cdiv(rows + 2 * STEPS, strips)
    return strips, deep, strips * deep


def log2(count):
    bits = count.bit_length() - 1
    assert 1 << bits == count
    return bits


def window_places(me_ref, ids_ref, slots, lon_count, lat_count):
    places = []
    for w in range(slots + 2):
        if w < slots:
            block = jnp.where(ids_ref[w] < 2 * lon_count * lat_count, ids_ref[w], 0)
        else:
            block = (me_ref[0] * lat_count + me_ref[1]) * 2 + (w - slots)
        pair = block >> 1
        column = (pair >> log2(lat_count)) * 2 + (block & 1)
        places.append((pair & (lat_count - 1), column))
    return places


def put_window(natural, base, rows, blocks, lane):
    for i in range(3):
        here, east, west = blocks[3 * i:3 * i + 3]
        sides = jnp.where(lane < STEPS, east, jnp.where(lane >= LANES - STEPS, west, 0.0))
        start = base + i * rows
        natural[0, start:start + rows, :] = here
        natural[1, start:start + rows, :] = sides


def turn(natural, deep, put):
    for i in range(deep):
        put(i, STEPS, natural[0, pl.ds(i, LANES, stride=deep), :].T)
        sides = natural[1, pl.ds(i, LANES, stride=deep), :].T
        put(i, STEPS + LANES, sides[:STEPS])
        put(i, 0, sides[LANES - STEPS:])


def rows_at(ref, start, shift=0):
    return ref[pl.ds(start + shift, SUBLANES), :]


def in_batches(chunks, work):
    late = []
    for start in range(0, len(chunks), BATCH):
        batch = [item for chunk in chunks[start:start + BATCH] for item in work(chunk)]
        for ref, a, value in late:
            ref[pl.ds(a, SUBLANES), :] = value
        late = batch
    for ref, a, value in late:
        ref[pl.ds(a, SUBLANES), :] = value


def strip_rows(ref, chunk, deep):
    at = [i * PITCH + PAD + chunk * SUBLANES for i in range(deep)]
    here = [rows_at(ref, a) for a in at]
    above = [pltpu.roll(here[-1], 1, 1)] + here[:-1]
    below = here[1:] + [pltpu.roll(here[0], LANES - 1, 1)]
    return here, above, below, at


def depth_kernel(ids_ref, bathymetry_ref, mask_ref, out_ref, ids, bathymetry, mask, sems):
    copies = [
        pltpu.make_async_copy(ids_ref, ids, sems.at[0]),
        pltpu.make_async_copy(bathymetry_ref, bathymetry, sems.at[1]),
        pltpu.make_async_copy(mask_ref, mask, sems.at[2]),
    ]
    for copy in copies:
        copy.start()
    for copy in copies:
        copy.wait()
    rows = bathymetry.shape[0]
    scaled = bathymetry[...] * mask[...].astype(jnp.float32)
    out_ref[0:rows, :] = scaled[:, :LANES]
    out_ref[rows:2 * rows, :] = scaled[:, LANES:]
    lane = lax.broadcasted_iota(jnp.int32, (SUBLANES, LANES), 1)
    listed = jnp.zeros((SUBLANES, LANES), jnp.int32)
    for s in range(ids.shape[0]):
        listed = jnp.where(lane == s, ids[s], listed)
    out_ref[2 * rows:2 * rows + SUBLANES, :] = listed.astype(jnp.float32)


def depth_payload(bathymetry, land_mask, block_ids):
    rows = bathymetry.shape[0]
    return pl.pallas_call(
        depth_kernel,
        in_specs=[HBM, HBM, HBM],
        out_specs=VMEM,
        out_shape=pltpu.VMEM((2 * rows + SUBLANES, LANES), jnp.float32),
        scratch_shapes=[
            pltpu.SMEM(block_ids.shape, jnp.int32),
            pltpu.VMEM(bathymetry.shape, jnp.float32),
            pltpu.VMEM(land_mask.shape, jnp.int32),
            pltpu.SemaphoreType.DMA((3,)),
        ],
        compiler_params=params(FIRST_VMEM),
        name="depth_payload",
    )(block_ids, bathymetry, land_mask)


def weights_kernel(slots, lon_count, lat_count, me_ref, ids_ref, near_ref, far_ref,
                   root_ref, centre_ref, around_ref, table_ref,
                   natural, all_ids, places_of, sems):
    half = lat_count // 2
    count = lon_count * half
    rows = (near_ref.shape[1] - SUBLANES) // 2
    strips, deep, tall = window_shape(slots, rows)
    column_count = 2 * lon_count
    parts = (near_ref, far_ref)
    copies = [
        pltpu.make_async_copy(
            parts[p].at[:, pl.ds(2 * rows, 1), :], all_ids.at[p], sems.at[p]
        )
        for p in range(2)
    ]
    for copy in copies:
        copy.start()
    natural[...] = jnp.zeros_like(natural)

    def load(lat, column):
        inside = (lat >= 0) & (lat < lat_count) & (column >= 0) & (column < column_count)
        lat_safe = jnp.clip(lat, 0, lat_count - 1)
        column_safe = jnp.clip(column, 0, column_count - 1)
        lon_xor = (column_safe >> 1) ^ me_ref[0]
        lat_xor = lat_safe ^ me_ref[1]
        place = lon_xor * half + (lat_xor >> 1)
        start = pl.multiple_of((column_safe & 1) * rows, SUBLANES)
        near = near_ref[place, pl.ds(start, rows), :]
        far = far_ref[place, pl.ds(start, rows), :]
        here = jnp.where((lat_xor & 1) == 0, near, far)
        return here * jnp.where(inside, 1.0, 0.0)

    lane = lax.broadcasted_iota(jnp.int32, (rows, LANES), 1)
    places = window_places(me_ref, ids_ref, slots, lon_count, lat_count)
    for w, (lat, column) in enumerate(places):
        blocks = [load(lat + down, column + right) for down, right in NEIGHBOURS]
        put_window(natural, w * tall, rows, blocks, lane)

    for copy in copies:
        copy.wait()

    def one_device(n, carry):
        for p in range(2):
            for s in range(slots):
                block = all_ids[p, n, 0, s].astype(jnp.int32)
                places_of[block] = (p * count + n) * slots + s
        return carry

    lax.fori_loop(0, count, one_device, 0)
    for w, (lat, column) in enumerate(places):
        for n, (down, right) in enumerate(NEIGHBOURS):
            lat_safe = jnp.clip(lat + down, 0, lat_count - 1)
            column_safe = jnp.clip(column + right, 0, column_count - 1)
            block = ((column_safe >> 1) * lat_count + lat_safe) * 2 + (column_safe & 1)
            table_ref[w * len(NEIGHBOURS) + n] = places_of[block]

    scale = chebyshev_sum(STEPS)[1]

    def put(i, x, values):
        start = i * PITCH + PAD + x
        root_ref[start:start + values.shape[0], :] = jnp.sqrt(values)
        around_ref[start:start + values.shape[0], :] = scale * values

    turn(natural, deep, put)
    zeros = jnp.zeros((PAD, LANES), jnp.float32)
    for i in range(deep):
        root_ref[i * PITCH:i * PITCH + PAD, :] = zeros
        root_ref[(i + 1) * PITCH - PAD:(i + 1) * PITCH, :] = zeros

    def work(chunk):
        here, above, below, at = strip_rows(root_ref, chunk, deep)
        out = []
        for i, a in enumerate(at):
            others = (rows_at(root_ref, a, 1) + rows_at(root_ref, a, -1)) + (above[i] + below[i])
            out.append((centre_ref, a, 2.0 - scale * here[i] * others))
        return out

    in_batches(range(WIDTH // SUBLANES), work)


def surface_weights(near, far, me, block_ids, rows, lon_count, lat_count):
    slots = block_ids.shape[0]
    assert near.shape[-1] == LANES
    strips, deep, tall = window_shape(slots, rows)
    shape = jax.ShapeDtypeStruct((deep * PITCH, LANES), jnp.float32)
    return pl.pallas_call(
        functools.partial(weights_kernel, slots, lon_count, lat_count),
        in_specs=[SMEM, SMEM, VMEM, VMEM],
        out_specs=[VMEM, VMEM, VMEM, SMEM],
        out_shape=[
            shape,
            shape,
            shape,
            jax.ShapeDtypeStruct(((slots + 2) * len(NEIGHBOURS),), jnp.int32),
        ],
        scratch_shapes=[
            pltpu.VMEM((2, LANES * deep, LANES), jnp.float32),
            pltpu.SMEM((2, near.shape[0], 1, LANES), jnp.float32),
            pltpu.SMEM((2 * lon_count * lat_count + 1,), jnp.int32),
            pltpu.SemaphoreType.DMA((2,)),
        ],
        compiler_params=params(WINDOW_VMEM),
        cost_estimate=pl.CostEstimate(
            flops=0, bytes_accessed=8 * MIB, transcendentals=0
        ),
        name="surface_weights",
    )(me, block_ids, near, far)


def solve_kernel(block_total, ids_ref, table_ref, coefs_ref, root_ref, centre_ref, around_ref,
                 levels_ref, bottom_ref, first_column_ref, last_column_ref, near_ref, far_ref,
                 corrected_ref, height_ref, sensitivity_ref,
                 natural, source, even, odd, extra, column, in_sems, out_sems):
    slots, comps, depth, rows, cols = column.shape
    strips, deep, tall = window_shape(slots, rows)

    middle = first_column_ref.shape[0]
    copies_in = [
        pltpu.make_async_copy(first_column_ref, column.at[pl.ds(0, middle)], in_sems.at[0]),
        pltpu.make_async_copy(
            last_column_ref, column.at[pl.ds(middle, slots - middle)], in_sems.at[1]
        ),
    ]
    for copy in copies_in:
        copy.start()

    count = near_ref.shape[0]

    def load(place):
        inner = place & (count - 1)
        return jnp.where(place < count, near_ref[inner], far_ref[inner])

    lane = lax.broadcasted_iota(jnp.int32, (rows, LANES), 1)
    for w in range(slots + 2):
        places = [table_ref[w * len(NEIGHBOURS) + n] for n in range(len(NEIGHBOURS))]
        put_window(natural, w * tall, rows, [load(place) for place in places], lane)

    coefs, step_scale = chebyshev_sum(STEPS)

    def put(i, x, values):
        start = i * PITCH + PAD + x
        stop = start + values.shape[0]
        root = root_ref[start:stop, :]
        values = jnp.where(root > 0.0, root * values, 0.0)
        source[start:stop, :] = values
        even[start:stop, :] = coefs[STEPS - 1] * values
        odd[start:stop, :] = jnp.zeros_like(values)

    zeros = jnp.zeros((PAD, LANES), jnp.float32)
    for ref in (even, odd):
        for i in range(deep):
            ref[i * PITCH:i * PITCH + PAD, :] = zeros
            ref[(i + 1) * PITCH - PAD:(i + 1) * PITCH, :] = zeros
    turn(natural, deep, put)

    chunks = WIDTH // SUBLANES

    def apply(current, target, coef, gain, m):
        def work(chunk):
            here, above, below, at = strip_rows(current, chunk, deep)
            out = []
            for i, a in enumerate(at):
                others = (rows_at(current, a, 1) + rows_at(current, a, -1)) + (
                    above[i] + below[i]
                )
                pushed = rows_at(centre_ref, a) * here[i] + rows_at(around_ref, a) * others
                if gain != 1.0:
                    pushed = gain * pushed
                kept = coef * rows_at(source, a) - rows_at(target, a)
                out.append((target, a, kept + pushed))
            return out

        in_batches(range(m // SUBLANES, chunks - m // SUBLANES), work)

    runs = []
    for m in range(1, STEPS - 1, 2):
        if runs and runs[-1][0] // SUBLANES == m // SUBLANES:
            runs[-1][1] += 1
        else:
            runs.append([m, 1])
    for first, pairs in runs:
        def two_steps(pair, carry, first=first):
            m = first + 2 * pair
            apply(even, odd, coefs_ref[m], 1.0, first)
            apply(odd, even, coefs_ref[m + 1], 1.0, first)
            return carry

        lax.fori_loop(0, pairs, two_steps, 0)
    apply(even, odd, coefs[0], 0.5, STEPS - 1)

    low = STEPS // SUBLANES - 1

    def one_height(chunk):
        out = []
        for i in range(deep):
            a = i * PITCH + PAD + chunk * SUBLANES
            root = rows_at(root_ref, a)
            out.append((extra, a, jnp.where(root > 0.0, rows_at(odd, a) / root, 0.0)))
        return out

    in_batches(range(low, chunks - low), one_height)

    def differences(chunk):
        here, above, below, at = strip_rows(extra, chunk, deep)
        root, root_above, root_below, _ = strip_rows(root_ref, chunk, deep)
        out = []
        for i, a in enumerate(at):
            east_step = rows_at(extra, a, 1) - here[i]
            west_step = here[i] - rows_at(extra, a, -1)
            south_step = below[i] - here[i]
            north_step = here[i] - above[i]
            energy = root[i] * (
                (rows_at(root_ref, a, 1) * east_step * east_step
                 + rows_at(root_ref, a, -1) * west_step * west_step)
                + (root_below[i] * south_step * south_step
                   + root_above[i] * north_step * north_step)
            )
            scaled = rows_at(around_ref, a) * (1.0 / step_scale)
            out.append((even, a, east_step))
            out.append((source, a, 0.25 * energy / jnp.maximum(scaled, 0.25)))
        return out

    in_batches(range(low + 1, chunks - low - 1), differences)

    def turn_back(ref, tile):
        for i in range(deep):
            start = i * PITCH + PAD + STEPS
            natural[tile, pl.ds(i, LANES, stride=deep), :] = ref[start:start + LANES, :].T

    def cut(tile, w, shift=0):
        return natural[tile, pl.ds(w * tall + STEPS + shift, rows), :]

    def copy_out(b, c):
        return pltpu.make_async_copy(column.at[b, c], corrected_ref.at[b, c], out_sems.at[b, c])

    def correct(b, c, step):
        levels = levels_ref[b] * jnp.where(ids_ref[b] < block_total, 1, 0)
        push = pressure_gain * step
        lowest = bottom_ref[b, c] - push

        late = []
        for low in range(0, depth, CHUNK):
            batch = []
            for k in range(low, min(low + CHUNK, depth)):
                value = jnp.where(levels == k + 1, lowest, column[b, c, k] - push)
                batch.append((k, jnp.where(levels > k, value, 0.0)))
            for k, value in late:
                column[b, c, k] = value
            late = batch
        for k, value in late:
            column[b, c, k] = value
        copy_out(b, c).start()

    turn_back(even, 0)
    for copy in copies_in:
        copy.wait()

    def correct_east(b, carry):
        correct(b, 0, cut(0, b))
        return carry

    def correct_north(b, carry):
        correct(b, 1, cut(1, b, 1) - cut(1, b))
        return carry

    lax.fori_loop(0, slots, correct_east, 0)
    turn_back(extra, 1)
    lax.fori_loop(0, slots, correct_north, 0)
    turn_back(source, 0)
    for h in range(2):
        height_ref[:, h * LANES:(h + 1) * LANES] = cut(1, slots + h)
        sensitivity_ref[:, h * LANES:(h + 1) * LANES] = cut(0, slots + h)

    for b in range(slots):
        for c in range(comps):
            copy_out(b, c).wait()


def surface_solve(near, far, weights, block_ids, level_count, bottom, columns, block_total):
    root, centre, around, table = weights
    comps, depth, rows, cols = columns[0].shape[1:]
    slots = level_count.shape[0]
    assert comps == 2
    full = (slots, comps, depth, rows, cols)
    deep = window_shape(slots, rows)[1]
    turned = pltpu.VMEM(root.shape, jnp.float32)
    coefs = jnp.array(chebyshev_sum(STEPS)[0][::-1], jnp.float32)
    return pl.pallas_call(
        functools.partial(solve_kernel, block_total),
        in_specs=[SMEM, SMEM, SMEM] + [VMEM] * 5 + [HBM] * 2 + [VMEM] * 2,
        out_specs=[HBM, VMEM, VMEM],
        out_shape=[
            jax.ShapeDtypeStruct(full, jnp.float32),
            jax.ShapeDtypeStruct((rows, 2 * cols), jnp.float32),
            jax.ShapeDtypeStruct((rows, 2 * cols), jnp.float32),
        ],
        scratch_shapes=[
            pltpu.VMEM((2, LANES * deep, LANES), jnp.float32),
            turned,
            turned,
            turned,
            turned,
            pltpu.VMEM(full, jnp.float32),
            pltpu.SemaphoreType.DMA((2,)),
            pltpu.SemaphoreType.DMA((slots, comps)),
        ],
        compiler_params=params(SOLVE_VMEM),
        cost_estimate=pl.CostEstimate(
            flops=9 * STEPS * root.size, bytes_accessed=16 * root.size, transcendentals=0
        ),
        name="surface_solve",
    )(block_ids, table, coefs, root, centre, around, level_count, bottom, *columns, near, far)


def stack_kernel(parts, *refs):
    out_ref = refs[-1]
    for p in range(parts):
        out_ref[p] = refs[p][...]


def stack_after(parts, *tokens):
    return pl.pallas_call(
        functools.partial(stack_kernel, len(parts)),
        in_specs=[VMEM] * len(parts) + [ANYWHERE] * len(tokens),
        out_specs=VMEM,
        out_shape=jax.ShapeDtypeStruct((len(parts),) + parts[0].shape, jnp.float32),
        compiler_params=params(WINDOW_VMEM),
        name="stack_after",
    )(*parts, *tokens)


FIRST_SLOTS = 1


def swap(values, axis, mask):
    count = lax.axis_size(axis)
    return lax.ppermute(values, axis, [(i, i ^ mask) for i in range(count)])


def per_device(adjoint_vel, velocity, drag_coef, level_count, block_ids, bathymetry, land_mask):
    slots = block_ids.shape[0]
    rows, cols = drag_coef.shape[1:]
    lon_count = lax.axis_size("gx")
    lat_count = lax.axis_size("gy")
    half = lat_count // 2
    block_total = 2 * lon_count * lat_count
    me = jnp.stack([lax.axis_index("gx"), lax.axis_index("gy")]).astype(jnp.int32)

    depths = depth_payload(bathymetry, land_mask, block_ids)
    depth_parts = [depths] + [swap(depths, "gy", 2 * m) for m in range(1, half)]
    forcing = column_forcing(adjoint_vel, level_count)

    parts = [forcing] + [swap(forcing, "gy", 2 * m) for m in range(1, half)]
    near_depths = stack_after(depth_parts, forcing)
    near_depths = [near_depths] + [swap(near_depths, "gx", m) for m in range(1, lon_count)]
    columns = (adjoint_vel, velocity, drag_coef, level_count, block_ids)
    first_column, *first_rest = column_mixing(*columns, forcing, block_total, 0, FIRST_SLOTS)
    line = stack_after(parts, first_rest[0])

    near = [line] + [swap(line, "gx", m) for m in range(1, lon_count)]
    near_depths = stack_after(near_depths, line)
    near_depths = near_depths.reshape((lon_count * half,) + depths.shape)
    far_depths = swap(near_depths, "gy", 1)
    last_column, bottom, drag_gradient = column_mixing(
        *columns, line, block_total, FIRST_SLOTS, slots, first_rest
    )
    weights = surface_weights(
        near_depths, far_depths, me, block_ids, rows, lon_count, lat_count
    )

    near = stack_after(near, bottom, weights[0])
    far = swap(near, "gy", 1)

    corrected, height, sensitivity = surface_solve(
        near.reshape((-1, rows, cols)), far.reshape((-1, rows, cols)), weights,
        block_ids, level_count, bottom, (first_column, last_column), block_total,
    )
    return corrected, drag_gradient, height, sensitivity


def solution(mesh):
    in_specs = (
        P(("gx", "gy"), None, None, None, None),
        P(("gx", "gy"), None, None, None, None),
        P(("gx", "gy"), None, None),
        P(("gx", "gy"), None, None),
        P(("gx", "gy")),
        P("gy", "gx"),
        P("gy", "gx"),
    )
    out_specs = (
        P(("gx", "gy"), None, None, None, None),
        P(("gx", "gy"), None, None),
        P("gy", "gx"),
        P("gy", "gx"),
    )
    return jax.shard_map(
        per_device, mesh=mesh, in_specs=in_specs, out_specs=out_specs, check_vma=False
    )
```

```python
import functools

import jax
import jax.numpy as jnp
import numpy as np
from jax import lax
from jax.experimental import pallas as pl
from jax.experimental.pallas import tpu as pltpu
from jax.sharding import PartitionSpec as P

STEPS = 32

mix_rate = 0.25
drag_step = 0.5
force_scale = 0.25
pressure_gain = 0.5
surface_shift = 1.0 / 64.0
speed_floor = 0.01

LANES = 128
SUBLANES = 8
MIB = 1024 * 1024
FIRST_VMEM = 61 * MIB
MIXING_VMEM = 52 * MIB
SOLVE_VMEM = 50 * MIB
WINDOW_VMEM = 16 * MIB


def chebyshev_sum(total_steps):
    highest = surface_shift + 8.0
    centre = 0.5 * (highest + surface_shift)
    radius = 0.5 * (highest - surface_shift)
    sigma_ratio = centre / radius

    def operate(series):
        shifted = np.zeros_like(series)
        shifted[1] += series[0]
        for k in range(1, len(series) - 1):
            shifted[k + 1] += 0.5 * series[k]
            shifted[k - 1] += 0.5 * series[k]
        return centre * series - radius * shifted

    height = np.zeros(total_steps + 2)
    residual = np.zeros(total_steps + 2)
    residual[0] = 1.0
    direction = residual / centre
    ratio_prev = 1.0 / sigma_ratio
    for _ in range(total_steps):
        height = height + direction
        residual = residual - operate(direction)
        ratio_next = 1.0 / (2.0 * sigma_ratio - ratio_prev)
        direction = ratio_next * ratio_prev * direction + 2.0 * ratio_next / radius * residual
        ratio_prev = ratio_next
    return [float(c) for c in height[:total_steps]], 2.0 / radius


def params(limit):
    return pltpu.CompilerParams(vmem_limit_bytes=limit)


SMEM = pl.BlockSpec(memory_space=pltpu.SMEM)
VMEM = pl.BlockSpec(memory_space=pltpu.VMEM)
ANYWHERE = pl.BlockSpec(memory_space=pl.ANY)
HBM = pl.BlockSpec(memory_space=pltpu.HBM)


def forcing_kernel(levels_ref, adjoint_ref, out_ref, levels_held, held, level_sem, sems):
    slots, comps, depth, rows, cols = held.shape
    level_copy = pltpu.make_async_copy(levels_ref, levels_held, level_sem)
    level_copy.start()

    def copy_in(b, c):
        return pltpu.make_async_copy(adjoint_ref.at[b, c], held.at[b, c], sems.at[b, c])

    for b in range(slots):
        for c in range(comps):
            copy_in(b, c).start()
    level_copy.wait()

    def one_slot(b, carry):
        levels = levels_held[b]
        totals = [jnp.zeros((rows, cols), jnp.float32) for _ in range(4)]
        for c in range(comps):
            copy_in(b, c).wait()
            for k in range(depth):
                totals[k % 4] = totals[k % 4] + jnp.where(levels > k, held[b, c, k], 0.0)
        out_ref[b] = force_scale * ((totals[0] + totals[1]) + (totals[2] + totals[3]))
        return carry

    lax.fori_loop(0, slots, one_slot, 0)


def column_forcing(adjoint_vel, level_count):
    slots, comps, depth, rows, cols = adjoint_vel.shape
    return pl.pallas_call(
        forcing_kernel,
        in_specs=[HBM, HBM],
        out_specs=VMEM,
        out_shape=pltpu.VMEM((slots, rows, cols), jnp.float32),
        scratch_shapes=[
            pltpu.VMEM(level_count.shape, jnp.int32),
            pltpu.VMEM(adjoint_vel.shape, jnp.float32),
            pltpu.SemaphoreType.DMA,
            pltpu.SemaphoreType.DMA((slots, comps)),
        ],
        compiler_params=params(FIRST_VMEM),
        cost_estimate=pl.CostEstimate(
            flops=2 * adjoint_vel.size, bytes_accessed=4 * adjoint_vel.size, transcendentals=0
        ),
        name="column_forcing",
    )(level_count, adjoint_vel)


CHUNK = 8


def mixing_kernel(block_total, first, earlier, ids_ref, levels_ref, drag_ref, adjoint_ref,
                  velocity_ref, after_ref, *rest):
    if earlier:
        for target, ref in zip(rest[3:5], rest[:2]):
            target[0:first] = ref[...]
        rest = rest[2:]
    column_ref, bottom_ref, gradient_ref, adjoint, velocity, column, in_sems, out_sems = rest
    slots, comps, depth, rows, cols = adjoint.shape
    group = 16
    parts = rows // group

    def copies_in(b, index):
        span = pl.ds(pl.multiple_of(index * group, group), group)
        return [
            pltpu.make_async_copy(
                source.at[first + b, :, :, span], target.at[b, :, :, span],
                in_sems.at[n, b, index],
            )
            for n, (source, target) in enumerate(
                ((adjoint_ref, adjoint), (velocity_ref, velocity))
            )
        ]

    def copy_out(b, index):
        span = pl.ds(pl.multiple_of(index * group, group), group)
        return pltpu.make_async_copy(
            column.at[b, :, :, span], column_ref.at[b, :, :, span], out_sems.at[b, index]
        )

    for b in range(slots):
        for index in range(parts):
            for copy in copies_in(b, index):
                copy.start()

    def one_group(b, index):
        flag = jnp.where(ids_ref[first + b] < block_total, 1.0, 0.0)
        span = pl.ds(pl.multiple_of(index * group, group), group)
        levels = levels_ref[first + b, span, :]
        zero = jnp.zeros(levels.shape, jnp.float32)
        x = [zero, zero]
        once = [zero, zero]
        first_flux = [zero, zero]
        second_flux = [zero, zero]
        flow = [zero, zero]
        field = [zero, zero]
        wets = []
        rates = []
        for low in range(0, depth + 2, CHUNK):
            here = range(low, min(low + CHUNK, depth + 2))
            loaded = {}
            for k in here:
                if k < depth:
                    for c in range(2):
                        loaded[k, c] = (adjoint[b, c, k, span, :], velocity[b, c, k, span, :])
            done = []
            for k in here:
                if k < depth:
                    wets.append(levels > k)
                    rates.append(jnp.where(wets[k], mix_rate, 0.0))
                for c in range(2):
                    fresh_once = None
                    if k < depth:
                        fresh = loaded[k, c][0]
                        flow[c] = jnp.where(
                            wets[k], loaded[k, c][1].astype(jnp.float32), flow[c]
                        )
                        if 1 <= k:
                            flux = (fresh - x[c]) * rates[k]
                            fresh_once = x[c] + (flux - first_flux[c])
                            first_flux[c] = flux
                        x[c] = fresh
                    elif k == depth:
                        fresh_once = x[c] - first_flux[c]
                    if 2 <= k:
                        if k <= depth:
                            flux = (fresh_once - once[c]) * rates[k - 1]
                            twice = once[c] + (flux - second_flux[c])
                            second_flux[c] = flux
                        else:
                            twice = once[c] - second_flux[c]
                        done.append((c, k - 2, twice))
                        field[c] = jnp.where(wets[k - 2], twice, field[c])
                    if fresh_once is not None:
                        once[c] = fresh_once
            for c, k, value in done:
                column[b, c, k, span, :] = value
        speed = jnp.sqrt(flow[0] * flow[0] + flow[1] * flow[1] + speed_floor)
        along = flow[0] * field[0] + flow[1] * field[1]
        ratio = along / speed
        drag = drag_ref[first + b, span, :]
        for c in range(2):
            bottom_ref[first + b, c, span, :] = field[c] - drag_step * drag * (
                speed * field[c] + flow[c] * ratio
            )
        gradient_ref[first + b, span, :] = -drag_step * speed * along * flag

    def one(step, carry):
        b = lax.div(step, parts)
        index = lax.rem(step, parts)

        for copy in copies_in(b, index):
            copy.wait()
        one_group(b, index)
        copy_out(b, index).start()
        return carry

    lax.fori_loop(0, slots * parts, one, 0)
    for b in range(slots):
        for index in range(parts):
            copy_out(b, index).wait()


def column_mixing(adjoint_vel, velocity, drag_coef, level_count, block_ids, after, block_total,
                  first, last, earlier=()):
    comps, depth, rows, cols = adjoint_vel.shape[1:]
    slots = last - first
    part = (slots, comps, depth, rows, cols)
    size = slots * comps * depth * rows * cols
    return pl.pallas_call(
        functools.partial(mixing_kernel, block_total, first, len(earlier)),
        in_specs=[SMEM, VMEM, VMEM, HBM, HBM, ANYWHERE] + [VMEM] * len(earlier),
        out_specs=[HBM, VMEM, VMEM],
        out_shape=[
            pltpu.HBM(part, jnp.float32),
            pltpu.VMEM((last, comps, rows, cols), jnp.float32),
            (pltpu.HBM if last == level_count.shape[0] else pltpu.VMEM)((last, rows, cols), jnp.float32),
        ],
        scratch_shapes=[
            pltpu.VMEM(part, adjoint_vel.dtype),
            pltpu.VMEM(part, velocity.dtype),
            pltpu.VMEM(part, jnp.float32),
            pltpu.SemaphoreType.DMA((2, slots, rows // 16)),
            pltpu.SemaphoreType.DMA((slots, rows // 16)),
        ],
        compiler_params=params(MIXING_VMEM),
        cost_estimate=pl.CostEstimate(
            flops=14 * size, bytes_accessed=10 * size, transcendentals=0
        ),
        name="column_mixing",
    )(block_ids, level_count, drag_coef, adjoint_vel, velocity, after, *earlier)


PAD = SUBLANES
BATCH = 2
WIDTH = LANES + 2 * STEPS
PITCH = WIDTH + 2 * PAD
NEIGHBOURS = [(down, right) for down in (-1, 0, 1) for right in (0, 1, -1)]


def window_shape(slots, rows):
    strips = LANES // (slots + 2)
    deep = pl.cdiv(rows + 2 * STEPS, strips)
    return strips, deep, strips * deep


def log2(count):
    bits = count.bit_length() - 1
    assert 1 << bits == count
    return bits


def window_places(me_ref, ids_ref, slots, lon_count, lat_count):
    places = []
    for w in range(slots + 2):
        if w < slots:
            block = jnp.where(ids_ref[w] < 2 * lon_count * lat_count, ids_ref[w], 0)
        else:
            block = (me_ref[0] * lat_count + me_ref[1]) * 2 + (w - slots)
        pair = block >> 1
        column = (pair >> log2(lat_count)) * 2 + (block & 1)
        places.append((pair & (lat_count - 1), column))
    return places


def put_window(natural, base, rows, blocks, lane):
    for i in range(3):
        here, east, west = blocks[3 * i:3 * i + 3]
        sides = jnp.where(lane < STEPS, east, jnp.where(lane >= LANES - STEPS, west, 0.0))
        start = base + i * rows
        natural[0, start:start + rows, :] = here
        natural[1, start:start + rows, :] = sides


def turn(natural, deep, put):
    for i in range(deep):
        put(i, STEPS, natural[0, pl.ds(i, LANES, stride=deep), :].T)
        sides = natural[1, pl.ds(i, LANES, stride=deep), :].T
        put(i, STEPS + LANES, sides[:STEPS])
        put(i, 0, sides[LANES - STEPS:])


def rows_at(ref, start, shift=0):
    return ref[pl.ds(start + shift, SUBLANES), :]


def in_batches(chunks, work):
    late = []
    for start in range(0, len(chunks), BATCH):
        batch = [item for chunk in chunks[start:start + BATCH] for item in work(chunk)]
        for ref, a, value in late:
            ref[pl.ds(a, SUBLANES), :] = value
        late = batch
    for ref, a, value in late:
        ref[pl.ds(a, SUBLANES), :] = value


def strip_rows(ref, chunk, deep):
    at = [i * PITCH + PAD + chunk * SUBLANES for i in range(deep)]
    here = [rows_at(ref, a) for a in at]
    above = [pltpu.roll(here[-1], 1, 1)] + here[:-1]
    below = here[1:] + [pltpu.roll(here[0], LANES - 1, 1)]
    return here, above, below, at


def depth_kernel(ids_ref, bathymetry_ref, mask_ref, out_ref, ids, bathymetry, mask, sems):
    copies = [
        pltpu.make_async_copy(ids_ref, ids, sems.at[0]),
        pltpu.make_async_copy(bathymetry_ref, bathymetry, sems.at[1]),
        pltpu.make_async_copy(mask_ref, mask, sems.at[2]),
    ]
    for copy in copies:
        copy.start()
    for copy in copies:
        copy.wait()
    rows = bathymetry.shape[0]
    scaled = bathymetry[...] * mask[...].astype(jnp.float32)
    out_ref[0:rows, :] = scaled[:, :LANES]
    out_ref[rows:2 * rows, :] = scaled[:, LANES:]
    lane = lax.broadcasted_iota(jnp.int32, (SUBLANES, LANES), 1)
    listed = jnp.zeros((SUBLANES, LANES), jnp.int32)
    for s in range(ids.shape[0]):
        listed = jnp.where(lane == s, ids[s], listed)
    out_ref[2 * rows:2 * rows + SUBLANES, :] = listed.astype(jnp.float32)


def depth_payload(bathymetry, land_mask, block_ids):
    rows = bathymetry.shape[0]
    return pl.pallas_call(
        depth_kernel,
        in_specs=[HBM, HBM, HBM],
        out_specs=VMEM,
        out_shape=pltpu.VMEM((2 * rows + SUBLANES, LANES), jnp.float32),
        scratch_shapes=[
            pltpu.SMEM(block_ids.shape, jnp.int32),
            pltpu.VMEM(bathymetry.shape, jnp.float32),
            pltpu.VMEM(land_mask.shape, jnp.int32),
            pltpu.SemaphoreType.DMA((3,)),
        ],
        compiler_params=params(FIRST_VMEM),
        name="depth_payload",
    )(block_ids, bathymetry, land_mask)


def weights_kernel(slots, lon_count, lat_count, me_ref, ids_ref, near_ref, far_ref,
                   root_ref, centre_ref, around_ref, table_ref,
                   natural, all_ids, places_of, sems):
    half = lat_count // 2
    count = lon_count * half
    rows = (near_ref.shape[1] - SUBLANES) // 2
    strips, deep, tall = window_shape(slots, rows)
    column_count = 2 * lon_count
    parts = (near_ref, far_ref)
    copies = [
        pltpu.make_async_copy(
            parts[p].at[:, pl.ds(2 * rows, 1), :], all_ids.at[p], sems.at[p]
        )
        for p in range(2)
    ]
    for copy in copies:
        copy.start()
    natural[...] = jnp.zeros_like(natural)

    def load(lat, column):
        inside = (lat >= 0) & (lat < lat_count) & (column >= 0) & (column < column_count)
        lat_safe = jnp.clip(lat, 0, lat_count - 1)
        column_safe = jnp.clip(column, 0, column_count - 1)
        lon_xor = (column_safe >> 1) ^ me_ref[0]
        lat_xor = lat_safe ^ me_ref[1]
        place = lon_xor * half + (lat_xor >> 1)
        start = pl.multiple_of((column_safe & 1) * rows, SUBLANES)
        near = near_ref[place, pl.ds(start, rows), :]
        far = far_ref[place, pl.ds(start, rows), :]
        here = jnp.where((lat_xor & 1) == 0, near, far)
        return here * jnp.where(inside, 1.0, 0.0)

    lane = lax.broadcasted_iota(jnp.int32, (rows, LANES), 1)
    places = window_places(me_ref, ids_ref, slots, lon_count, lat_count)
    for w, (lat, column) in enumerate(places):
        blocks = [load(lat + down, column + right) for down, right in NEIGHBOURS]
        put_window(natural, w * tall, rows, blocks, lane)

    for copy in copies:
        copy.wait()

    def one_device(n, carry):
        for p in range(2):
            for s in range(slots):
                block = all_ids[p, n, 0, s].astype(jnp.int32)
                places_of[block] = (p * count + n) * slots + s
        return carry

    lax.fori_loop(0, count, one_device, 0)
    for w, (lat, column) in enumerate(places):
        for n, (down, right) in enumerate(NEIGHBOURS):
            lat_safe = jnp.clip(lat + down, 0, lat_count - 1)
            column_safe = jnp.clip(column + right, 0, column_count - 1)
            block = ((column_safe >> 1) * lat_count + lat_safe) * 2 + (column_safe & 1)
            table_ref[w * len(NEIGHBOURS) + n] = places_of[block]

    scale = chebyshev_sum(STEPS)[1]

    def put(i, x, values):
        start = i * PITCH + PAD + x
        root_ref[start:start + values.shape[0], :] = jnp.sqrt(values)
        around_ref[start:start + values.shape[0], :] = scale * values

    turn(natural, deep, put)
    zeros = jnp.zeros((PAD, LANES), jnp.float32)
    for i in range(deep):
        root_ref[i * PITCH:i * PITCH + PAD, :] = zeros
        root_ref[(i + 1) * PITCH - PAD:(i + 1) * PITCH, :] = zeros

    def work(chunk):
        here, above, below, at = strip_rows(root_ref, chunk, deep)
        out = []
        for i, a in enumerate(at):
            others = (rows_at(root_ref, a, 1) + rows_at(root_ref, a, -1)) + (above[i] + below[i])
            out.append((centre_ref, a, 2.0 - scale * here[i] * others))
        return out

    in_batches(range(WIDTH // SUBLANES), work)


def surface_weights(near, far, me, block_ids, rows, lon_count, lat_count):
    slots = block_ids.shape[0]
    assert near.shape[-1] == LANES
    strips, deep, tall = window_shape(slots, rows)
    shape = jax.ShapeDtypeStruct((deep * PITCH, LANES), jnp.float32)
    return pl.pallas_call(
        functools.partial(weights_kernel, slots, lon_count, lat_count),
        in_specs=[SMEM, SMEM, VMEM, VMEM],
        out_specs=[VMEM, VMEM, VMEM, SMEM],
        out_shape=[
            shape,
            shape,
            shape,
            jax.ShapeDtypeStruct(((slots + 2) * len(NEIGHBOURS),), jnp.int32),
        ],
        scratch_shapes=[
            pltpu.VMEM((2, LANES * deep, LANES), jnp.float32),
            pltpu.SMEM((2, near.shape[0], 1, LANES), jnp.float32),
            pltpu.SMEM((2 * lon_count * lat_count + 1,), jnp.int32),
            pltpu.SemaphoreType.DMA((2,)),
        ],
        compiler_params=params(WINDOW_VMEM),
        cost_estimate=pl.CostEstimate(
            flops=0, bytes_accessed=8 * MIB, transcendentals=0
        ),
        name="surface_weights",
    )(me, block_ids, near, far)


def solve_kernel(block_total, ids_ref, table_ref, coefs_ref, root_ref, centre_ref, around_ref,
                 levels_ref, bottom_ref, first_column_ref, last_column_ref, near_ref, far_ref,
                 corrected_ref, height_ref, sensitivity_ref,
                 natural, source, even, odd, extra, column, in_sems, out_sems):
    slots, comps, depth, rows, cols = column.shape
    strips, deep, tall = window_shape(slots, rows)

    middle = first_column_ref.shape[0]
    copies_in = [
        pltpu.make_async_copy(first_column_ref, column.at[pl.ds(0, middle)], in_sems.at[0]),
        pltpu.make_async_copy(
            last_column_ref, column.at[pl.ds(middle, slots - middle)], in_sems.at[1]
        ),
    ]
    for copy in copies_in:
        copy.start()

    count = near_ref.shape[0]

    def load(place):
        inner = place & (count - 1)
        return jnp.where(place < count, near_ref[inner], far_ref[inner])

    lane = lax.broadcasted_iota(jnp.int32, (rows, LANES), 1)
    for w in range(slots + 2):
        places = [table_ref[w * len(NEIGHBOURS) + n] for n in range(len(NEIGHBOURS))]
        put_window(natural, w * tall, rows, [load(place) for place in places], lane)

    coefs, step_scale = chebyshev_sum(STEPS)

    def put(i, x, values):
        start = i * PITCH + PAD + x
        stop = start + values.shape[0]
        root = root_ref[start:stop, :]
        values = jnp.where(root > 0.0, root * values, 0.0)
        source[start:stop, :] = values
        even[start:stop, :] = coefs[STEPS - 1] * values
        odd[start:stop, :] = jnp.zeros_like(values)

    zeros = jnp.zeros((PAD, LANES), jnp.float32)
    for ref in (even, odd):
        for i in range(deep):
            ref[i * PITCH:i * PITCH + PAD, :] = zeros
            ref[(i + 1) * PITCH - PAD:(i + 1) * PITCH, :] = zeros
    turn(natural, deep, put)

    chunks = WIDTH // SUBLANES

    def apply(current, target, coef, gain, m):
        def work(chunk):
            here, above, below, at = strip_rows(current, chunk, deep)
            out = []
            for i, a in enumerate(at):
                others = (rows_at(current, a, 1) + rows_at(current, a, -1)) + (
                    above[i] + below[i]
                )
                pushed = rows_at(centre_ref, a) * here[i] + rows_at(around_ref, a) * others
                if gain != 1.0:
                    pushed = gain * pushed
                kept = coef * rows_at(source, a) - rows_at(target, a)
                out.append((target, a, kept + pushed))
            return out

        in_batches(range(m // SUBLANES, chunks - m // SUBLANES), work)

    runs = []
    for m in range(1, STEPS - 1, 2):
        if runs and runs[-1][0] // SUBLANES == m // SUBLANES:
            runs[-1][1] += 1
        else:
            runs.append([m, 1])
    for first, pairs in runs:
        def two_steps(pair, carry, first=first):
            m = first + 2 * pair
            apply(even, odd, coefs_ref[m], 1.0, first)
            apply(odd, even, coefs_ref[m + 1], 1.0, first)
            return carry

        lax.fori_loop(0, pairs, two_steps, 0)
    apply(even, odd, coefs[0], 0.5, STEPS - 1)

    low = STEPS // SUBLANES - 1

    def one_height(chunk):
        out = []
        for i in range(deep):
            a = i * PITCH + PAD + chunk * SUBLANES
            root = rows_at(root_ref, a)
            out.append((extra, a, jnp.where(root > 0.0, rows_at(odd, a) / root, 0.0)))
        return out

    in_batches(range(low, chunks - low), one_height)

    def east_steps(chunk):
        here, _, _, at = strip_rows(extra, chunk, deep)
        return [(even, a, rows_at(extra, a, 1) - here[i]) for i, a in enumerate(at)]

    def sensitivity(chunk):
        here, above, below, at = strip_rows(extra, chunk, deep)
        root, root_above, root_below, _ = strip_rows(root_ref, chunk, deep)
        out = []
        for i, a in enumerate(at):
            east_step = rows_at(extra, a, 1) - here[i]
            west_step = here[i] - rows_at(extra, a, -1)
            south_step = below[i] - here[i]
            north_step = here[i] - above[i]
            energy = root[i] * (
                (rows_at(root_ref, a, 1) * east_step * east_step
                 + rows_at(root_ref, a, -1) * west_step * west_step)
                + (root_below[i] * south_step * south_step
                   + root_above[i] * north_step * north_step)
            )
            scaled = rows_at(around_ref, a) * (1.0 / step_scale)
            out.append((source, a, 0.25 * energy / jnp.maximum(scaled, 0.25)))
        return out

    middle_chunks = range(low + 1, chunks - low - 1)

    def turn_back(ref, tile):
        for i in range(deep):
            start = i * PITCH + PAD + STEPS
            natural[tile, pl.ds(i, LANES, stride=deep), :] = ref[start:start + LANES, :].T

    def cut(tile, w, shift=0):
        return natural[tile, pl.ds(w * tall + STEPS + shift, rows), :]

    def copy_out(b, c):
        return pltpu.make_async_copy(column.at[b, c], corrected_ref.at[b, c], out_sems.at[b, c])

    def correct(b, c, step):
        levels = levels_ref[b] * jnp.where(ids_ref[b] < block_total, 1, 0)
        push = pressure_gain * step
        lowest = bottom_ref[b, c] - push

        late = []
        for low in range(0, depth, CHUNK):
            batch = []
            for k in range(low, min(low + CHUNK, depth)):
                value = jnp.where(levels == k + 1, lowest, column[b, c, k] - push)
                batch.append((k, jnp.where(levels > k, value, 0.0)))
            for k, value in late:
                column[b, c, k] = value
            late = batch
        for k, value in late:
            column[b, c, k] = value
        copy_out(b, c).start()

    def correct_north(b, carry):
        correct(b, 1, cut(1, b, 1) - cut(1, b))
        return carry

    def correct_east(b, carry):
        correct(b, 0, cut(0, b))
        return carry

    turn_back(extra, 1)
    for copy in copies_in:
        copy.wait()
    lax.fori_loop(0, slots, correct_north, 0)
    in_batches(middle_chunks, east_steps)
    turn_back(even, 0)
    lax.fori_loop(0, slots, correct_east, 0)
    in_batches(middle_chunks, sensitivity)
    turn_back(source, 0)
    for h in range(2):
        height_ref[:, h * LANES:(h + 1) * LANES] = cut(1, slots + h)
        sensitivity_ref[:, h * LANES:(h + 1) * LANES] = cut(0, slots + h)

    for b in range(slots):
        for c in range(comps):
            copy_out(b, c).wait()


def surface_solve(near, far, weights, block_ids, level_count, bottom, columns, block_total):
    root, centre, around, table = weights
    comps, depth, rows, cols = columns[0].shape[1:]
    slots = level_count.shape[0]
    assert comps == 2
    full = (slots, comps, depth, rows, cols)
    deep = window_shape(slots, rows)[1]
    turned = pltpu.VMEM(root.shape, jnp.float32)
    coefs = jnp.array(chebyshev_sum(STEPS)[0][::-1], jnp.float32)
    return pl.pallas_call(
        functools.partial(solve_kernel, block_total),
        in_specs=[SMEM, SMEM, SMEM] + [VMEM] * 5 + [HBM] * 2 + [VMEM] * 2,
        out_specs=[HBM, VMEM, VMEM],
        out_shape=[
            jax.ShapeDtypeStruct(full, jnp.float32),
            jax.ShapeDtypeStruct((rows, 2 * cols), jnp.float32),
            jax.ShapeDtypeStruct((rows, 2 * cols), jnp.float32),
        ],
        scratch_shapes=[
            pltpu.VMEM((2, LANES * deep, LANES), jnp.float32),
            turned,
            turned,
            turned,
            turned,
            pltpu.VMEM(full, jnp.float32),
            pltpu.SemaphoreType.DMA((2,)),
            pltpu.SemaphoreType.DMA((slots, comps)),
        ],
        compiler_params=params(SOLVE_VMEM),
        cost_estimate=pl.CostEstimate(
            flops=9 * STEPS * root.size, bytes_accessed=16 * root.size, transcendentals=0
        ),
        name="surface_solve",
    )(block_ids, table, coefs, root, centre, around, level_count, bottom, *columns, near, far)


def stack_kernel(parts, *refs):
    out_ref = refs[-1]
    for p in range(parts):
        out_ref[p] = refs[p][...]


def stack_after(parts, *tokens):
    return pl.pallas_call(
        functools.partial(stack_kernel, len(parts)),
        in_specs=[VMEM] * len(parts) + [ANYWHERE] * len(tokens),
        out_specs=VMEM,
        out_shape=jax.ShapeDtypeStruct((len(parts),) + parts[0].shape, jnp.float32),
        compiler_params=params(WINDOW_VMEM),
        name="stack_after",
    )(*parts, *tokens)


FIRST_SLOTS = 1


def swap(values, axis, mask):
    count = lax.axis_size(axis)
    return lax.ppermute(values, axis, [(i, i ^ mask) for i in range(count)])


def per_device(adjoint_vel, velocity, drag_coef, level_count, block_ids, bathymetry, land_mask):
    slots = block_ids.shape[0]
    rows, cols = drag_coef.shape[1:]
    lon_count = lax.axis_size("gx")
    lat_count = lax.axis_size("gy")
    half = lat_count // 2
    block_total = 2 * lon_count * lat_count
    me = jnp.stack([lax.axis_index("gx"), lax.axis_index("gy")]).astype(jnp.int32)

    depths = depth_payload(bathymetry, land_mask, block_ids)
    depth_parts = [depths] + [swap(depths, "gy", 2 * m) for m in range(1, half)]
    forcing = column_forcing(adjoint_vel, level_count)

    parts = [forcing] + [swap(forcing, "gy", 2 * m) for m in range(1, half)]
    near_depths = stack_after(depth_parts, forcing)
    near_depths = [near_depths] + [swap(near_depths, "gx", m) for m in range(1, lon_count)]
    columns = (adjoint_vel, velocity, drag_coef, level_count, block_ids)
    first_column, *first_rest = column_mixing(*columns, forcing, block_total, 0, FIRST_SLOTS)
    line = stack_after(parts, first_rest[0])

    near = [line] + [swap(line, "gx", m) for m in range(1, lon_count)]
    near_depths = stack_after(near_depths, line)
    near_depths = near_depths.reshape((lon_count * half,) + depths.shape)
    far_depths = swap(near_depths, "gy", 1)
    last_column, bottom, drag_gradient = column_mixing(
        *columns, line, block_total, FIRST_SLOTS, slots, first_rest
    )
    weights = surface_weights(
        near_depths, far_depths, me, block_ids, rows, lon_count, lat_count
    )

    near = stack_after(near, bottom)
    far = swap(near, "gy", 1)

    corrected, height, sensitivity = surface_solve(
        near.reshape((-1, rows, cols)), far.reshape((-1, rows, cols)), weights,
        block_ids, level_count, bottom, (first_column, last_column), block_total,
    )
    return corrected, drag_gradient, height, sensitivity


def solution(mesh):
    in_specs = (
        P(("gx", "gy"), None, None, None, None),
        P(("gx", "gy"), None, None, None, None),
        P(("gx", "gy"), None, None),
        P(("gx", "gy"), None, None),
        P(("gx", "gy")),
        P("gy", "gx"),
        P("gy", "gx"),
    )
    out_specs = (
        P(("gx", "gy"), None, None, None, None),
        P(("gx", "gy"), None, None),
        P("gy", "gx"),
        P("gy", "gx"),
    )
    return jax.shard_map(
        per_device, mesh=mesh, in_specs=in_specs, out_specs=out_specs, check_vma=False
    )
```

```python
import functools

import jax
import jax.numpy as jnp
import numpy as np
from jax import lax
from jax.experimental import pallas as pl
from jax.experimental.pallas import tpu as pltpu
from jax.sharding import PartitionSpec as P

STEPS = 32

mix_rate = 0.25
drag_step = 0.5
force_scale = 0.25
pressure_gain = 0.5
surface_shift = 1.0 / 64.0
speed_floor = 0.01

LANES = 128
SUBLANES = 8
MIB = 1024 * 1024
FIRST_VMEM = 61 * MIB
MIXING_VMEM = 52 * MIB
SOLVE_VMEM = 50 * MIB
WINDOW_VMEM = 16 * MIB


def chebyshev_sum(total_steps):
    highest = surface_shift + 8.0
    centre = 0.5 * (highest + surface_shift)
    radius = 0.5 * (highest - surface_shift)
    sigma_ratio = centre / radius

    def operate(series):
        shifted = np.zeros_like(series)
        shifted[1] += series[0]
        for k in range(1, len(series) - 1):
            shifted[k + 1] += 0.5 * series[k]
            shifted[k - 1] += 0.5 * series[k]
        return centre * series - radius * shifted

    height = np.zeros(total_steps + 2)
    residual = np.zeros(total_steps + 2)
    residual[0] = 1.0
    direction = residual / centre
    ratio_prev = 1.0 / sigma_ratio
    for _ in range(total_steps):
        height = height + direction
        residual = residual - operate(direction)
        ratio_next = 1.0 / (2.0 * sigma_ratio - ratio_prev)
        direction = ratio_next * ratio_prev * direction + 2.0 * ratio_next / radius * residual
        ratio_prev = ratio_next
    return [float(c) for c in height[:total_steps]], 2.0 / radius


def params(limit):
    return pltpu.CompilerParams(vmem_limit_bytes=limit)


SMEM = pl.BlockSpec(memory_space=pltpu.SMEM)
VMEM = pl.BlockSpec(memory_space=pltpu.VMEM)
ANYWHERE = pl.BlockSpec(memory_space=pl.ANY)
HBM = pl.BlockSpec(memory_space=pltpu.HBM)


def forcing_kernel(levels_ref, adjoint_ref, out_ref, levels_held, held, level_sem, sems):
    slots, comps, depth, rows, cols = held.shape
    level_copy = pltpu.make_async_copy(levels_ref, levels_held, level_sem)
    level_copy.start()

    def copy_in(b, c):
        return pltpu.make_async_copy(adjoint_ref.at[b, c], held.at[b, c], sems.at[b, c])

    for b in range(slots):
        for c in range(comps):
            copy_in(b, c).start()
    level_copy.wait()

    def one_slot(b, carry):
        levels = levels_held[b]
        totals = [jnp.zeros((rows, cols), jnp.float32) for _ in range(4)]
        for c in range(comps):
            copy_in(b, c).wait()
            for k in range(depth):
                totals[k % 4] = totals[k % 4] + jnp.where(levels > k, held[b, c, k], 0.0)
        out_ref[b] = force_scale * ((totals[0] + totals[1]) + (totals[2] + totals[3]))
        return carry

    lax.fori_loop(0, slots, one_slot, 0)


def column_forcing(adjoint_vel, level_count):
    slots, comps, depth, rows, cols = adjoint_vel.shape
    return pl.pallas_call(
        forcing_kernel,
        in_specs=[HBM, HBM],
        out_specs=VMEM,
        out_shape=pltpu.VMEM((slots, rows, cols), jnp.float32),
        scratch_shapes=[
            pltpu.VMEM(level_count.shape, jnp.int32),
            pltpu.VMEM(adjoint_vel.shape, jnp.float32),
            pltpu.SemaphoreType.DMA,
            pltpu.SemaphoreType.DMA((slots, comps)),
        ],
        compiler_params=params(FIRST_VMEM),
        cost_estimate=pl.CostEstimate(
            flops=2 * adjoint_vel.size, bytes_accessed=4 * adjoint_vel.size, transcendentals=0
        ),
        name="column_forcing",
    )(level_count, adjoint_vel)


CHUNK = 8


def mixing_kernel(block_total, first, earlier, ids_ref, levels_ref, drag_ref, adjoint_ref,
                  velocity_ref, after_ref, *rest):
    if earlier:
        for target, ref in zip(rest[3:5], rest[:2]):
            target[0:first] = ref[...]
        rest = rest[2:]
    column_ref, bottom_ref, gradient_ref, adjoint, velocity, column, in_sems, out_sems = rest
    slots, comps, depth, rows, cols = adjoint.shape
    group = 16
    parts = rows // group

    def copies_in(b, index):
        span = pl.ds(pl.multiple_of(index * group, group), group)
        return [
            pltpu.make_async_copy(
                source.at[first + b, :, :, span], target.at[b, :, :, span],
                in_sems.at[n, b, index],
            )
            for n, (source, target) in enumerate(
                ((adjoint_ref, adjoint), (velocity_ref, velocity))
            )
        ]

    def copy_out(b, index):
        span = pl.ds(pl.multiple_of(index * group, group), group)
        return pltpu.make_async_copy(
            column.at[b, :, :, span], column_ref.at[b, :, :, span], out_sems.at[b, index]
        )

    for b in range(slots):
        for index in range(parts):
            for copy in copies_in(b, index):
                copy.start()

    def one_group(b, index):
        flag = jnp.where(ids_ref[first + b] < block_total, 1.0, 0.0)
        span = pl.ds(pl.multiple_of(index * group, group), group)
        levels = levels_ref[first + b, span, :]
        zero = jnp.zeros(levels.shape, jnp.float32)
        x = [zero, zero]
        once = [zero, zero]
        first_flux = [zero, zero]
        second_flux = [zero, zero]
        flow = [zero, zero]
        field = [zero, zero]
        wets = []
        rates = []
        for low in range(0, depth + 2, CHUNK):
            here = range(low, min(low + CHUNK, depth + 2))
            loaded = {}
            for k in here:
                if k < depth:
                    for c in range(2):
                        loaded[k, c] = (adjoint[b, c, k, span, :], velocity[b, c, k, span, :])
            done = []
            for k in here:
                if k < depth:
                    wets.append(levels > k)
                    rates.append(jnp.where(wets[k], mix_rate, 0.0))
                for c in range(2):
                    fresh_once = None
                    if k < depth:
                        fresh = loaded[k, c][0]
                        flow[c] = jnp.where(
                            wets[k], loaded[k, c][1].astype(jnp.float32), flow[c]
                        )
                        if 1 <= k:
                            flux = (fresh - x[c]) * rates[k]
                            fresh_once = x[c] + (flux - first_flux[c])
                            first_flux[c] = flux
                        x[c] = fresh
                    elif k == depth:
                        fresh_once = x[c] - first_flux[c]
                    if 2 <= k:
                        if k <= depth:
                            flux = (fresh_once - once[c]) * rates[k - 1]
                            twice = once[c] + (flux - second_flux[c])
                            second_flux[c] = flux
                        else:
                            twice = once[c] - second_flux[c]
                        done.append((c, k - 2, twice))
                        field[c] = jnp.where(wets[k - 2], twice, field[c])
                    if fresh_once is not None:
                        once[c] = fresh_once
            for c, k, value in done:
                column[b, c, k, span, :] = value
        speed = jnp.sqrt(flow[0] * flow[0] + flow[1] * flow[1] + speed_floor)
        along = flow[0] * field[0] + flow[1] * field[1]
        ratio = along / speed
        drag = drag_ref[first + b, span, :]
        for c in range(2):
            bottom_ref[first + b, c, span, :] = field[c] - drag_step * drag * (
                speed * field[c] + flow[c] * ratio
            )
        gradient_ref[first + b, span, :] = -drag_step * speed * along * flag

    def one(step, carry):
        b = lax.div(step, parts)
        index = lax.rem(step, parts)

        for copy in copies_in(b, index):
            copy.wait()
        one_group(b, index)
        copy_out(b, index).start()
        return carry

    lax.fori_loop(0, slots * parts, one, 0)
    for b in range(slots):
        for index in range(parts):
            copy_out(b, index).wait()


def column_mixing(adjoint_vel, velocity, drag_coef, level_count, block_ids, after, block_total,
                  first, last, earlier=()):
    comps, depth, rows, cols = adjoint_vel.shape[1:]
    slots = last - first
    part = (slots, comps, depth, rows, cols)
    size = slots * comps * depth * rows * cols
    return pl.pallas_call(
        functools.partial(mixing_kernel, block_total, first, len(earlier)),
        in_specs=[SMEM, VMEM, VMEM, HBM, HBM, ANYWHERE] + [VMEM] * len(earlier),
        out_specs=[HBM, VMEM, VMEM],
        out_shape=[
            pltpu.HBM(part, jnp.float32),
            pltpu.VMEM((last, comps, rows, cols), jnp.float32),
            (pltpu.HBM if last == level_count.shape[0] else pltpu.VMEM)((last, rows, cols), jnp.float32),
        ],
        scratch_shapes=[
            pltpu.VMEM(part, adjoint_vel.dtype),
            pltpu.VMEM(part, velocity.dtype),
            pltpu.VMEM(part, jnp.float32),
            pltpu.SemaphoreType.DMA((2, slots, rows // 16)),
            pltpu.SemaphoreType.DMA((slots, rows // 16)),
        ],
        compiler_params=params(MIXING_VMEM),
        cost_estimate=pl.CostEstimate(
            flops=14 * size, bytes_accessed=10 * size, transcendentals=0
        ),
        name="column_mixing",
    )(block_ids, level_count, drag_coef, adjoint_vel, velocity, after, *earlier)


PAD = SUBLANES
BATCH = 2
WIDTH = LANES + 2 * STEPS
PITCH = WIDTH + 2 * PAD
NEIGHBOURS = [(down, right) for down in (-1, 0, 1) for right in (0, 1, -1)]


def window_shape(slots, rows):
    strips = LANES // (slots + 2)
    deep = pl.cdiv(rows + 2 * STEPS, strips)
    return strips, deep, strips * deep


def log2(count):
    bits = count.bit_length() - 1
    assert 1 << bits == count
    return bits


def window_places(me_ref, ids_ref, slots, lon_count, lat_count):
    places = []
    for w in range(slots + 2):
        if w < slots:
            block = jnp.where(ids_ref[w] < 2 * lon_count * lat_count, ids_ref[w], 0)
        else:
            block = (me_ref[0] * lat_count + me_ref[1]) * 2 + (w - slots)
        pair = block >> 1
        column = (pair >> log2(lat_count)) * 2 + (block & 1)
        places.append((pair & (lat_count - 1), column))
    return places


def put_window(natural, base, rows, blocks, lane):
    for i in range(3):
        here, east, west = blocks[3 * i:3 * i + 3]
        sides = jnp.where(lane < STEPS, east, jnp.where(lane >= LANES - STEPS, west, 0.0))
        start = base + i * rows
        natural[0, start:start + rows, :] = here
        natural[1, start:start + rows, :] = sides


def turn(natural, deep, put):
    for i in range(deep):
        put(i, STEPS, natural[0, pl.ds(i, LANES, stride=deep), :].T)
        sides = natural[1, pl.ds(i, LANES, stride=deep), :].T
        put(i, STEPS + LANES, sides[:STEPS])
        put(i, 0, sides[LANES - STEPS:])


def rows_at(ref, start, shift=0):
    return ref[pl.ds(start + shift, SUBLANES), :]


def in_batches(chunks, work):
    late = []
    for start in range(0, len(chunks), BATCH):
        batch = [item for chunk in chunks[start:start + BATCH] for item in work(chunk)]
        for ref, a, value in late:
            ref[pl.ds(a, SUBLANES), :] = value
        late = batch
    for ref, a, value in late:
        ref[pl.ds(a, SUBLANES), :] = value


def strip_rows(ref, chunk, deep):
    at = [i * PITCH + PAD + chunk * SUBLANES for i in range(deep)]
    here = [rows_at(ref, a) for a in at]
    above = [pltpu.roll(here[-1], 1, 1)] + here[:-1]
    below = here[1:] + [pltpu.roll(here[0], LANES - 1, 1)]
    return here, above, below, at


def depth_kernel(ids_ref, bathymetry_ref, mask_ref, out_ref, ids, bathymetry, mask, sems):
    copies = [
        pltpu.make_async_copy(ids_ref, ids, sems.at[0]),
        pltpu.make_async_copy(bathymetry_ref, bathymetry, sems.at[1]),
        pltpu.make_async_copy(mask_ref, mask, sems.at[2]),
    ]
    for copy in copies:
        copy.start()
    for copy in copies:
        copy.wait()
    rows = bathymetry.shape[0]
    scaled = bathymetry[...] * mask[...].astype(jnp.float32)
    out_ref[0:rows, :] = scaled[:, :LANES]
    out_ref[rows:2 * rows, :] = scaled[:, LANES:]
    lane = lax.broadcasted_iota(jnp.int32, (SUBLANES, LANES), 1)
    listed = jnp.zeros((SUBLANES, LANES), jnp.int32)
    for s in range(ids.shape[0]):
        listed = jnp.where(lane == s, ids[s], listed)
    out_ref[2 * rows:2 * rows + SUBLANES, :] = listed.astype(jnp.float32)


def depth_payload(bathymetry, land_mask, block_ids):
    rows = bathymetry.shape[0]
    return pl.pallas_call(
        depth_kernel,
        in_specs=[HBM, HBM, HBM],
        out_specs=VMEM,
        out_shape=pltpu.VMEM((2 * rows + SUBLANES, LANES), jnp.float32),
        scratch_shapes=[
            pltpu.SMEM(block_ids.shape, jnp.int32),
            pltpu.VMEM(bathymetry.shape, jnp.float32),
            pltpu.VMEM(land_mask.shape, jnp.int32),
            pltpu.SemaphoreType.DMA((3,)),
        ],
        compiler_params=params(FIRST_VMEM),
        name="depth_payload",
    )(block_ids, bathymetry, land_mask)


def weights_kernel(slots, lon_count, lat_count, me_ref, ids_ref, near_ref, far_ref,
                   root_ref, centre_ref, around_ref, table_ref,
                   natural, all_ids, places_of, sems):
    half = lat_count // 2
    count = lon_count * half
    rows = (near_ref.shape[1] - SUBLANES) // 2
    strips, deep, tall = window_shape(slots, rows)
    column_count = 2 * lon_count
    parts = (near_ref, far_ref)
    copies = [
        pltpu.make_async_copy(
            parts[p].at[:, pl.ds(2 * rows, 1), :], all_ids.at[p], sems.at[p]
        )
        for p in range(2)
    ]
    for copy in copies:
        copy.start()
    natural[...] = jnp.zeros_like(natural)

    def load(lat, column):
        inside = (lat >= 0) & (lat < lat_count) & (column >= 0) & (column < column_count)
        lat_safe = jnp.clip(lat, 0, lat_count - 1)
        column_safe = jnp.clip(column, 0, column_count - 1)
        lon_xor = (column_safe >> 1) ^ me_ref[0]
        lat_xor = lat_safe ^ me_ref[1]
        place = lon_xor * half + (lat_xor >> 1)
        start = pl.multiple_of((column_safe & 1) * rows, SUBLANES)
        near = near_ref[place, pl.ds(start, rows), :]
        far = far_ref[place, pl.ds(start, rows), :]
        here = jnp.where((lat_xor & 1) == 0, near, far)
        return here * jnp.where(inside, 1.0, 0.0)

    lane = lax.broadcasted_iota(jnp.int32, (rows, LANES), 1)
    places = window_places(me_ref, ids_ref, slots, lon_count, lat_count)
    for w, (lat, column) in enumerate(places):
        blocks = [load(lat + down, column + right) for down, right in NEIGHBOURS]
        put_window(natural, w * tall, rows, blocks, lane)

    for copy in copies:
        copy.wait()

    def one_device(n, carry):
        for p in range(2):
            for s in range(slots):
                block = all_ids[p, n, 0, s].astype(jnp.int32)
                places_of[block] = (p * count + n) * slots + s
        return carry

    lax.fori_loop(0, count, one_device, 0)
    for w, (lat, column) in enumerate(places):
        for n, (down, right) in enumerate(NEIGHBOURS):
            lat_safe = jnp.clip(lat + down, 0, lat_count - 1)
            column_safe = jnp.clip(column + right, 0, column_count - 1)
            block = ((column_safe >> 1) * lat_count + lat_safe) * 2 + (column_safe & 1)
            table_ref[w * len(NEIGHBOURS) + n] = places_of[block]

    scale = chebyshev_sum(STEPS)[1]

    def put(i, x, values):
        start = i * PITCH + PAD + x
        root_ref[start:start + values.shape[0], :] = jnp.sqrt(values)
        around_ref[start:start + values.shape[0], :] = scale * values

    turn(natural, deep, put)
    zeros = jnp.zeros((PAD, LANES), jnp.float32)
    for i in range(deep):
        root_ref[i * PITCH:i * PITCH + PAD, :] = zeros
        root_ref[(i + 1) * PITCH - PAD:(i + 1) * PITCH, :] = zeros

    def work(chunk):
        here, above, below, at = strip_rows(root_ref, chunk, deep)
        out = []
        for i, a in enumerate(at):
            others = (rows_at(root_ref, a, 1) + rows_at(root_ref, a, -1)) + (above[i] + below[i])
            out.append((centre_ref, a, 2.0 - scale * here[i] * others))
        return out

    in_batches(range(WIDTH // SUBLANES), work)


def surface_weights(near, far, me, block_ids, rows, lon_count, lat_count):
    slots = block_ids.shape[0]
    assert near.shape[-1] == LANES
    strips, deep, tall = window_shape(slots, rows)
    shape = jax.ShapeDtypeStruct((deep * PITCH, LANES), jnp.float32)
    return pl.pallas_call(
        functools.partial(weights_kernel, slots, lon_count, lat_count),
        in_specs=[SMEM, SMEM, VMEM, VMEM],
        out_specs=[VMEM, VMEM, VMEM, SMEM],
        out_shape=[
            shape,
            shape,
            shape,
            jax.ShapeDtypeStruct(((slots + 2) * len(NEIGHBOURS),), jnp.int32),
        ],
        scratch_shapes=[
            pltpu.VMEM((2, LANES * deep, LANES), jnp.float32),
            pltpu.SMEM((2, near.shape[0], 1, LANES), jnp.float32),
            pltpu.SMEM((2 * lon_count * lat_count + 1,), jnp.int32),
            pltpu.SemaphoreType.DMA((2,)),
        ],
        compiler_params=params(WINDOW_VMEM),
        cost_estimate=pl.CostEstimate(
            flops=0, bytes_accessed=8 * MIB, transcendentals=0
        ),
        name="surface_weights",
    )(me, block_ids, near, far)


def solve_kernel(block_total, ids_ref, table_ref, coefs_ref, root_ref, centre_ref, around_ref,
                 levels_ref, bottom_ref, first_column_ref, last_column_ref, near_ref, far_ref,
                 corrected_ref, height_ref, sensitivity_ref,
                 natural, source, even, odd, extra, column, in_sems, out_sems):
    slots, comps, depth, rows, cols = column.shape
    strips, deep, tall = window_shape(slots, rows)

    middle = first_column_ref.shape[0]
    copies_in = [
        pltpu.make_async_copy(first_column_ref, column.at[pl.ds(0, middle)], in_sems.at[0]),
        pltpu.make_async_copy(
            last_column_ref, column.at[pl.ds(middle, slots - middle)], in_sems.at[1]
        ),
    ]
    for copy in copies_in:
        copy.start()

    count = near_ref.shape[0]

    def load(place):
        inner = place & (count - 1)
        return jnp.where(place < count, near_ref[inner], far_ref[inner])

    lane = lax.broadcasted_iota(jnp.int32, (rows, LANES), 1)
    for w in range(slots + 2):
        places = [table_ref[w * len(NEIGHBOURS) + n] for n in range(len(NEIGHBOURS))]
        put_window(natural, w * tall, rows, [load(place) for place in places], lane)

    coefs, step_scale = chebyshev_sum(STEPS)

    def put(i, x, values):
        start = i * PITCH + PAD + x
        stop = start + values.shape[0]
        root = root_ref[start:stop, :]
        values = jnp.where(root > 0.0, root * values, 0.0)
        source[start:stop, :] = values
        even[start:stop, :] = coefs[STEPS - 1] * values
        odd[start:stop, :] = jnp.zeros_like(values)

    zeros = jnp.zeros((PAD, LANES), jnp.float32)
    for ref in (even, odd):
        for i in range(deep):
            ref[i * PITCH:i * PITCH + PAD, :] = zeros
            ref[(i + 1) * PITCH - PAD:(i + 1) * PITCH, :] = zeros
    turn(natural, deep, put)

    chunks = WIDTH // SUBLANES

    def apply(current, target, coef, gain, m):
        def work(chunk):
            here, above, below, at = strip_rows(current, chunk, deep)
            out = []
            for i, a in enumerate(at):
                others = (rows_at(current, a, 1) + rows_at(current, a, -1)) + (
                    above[i] + below[i]
                )
                pushed = rows_at(centre_ref, a) * here[i] + rows_at(around_ref, a) * others
                if gain != 1.0:
                    pushed = gain * pushed
                kept = coef * rows_at(source, a) - rows_at(target, a)
                out.append((target, a, kept + pushed))
            return out

        in_batches(range(m // SUBLANES, chunks - m // SUBLANES), work)

    runs = []
    for m in range(1, STEPS - 1, 2):
        if runs and runs[-1][0] // SUBLANES == m // SUBLANES:
            runs[-1][1] += 1
        else:
            runs.append([m, 1])
    for first, pairs in runs:
        def two_steps(pair, carry, first=first):
            m = first + 2 * pair
            apply(even, odd, coefs_ref[m], 1.0, first)
            apply(odd, even, coefs_ref[m + 1], 1.0, first)
            return carry

        lax.fori_loop(0, pairs, two_steps, 0)
    apply(even, odd, coefs[0], 0.5, STEPS - 1)

    low = STEPS // SUBLANES - 1

    def one_height(chunk):
        out = []
        for i in range(deep):
            a = i * PITCH + PAD + chunk * SUBLANES
            root = rows_at(root_ref, a)
            out.append((extra, a, jnp.where(root > 0.0, rows_at(odd, a) / root, 0.0)))
        return out

    in_batches(range(low, chunks - low), one_height)

    def east_steps(chunk):
        here, _, _, at = strip_rows(extra, chunk, deep)
        return [(even, a, rows_at(extra, a, 1) - here[i]) for i, a in enumerate(at)]

    def sensitivity(chunk):
        here, above, below, at = strip_rows(extra, chunk, deep)
        root, root_above, root_below, _ = strip_rows(root_ref, chunk, deep)
        out = []
        for i, a in enumerate(at):
            east_step = rows_at(extra, a, 1) - here[i]
            west_step = here[i] - rows_at(extra, a, -1)
            south_step = below[i] - here[i]
            north_step = here[i] - above[i]
            energy = root[i] * (
                (rows_at(root_ref, a, 1) * east_step * east_step
                 + rows_at(root_ref, a, -1) * west_step * west_step)
                + (root_below[i] * south_step * south_step
                   + root_above[i] * north_step * north_step)
            )
            scaled = rows_at(around_ref, a) * (1.0 / step_scale)
            out.append((source, a, 0.25 * energy / jnp.maximum(scaled, 0.25)))
        return out

    middle_chunks = range(low + 1, chunks - low - 1)

    def turn_back(ref, tile):
        for i in range(deep):
            start = i * PITCH + PAD + STEPS
            natural[tile, pl.ds(i, LANES, stride=deep), :] = ref[start:start + LANES, :].T

    def cut(tile, w, shift=0):
        return natural[tile, pl.ds(w * tall + STEPS + shift, rows), :]

    def copy_out(b, c):
        return pltpu.make_async_copy(column.at[b, c], corrected_ref.at[b, c], out_sems.at[b, c])

    def correct(b, c, step):
        levels = levels_ref[b] * jnp.where(ids_ref[b] < block_total, 1, 0)
        push = pressure_gain * step
        lowest = bottom_ref[b, c] - push

        late = []
        for low in range(0, depth, CHUNK):
            batch = []
            for k in range(low, min(low + CHUNK, depth)):
                value = jnp.where(levels == k + 1, lowest, column[b, c, k] - push)
                batch.append((k, jnp.where(levels > k, value, 0.0)))
            for k, value in late:
                column[b, c, k] = value
            late = batch
        for k, value in late:
            column[b, c, k] = value
        copy_out(b, c).start()

    def correct_north(b, carry):
        correct(b, 1, cut(1, b, 1) - cut(1, b))
        return carry

    def correct_east(b, carry):
        correct(b, 0, cut(0, b))
        return carry

    turn_back(extra, 1)
    for copy in copies_in:
        copy.wait()
    lax.fori_loop(0, slots, correct_north, 0)
    in_batches(middle_chunks, east_steps)
    turn_back(even, 0)
    lax.fori_loop(0, slots, correct_east, 0)
    in_batches(middle_chunks, sensitivity)
    turn_back(source, 0)
    for h in range(2):
        height_ref[:, h * LANES:(h + 1) * LANES] = cut(1, slots + h)
        sensitivity_ref[:, h * LANES:(h + 1) * LANES] = cut(0, slots + h)

    for b in range(slots):
        for c in range(comps):
            copy_out(b, c).wait()


def surface_solve(near, far, weights, block_ids, level_count, bottom, columns, block_total):
    root, centre, around, table = weights
    comps, depth, rows, cols = columns[0].shape[1:]
    slots = level_count.shape[0]
    assert comps == 2
    full = (slots, comps, depth, rows, cols)
    deep = window_shape(slots, rows)[1]
    turned = pltpu.VMEM(root.shape, jnp.float32)
    coefs = jnp.array(chebyshev_sum(STEPS)[0][::-1], jnp.float32)
    return pl.pallas_call(
        functools.partial(solve_kernel, block_total),
        in_specs=[SMEM, SMEM, SMEM] + [VMEM] * 5 + [HBM] * 2 + [VMEM] * 2,
        out_specs=[HBM, VMEM, VMEM],
        out_shape=[
            jax.ShapeDtypeStruct(full, jnp.float32),
            jax.ShapeDtypeStruct((rows, 2 * cols), jnp.float32),
            jax.ShapeDtypeStruct((rows, 2 * cols), jnp.float32),
        ],
        scratch_shapes=[
            pltpu.VMEM((2, LANES * deep, LANES), jnp.float32),
            turned,
            turned,
            turned,
            turned,
            pltpu.VMEM(full, jnp.float32),
            pltpu.SemaphoreType.DMA((2,)),
            pltpu.SemaphoreType.DMA((slots, comps)),
        ],
        compiler_params=params(SOLVE_VMEM),
        cost_estimate=pl.CostEstimate(
            flops=9 * STEPS * root.size, bytes_accessed=16 * root.size, transcendentals=0
        ),
        name="surface_solve",
    )(block_ids, table, coefs, root, centre, around, level_count, bottom, *columns, near, far)


def stack_kernel(parts, *refs):
    out_ref = refs[-1]
    for p in range(parts):
        out_ref[p] = refs[p][...]


def stack_after(parts, *tokens):
    return pl.pallas_call(
        functools.partial(stack_kernel, len(parts)),
        in_specs=[VMEM] * len(parts) + [ANYWHERE] * len(tokens),
        out_specs=VMEM,
        out_shape=jax.ShapeDtypeStruct((len(parts),) + parts[0].shape, jnp.float32),
        compiler_params=params(WINDOW_VMEM),
        name="stack_after",
    )(*parts, *tokens)


FIRST_SLOTS = 1


def swap(values, axis, mask):
    count = lax.axis_size(axis)
    return lax.ppermute(values, axis, [(i, i ^ mask) for i in range(count)])


def per_device(adjoint_vel, velocity, drag_coef, level_count, block_ids, bathymetry, land_mask):
    slots = block_ids.shape[0]
    rows, cols = drag_coef.shape[1:]
    lon_count = lax.axis_size("gx")
    lat_count = lax.axis_size("gy")
    half = lat_count // 2
    block_total = 2 * lon_count * lat_count
    me = jnp.stack([lax.axis_index("gx"), lax.axis_index("gy")]).astype(jnp.int32)

    depths = depth_payload(bathymetry, land_mask, block_ids)
    depth_parts = [depths] + [swap(depths, "gy", 2 * m) for m in range(1, half)]
    forcing = column_forcing(adjoint_vel, level_count)

    parts = [forcing] + [swap(forcing, "gy", 2 * m) for m in range(1, half)]
    near_depths = stack_after(depth_parts, forcing)
    near_depths = [near_depths] + [swap(near_depths, "gx", m) for m in range(1, lon_count)]
    columns = (adjoint_vel, velocity, drag_coef, level_count, block_ids)
    first_column, *first_rest = column_mixing(*columns, forcing, block_total, 0, FIRST_SLOTS)
    line = stack_after(parts, first_rest[0])

    near = [line] + [swap(line, "gx", m) for m in range(1, lon_count)]
    near_depths = stack_after(near_depths, line)
    near_depths = near_depths.reshape((lon_count * half,) + depths.shape)
    far_depths = swap(near_depths, "gy", 1)
    last_column, bottom, drag_gradient = column_mixing(
        *columns, line, block_total, FIRST_SLOTS, slots, first_rest
    )
    weights = surface_weights(
        near_depths, far_depths, me, block_ids, rows, lon_count, lat_count
    )

    near = stack_after(near, bottom, far_depths)
    far = swap(near, "gy", 1)

    corrected, height, sensitivity = surface_solve(
        near.reshape((-1, rows, cols)), far.reshape((-1, rows, cols)), weights,
        block_ids, level_count, bottom, (first_column, last_column), block_total,
    )
    return corrected, drag_gradient, height, sensitivity


def solution(mesh):
    in_specs = (
        P(("gx", "gy"), None, None, None, None),
        P(("gx", "gy"), None, None, None, None),
        P(("gx", "gy"), None, None),
        P(("gx", "gy"), None, None),
        P(("gx", "gy")),
        P("gy", "gx"),
        P("gy", "gx"),
    )
    out_specs = (
        P(("gx", "gy"), None, None, None, None),
        P(("gx", "gy"), None, None),
        P("gy", "gx"),
        P("gy", "gx"),
    )
    return jax.shard_map(
        per_device, mesh=mesh, in_specs=in_specs, out_specs=out_specs, check_vma=False
    )
```
